32 devices in a mesh: patch: 4 (over y, x), member: 8 (over z, core).
Axes of the slice: x: 2, y: 2, z: 4, core: 2. Of those that a mesh axis runs over, the one named last changes fastest.
Arguments:
- init_field: float32 [1024, 32, 256], P('member', 'patch'), may hold values from -6 to 6
- flow_fields: float32 [4, 32, 256], P(None, 'patch'), may hold values from -6 to 6, as said below
- emission: float32 [1024], P('member'), may hold values from 0.5 to 2
- observed_cell: int32 [32, 512], P(('patch', 'member')), may hold values from 0 to 767
- observed_count: int32 [32], P(('patch', 'member')), may hold values from 1 to 512, as said below
- observed_value: float32 [32, 512], P(('patch', 'member')), may hold values from -6 to 6
- observed_scale: float32 [32, 512], P(('patch', 'member')), may hold values from 0.1 to 10
Outputs:
- analysis: float32 [1024, 32, 256], P('member', 'patch')
The draws below stay inside these ranges and needn't reach their ends.
Inputs may be any that keep to these rules, and one draw needn't show every extreme that they name: `observed_cell`: A position is (row offset + 1) * 256 + column with row offset -1, 0 or 1 from the region's row; slots from observed_count on are not read. `observed_count`: some region has 512 observations and some region has one. `flow_fields`: rows 0 and 1 lie in -0.5 to 0.5, row 2 in 0.02 to 0.5.
All inputs are finite; a program needn't handle non-finite values.
Results may differ from the reference program's by a relative error of at most 0.0012.
Values sent between devices are 32-bit elements; how exact they have to be, the bound alone decides.
No kernel may reach another device: no remote copies, remote signals or barrier semaphores. Data moves between devices by JAX's collectives and lax.ppermute only.
A program may use at most 64 MiB of HBM per device.

```python
import math
import jax
import jax.numpy as jnp
from jax import lax

ENSEMBLE = 1024
NY = 256
SLOTS = 512
STEPS = 2
NX = 32


def draw_flow_fields(key, part):
    keys = jax.random.split(jax.random.fold_in(key, 7), 4)
    shape = (NX, NY)
    row_flow = jax.random.uniform(keys[0], shape, jnp.float32, -0.5, 0.5)
    col_flow = jax.random.uniform(keys[1], shape, jnp.float32, -0.5, 0.5)
    decay_rate = jnp.exp(jax.random.uniform(keys[2], shape, jnp.float32, math.log(0.02), math.log(0.5)))
    source = jax.random.normal(keys[3], shape, jnp.float32)
    row_flow = jnp.clip(row_flow, -0.5, 0.5)
    col_flow = jnp.clip(col_flow, -0.5, 0.5)
    decay_rate = jnp.clip(decay_rate, 0.02, 0.5)
    source = jnp.clip(source, -6.0, 6.0)
    return jnp.stack([row_flow, col_flow, decay_rate, source]).astype(jnp.float32)


def draw_observed_count(key, part):
    first, second = jax.random.split(jax.random.fold_in(key, 11))
    counts = jax.random.randint(first, (NX,), 1, SLOTS + 1)
    order = jax.random.permutation(second, NX)
    counts = counts.at[order[0]].set(SLOTS)
    counts = counts.at[order[1]].set(1)
    return counts.astype(jnp.int32)


def with_ends(entries, rng, low, largest):
    longest = entries.shape.index(max(entries.shape))
    spots = []
    for shift in (0, 1):
        where = [jax.random.randint(jax.random.fold_in(rng, axis), (), 0, length) for axis, length in enumerate(entries.shape)]
        where[longest] = (where[longest] + shift) % entries.shape[longest]
        spots.append(tuple(where))
    return entries.at[spots[0]].set(low).at[spots[1]].set(largest)


def level_of(rng, extent, pieces, least, top_value):
    gain, own = 1.0, jax.random.fold_in(rng, 6)
    for dim, shards_of in pieces:
        heights = jnp.exp(jax.random.uniform(jax.random.fold_in(own, dim), (shards_of,), jnp.float32, least / len(pieces), top_value / len(pieces)))
        gain = gain * jnp.repeat(heights, extent[dim] // shards_of).reshape([-1 if axis == dim else 1 for axis in range(len(extent))])
    return gain


def noise(stream_key, dims, deviation, limit, shards=(), held_as=jnp.bfloat16):
    factor_of = level_of(stream_key, dims, shards, -0.22, 0.18) if shards else 1.0
    drawn = jax.random.normal(stream_key, dims, jnp.float32) * deviation * factor_of
    return jnp.minimum(jnp.maximum(drawn, -limit), limit).astype(held_as)


def setup_inputs(seed: int = 0) -> dict:
    key_of = jax.random.split(jax.random.key(seed), 8)
    return {
        "init_field": noise(key_of[0], (ENSEMBLE, NX, NY), 1.0, 6.0, ((0, 8), (1, 4)), jnp.float32),
        "flow_fields": draw_flow_fields(jax.random.fold_in(key_of[7], 71), 0),
        "emission": jnp.clip(jnp.exp(math.log(2.0) - 1.3862944 * jax.random.uniform(key_of[2], (ENSEMBLE,), jnp.float32) ** level_of(key_of[2], (ENSEMBLE,), ((0, 8),), -0.2, 0.2)), 0.5, 2.0),
        "observed_cell": with_ends(jax.random.randint(key_of[3], (NX, SLOTS), 0, 3 * NY), jax.random.fold_in(key_of[3], 1), 0, (3 * NY) - 1).astype(jnp.int32),
        "observed_count": draw_observed_count(jax.random.fold_in(key_of[7], 71), 0),
        "observed_value": noise(key_of[5], (NX, SLOTS), 1.0, 6.0, ((0, 32),), jnp.float32),
        "observed_scale": jnp.clip(jnp.exp(math.log(10.0) - 4.6051702 * jax.random.uniform(key_of[6], (NX, SLOTS), jnp.float32) ** level_of(key_of[6], (NX, SLOTS), ((0, 32),), -0.2, 0.2)), 0.1, 10.0),
    }


HIGH = lax.Precision.HIGHEST

def advance(extended, flow_piece, emission):
    field = extended[:, 1:-1, :]
    behind_rows = extended[:, :-2, :]
    ahead_rows = extended[:, 2:, :]
    behind_cols = jnp.roll(field, 1, axis=2)
    ahead_cols = jnp.roll(field, -1, axis=2)
    row_flow = flow_piece[0]
    col_flow = flow_piece[1]
    advected = field - jnp.maximum(row_flow, 0.0) * (field - behind_rows) - jnp.minimum(row_flow, 0.0) * (ahead_rows - field) - jnp.maximum(col_flow, 0.0) * (field - behind_cols) - jnp.minimum(col_flow, 0.0) * (ahead_cols - field)
    return (1.0 - flow_piece[2]) * advected + emission[:, None, None] * flow_piece[3]

def analyse(window, cells, count, values, scales):
    members = window.shape[0]
    width = window.shape[1] // 3
    root = math.sqrt(members - 1)
    predicted = jnp.take(window, cells, axis=1)
    active_slot = (jnp.arange(cells.shape[0], dtype=jnp.int32) < count).astype(jnp.float32)
    slot_weight = active_slot * scales
    predicted_mean = lax.optimization_barrier(jnp.mean(predicted, axis=0))
    spread = (predicted - predicted_mean) * (slot_weight / root)
    innovation = slot_weight * (values - predicted_mean)
    own_row = window[:, width:2 * width]
    mean_row = lax.optimization_barrier(jnp.mean(own_row, axis=0))
    anomaly = own_row - mean_row
    forcing = jnp.dot(spread, innovation, precision=HIGH) / root
    weight_matrix = jnp.eye(members, dtype=jnp.float32) + jnp.dot(spread, spread.T, precision=HIGH)
    factor = jnp.linalg.cholesky(weight_matrix)
    solved = jax.scipy.linalg.cho_solve((factor, True), anomaly)
    weights = jax.scipy.linalg.cho_solve((factor, True), forcing)
    offset_term = jnp.dot(weights, anomaly, precision=HIGH)
    return mean_row + 0.5 * anomaly + 0.5 * solved + offset_term

def reference(init_field, flow_fields, emission, observed_cell, observed_count, observed_value, observed_scale):
    field = init_field
    for step_index in range(STEPS):
        padded = jnp.pad(field, ((0, 0), (1, 1), (0, 0)))
        field = advance(padded, flow_fields, emission)
    bordered = jnp.pad(field, ((0, 0), (1, 1), (0, 0)))

    def region(inputs):
        index, cells, count, values, scales = inputs
        window = lax.dynamic_slice_in_dim(bordered, index, 3, 1)
        window = window.reshape(ENSEMBLE, 3 * NY)
        return analyse(window, cells, count, values, scales)
    result = lax.map(region, (jnp.arange(NX, dtype=jnp.int32), observed_cell, observed_count, observed_value, observed_scale))
    return jnp.transpose(result, (1, 0, 2))
```

```python
import functools
import math

import jax
import jax.numpy as jnp
from jax import lax
from jax.experimental import pallas as pl
from jax.experimental.pallas import tpu as pltpu
from jax.sharding import PartitionSpec as P

STEPS = 2
COARSE = 0.06
DONE = 1e-4
LARGE = 2e4
F32 = jnp.float32
BF16 = jnp.bfloat16


def padded(cells, sides, width):
    for axis, dim in sides:
        count = lax.axis_size(axis)
        ends = count - 1
        head = lax.slice_in_dim(cells, 0, width, axis=dim)
        tail = lax.slice_in_dim(cells, cells.shape[dim] - width, cells.shape[dim], axis=dim)
        cells = jnp.concatenate(
            [
                lax.ppermute(tail, axis, [(i, (i + 1) % count) for i in range(ends)]),
                cells,
                lax.ppermute(head, axis, [((i + 1) % count, i) for i in range(ends)]),
            ],
            axis=dim,
        )
    return cells


def advance(extended, flow_piece, emission):
    field = extended[1:-1]
    behind_rows = extended[:-2]
    ahead_rows = extended[2:]
    behind_cols = jnp.roll(field, 1, axis=2)
    ahead_cols = jnp.roll(field, -1, axis=2)
    row_flow = flow_piece[0][:, None, :]
    col_flow = flow_piece[1][:, None, :]
    advected = (
        field
        - jnp.maximum(row_flow, 0.0) * (field - behind_rows)
        - jnp.minimum(row_flow, 0.0) * (ahead_rows - field)
        - jnp.maximum(col_flow, 0.0) * (field - behind_cols)
        - jnp.minimum(col_flow, 0.0) * (ahead_cols - field)
    )
    return (1.0 - flow_piece[2][:, None, :]) * advected + emission[None, :, None] * flow_piece[3][:, None, :]


def pieces(x, count):
    parts = []
    for _ in range(count - 1):
        part = x.astype(BF16)
        parts.append(part)
        x = x - part.astype(F32)
    return parts + [x.astype(BF16)]


def dot(a, b):
    return lax.dot_general(a, b, (((1,), (0,)), ((), ())), preferred_element_type=F32)


def dot_t(a, b):
    return lax.dot_general(a, b, (((0,), (0,)), ((), ())), preferred_element_type=F32)


def product(a, b):
    total = None
    for i, left in enumerate(a):
        for j, right in enumerate(b):
            if i + j < max(len(a), len(b)):
                term = dot(left, right)
                total = term if total is None else total + term
    return total


def region_kernel(
    up_ref, own_ref, down_ref, cells_ref, count_ref, values_ref, scales_ref, out_ref,
    high_ref, low_ref, spread_high, spread_low, factor, answer,
):
    members, width = own_ref.shape
    slots = cells_ref.shape[1]
    root = math.sqrt(members - 1)
    step = 256

    means = []
    for place, row in enumerate((up_ref, own_ref, down_ref)):
        mean = jnp.sum(row[...], axis=0, keepdims=True) * (1.0 / members)
        means.append(mean)
        for first in range(0, members, step):
            at = (pl.ds(first, step), pl.ds(place * width, width))
            high, low = pieces(row[pl.ds(first, step), :] - mean, 2)
            high_ref[at] = high
            low_ref[at] = low
    chosen = (
        lax.broadcasted_iota(jnp.int32, (3 * width, slots), 0) == cells_ref[...]
    ).astype(F32).astype(BF16)
    active = lax.broadcasted_iota(jnp.int32, (1, slots), 1) < count_ref[0]
    slot_weight = jnp.where(active, scales_ref[...], 0.0)
    scale = slot_weight * (1.0 / root)
    mean_parts = pieces(jnp.broadcast_to(jnp.concatenate(means, axis=1), (8, 3 * width)), 3)
    predicted_mean = (dot(mean_parts[0], chosen) + (dot(mean_parts[1], chosen) + dot(mean_parts[2], chosen)))[:1]
    innovation = slot_weight * (values_ref[...] - predicted_mean)
    for first in range(0, members, step):
        rows = pl.ds(first, step)
        spread = (dot(high_ref[rows, :], chosen) + dot(low_ref[rows, :], chosen)) * scale
        high, low = pieces(spread, 2)
        spread_high[rows, :] = high
        spread_low[rows, :] = low

    high, low = spread_high[...], spread_low[...]
    middle = pl.ds(width, width)
    eye = lax.broadcasted_iota(jnp.int32, (slots, slots), 0) == lax.broadcasted_iota(
        jnp.int32, (slots, slots), 1
    )
    cross = dot_t(high, low)
    matrix = dot_t(high, high) + (cross + cross.T) + jnp.where(eye, 1.0, 0.0)
    right = dot_t(high, high_ref[:, middle]) + (dot_t(high, low_ref[:, middle]) + dot_t(low, high_ref[:, middle]))

    norm = jnp.max(jnp.sum(jnp.abs(matrix), axis=0, keepdims=True))
    start = 2.0 / (1.0 + norm)
    factor[...] = matrix * start
    answer[...] = right * start

    def refine(bound, count):
        gain = 2.0 / (2.0 - bound * bound)
        parts = pieces(factor[...], count)
        answer[...] = gain * (2.0 * answer[...] - product(parts, pieces(answer[...], count)))
        factor[...] = gain * (2.0 * factor[...] - product(parts, parts))
        return bound * bound / (2.0 - bound * bound)

    def finish(bound):
        gain = 2.0 / (2.0 - bound * bound)
        rest = factor[...].astype(BF16)
        answer[...] = gain * (answer[...] + dot(rest, answer[...].astype(BF16)))
        factor[...] = gain * (dot(rest, rest) - jnp.where(eye, 0.5 * bound * bound, 0.0))
        return bound * bound / (2.0 - bound * bound)

    bound = 1.0 - start
    bound = lax.while_loop(
        lambda b: jnp.logical_and(b > COARSE, norm > LARGE), lambda b: refine(b, 3), bound
    )
    bound = lax.while_loop(lambda b: b > COARSE, lambda b: refine(b, 2), bound)
    factor[...] = jnp.where(eye, 1.0, 0.0) - factor[...]
    lax.while_loop(lambda b: b > DONE, finish, bound)

    solved = answer[...]
    solved_parts = pieces(solved, 2)
    innovation_parts = pieces(jnp.broadcast_to(innovation * (1.0 / root), (8, slots)), 3)
    shift = product(innovation_parts, pieces(solved, 3))[:1]
    half = [part * jnp.asarray(-0.5, BF16) for part in solved_parts]
    for first in range(0, members, step):
        rows = pl.ds(first, step)
        moved = product([spread_high[rows, :], spread_low[rows, :]], half)
        out_ref[rows, :] = own_ref[rows, :] + shift + moved


def analyse(up, own, down, cells, count, values, scales):
    members, width = own.shape
    slots = cells.shape[1]
    vmem = pl.BlockSpec(memory_space=pltpu.VMEM)
    return pl.pallas_call(
        region_kernel,
        out_shape=jax.ShapeDtypeStruct((members, width), F32),
        in_specs=[vmem] * 4 + [pl.BlockSpec(memory_space=pltpu.SMEM)] + [vmem] * 2,
        out_specs=vmem,
        scratch_shapes=[
            pltpu.VMEM((members, 3 * width), BF16),
            pltpu.VMEM((members, 3 * width), BF16),
            pltpu.VMEM((members, slots), BF16),
            pltpu.VMEM((members, slots), BF16),
            pltpu.VMEM((slots, slots), F32),
            pltpu.VMEM((slots, width), F32),
        ],
        compiler_params=pltpu.CompilerParams(vmem_limit_bytes=48 * 1024 * 1024),
        name="region",
    )(up, own, down, cells, count, values, scales)


def per_device(
    init_field, flow_fields, emission, observed_cell, observed_count, observed_value, observed_scale
):
    rows = init_field.shape[1]
    width = init_field.shape[2]
    field = jnp.transpose(init_field, (1, 0, 2))
    extended = padded(field, (("patch", 0),), STEPS)
    flow_wide = padded(flow_fields, (("patch", 1),), STEPS - 1)
    for step_index in range(STEPS):
        margin = STEPS - 1 - step_index
        extended = advance(
            extended, flow_wide[:, step_index : step_index + rows + 2 * margin, :], emission
        )
    regrouped = lax.all_to_all(extended, "member", split_axis=0, concat_axis=0, tiled=True)
    own = regrouped.reshape(-1, width)
    count = lax.axis_size("patch") * lax.axis_size("member")
    axes = ("patch", "member")
    up = lax.ppermute(own, axes, [(i, i + 1) for i in range(count - 1)])
    down = lax.ppermute(own, axes, [(i + 1, i) for i in range(count - 1)])
    analysed = analyse(up, own, down, observed_cell, observed_count, observed_value, observed_scale)
    returned = lax.all_to_all(
        analysed.reshape(rows, -1, width), "member", split_axis=0, concat_axis=0, tiled=True
    )
    return jnp.transpose(returned, (1, 0, 2))


def solution(mesh):
    return jax.shard_map(
        per_device,
        mesh=mesh,
        in_specs=(
            P("member", "patch", None),
            P(None, "patch", None),
            P("member"),
            P(("patch", "member"), None),
            P(("patch", "member")),
            P(("patch", "member"), None),
            P(("patch", "member"), None),
        ),
        out_specs=P("member", "patch", None),
        check_vma=False,
    )
```

```python
import functools
import math

import jax
import jax.numpy as jnp
from jax import lax
from jax.experimental import pallas as pl
from jax.experimental.pallas import tpu as pltpu
from jax.sharding import PartitionSpec as P

STEPS = 2
COARSE = 0.06
DONE = 1e-4
LARGE = 2e4
PART = 256
F32 = jnp.float32
BF16 = jnp.bfloat16


def pack_kernel(field_ref, flow_ref, tail_ref, head_ref):
    members, rows, width = field_ref.shape
    for out_ref, first, edge in ((tail_ref, rows - STEPS, rows - 1), (head_ref, 0, 0)):
        for place in range(STEPS):
            out_ref[pl.ds(place * members, members), :] = field_ref[:, first + place, :]
        out_ref[pl.ds(STEPS * members, 8), :] = jnp.concatenate([flow_ref[:, edge, :]] * 2, axis=0)


def forecast_kernel(field_ref, flow_ref, emission_ref, before_ref, after_ref, out_ref, wide_ref):
    members, rows, width = field_ref.shape
    diagonal = lax.broadcasted_iota(jnp.int32, (members, members), 0) == lax.broadcasted_iota(
        jnp.int32, (members, members), 1
    )
    emission = jnp.sum(jnp.where(diagonal, emission_ref[...], 0.0), axis=1, keepdims=True)

    def flow_row(row):
        if row < 0:
            return before_ref[pl.ds(STEPS * members, 4), :]
        if row >= rows:
            return after_ref[pl.ds(STEPS * members, 4), :]
        return flow_ref[:, row, :]

    def start_row(row):
        if row < 0:
            return before_ref[pl.ds((row + STEPS) * members, members), :]
        if row >= rows:
            return after_ref[pl.ds((row - rows) * members, members), :]
        return field_ref[:, row, :]

    def advance(row, behind, field, ahead):
        flow = flow_row(row)
        row_flow, col_flow, kept, source = flow[0:1], flow[1:2], 1.0 - flow[2:3], flow[3:4]
        from_behind, from_ahead = jnp.maximum(row_flow, 0.0), -jnp.minimum(row_flow, 0.0)
        from_left, from_right = jnp.maximum(col_flow, 0.0), -jnp.minimum(col_flow, 0.0)
        stays = 1.0 - from_behind - from_ahead - from_left - from_right
        return (
            (kept * stays) * field
            + (kept * from_behind) * behind
            + (kept * from_ahead) * ahead
            + (kept * from_left) * pltpu.roll(field, 1, 1)
            + (kept * from_right) * pltpu.roll(field, width - 1, 1)
            + emission * source
        )

    margin = STEPS - 1
    for row in range(-margin, rows + margin):
        wide_ref[row + margin] = advance(row, start_row(row - 1), start_row(row), start_row(row + 1))
    for row in range(rows):
        place = row + margin
        out_ref[row] = advance(row, wide_ref[place - 1], wide_ref[place], wide_ref[place + 1])


def unpack_kernel(rows_ref, out_ref):
    for row in range(rows_ref.shape[0]):
        out_ref[:, row, :] = rows_ref[row]


def pieces(x, count):
    parts = []
    for _ in range(count - 1):
        part = x.astype(BF16)
        parts.append(part)
        x = x - part.astype(F32)
    return parts + [x.astype(BF16)]


def dot(a, b):
    return lax.dot_general(a, b, (((1,), (0,)), ((), ())), preferred_element_type=F32)


def dot_t(a, b):
    return lax.dot_general(a, b, (((0,), (0,)), ((), ())), preferred_element_type=F32)


def product(a, b):
    total = None
    for i, left in enumerate(a):
        for j, right in enumerate(b):
            if i + j < max(len(a), len(b)):
                term = dot(left, right)
                total = term if total is None else total + term
    return total


def region_kernel(
    turned_ref, up_ref, own_ref, down_ref, mine_ref, other_ref, out_ref,
    high_ref, low_ref, spread_high, spread_low, factor, answer,
):
    blocks, step, width = own_ref.shape
    members = blocks * step
    slots = mine_ref.shape[1]
    root = math.sqrt(members - 1)

    def at_block(which, block):
        return block + turned_ref[which] * (blocks - 1 - 2 * block)

    observed = jnp.where(turned_ref[1] == 1, other_ref[...], mine_ref[...])
    cells, values, scales, count = (observed[i : i + 1] for i in range(4))
    means = []
    for place, row in enumerate((up_ref, own_ref, down_ref)):
        mean = jnp.sum(jnp.sum(row[...], axis=0), axis=0, keepdims=True) * (1.0 / members)
        means.append(mean)
        for block in range(blocks):
            at = (pl.ds(block * step, step), pl.ds(place * width, width))
            high, low = pieces(row[at_block(place, block)] - mean, 2)
            high_ref[at] = high
            low_ref[at] = low
    chosen = (
        lax.broadcasted_iota(jnp.int32, (3 * width, slots), 0) == cells.astype(jnp.int32)
    ).astype(F32).astype(BF16)
    active = lax.broadcasted_iota(jnp.int32, (1, slots), 1) < count.astype(jnp.int32)
    slot_weight = jnp.where(active, scales, 0.0)
    scale = slot_weight * (1.0 / root)
    mean_parts = pieces(jnp.broadcast_to(jnp.concatenate(means, axis=1), (8, 3 * width)), 3)
    predicted_mean = (dot(mean_parts[0], chosen) + (dot(mean_parts[1], chosen) + dot(mean_parts[2], chosen)))[:1]
    innovation = slot_weight * (values - predicted_mean)
    for first in range(0, members, PART):
        rows = pl.ds(first, PART)
        spread = (dot(high_ref[rows, :], chosen) + dot(low_ref[rows, :], chosen)) * scale
        high, low = pieces(spread, 2)
        spread_high[rows, :] = high
        spread_low[rows, :] = low

    high, low = spread_high[...], spread_low[...]
    middle = pl.ds(width, width)
    eye = lax.broadcasted_iota(jnp.int32, (slots, slots), 0) == lax.broadcasted_iota(
        jnp.int32, (slots, slots), 1
    )
    cross = dot_t(high, low)
    matrix = dot_t(high, high) + (cross + cross.T) + jnp.where(eye, 1.0, 0.0)
    right = dot_t(high, high_ref[:, middle]) + (dot_t(high, low_ref[:, middle]) + dot_t(low, high_ref[:, middle]))

    norm = jnp.max(jnp.sum(jnp.abs(matrix), axis=0, keepdims=True))
    start = 2.0 / (1.0 + norm)
    factor[...] = matrix * start
    answer[...] = right * start

    def refine(bound, count):
        gain = 2.0 / (2.0 - bound * bound)
        parts = pieces(factor[...], count)
        answer[...] = gain * (2.0 * answer[...] - product(parts, pieces(answer[...], count)))
        factor[...] = gain * (2.0 * factor[...] - product(parts, parts))
        return bound * bound / (2.0 - bound * bound)

    def finish(bound):
        gain = 2.0 / (2.0 - bound * bound)
        rest = factor[...].astype(BF16)
        answer[...] = gain * (answer[...] + dot(rest, answer[...].astype(BF16)))
        factor[...] = gain * (dot(rest, rest) - jnp.where(eye, 0.5 * bound * bound, 0.0))
        return bound * bound / (2.0 - bound * bound)

    bound = 1.0 - start
    bound = lax.while_loop(
        lambda b: jnp.logical_and(b > COARSE, norm > LARGE), lambda b: refine(b, 3), bound
    )
    bound = lax.while_loop(lambda b: b > COARSE, lambda b: refine(b, 2), bound)
    factor[...] = jnp.where(eye, 1.0, 0.0) - factor[...]
    lax.while_loop(lambda b: b > DONE, finish, bound)

    solved = answer[...]
    solved_parts = pieces(solved, 2)
    innovation_parts = pieces(jnp.broadcast_to(innovation * (1.0 / root), (8, slots)), 3)
    shift = product(innovation_parts, pieces(solved, 3))[:1]
    half = [part * jnp.asarray(-0.5, BF16) for part in solved_parts]
    for block in range(blocks):
        rows = pl.ds(block * step, step)
        moved = product([spread_high[rows, :], spread_low[rows, :]], half)
        at = at_block(1, block)
        out_ref[at] = own_ref[at] + shift + moved


VMEM = pl.BlockSpec(memory_space=pltpu.VMEM)
LIMIT = pltpu.CompilerParams(vmem_limit_bytes=48 * 1024 * 1024)


def analyse(turned, up, own, down, mine, other):
    blocks, step, width = own.shape
    members = blocks * step
    slots = mine.shape[1]
    return pl.pallas_call(
        region_kernel,
        out_shape=jax.ShapeDtypeStruct(own.shape, F32),
        in_specs=[pl.BlockSpec(memory_space=pltpu.SMEM)] + [VMEM] * 5,
        out_specs=VMEM,
        scratch_shapes=[
            pltpu.VMEM((members, 3 * width), BF16),
            pltpu.VMEM((members, 3 * width), BF16),
            pltpu.VMEM((members, slots), BF16),
            pltpu.VMEM((members, slots), BF16),
            pltpu.VMEM((slots, slots), F32),
            pltpu.VMEM((slots, width), F32),
        ],
        compiler_params=LIMIT,
        name="region",
    )(turned, up, own, down, mine, other)


def per_device(
    init_field, flow_fields, emission, observed_cell, observed_count, observed_value, observed_scale
):
    members, rows, width = init_field.shape
    patches, lanes = lax.axis_size("patch"), lax.axis_size("member")
    axes = ("patch", "member")
    count = patches * lanes

    edge = jax.ShapeDtypeStruct((STEPS * members + 8, width), F32)
    tail, head = pl.pallas_call(
        pack_kernel, out_shape=(edge, edge), in_specs=[VMEM] * 2, out_specs=(VMEM, VMEM),
        compiler_params=LIMIT, name="pack",
    )(init_field, flow_fields)
    before = lax.ppermute(tail, "patch", [(i, i + 1) for i in range(patches - 1)])
    after = lax.ppermute(head, "patch", [(i + 1, i) for i in range(patches - 1)])

    def holder(region):
        patch, row = divmod(region, lanes)
        return patch * lanes + (lanes - 1 - row if patch % 2 else row)

    groups = [[holder(patch * lanes + row) for row in range(lanes)] for patch in range(patches)]
    mine = jnp.concatenate(
        [
            observed_cell.astype(F32),
            observed_value,
            observed_scale,
            jnp.broadcast_to(observed_count.astype(F32)[:, None], observed_cell.shape),
        ]
        * 2,
        axis=0,
    )
    other = lax.ppermute(
        mine, axes, [(g, holder(g)) for g in range(count) if (g // lanes) % 2]
    )

    forecast = pl.pallas_call(
        forecast_kernel, out_shape=jax.ShapeDtypeStruct((rows, members, width), F32),
        in_specs=[VMEM] * 5, out_specs=VMEM,
        scratch_shapes=[pltpu.VMEM((rows + 2 * (STEPS - 1), members, width), F32)],
        compiler_params=LIMIT, name="forecast",
    )(init_field, flow_fields, emission[None, :], before, after)
    own = lax.all_to_all(
        forecast, axes, split_axis=0, concat_axis=0, tiled=True, axis_index_groups=groups
    )
    up = lax.ppermute(own, axes, [(holder(g), holder(g + 1)) for g in range(count - 1)])
    down = lax.ppermute(own, axes, [(holder(g + 1), holder(g)) for g in range(count - 1)])
    patch, lane = lax.axis_index("patch"), lax.axis_index("member")
    region = patch * lanes + jnp.where(patch % 2 == 1, lanes - 1 - lane, lane)
    turned = ((region + jnp.arange(-1, 2, dtype=jnp.int32) + lanes) // lanes + 1) % 2
    analysed = analyse(turned, up, own, down, mine, other)
    returned = lax.all_to_all(
        analysed, axes, split_axis=0, concat_axis=0, tiled=True, axis_index_groups=groups
    )
    return pl.pallas_call(
        unpack_kernel, out_shape=jax.ShapeDtypeStruct((members, rows, width), F32),
        in_specs=[VMEM], out_specs=VMEM, compiler_params=LIMIT, name="unpack",
    )(returned)


def solution(mesh):
    return jax.shard_map(
        per_device,
        mesh=mesh,
        in_specs=(
            P("member", "patch", None),
            P(None, "patch", None),
            P("member"),
            P(("patch", "member"), None),
            P(("patch", "member")),
            P(("patch", "member"), None),
            P(("patch", "member"), None),
        ),
        out_specs=P("member", "patch", None),
        check_vma=False,
    )
```

```python
import functools
import math

import jax
import jax.numpy as jnp
from jax import lax
from jax.experimental import pallas as pl
from jax.experimental.pallas import tpu as pltpu
from jax.sharding import PartitionSpec as P

STEPS = 2
COARSE = 0.06
DONE = 1e-4
LARGE = 2e4
PART = 256
F32 = jnp.float32
BF16 = jnp.bfloat16


def pack_kernel(field_ref, flow_ref, tail_ref, head_ref):
    members, rows, width = field_ref.shape
    for out_ref, first, edge in ((tail_ref, rows - STEPS, rows - 1), (head_ref, 0, 0)):
        for place in range(STEPS):
            out_ref[pl.ds(place * members, members), :] = field_ref[:, first + place, :]
        out_ref[pl.ds(STEPS * members, 8), :] = jnp.concatenate([flow_ref[:, edge, :]] * 2, axis=0)


def weights_of(flow):
    row_flow, col_flow, kept, source = flow[0:1], flow[1:2], 1.0 - flow[2:3], flow[3:4]
    behind, ahead = jnp.maximum(row_flow, 0.0), -jnp.minimum(row_flow, 0.0)
    left, right = jnp.maximum(col_flow, 0.0), -jnp.minimum(col_flow, 0.0)
    stays = 1.0 - behind - ahead - left - right
    return [kept * stays, kept * behind, kept * ahead, kept * left, kept * right, source]


def advance(weights, emission, behind, field, ahead):
    width = field.shape[1]
    return (
        weights[0] * field
        + weights[1] * behind
        + weights[2] * ahead
        + weights[3] * pltpu.roll(field, 1, 1)
        + weights[4] * pltpu.roll(field, width - 1, 1)
        + emission * weights[5]
    )


def emission_column(emission_ref):
    members = emission_ref.shape[1]
    diagonal = lax.broadcasted_iota(jnp.int32, (members, members), 0) == lax.broadcasted_iota(
        jnp.int32, (members, members), 1
    )
    return jnp.sum(jnp.where(diagonal, emission_ref[...], 0.0), axis=1, keepdims=True)


def second_step(info_ref, wanted, shift, emission, wide_ref, weight_ref, out_refs):
    chips = len(out_refs)
    rows = weight_ref.shape[0]
    for s, out_ref in enumerate(out_refs):
        chip = lax.rem(info_ref[0] + s, chips)

        @pl.when(wanted(chip))
        def _():
            for place in range(2):
                position = 2 * chip + place
                row = position + info_ref[2] * (rows - 1 - 2 * position)
                weights = weight_ref[row]
                at = row + shift
                out_ref[place] = advance(
                    [weights[i : i + 1] for i in range(6)],
                    emission, wide_ref[at - 1], wide_ref[at], wide_ref[at + 1],
                )


def store_weights(flow_ref, weight_ref, rows):
    for row in rows:
        for i, weight in enumerate(weights_of(flow_ref[:, row, :])):
            weight_ref[row, pl.ds(i, 1), :] = weight


def inner_kernel(info_ref, field_ref, flow_ref, emission_ref, *refs):
    out_refs, (wide_ref, weight_ref) = refs[:-2], refs[-2:]
    rows = field_ref.shape[1]
    chips = len(out_refs)
    emission = emission_column(emission_ref)
    store_weights(flow_ref, weight_ref, range(rows))
    for row in range(1, rows - 1):
        wide_ref[row] = advance(
            weights_of(flow_ref[:, row, :]), emission,
            field_ref[:, row - 1, :], field_ref[:, row, :], field_ref[:, row + 1, :],
        )
    wanted = lambda chip: jnp.logical_and(chip > 0, chip < chips - 1)
    second_step(info_ref, wanted, 0, emission, wide_ref, weight_ref, out_refs)


def edge_kernel(info_ref, field_ref, flow_ref, emission_ref, before_ref, after_ref, *refs):
    out_refs, (wide_ref, weight_ref) = refs[:-2], refs[-2:]
    members, rows, width = field_ref.shape
    chips = len(out_refs)
    emission = emission_column(emission_ref)
    store_weights(flow_ref, weight_ref, (0, 1, rows - 2, rows - 1))

    def flow_row(row):
        if row < 0:
            return before_ref[pl.ds(STEPS * members, 4), :]
        if row >= rows:
            return after_ref[pl.ds(STEPS * members, 4), :]
        return flow_ref[:, row, :]

    def start_row(row):
        if row < 0:
            return before_ref[pl.ds((row + STEPS) * members, members), :]
        if row >= rows:
            return after_ref[pl.ds((row - rows) * members, members), :]
        return field_ref[:, row, :]

    for row in (-1, 0, 1, 2, rows - 3, rows - 2, rows - 1, rows):
        wide_ref[row + 1] = advance(
            weights_of(flow_row(row)), emission, start_row(row - 1), start_row(row), start_row(row + 1)
        )
    wanted = lambda chip: jnp.logical_or(chip == 0, chip == chips - 1)
    second_step(info_ref, wanted, 1, emission, wide_ref, weight_ref, out_refs)


def collect_kernel(info_ref, *refs):
    chips = (len(refs) - 3) // 2
    both_ref, first_ref, second_ref = refs[-3:]
    chip, core = info_ref[0], info_ref[1]
    at_edge = jnp.logical_or(chip == 0, chip == chips - 1)
    for s in range(chips):
        block = lax.rem(chip + chips - s, chips)
        for ref, here in ((refs[s], jnp.logical_not(at_edge)), (refs[chips + s], at_edge)):

            @pl.when(here)
            def _():
                other, own = ref[1 - core], ref[core]
                both_ref[0, block] = other
                both_ref[1, block] = own
                first_ref[block] = other
                second_ref[block] = own


def unpack_kernel(info_ref, rows_ref, out_ref):
    rows = rows_ref.shape[0]
    for row in range(rows):
        out_ref[:, row, :] = rows_ref[row + info_ref[2] * (rows - 1 - 2 * row)]


def pieces(x, count):
    parts = []
    for _ in range(count - 1):
        part = x.astype(BF16)
        parts.append(part)
        x = x - part.astype(F32)
    return parts + [x.astype(BF16)]


def dot(a, b):
    return lax.dot_general(a, b, (((1,), (0,)), ((), ())), preferred_element_type=F32)


def dot_t(a, b):
    return lax.dot_general(a, b, (((0,), (0,)), ((), ())), preferred_element_type=F32)


def product(a, b):
    total = None
    for i, left in enumerate(a):
        for j, right in enumerate(b):
            if i + j < max(len(a), len(b)):
                term = dot(left, right)
                total = term if total is None else total + term
    return total


def region_kernel(
    info_ref, mine_ref, other_ref, near_ref, far_ref, first_ref, second_ref, out_ref,
    high_ref, low_ref, spread_high, spread_low, factor, answer,
):
    _, chips, step, width = near_ref.shape
    half_of = chips * step
    members = 2 * half_of
    slots = mine_ref.shape[1]
    root = math.sqrt(members - 1)
    core, turned = info_ref[1], info_ref[2] == 1
    swapped = jnp.logical_or(
        jnp.logical_and(info_ref[0] == 0, core == 0), jnp.logical_and(info_ref[0] == chips - 1, core == 1)
    )

    observed = jnp.where(turned, other_ref[...], mine_ref[...])
    cells, values, scales, count = (observed[i : i + 1] for i in range(4))
    cells = cells.astype(jnp.int32)
    offset = sum((cells >= i * width).astype(jnp.int32) for i in (1, 2)) - 1
    column = cells - (offset + 1) * width
    side = offset * jnp.where(turned, -1, 1) * (1 - 2 * core)
    cells = column + width * jnp.where(side == 0, 2, jnp.where(side < 0, 0, 1))

    def block_of(place, part, chip):
        if place == 0:
            pair = (first_ref[chip], second_ref[chip])
            return jnp.where(swapped, pair[1 - part], pair[part])
        if part == 0:
            return near_ref[place - 1, chip]
        return far_ref[2 - place, chip]

    blocks = [(part, chip) for part in range(2) for chip in range(chips)]
    means = []
    for place in range(3):
        total = None
        for part, chip in blocks:
            block = block_of(place, part, chip)
            total = block if total is None else total + block
        mean = jnp.sum(total, axis=0, keepdims=True) * (1.0 / members)
        means.append(mean)
        for index, (part, chip) in enumerate(blocks):
            at = (pl.ds(index * step, step), pl.ds(place * width, width))
            high, low = pieces(block_of(place, part, chip) - mean, 2)
            high_ref[at] = high
            low_ref[at] = low
    chosen = (
        lax.broadcasted_iota(jnp.int32, (3 * width, slots), 0) == cells
    ).astype(F32).astype(BF16)
    active = lax.broadcasted_iota(jnp.int32, (1, slots), 1) < count.astype(jnp.int32)
    slot_weight = jnp.where(active, scales, 0.0)
    scale = slot_weight * (1.0 / root)
    mean_parts = pieces(jnp.broadcast_to(jnp.concatenate(means, axis=1), (8, 3 * width)), 3)
    predicted_mean = (dot(mean_parts[0], chosen) + (dot(mean_parts[1], chosen) + dot(mean_parts[2], chosen)))[:1]
    innovation = slot_weight * (values - predicted_mean)
    for first in range(0, members, PART):
        rows = pl.ds(first, PART)
        spread = (dot(high_ref[rows, :], chosen) + dot(low_ref[rows, :], chosen)) * scale
        high, low = pieces(spread, 2)
        spread_high[rows, :] = high
        spread_low[rows, :] = low

    high, low = spread_high[...], spread_low[...]
    middle = pl.ds(2 * width, width)
    eye = lax.broadcasted_iota(jnp.int32, (slots, slots), 0) == lax.broadcasted_iota(
        jnp.int32, (slots, slots), 1
    )
    cross = dot_t(high, low)
    matrix = dot_t(high, high) + (cross + cross.T) + jnp.where(eye, 1.0, 0.0)
    right = dot_t(high, high_ref[:, middle]) + (dot_t(high, low_ref[:, middle]) + dot_t(low, high_ref[:, middle]))

    norm = jnp.max(jnp.sum(jnp.abs(matrix), axis=0, keepdims=True))
    start = 2.0 / (1.0 + norm)
    factor[...] = matrix * start
    answer[...] = right * start

    def refine(bound, count):
        gain = 2.0 / (2.0 - bound * bound)
        parts = pieces(factor[...], count)
        answer[...] = gain * (2.0 * answer[...] - product(parts, pieces(answer[...], count)))
        factor[...] = gain * (2.0 * factor[...] - product(parts, parts))
        return bound * bound / (2.0 - bound * bound)

    def finish(bound):
        gain = 2.0 / (2.0 - bound * bound)
        rest = factor[...].astype(BF16)
        answer[...] = gain * (answer[...] + dot(rest, answer[...].astype(BF16)))
        factor[...] = gain * (dot(rest, rest) - jnp.where(eye, 0.5 * bound * bound, 0.0))
        return bound * bound / (2.0 - bound * bound)

    bound = 1.0 - start
    bound = lax.while_loop(
        lambda b: jnp.logical_and(b > COARSE, norm > LARGE), lambda b: refine(b, 3), bound
    )
    bound = lax.while_loop(lambda b: b > COARSE, lambda b: refine(b, 2), bound)
    factor[...] = jnp.where(eye, 1.0, 0.0) - factor[...]
    lax.while_loop(lambda b: b > DONE, finish, bound)

    solved = answer[...]
    solved_parts = pieces(solved, 2)
    innovation_parts = pieces(jnp.broadcast_to(innovation * (1.0 / root), (8, slots)), 3)
    shift = product(innovation_parts, pieces(solved, 3))[:1]
    half = [part * jnp.asarray(-0.5, BF16) for part in solved_parts]
    for index, (part, chip) in enumerate(blocks):
        rows = pl.ds(index * step, step)
        moved = product([spread_high[rows, :], spread_low[rows, :]], half)
        out_ref[2 * chip + jnp.abs(core - part)] = block_of(2, part, chip) + shift + moved


VMEM = pl.BlockSpec(memory_space=pltpu.VMEM)
LIMIT = pltpu.CompilerParams(vmem_limit_bytes=48 * 1024 * 1024)


SMEM = pl.BlockSpec(memory_space=pltpu.SMEM)


def call(kernel, name, out_shape, args, scratch=()):
    several = isinstance(out_shape, (list, tuple))
    return pl.pallas_call(
        kernel,
        out_shape=out_shape,
        in_specs=[SMEM] + [VMEM] * (len(args) - 1),
        out_specs=[VMEM] * len(out_shape) if several else VMEM,
        scratch_shapes=scratch,
        compiler_params=LIMIT,
        name=name,
    )(*args)


def array(*shape):
    return jax.ShapeDtypeStruct(shape, F32)


def per_device(
    init_field, flow_fields, emission, observed_cell, observed_count, observed_value, observed_scale
):
    step, rows, width = init_field.shape
    slots = observed_cell.shape[1]
    patches, lanes = lax.axis_size("patch"), lax.axis_size("member")
    chips = lanes // 2
    members = lanes * step
    axes = ("patch", "member")
    count = patches * lanes
    patch, lane = lax.axis_index("patch"), lax.axis_index("member")
    info = jnp.stack([lane // 2, lane % 2, patch % 2]).astype(jnp.int32)

    edge = array(STEPS * step + 8, width)
    tail, head = pl.pallas_call(
        pack_kernel, out_shape=(edge, edge), in_specs=[VMEM] * 2, out_specs=(VMEM, VMEM),
        compiler_params=LIMIT, name="pack",
    )(init_field, flow_fields)
    before = lax.ppermute(tail, "patch", [(i, i + 1) for i in range(patches - 1)])
    after = lax.ppermute(head, "patch", [(i + 1, i) for i in range(patches - 1)])

    mine = jnp.concatenate(
        [
            observed_cell.astype(F32),
            observed_value,
            observed_scale,
            jnp.broadcast_to(observed_count.astype(F32)[:, None], observed_cell.shape),
        ]
        * 2,
        axis=0,
    )
    other = lax.ppermute(
        mine, axes,
        [(p * lanes + i, p * lanes + lanes - 1 - i) for p in range(1, patches, 2) for i in range(lanes)],
    )

    def along(piece, s, ends):
        pairs = []
        for chip in range(chips):
            to = (chip + s) % chips
            if (to in (0, chips - 1)) == ends:
                pairs += [(2 * chip + core, 2 * to + core) for core in range(2)]
        return lax.ppermute(piece, "member", pairs)

    pair = array(2, step, width)
    wide = [pltpu.VMEM((rows + 2, step, width), F32), pltpu.VMEM((rows, 8, width), F32)]
    args = [info, init_field, flow_fields, emission[None, :]]
    inner = call(inner_kernel, "inner", [pair] * chips, args, wide)
    order = [s for near in range(chips // 2, 0, -1) for s in sorted({near, chips - near})]
    got_inner = {s: along(inner[s], s, False) for s in order}
    outer = call(edge_kernel, "edge", [pair] * chips, args + [before, after], wide)
    got_outer = {s: along(outer[s], s, True) for s in order}
    pieces_in = [inner[0]] + [got_inner[s] for s in range(1, chips)]
    pieces_in += [outer[0]] + [got_outer[s] for s in range(1, chips)]
    half_row = array(chips, step, width)
    near, first, second = call(
        collect_kernel, "collect", [array(2, chips, step, width), half_row, half_row], [info] + pieces_in
    )

    def device(p, chip, core):
        return p * lanes + 2 * chip + core

    first_pairs, second_pairs, siblings = [], [], []
    for p in range(patches):
        for chip in range(chips):
            siblings += [(device(p, chip, core), device(p, chip, 1 - core)) for core in range(2)]
            for core, away in ((0, 1), (1, -1)):
                if 0 <= chip + away < chips:
                    to_first, to_second = device(p, chip + away, core), device(p, chip + away, core)
                    to = p
                else:
                    to = p + 1 if (p % 2 == 0) == (away == 1) else p - 1
                    if not 0 <= to < patches:
                        continue
                    to_first = to_second = device(to, chip, 1 - core)
                first_pairs.append((device(p, chip, core), to_first))
                second_pairs.append((device(p, chip, 1 - core), to_second))
    got_first = lax.ppermute(first, axes, first_pairs)
    got_second = lax.ppermute(second, axes, second_pairs)
    far = lax.ppermute(near, axes, siblings)

    analysed = call(
        region_kernel, "region", array(lanes, step, width),
        [info, mine, other, near, far, got_first, got_second],
        [
            pltpu.VMEM((members, 3 * width), BF16),
            pltpu.VMEM((members, 3 * width), BF16),
            pltpu.VMEM((members, slots), BF16),
            pltpu.VMEM((members, slots), BF16),
            pltpu.VMEM((slots, slots), F32),
            pltpu.VMEM((slots, width), F32),
        ],
    )
    returned = lax.all_to_all(analysed, "member", split_axis=0, concat_axis=0, tiled=True)
    return call(unpack_kernel, "unpack", array(step, rows, width), [info, returned])


def solution(mesh):
    return jax.shard_map(
        per_device,
        mesh=mesh,
        in_specs=(
            P("member", "patch", None),
            P(None, "patch", None),
            P("member"),
            P(("patch", "member"), None),
            P(("patch", "member")),
            P(("patch", "member"), None),
            P(("patch", "member"), None),
        ),
        out_specs=P("member", "patch", None),
        check_vma=False,
    )
```

```python
import functools
import math

import jax
import jax.numpy as jnp
from jax import lax
from jax.experimental import pallas as pl
from jax.experimental.pallas import tpu as pltpu
from jax.sharding import PartitionSpec as P

STEPS = 2
COARSE = 0.06
DONE = 0.01
LARGE = 2e4
PART = 256
F32 = jnp.float32
BF16 = jnp.bfloat16


def pack_kernel(field_ref, flow_ref, tail_ref, head_ref):
    members, rows, width = field_ref.shape
    for out_ref, first, edge in ((tail_ref, rows - STEPS, rows - 1), (head_ref, 0, 0)):
        for place in range(STEPS):
            out_ref[pl.ds(place * members, members), :] = field_ref[:, first + place, :]
        out_ref[pl.ds(STEPS * members, 8), :] = jnp.concatenate([flow_ref[:, edge, :]] * 2, axis=0)


def weights_of(flow):
    row_flow, col_flow, kept, source = flow[0:1], flow[1:2], 1.0 - flow[2:3], flow[3:4]
    behind, ahead = jnp.maximum(row_flow, 0.0), -jnp.minimum(row_flow, 0.0)
    left, right = jnp.maximum(col_flow, 0.0), -jnp.minimum(col_flow, 0.0)
    stays = 1.0 - behind - ahead - left - right
    return [kept * stays, kept * behind, kept * ahead, kept * left, kept * right, source]


def advance(weights, emission, behind, field, ahead):
    width = field.shape[1]
    return (
        weights[0] * field
        + weights[1] * behind
        + weights[2] * ahead
        + weights[3] * pltpu.roll(field, 1, 1)
        + weights[4] * pltpu.roll(field, width - 1, 1)
        + emission * weights[5]
    )


def emission_column(emission_ref):
    members = emission_ref.shape[1]
    diagonal = lax.broadcasted_iota(jnp.int32, (members, members), 0) == lax.broadcasted_iota(
        jnp.int32, (members, members), 1
    )
    return jnp.sum(jnp.where(diagonal, emission_ref[...], 0.0), axis=1, keepdims=True)


def second_step(info_ref, wanted, shift, emission, wide_ref, weight_ref, out_refs):
    chips = len(out_refs)
    rows = weight_ref.shape[0]
    for s, out_ref in enumerate(out_refs):
        chip = lax.rem(info_ref[0] + s, chips)

        @pl.when(wanted(chip))
        def _():
            for place in range(2):
                position = 2 * chip + place
                row = position + info_ref[2] * (rows - 1 - 2 * position)
                weights = weight_ref[row]
                at = row + shift
                out_ref[place] = advance(
                    [weights[i : i + 1] for i in range(6)],
                    emission, wide_ref[at - 1], wide_ref[at], wide_ref[at + 1],
                )


def store_weights(flow_ref, weight_ref, rows):
    for row in rows:
        for i, weight in enumerate(weights_of(flow_ref[:, row, :])):
            weight_ref[row, pl.ds(i, 1), :] = weight


def inner_kernel(info_ref, field_ref, flow_ref, emission_ref, *refs):
    out_refs, (wide_ref, weight_ref) = refs[:-2], refs[-2:]
    rows = field_ref.shape[1]
    chips = len(out_refs)
    emission = emission_column(emission_ref)
    store_weights(flow_ref, weight_ref, range(rows))
    for row in range(1, rows - 1):
        wide_ref[row] = advance(
            weights_of(flow_ref[:, row, :]), emission,
            field_ref[:, row - 1, :], field_ref[:, row, :], field_ref[:, row + 1, :],
        )
    wanted = lambda chip: jnp.logical_and(chip > 0, chip < chips - 1)
    second_step(info_ref, wanted, 0, emission, wide_ref, weight_ref, out_refs)


def edge_kernel(info_ref, field_ref, flow_ref, emission_ref, before_ref, after_ref, *refs):
    out_refs, (wide_ref, weight_ref) = refs[:-2], refs[-2:]
    members, rows, width = field_ref.shape
    chips = len(out_refs)
    emission = emission_column(emission_ref)
    store_weights(flow_ref, weight_ref, (0, 1, rows - 2, rows - 1))

    def flow_row(row):
        if row < 0:
            return before_ref[pl.ds(STEPS * members, 4), :]
        if row >= rows:
            return after_ref[pl.ds(STEPS * members, 4), :]
        return flow_ref[:, row, :]

    def start_row(row):
        if row < 0:
            return before_ref[pl.ds((row + STEPS) * members, members), :]
        if row >= rows:
            return after_ref[pl.ds((row - rows) * members, members), :]
        return field_ref[:, row, :]

    for row in (-1, 0, 1, 2, rows - 3, rows - 2, rows - 1, rows):
        wide_ref[row + 1] = advance(
            weights_of(flow_row(row)), emission, start_row(row - 1), start_row(row), start_row(row + 1)
        )
    wanted = lambda chip: jnp.logical_or(chip == 0, chip == chips - 1)
    second_step(info_ref, wanted, 1, emission, wide_ref, weight_ref, out_refs)


def collect_kernel(info_ref, mine_ref, other_ref, *refs):
    chips = (len(refs) - 4) // 2
    both_ref, first_ref, second_ref, observed_ref = refs[-4:]
    observed_ref[...] = jnp.where(info_ref[2] == 1, other_ref[...], mine_ref[...])
    chip, core = info_ref[0], info_ref[1]
    at_edge = jnp.logical_or(chip == 0, chip == chips - 1)
    for s in range(chips):
        block = lax.rem(chip + chips - s, chips)
        for ref, here in ((refs[s], jnp.logical_not(at_edge)), (refs[chips + s], at_edge)):

            @pl.when(here)
            def _():
                other, own = ref[1 - core], ref[core]
                both_ref[0, block] = other
                both_ref[1, block] = own
                first_ref[block] = other
                second_ref[block] = own


def unpack_kernel(info_ref, rows_ref, out_ref):
    rows = rows_ref.shape[0]
    for row in range(rows):
        out_ref[:, row, :] = rows_ref[row + info_ref[2] * (rows - 1 - 2 * row)]


def pieces(x, count):
    parts = []
    for _ in range(count - 1):
        part = x.astype(BF16)
        parts.append(part)
        x = x - part.astype(F32)
    return parts + [x.astype(BF16)]


def dot(a, b):
    return lax.dot_general(a, b, (((1,), (0,)), ((), ())), preferred_element_type=F32)


def dot_t(a, b):
    return lax.dot_general(a, b, (((0,), (0,)), ((), ())), preferred_element_type=F32)


def product(a, b):
    total = None
    for i, left in enumerate(a):
        for j, right in enumerate(b):
            if i + j < max(len(a), len(b)):
                term = dot(left, right)
                total = term if total is None else total + term
    return total


def observations(info_ref, observed_ref, width, root):
    slots = observed_ref.shape[1]
    cells, values, scales, count = (observed_ref[pl.ds(i, 1), :] for i in range(4))
    cells = cells.astype(jnp.int32)
    offset = sum((cells >= i * width).astype(jnp.int32) for i in (1, 2)) - 1
    column = cells - (offset + 1) * width
    side = offset * jnp.where(info_ref[2] == 1, -1, 1) * (1 - 2 * info_ref[1])
    cells = column + width * jnp.where(side == 0, 2, jnp.where(side < 0, 0, 1))
    active = lax.broadcasted_iota(jnp.int32, (1, slots), 1) < count.astype(jnp.int32)
    slot_weight = jnp.where(active, scales, 0.0)
    return cells, slot_weight, values, slot_weight * (1.0 / root)


def one_hot(cells, first, count):
    return (
        lax.broadcasted_iota(jnp.int32, (count, cells.shape[1]), 0) + first == cells
    ).astype(F32).astype(BF16)


def mean_of(blocks, members):
    total = blocks[0]
    for block in blocks[1:]:
        total = total + block
    return jnp.sum(total, axis=0, keepdims=True) * (1.0 / members)


def at_cells(row, chosen):
    parts = pieces(jnp.broadcast_to(row, (8, row.shape[1])), 3)
    return (dot(parts[0], chosen) + (dot(parts[1], chosen) + dot(parts[2], chosen)))[:1]


def prepare_kernel(
    info_ref, observed_ref, near_ref, far_ref,
    spread_high, spread_low, own_high, own_low, mean_ref, high_ref, low_ref,
):
    _, chips, step, width = near_ref.shape
    members = 2 * chips * step
    cells, _, _, scale = observations(info_ref, observed_ref, width, math.sqrt(members - 1))
    chosen = one_hot(cells, width, 2 * width)
    means = []
    for place in range(2):
        blocks = [near_ref[place, chip] for chip in range(chips)] + [far_ref[1 - place, chip] for chip in range(chips)]
        means.append(mean_of(blocks, members))
        for index in range(2 * chips):
            block = near_ref[place, index] if index < chips else far_ref[1 - place, index - chips]
            rows = pl.ds(index * step, step)
            high, low = pieces(block - means[-1], 2)
            high_ref[rows, pl.ds(place * width, width)] = high
            low_ref[rows, pl.ds(place * width, width)] = low
            if place == 1:
                own_high[rows, :] = high
                own_low[rows, :] = low
    mean_ref[...] = jnp.broadcast_to(at_cells(jnp.concatenate(means, axis=1), chosen), mean_ref.shape)
    for first in range(0, members, PART):
        rows = pl.ds(first, PART)
        spread = (dot(high_ref[rows, :], chosen) + dot(low_ref[rows, :], chosen)) * scale
        high, low = pieces(spread, 2)
        spread_high[rows, :] = high
        spread_low[rows, :] = low


def square(parts):
    half = parts[0].shape[0] // 2
    upper = product([part[:half] for part in parts], parts)
    lower = product([part[half:] for part in parts], [part[:, half:] for part in parts])
    return upper, jnp.concatenate([upper[:, half:].T, lower], axis=1)


def region_kernel(
    info_ref, observed_ref, near_ref, far_ref, high_in, low_in, own_high, own_low, mean_ref, first_ref, second_ref,
    out_ref, spread_high, spread_low, factor, answer,
):
    _, chips, step, width = near_ref.shape
    members = 2 * chips * step
    slots = observed_ref.shape[1]
    root = math.sqrt(members - 1)
    core = info_ref[1]
    swapped = jnp.logical_or(
        jnp.logical_and(info_ref[0] == 0, core == 0), jnp.logical_and(info_ref[0] == chips - 1, core == 1)
    )
    cells, slot_weight, values, scale = observations(info_ref, observed_ref, width, root)
    chosen = one_hot(cells, 0, width)

    def outer_block(index):
        pair = (first_ref[index % chips], second_ref[index % chips])
        part = index // chips
        return jnp.where(swapped, pair[1 - part], pair[part])

    mean = mean_of([ref[chip] for ref in (first_ref, second_ref) for chip in range(chips)], members)
    innovation = slot_weight * (values - (mean_ref[pl.ds(0, 1), :] + at_cells(mean, chosen)))
    for index in range(2 * chips):
        rows = pl.ds(index * step, step)
        high, low = pieces(outer_block(index) - mean, 2)
        high, low = pieces((dot(high, chosen) + dot(low, chosen)) * scale, 2)
        spread_high[rows, :] = high + high_in[rows, :]
        spread_low[rows, :] = low + low_in[rows, :]

    high, low = spread_high[...], spread_low[...]
    eye = lax.broadcasted_iota(jnp.int32, (slots, slots), 0) == lax.broadcasted_iota(
        jnp.int32, (slots, slots), 1
    )
    cross = dot_t(high, low)
    matrix = dot_t(high, high) + (cross + cross.T) + jnp.where(eye, 1.0, 0.0)
    right = dot_t(high, own_high[...]) + (dot_t(high, own_low[...]) + dot_t(low, own_high[...]))

    norm = jnp.max(jnp.sum(jnp.abs(matrix), axis=0, keepdims=True))
    start = 2.0 / (1.0 + norm)
    factor[...] = matrix * start
    answer[...] = right * start
    half = slots // 2
    upper, lower = pl.ds(0, half), pl.ds(half, half)

    def refine(bound, count):
        gain = 2.0 / (2.0 - bound * bound)
        parts = pieces(factor[...], count)
        answer[...] = gain * (2.0 * answer[...] - product(parts, pieces(answer[...], count)))
        top, bottom = square(parts)
        factor[upper, :] = gain * (2.0 * factor[upper, :] - top)
        factor[lower, :] = gain * (2.0 * factor[lower, :] - bottom)
        return bound * bound / (2.0 - bound * bound)

    def close(bound, rest):
        gain = 2.0 / (2.0 - bound * bound)
        answer[...] = gain * (answer[...] + dot(rest, answer[...].astype(BF16)))
        return gain

    def finish(bound):
        rest = factor[...].astype(BF16)
        gain = close(bound, rest)
        factor[...] = gain * (dot(rest, rest) - jnp.where(eye, 0.5 * bound * bound, 0.0))
        return bound * bound / (2.0 - bound * bound)

    bound = 1.0 - start
    bound = lax.while_loop(
        lambda b: jnp.logical_and(b > COARSE, norm > LARGE), lambda b: refine(b, 3), bound
    )
    bound = lax.while_loop(lambda b: b > COARSE, lambda b: refine(b, 2), bound)
    factor[...] = jnp.where(eye, 1.0, 0.0) - factor[...]
    bound = lax.while_loop(lambda b: b > DONE, finish, bound)
    close(bound, factor[...].astype(BF16))

    solved = answer[...]
    solved_parts = pieces(solved, 2)
    innovation_parts = pieces(jnp.broadcast_to(innovation * (1.0 / root), (8, slots)), 3)
    shift = product(innovation_parts, pieces(solved, 3))[:1]
    halved = [part * jnp.asarray(-0.5, BF16) for part in solved_parts]
    for part, ref, place in ((0, near_ref, 1), (1, far_ref, 0)):
        for chip in range(chips):
            rows = pl.ds((part * chips + chip) * step, step)
            moved = product([spread_high[rows, :], spread_low[rows, :]], halved)
            out_ref[2 * chip + jnp.abs(core - part)] = ref[place, chip] + shift + moved


VMEM = pl.BlockSpec(memory_space=pltpu.VMEM)
LIMIT = pltpu.CompilerParams(vmem_limit_bytes=32 * 1024 * 1024)


SMEM = pl.BlockSpec(memory_space=pltpu.SMEM)


def call(kernel, name, out_shape, args, scratch=(), flops=None):
    several = isinstance(out_shape, (list, tuple))
    return pl.pallas_call(
        kernel,
        out_shape=out_shape,
        in_specs=[SMEM] + [VMEM] * (len(args) - 1),
        out_specs=[VMEM] * len(out_shape) if several else VMEM,
        scratch_shapes=scratch,
        compiler_params=LIMIT,
        cost_estimate=flops and pl.CostEstimate(flops=flops, bytes_accessed=0, transcendentals=0),
        name=name,
    )(*args)


def bfloat(*shape):
    return jax.ShapeDtypeStruct(shape, BF16)


def array(*shape):
    return jax.ShapeDtypeStruct(shape, F32)


def per_device(
    init_field, flow_fields, emission, observed_cell, observed_count, observed_value, observed_scale
):
    step, rows, width = init_field.shape
    slots = observed_cell.shape[1]
    patches, lanes = lax.axis_size("patch"), lax.axis_size("member")
    chips = lanes // 2
    members = lanes * step
    axes = ("patch", "member")
    count = patches * lanes
    patch, lane = lax.axis_index("patch"), lax.axis_index("member")
    info = jnp.stack([lane // 2, lane % 2, patch % 2]).astype(jnp.int32)

    edge = array(STEPS * step + 8, width)
    tail, head = pl.pallas_call(
        pack_kernel, out_shape=(edge, edge), in_specs=[VMEM] * 2, out_specs=(VMEM, VMEM),
        compiler_params=LIMIT, name="pack",
    )(init_field, flow_fields)
    before = lax.ppermute(tail, "patch", [(i, i + 1) for i in range(patches - 1)])
    after = lax.ppermute(head, "patch", [(i + 1, i) for i in range(patches - 1)])

    mine = jnp.concatenate(
        [
            observed_cell.astype(F32),
            observed_value,
            observed_scale,
            jnp.broadcast_to(observed_count.astype(F32)[:, None], observed_cell.shape),
        ]
        * 2,
        axis=0,
    )

    def along(piece, s, ends):
        pairs = []
        for chip in range(chips):
            to = (chip + s) % chips
            if (to in (0, chips - 1)) == ends:
                pairs += [(2 * chip + core, 2 * to + core) for core in range(2)]
        return lax.ppermute(piece, "member", pairs)

    pair = array(2, step, width)
    wide = [pltpu.VMEM((rows + 2, step, width), F32), pltpu.VMEM((rows, 8, width), F32)]
    args = [info, init_field, flow_fields, emission[None, :]]
    inner = call(inner_kernel, "inner", [pair] * chips, args, wide)
    order = [s for near in range(chips // 2, 0, -1) for s in sorted({near, chips - near})]
    got_inner = {s: along(inner[s], s, False) for s in order}
    outer = call(edge_kernel, "edge", [pair] * chips, args + [before, after], wide)
    mine, _ = lax.optimization_barrier((mine, outer[0]))
    other = lax.ppermute(
        mine, axes,
        [(p * lanes + i, p * lanes + lanes - 1 - i) for p in range(1, patches, 2) for i in range(lanes)],
    )
    got_outer = {s: along(outer[s], s, True) for s in order}
    pieces_in = [inner[0]] + [got_inner[s] for s in range(1, chips)]
    pieces_in += [outer[0]] + [got_outer[s] for s in range(1, chips)]
    half_row = array(chips, step, width)
    near, first, second, observed = call(
        collect_kernel, "collect", [array(2, chips, step, width), half_row, half_row, array(8, slots)],
        [info, mine, other] + pieces_in,
    )

    def device(p, chip, core):
        return p * lanes + 2 * chip + core

    first_pairs, second_pairs, siblings = [], [], []
    for p in range(patches):
        for chip in range(chips):
            siblings += [(device(p, chip, core), device(p, chip, 1 - core)) for core in range(2)]
            for core, away in ((0, 1), (1, -1)):
                if 0 <= chip + away < chips:
                    to_first, to_second = device(p, chip + away, core), device(p, chip + away, core)
                    to = p
                else:
                    to = p + 1 if (p % 2 == 0) == (away == 1) else p - 1
                    if not 0 <= to < patches:
                        continue
                    to_first = to_second = device(to, chip, 1 - core)
                first_pairs.append((device(p, chip, core), to_first))
                second_pairs.append((device(p, chip, 1 - core), to_second))
    far = lax.ppermute(near, axes, siblings)
    got_first = lax.ppermute(first, axes, first_pairs)
    got_second = lax.ppermute(second, axes, second_pairs)

    split = [pltpu.VMEM((members, slots), BF16)] * 2
    prepared = call(
        prepare_kernel, "prepare",
        [bfloat(members, slots)] * 2 + [bfloat(members, width)] * 2 + [array(8, slots)],
        [info, observed, near, far],
        [pltpu.VMEM((members, 2 * width), BF16)] * 2,
        flops=8 * members * slots * width,
    )
    analysed = call(
        region_kernel, "region", array(lanes, step, width),
        [info, observed, near, far, *prepared, got_first, got_second],
        split + [pltpu.VMEM((slots, slots), F32), pltpu.VMEM((slots, width), F32)],
    )
    returned = lax.all_to_all(analysed, "member", split_axis=0, concat_axis=0, tiled=True)
    return call(unpack_kernel, "unpack", array(step, rows, width), [info, returned])


def solution(mesh):
    return jax.shard_map(
        per_device,
        mesh=mesh,
        in_specs=(
            P("member", "patch", None),
            P(None, "patch", None),
            P("member"),
            P(("patch", "member"), None),
            P(("patch", "member")),
            P(("patch", "member"), None),
            P(("patch", "member"), None),
        ),
        out_specs=P("member", "patch", None),
        check_vma=False,
    )
```

```python
import functools
import math

import jax
import jax.numpy as jnp
from jax import lax
from jax.experimental import pallas as pl
from jax.experimental.pallas import tpu as pltpu
from jax.sharding import PartitionSpec as P

STEPS = 2
COARSE = 0.06
DONE = 0.01
LARGE = 2e4
PART = 256
F32 = jnp.float32
BF16 = jnp.bfloat16


def pack_kernel(field_ref, flow_ref, tail_ref, head_ref):
    members, rows, width = field_ref.shape
    for out_ref, first, edge in ((tail_ref, rows - STEPS, rows - 1), (head_ref, 0, 0)):
        for place in range(STEPS):
            out_ref[pl.ds(place * members, members), :] = field_ref[:, first + place, :]
        out_ref[pl.ds(STEPS * members, 8), :] = jnp.concatenate([flow_ref[:, edge, :]] * 2, axis=0)


def weights_of(flow):
    row_flow, col_flow, kept, source = flow[0:1], flow[1:2], 1.0 - flow[2:3], flow[3:4]
    behind, ahead = jnp.maximum(row_flow, 0.0), -jnp.minimum(row_flow, 0.0)
    left, right = jnp.maximum(col_flow, 0.0), -jnp.minimum(col_flow, 0.0)
    stays = 1.0 - behind - ahead - left - right
    return [kept * stays, kept * behind, kept * ahead, kept * left, kept * right, source]


def advance(weights, emission, behind, field, ahead):
    width = field.shape[1]
    return (
        weights[0] * field
        + weights[1] * behind
        + weights[2] * ahead
        + weights[3] * pltpu.roll(field, 1, 1)
        + weights[4] * pltpu.roll(field, width - 1, 1)
        + emission * weights[5]
    )


def emission_column(emission_ref):
    members = emission_ref.shape[1]
    diagonal = lax.broadcasted_iota(jnp.int32, (members, members), 0) == lax.broadcasted_iota(
        jnp.int32, (members, members), 1
    )
    return jnp.sum(jnp.where(diagonal, emission_ref[...], 0.0), axis=1, keepdims=True)


def second_step(info_ref, target, shift, emission, wide_ref, weight_ref, out_refs):
    rows = weight_ref.shape[0]
    for s, out_ref in enumerate(out_refs):
        chip, wanted = target(s)

        @pl.when(wanted)
        def _():
            for place in range(2):
                position = 2 * chip + place
                row = position + info_ref[2] * (rows - 1 - 2 * position)
                weights = weight_ref[row]
                at = row + shift
                out_ref[place] = advance(
                    [weights[i : i + 1] for i in range(6)],
                    emission, wide_ref[at - 1], wide_ref[at], wide_ref[at + 1],
                )


def store_weights(flow_ref, weight_ref, rows):
    for row in rows:
        for i, weight in enumerate(weights_of(flow_ref[:, row, :])):
            weight_ref[row, pl.ds(i, 1), :] = weight


def inner_kernel(info_ref, field_ref, flow_ref, emission_ref, *refs):
    out_refs, (wide_ref, weight_ref) = refs[:-2], refs[-2:]
    rows = field_ref.shape[1]
    chips = len(out_refs)
    emission = emission_column(emission_ref)
    store_weights(flow_ref, weight_ref, range(rows))
    for row in range(1, rows - 1):
        wide_ref[row] = advance(
            weights_of(flow_ref[:, row, :]), emission,
            field_ref[:, row - 1, :], field_ref[:, row, :], field_ref[:, row + 1, :],
        )

    def target(s):
        chip = lax.rem(info_ref[0] + s, chips)
        return chip, jnp.logical_and(chip > 0, chip < chips - 1)

    second_step(info_ref, target, 0, emission, wide_ref, weight_ref, out_refs)


def edge_kernel(info_ref, field_ref, flow_ref, emission_ref, before_ref, after_ref, *refs):
    out_refs, (wide_ref, weight_ref) = refs[:-2], refs[-2:]
    members, rows, width = field_ref.shape
    chips = len(out_refs)
    emission = emission_column(emission_ref)
    store_weights(flow_ref, weight_ref, (0, 1, rows - 2, rows - 1))

    def flow_row(row):
        if row < 0:
            return before_ref[pl.ds(STEPS * members, 4), :]
        if row >= rows:
            return after_ref[pl.ds(STEPS * members, 4), :]
        return flow_ref[:, row, :]

    def start_row(row):
        if row < 0:
            return before_ref[pl.ds((row + STEPS) * members, members), :]
        if row >= rows:
            return after_ref[pl.ds((row - rows) * members, members), :]
        return field_ref[:, row, :]

    for row in (-1, 0, 1, 2, rows - 3, rows - 2, rows - 1, rows):
        wide_ref[row + 1] = advance(
            weights_of(flow_row(row)), emission, start_row(row - 1), start_row(row), start_row(row + 1)
        )

    def target(s):
        first, last = info_ref[0] == s, info_ref[0] == chips - 1 - s
        return jnp.where(first, 0, chips - 1), jnp.logical_or(first, last)

    second_step(info_ref, target, 1, emission, wide_ref, weight_ref, out_refs)


def collect_kernel(info_ref, mine_ref, other_ref, *refs):
    chips = (len(refs) - 4) // 2
    both_ref, first_ref, second_ref, observed_ref = refs[-4:]
    observed_ref[...] = jnp.where(info_ref[2] == 1, other_ref[...], mine_ref[...])
    chip, core = info_ref[0], info_ref[1]
    at_edge = jnp.logical_or(chip == 0, chip == chips - 1)
    for s in range(chips):
        turn, mirror = lax.rem(chip + chips - s, chips), jnp.where(chip == 0, s, chips - 1 - s)
        for ref, here, block in (
            (refs[s], jnp.logical_not(at_edge), turn), (refs[chips + s], at_edge, mirror)
        ):

            @pl.when(here)
            def _():
                other, own = ref[1 - core], ref[core]
                both_ref[0, block] = other
                both_ref[1, block] = own
                first_ref[block] = other
                second_ref[block] = own


def unpack_kernel(info_ref, rows_ref, out_ref):
    rows = rows_ref.shape[0]
    for row in range(rows):
        out_ref[:, row, :] = rows_ref[row + info_ref[2] * (rows - 1 - 2 * row)]


def pieces(x, count):
    parts = []
    for _ in range(count - 1):
        part = x.astype(BF16)
        parts.append(part)
        x = x - part.astype(F32)
    return parts + [x.astype(BF16)]


def dot(a, b):
    return lax.dot_general(a, b, (((1,), (0,)), ((), ())), preferred_element_type=F32)


def dot_t(a, b):
    return lax.dot_general(a, b, (((0,), (0,)), ((), ())), preferred_element_type=F32)


def product(a, b):
    total = None
    for i, left in enumerate(a):
        for j, right in enumerate(b):
            if i + j < max(len(a), len(b)):
                term = dot(left, right)
                total = term if total is None else total + term
    return total


def observations(info_ref, observed_ref, width, root):
    slots = observed_ref.shape[1]
    cells, values, scales, count = (observed_ref[pl.ds(i, 1), :] for i in range(4))
    cells = cells.astype(jnp.int32)
    offset = sum((cells >= i * width).astype(jnp.int32) for i in (1, 2)) - 1
    column = cells - (offset + 1) * width
    side = offset * jnp.where(info_ref[2] == 1, -1, 1) * (1 - 2 * info_ref[1])
    cells = column + width * jnp.where(side == 0, 2, jnp.where(side < 0, 0, 1))
    active = lax.broadcasted_iota(jnp.int32, (1, slots), 1) < count.astype(jnp.int32)
    slot_weight = jnp.where(active, scales, 0.0)
    return cells, slot_weight, values, slot_weight * (1.0 / root)


def one_hot(cells, first, count):
    return (
        lax.broadcasted_iota(jnp.int32, (count, cells.shape[1]), 0) + first == cells
    ).astype(F32).astype(BF16)


def mean_of(blocks, members):
    total = blocks[0]
    for block in blocks[1:]:
        total = total + block
    return jnp.sum(total, axis=0, keepdims=True) * (1.0 / members)


def at_cells(row, chosen):
    parts = pieces(jnp.broadcast_to(row, (8, row.shape[1])), 3)
    return (dot(parts[0], chosen) + (dot(parts[1], chosen) + dot(parts[2], chosen)))[:1]


def doubled(x):
    return jnp.concatenate([x, x], axis=1)


def prepare_kernel(
    info_ref, observed_ref, near_ref, far_ref,
    spread_high, spread_low, own_high, own_low, own_part, seen_ref, direction_ref,
    anomaly, high_ref, low_ref,
):
    _, chips, step, width = near_ref.shape
    members = 2 * chips * step
    cells, _, _, scale = observations(info_ref, observed_ref, width, math.sqrt(members - 1))
    chosen = one_hot(cells, width, 2 * width)
    blocks = [pl.ds(index * step, step) for index in range(2 * chips)]
    means = []
    for place in range(2):
        columns = pl.ds(place * width, width)
        rows = [near_ref.at[place, chip] for chip in range(chips)] + [far_ref.at[1 - place, chip] for chip in range(chips)]
        means.append(mean_of([row[...] for row in rows], members))
        for block, row in zip(blocks, rows):
            part = row[...] - means[-1]
            anomaly[block, columns] = part
            high_ref[block, columns] = part.astype(BF16)

    def unit(x):
        return x * (1.0 / jnp.maximum(jnp.max(jnp.abs(x)), 1e-30))

    high = high_ref[...]
    along = lax.dot_general(high[:16], high, (((1,), (1,)), ((), ())), preferred_element_type=F32)
    rows = unit(dot(unit(along).astype(BF16), high))
    weight = jnp.sum(rows * rows[:1], axis=1, keepdims=True)
    weight = weight + jnp.where(jnp.max(jnp.abs(weight)) > 0.0, 0.0, 1.0)
    pattern = unit(jnp.sum(rows * weight, axis=0, keepdims=True))
    total = jnp.zeros((1, 1), F32)
    for block in blocks:
        along = jnp.sum(anomaly[block, :] * pattern, axis=1, keepdims=True)
        total = total + jnp.sum(along * along, axis=0, keepdims=True)
        direction_ref[block, :] = jnp.broadcast_to(along, (step, direction_ref.shape[1]))
    length = lax.rsqrt(jnp.maximum(total, 1e-30))
    taken = None
    for block in blocks:
        direction = direction_ref[block, :] * length
        direction_ref[block, :] = direction
        term = anomaly[block, :] * doubled(doubled(direction))
        taken = term if taken is None else taken + term
    taken = jnp.sum(taken, axis=0, keepdims=True)
    own_part[...] = jnp.broadcast_to(taken[:, width:], (own_part.shape[1], width)).T

    for block in blocks:
        rest = anomaly[block, :] - doubled(doubled(direction_ref[block, :])) * taken
        high, low = pieces(rest, 2)
        high_ref[block, :] = high
        low_ref[block, :] = low
        own = rest[:, width:].T
        own_high[:, block], own_low[:, block] = pieces(own, 2)
    seen_ref[pl.ds(0, 1), :] = at_cells(jnp.concatenate(means, axis=1), chosen)
    seen_ref[pl.ds(1, 1), :] = at_cells(taken, chosen)
    for first in range(0, members, PART):
        rows = pl.ds(first, PART)
        spread = (dot(high_ref[rows, :], chosen) + dot(low_ref[rows, :], chosen)) * scale
        high, low = pieces(spread, 2)
        spread_high[rows, :] = high
        spread_low[rows, :] = low


def square(parts):
    half = parts[0].shape[0] // 2
    upper = product([part[:half] for part in parts], parts)
    lower = product([part[half:] for part in parts], [part[:, half:] for part in parts])
    return upper, jnp.concatenate([upper[:, half:].T, lower], axis=1)


def region_kernel(
    info_ref, observed_ref, near_ref, far_ref, high_in, low_in, own_high, own_low, own_part, seen_ref, direction_ref,
    first_ref, second_ref, out_ref, spread_high, spread_low, factor, answer,
):
    _, chips, step, width = near_ref.shape
    members = 2 * chips * step
    slots = observed_ref.shape[1]
    root = math.sqrt(members - 1)
    core = info_ref[1]
    swapped = jnp.logical_or(
        jnp.logical_and(info_ref[0] == 0, core == 0), jnp.logical_and(info_ref[0] == chips - 1, core == 1)
    )
    cells, slot_weight, values, scale = observations(info_ref, observed_ref, width, root)
    chosen = one_hot(cells, 0, width)

    def outer_block(index):
        pair = (first_ref[index % chips], second_ref[index % chips])
        part = index // chips
        return jnp.where(swapped, pair[1 - part], pair[part])

    blocks = [pl.ds(index * step, step) for index in range(2 * chips)]
    mean = mean_of([ref[chip] for ref in (first_ref, second_ref) for chip in range(chips)], members)
    taken = None
    for index, block in enumerate(blocks):
        term = (outer_block(index) - mean) * doubled(direction_ref[block, :])
        taken = term if taken is None else taken + term
    taken = jnp.sum(taken, axis=0, keepdims=True)
    seen_mean = seen_ref[pl.ds(0, 1), :] + at_cells(mean, chosen)
    common = (seen_ref[pl.ds(1, 1), :] + at_cells(taken, chosen)) * scale
    innovation = slot_weight * (values - seen_mean)
    for index, block in enumerate(blocks):
        rest = outer_block(index) - mean - doubled(direction_ref[block, :]) * taken
        high, low = pieces(rest, 2)
        high, low = pieces((dot(high, chosen) + dot(low, chosen)) * scale, 2)
        spread_high[block, :] = high + high_in[block, :]
        spread_low[block, :] = low + low_in[block, :]

    high, low = spread_high[...], spread_low[...]
    eye = lax.broadcasted_iota(jnp.int32, (slots, slots), 0) == lax.broadcasted_iota(
        jnp.int32, (slots, slots), 1
    )
    turned = high.T
    cross = dot(turned, low)
    factor[...] = dot(turned, high) + (cross + cross.T) + jnp.where(eye, 1.0, 0.0)
    answer[pl.ds(0, width), :] = product([own_high[...], own_low[...]], [high, low])
    answer[pl.ds(width, 8), :] = jnp.where(
        lax.broadcasted_iota(jnp.int32, (8, slots), 0) == 0, jnp.broadcast_to(common, (8, slots)), 0.0
    )
    half = slots // 2
    upper, lower = pl.ds(0, half), pl.ds(half, half)

    def after(bound):
        return bound * bound / (2.0 - bound * bound)

    def size(matrix):
        return jnp.sum(jnp.sum(matrix * matrix, axis=0, keepdims=True))

    def begin(count):
        parts = pieces(factor[...], count)
        top, bottom = square(parts)
        limit = 1.0001 * jnp.sqrt(jnp.sqrt(size(top) + size(bottom)))
        start = 2.0 / (1.0 + limit)
        bound = 1.0 - start
        gain = 2.0 / (2.0 - bound * bound)
        answer[...] = (gain * start) * (2.0 * answer[...] - start * product(pieces(answer[...], count), parts))
        factor[upper, :] = (gain * start) * (2.0 * factor[upper, :] - start * top)
        factor[lower, :] = (gain * start) * (2.0 * factor[lower, :] - start * bottom)
        return after(bound)

    def refine(bound, count):
        gain = 2.0 / (2.0 - bound * bound)
        parts = pieces(factor[...], count)
        answer[...] = gain * (2.0 * answer[...] - product(pieces(answer[...], count), parts))
        top, bottom = square(parts)
        factor[upper, :] = gain * (2.0 * factor[upper, :] - top)
        factor[lower, :] = gain * (2.0 * factor[lower, :] - bottom)
        return after(bound)

    def close(bound, rest):
        gain = 2.0 / (2.0 - bound * bound)
        answer[...] = gain * (answer[...] + dot(answer[...].astype(BF16), rest))
        return gain

    def finish(bound):
        rest = factor[...].astype(BF16)
        gain = close(bound, rest)
        factor[...] = gain * (dot(rest, rest) - jnp.where(eye, 0.5 * bound * bound, 0.0))
        return after(bound)

    large = size(factor[...]) > LARGE * LARGE
    bound = lax.cond(large, lambda: begin(3), lambda: begin(2))
    bound = lax.while_loop(lambda b: jnp.logical_and(b > COARSE, large), lambda b: refine(b, 3), bound)
    bound = lax.while_loop(lambda b: b > COARSE, lambda b: refine(b, 2), bound)
    factor[...] = jnp.where(eye, 1.0, 0.0) - factor[...]
    bound = lax.while_loop(lambda b: b > DONE, finish, bound)
    close(bound, factor[...].astype(BF16))

    solved = answer[pl.ds(0, width), :]
    alone = answer[pl.ds(width, 1), :]
    share = own_part[:, :1] - jnp.sum(solved * common, axis=1, keepdims=True)
    solved = solved + (share / (1.0 + jnp.sum(common * alone, axis=1, keepdims=True))) * alone
    solved = solved.T
    which = lax.broadcasted_iota(jnp.int32, (8, slots), 0)
    sides = jnp.where(which == 0, innovation * (1.0 / root), jnp.where(which == 1, -0.5 * common, 0.0))
    parts = pieces(solved, 3)
    sides = product(pieces(sides, 3), parts)
    shift, along = sides[0:1], sides[1:2]
    halved = [part * jnp.asarray(-0.5, BF16) for part in pieces(solved, 2)]
    for part, ref, place in ((0, near_ref, 1), (1, far_ref, 0)):
        for chip in range(chips):
            block = blocks[part * chips + chip]
            moved = product([spread_high[block, :], spread_low[block, :]], halved)
            moved = moved + doubled(direction_ref[block, :]) * along
            out_ref[2 * chip + jnp.abs(core - part)] = ref[place, chip] + shift + moved


VMEM = pl.BlockSpec(memory_space=pltpu.VMEM)
LIMIT = pltpu.CompilerParams(vmem_limit_bytes=32 * 1024 * 1024)


SMEM = pl.BlockSpec(memory_space=pltpu.SMEM)


def call(kernel, name, out_shape, args, scratch=(), flops=None):
    several = isinstance(out_shape, (list, tuple))
    return pl.pallas_call(
        kernel,
        out_shape=out_shape,
        in_specs=[SMEM] + [VMEM] * (len(args) - 1),
        out_specs=[VMEM] * len(out_shape) if several else VMEM,
        scratch_shapes=scratch,
        compiler_params=LIMIT,
        cost_estimate=flops and pl.CostEstimate(flops=flops, bytes_accessed=0, transcendentals=0),
        name=name,
    )(*args)


def bfloat(*shape):
    return jax.ShapeDtypeStruct(shape, BF16)


def array(*shape):
    return jax.ShapeDtypeStruct(shape, F32)


def per_device(
    init_field, flow_fields, emission, observed_cell, observed_count, observed_value, observed_scale
):
    step, rows, width = init_field.shape
    slots = observed_cell.shape[1]
    patches, lanes = lax.axis_size("patch"), lax.axis_size("member")
    chips = lanes // 2
    members = lanes * step
    axes = ("patch", "member")
    count = patches * lanes
    patch, lane = lax.axis_index("patch"), lax.axis_index("member")
    info = jnp.stack([lane // 2, lane % 2, patch % 2]).astype(jnp.int32)

    edge = array(STEPS * step + 8, width)
    tail, head = pl.pallas_call(
        pack_kernel, out_shape=(edge, edge), in_specs=[VMEM] * 2, out_specs=(VMEM, VMEM),
        compiler_params=LIMIT, name="pack",
    )(init_field, flow_fields)
    before = lax.ppermute(tail, "patch", [(i, i + 1) for i in range(patches - 1)])
    after = lax.ppermute(head, "patch", [(i + 1, i) for i in range(patches - 1)])

    mine = jnp.concatenate(
        [
            observed_cell.astype(F32),
            observed_value,
            observed_scale,
            jnp.broadcast_to(observed_count.astype(F32)[:, None], observed_cell.shape),
        ]
        * 2,
        axis=0,
    )

    def along(piece, s, ends):
        if ends:
            hops = [(s, 0), (chips - 1 - s, chips - 1)]
        else:
            hops = [(chip, (chip + s) % chips) for chip in range(chips)]
            hops = [(chip, to) for chip, to in hops if 0 < to < chips - 1]
        return lax.ppermute(piece, "member", [(2 * a + core, 2 * b + core) for a, b in hops for core in range(2)])

    pair = array(2, step, width)
    wide = [pltpu.VMEM((rows + 2, step, width), F32), pltpu.VMEM((rows, 8, width), F32)]
    args = [info, init_field, flow_fields, emission[None, :]]
    inner = call(inner_kernel, "inner", [pair] * chips, args, wide)
    order = [s for near in range(chips // 2, 0, -1) for s in sorted({near, chips - near})]
    got_inner = {s: along(inner[s], s, False) for s in order}
    outer = call(edge_kernel, "edge", [pair] * chips, args + [before, after], wide)
    mine, _ = lax.optimization_barrier((mine, outer[0]))
    other = lax.ppermute(
        mine, axes,
        [(p * lanes + i, p * lanes + lanes - 1 - i) for p in range(1, patches, 2) for i in range(lanes)],
    )
    got_outer = {s: along(outer[s], s, True) for s in range(chips - 1, 0, -1)}
    pieces_in = [inner[0]] + [got_inner[s] for s in range(1, chips)]
    pieces_in += [outer[0]] + [got_outer[s] for s in range(1, chips)]
    half_row = array(chips, step, width)
    near, first, second, observed = call(
        collect_kernel, "collect", [array(2, chips, step, width), half_row, half_row, array(8, slots)],
        [info, mine, other] + pieces_in,
    )

    def device(p, chip, core):
        return p * lanes + 2 * chip + core

    first_pairs, second_pairs, siblings = [], [], []
    for p in range(patches):
        for chip in range(chips):
            siblings += [(device(p, chip, core), device(p, chip, 1 - core)) for core in range(2)]
            for core, away in ((0, 1), (1, -1)):
                if 0 <= chip + away < chips:
                    to_first, to_second = device(p, chip + away, core), device(p, chip + away, core)
                    to = p
                else:
                    to = p + 1 if (p % 2 == 0) == (away == 1) else p - 1
                    if not 0 <= to < patches:
                        continue
                    to_first = to_second = device(to, chip, 1 - core)
                first_pairs.append((device(p, chip, core), to_first))
                second_pairs.append((device(p, chip, 1 - core), to_second))
    far = lax.ppermute(near, axes, siblings)
    got_first = lax.ppermute(first, axes, first_pairs)
    got_second = lax.ppermute(second, axes, second_pairs)

    split = [pltpu.VMEM((members, slots), BF16)] * 2
    prepared = call(
        prepare_kernel, "prepare",
        [bfloat(members, slots)] * 2 + [bfloat(width, members)] * 2
        + [array(width, width // 2), array(8, slots), array(members, width // 2)],
        [info, observed, near, far],
        [pltpu.VMEM((members, 2 * width), F32)] + [pltpu.VMEM((members, 2 * width), BF16)] * 2,
        flops=8 * members * slots * width,
    )
    analysed = call(
        region_kernel, "region", array(lanes, step, width),
        [info, observed, near, far, *prepared, got_first, got_second],
        split + [pltpu.VMEM((slots, slots), F32), pltpu.VMEM((width + 8, slots), F32)],
    )
    returned = lax.all_to_all(analysed, "member", split_axis=0, concat_axis=0, tiled=True)
    return call(unpack_kernel, "unpack", array(step, rows, width), [info, returned])


def solution(mesh):
    return jax.shard_map(
        per_device,
        mesh=mesh,
        in_specs=(
            P("member", "patch", None),
            P(None, "patch", None),
            P("member"),
            P(("patch", "member"), None),
            P(("patch", "member")),
            P(("patch", "member"), None),
            P(("patch", "member"), None),
        ),
        out_specs=P("member", "patch", None),
        check_vma=False,
    )
```

```python
import functools
import math

import jax
import jax.numpy as jnp
from jax import lax
from jax.experimental import pallas as pl
from jax.experimental.pallas import tpu as pltpu
from jax.sharding import PartitionSpec as P

STEPS = 2
COARSE = 0.2
DONE = 0.01
LARGE = 2e4
PART = 256
F32 = jnp.float32
BF16 = jnp.bfloat16


def pack_kernel(info_ref, field_ref, flow_ref, first_ref, second_ref):
    members, rows, width = field_ref.shape
    for out_ref, last in ((first_ref, 0), (second_ref, 1)):
        for parity in range(2):

            @pl.when(info_ref[2] == parity)
            def _():
                first, edge = (rows - STEPS, rows - 1) if parity == last else (0, 0)
                for place in range(STEPS):
                    out_ref[pl.ds(place * members, members), :] = field_ref[:, first + place, :]
                out_ref[pl.ds(STEPS * members, 8), :] = jnp.concatenate([flow_ref[:, edge, :]] * 2, axis=0)


def weights_of(flow):
    row_flow, col_flow, kept, source = flow[0:1], flow[1:2], 1.0 - flow[2:3], flow[3:4]
    behind, ahead = jnp.maximum(row_flow, 0.0), -jnp.minimum(row_flow, 0.0)
    left, right = jnp.maximum(col_flow, 0.0), -jnp.minimum(col_flow, 0.0)
    stays = 1.0 - behind - ahead - left - right
    return [kept * stays, kept * behind, kept * ahead, kept * left, kept * right, source]


def advance(weights, emission, behind, field, ahead):
    width = field.shape[1]
    return (
        weights[0] * field
        + weights[1] * behind
        + weights[2] * ahead
        + weights[3] * pltpu.roll(field, 1, 1)
        + weights[4] * pltpu.roll(field, width - 1, 1)
        + emission * weights[5]
    )


def emission_column(emission_ref):
    members = emission_ref.shape[1]
    diagonal = lax.broadcasted_iota(jnp.int32, (members, members), 0) == lax.broadcasted_iota(
        jnp.int32, (members, members), 1
    )
    return jnp.sum(jnp.where(diagonal, emission_ref[...], 0.0), axis=1, keepdims=True)


def inner_kernel(info_ref, field_ref, flow_ref, emission_ref, kept_ref, *refs):
    out_refs, (wide_ref, weight_ref) = refs[:-2], refs[-2:]
    rows = field_ref.shape[1]
    chips = len(out_refs)
    emission = emission_column(emission_ref)
    for row in range(1, rows - 1):
        weights = weights_of(flow_ref[:, row, :])
        for i, weight in enumerate(weights):
            weight_ref[row, pl.ds(i, 1), :] = weight
        wide_ref[row] = advance(
            weights, emission, field_ref[:, row - 1, :], field_ref[:, row, :], field_ref[:, row + 1, :]
        )
    for place, row in enumerate((1, 2, rows - 3, rows - 2)):
        kept_ref[place] = wide_ref[row]
    for s, out_ref in enumerate(out_refs):
        chip = lax.rem(info_ref[0] + s, chips)

        @pl.when(jnp.logical_and(chip > 0, chip < chips - 1))
        def _():
            for place in range(2):
                position = 2 * chip + place
                row = position + info_ref[2] * (rows - 1 - 2 * position)
                weights = weight_ref[row]
                out_ref[place] = advance(
                    [weights[i : i + 1] for i in range(6)],
                    emission, wide_ref[row - 1], wide_ref[row], wide_ref[row + 1],
                )


def end_rows(info_ref, last, field_ref, flow_ref, emission_ref, kept_ref, halo_ref, out_ref):
    members, rows, width = field_ref.shape
    emission = emission_column(emission_ref)

    def halo_row(place):
        return halo_ref[pl.ds(place * members, members), :]

    halo_weights = weights_of(halo_ref[pl.ds(STEPS * members, 4), :])
    for parity in range(2):

        @pl.when(info_ref[2] == parity)
        def _():
            if parity == last:
                end, near, outside, beyond = 0, 1, halo_row(1), halo_row(0)
                inside, further = kept_ref[0], kept_ref[1]
            else:
                end, near, outside, beyond = rows - 1, rows - 2, halo_row(0), halo_row(1)
                inside, further = kept_ref[3], kept_ref[2]

            def ordered(weights, outer, own, inner):
                behind, ahead = (outer, inner) if end == 0 else (inner, outer)
                return advance(weights, emission, behind, own, ahead)

            end_weights = weights_of(flow_ref[:, end, :])
            end_field = field_ref[:, end, :]
            outer = ordered(halo_weights, beyond, outside, end_field)
            own = ordered(end_weights, outside, end_field, field_ref[:, near, :])
            out_ref[last] = ordered(end_weights, outer, own, inside)
            out_ref[1 - last] = ordered(weights_of(flow_ref[:, near, :]), own, inside, further)


def last_kernel(info_ref, field_ref, flow_ref, emission_ref, kept_ref, halo_ref, *refs):
    chips = (len(refs) - 1) // 2
    scratch = refs[-1]
    end_rows(info_ref, 1, field_ref, flow_ref, emission_ref, kept_ref, halo_ref, scratch)
    for s, out_ref in enumerate(refs[chips:-1]):

        @pl.when(info_ref[0] == chips - 1 - s)
        def _():
            out_ref[...] = scratch[...]


def first_kernel(info_ref, field_ref, flow_ref, emission_ref, kept_ref, halo_ref, out_ref):
    end_rows(info_ref, 0, field_ref, flow_ref, emission_ref, kept_ref, halo_ref, out_ref)


def collect_kernel(info_ref, mine_ref, other_ref, *refs):
    chips = (len(refs) - 4) // 2
    both_ref, first_ref, second_ref, observed_ref = refs[-4:]
    observed_ref[...] = jnp.where(info_ref[2] == 1, other_ref[...], mine_ref[...])
    chip, core = info_ref[0], info_ref[1]
    for s in range(chips):
        turn = lax.rem(chip + chips - s, chips)
        for ref, here, block in ((refs[s], chip > 0, turn), (refs[chips + s], chip == 0, s)):

            @pl.when(here)
            def _():
                other, own = ref[1 - core], ref[core]
                both_ref[0, block] = other
                both_ref[1, block] = own
                first_ref[block] = other
                second_ref[block] = own


def unpack_kernel(info_ref, rows_ref, out_ref):
    rows = rows_ref.shape[0]
    for row in range(rows):
        out_ref[:, row, :] = rows_ref[row + info_ref[2] * (rows - 1 - 2 * row)]


def pieces(x, count):
    parts = []
    for _ in range(count - 1):
        part = x.astype(BF16)
        parts.append(part)
        x = x - part.astype(F32)
    return parts + [x.astype(BF16)]


def dot(a, b):
    return lax.dot_general(a, b, (((1,), (0,)), ((), ())), preferred_element_type=F32)


def dot_t(a, b):
    return lax.dot_general(a, b, (((0,), (0,)), ((), ())), preferred_element_type=F32)


def product(a, b):
    total = None
    for i, left in enumerate(a):
        for j, right in enumerate(b):
            if i + j < max(len(a), len(b)):
                term = dot(left, right)
                total = term if total is None else total + term
    return total


def observations(info_ref, observed_ref, width, root):
    slots = observed_ref.shape[1]
    cells, values, scales, count = (observed_ref[pl.ds(i, 1), :] for i in range(4))
    cells = cells.astype(jnp.int32)
    offset = sum((cells >= i * width).astype(jnp.int32) for i in (1, 2)) - 1
    column = cells - (offset + 1) * width
    side = offset * jnp.where(info_ref[2] == 1, -1, 1) * (1 - 2 * info_ref[1])
    cells = column + width * jnp.where(side == 0, 2, jnp.where(side < 0, 0, 1))
    active = lax.broadcasted_iota(jnp.int32, (1, slots), 1) < count.astype(jnp.int32)
    slot_weight = jnp.where(active, scales, 0.0)
    return cells, slot_weight, values, slot_weight * (1.0 / root)


def one_hot(cells, first, count):
    return (
        lax.broadcasted_iota(jnp.int32, (count, cells.shape[1]), 0) + first == cells
    ).astype(F32).astype(BF16)


def mean_of(blocks, members):
    total = blocks[0]
    for block in blocks[1:]:
        total = total + block
    return jnp.sum(total, axis=0, keepdims=True) * (1.0 / members)


def at_cells(row, chosen):
    parts = pieces(jnp.broadcast_to(row, (8, row.shape[1])), 3)
    return (dot(parts[0], chosen) + (dot(parts[1], chosen) + dot(parts[2], chosen)))[:1]


def doubled(x):
    return jnp.concatenate([x, x], axis=1)


def prepare_kernel(
    info_ref, observed_ref, near_ref, far_ref,
    spread_high, spread_low, own_high, own_low, own_part, seen_ref, direction_ref,
    anomaly, high_ref, low_ref,
):
    _, chips, step, width = near_ref.shape
    members = 2 * chips * step
    cells, _, _, scale = observations(info_ref, observed_ref, width, math.sqrt(members - 1))
    chosen = one_hot(cells, width, 2 * width)
    blocks = [pl.ds(index * step, step) for index in range(2 * chips)]
    means = []
    for place in range(2):
        columns = pl.ds(place * width, width)
        rows = [near_ref.at[place, chip] for chip in range(chips)] + [far_ref.at[1 - place, chip] for chip in range(chips)]
        means.append(mean_of([row[...] for row in rows], members))
        for block, row in zip(blocks, rows):
            part = row[...] - means[-1]
            anomaly[block, columns] = part
            high_ref[block, columns] = part.astype(BF16)

    def unit(x):
        return x * (1.0 / jnp.maximum(jnp.max(jnp.abs(x)), 1e-30))

    high = high_ref[...]
    along = lax.dot_general(high[:16], high, (((1,), (1,)), ((), ())), preferred_element_type=F32)
    rows = unit(dot(unit(along).astype(BF16), high))
    weight = jnp.sum(rows * rows[:1], axis=1, keepdims=True)
    weight = weight + jnp.where(jnp.max(jnp.abs(weight)) > 0.0, 0.0, 1.0)
    pattern = unit(jnp.sum(rows * weight, axis=0, keepdims=True))
    total = jnp.zeros((1, 1), F32)
    for block in blocks:
        along = jnp.sum(anomaly[block, :] * pattern, axis=1, keepdims=True)
        total = total + jnp.sum(along * along, axis=0, keepdims=True)
        direction_ref[block, :] = jnp.broadcast_to(along, (step, direction_ref.shape[1]))
    length = lax.rsqrt(jnp.maximum(total, 1e-30))
    taken = None
    for block in blocks:
        direction = direction_ref[block, :] * length
        direction_ref[block, :] = direction
        term = anomaly[block, :] * doubled(doubled(direction))
        taken = term if taken is None else taken + term
    taken = jnp.sum(taken, axis=0, keepdims=True)
    own_part[...] = jnp.broadcast_to(taken[:, width:], (own_part.shape[1], width)).T

    for block in blocks:
        rest = anomaly[block, :] - doubled(doubled(direction_ref[block, :])) * taken
        high, low = pieces(rest, 2)
        high_ref[block, :] = high
        low_ref[block, :] = low
        own = rest[:, width:].T
        own_high[:, block], own_low[:, block] = pieces(own, 2)
    seen_ref[pl.ds(0, 1), :] = at_cells(jnp.concatenate(means, axis=1), chosen)
    seen_ref[pl.ds(1, 1), :] = at_cells(taken, chosen)
    for first in range(0, members, PART):
        rows = pl.ds(first, PART)
        spread = (dot(high_ref[rows, :], chosen) + dot(low_ref[rows, :], chosen)) * scale
        high, low = pieces(spread, 2)
        spread_high[rows, :] = high
        spread_low[rows, :] = low


def square(parts):
    half = parts[0].shape[0] // 2
    upper = product([part[:half] for part in parts], parts)
    lower = product([part[half:] for part in parts], [part[:, half:] for part in parts])
    return upper, jnp.concatenate([upper[:, half:].T, lower], axis=1)


def region_kernel(
    info_ref, observed_ref, near_ref, far_ref, high_in, low_in, own_high, own_low, own_part, seen_ref, direction_ref,
    first_ref, second_ref, out_ref, spread_high, spread_low, factor, answer,
):
    _, chips, step, width = near_ref.shape
    members = 2 * chips * step
    slots = observed_ref.shape[1]
    root = math.sqrt(members - 1)
    core = info_ref[1]
    swapped = jnp.logical_or(
        jnp.logical_and(info_ref[0] == 0, core == 0), jnp.logical_and(info_ref[0] == chips - 1, core == 1)
    )
    cells, slot_weight, values, scale = observations(info_ref, observed_ref, width, root)
    chosen = one_hot(cells, 0, width)

    def outer_block(index):
        pair = (first_ref[index % chips], second_ref[index % chips])
        part = index // chips
        return jnp.where(swapped, pair[1 - part], pair[part])

    blocks = [pl.ds(index * step, step) for index in range(2 * chips)]
    mean = mean_of([ref[chip] for ref in (first_ref, second_ref) for chip in range(chips)], members)
    taken = None
    for index, block in enumerate(blocks):
        term = (outer_block(index) - mean) * doubled(direction_ref[block, :])
        taken = term if taken is None else taken + term
    taken = jnp.sum(taken, axis=0, keepdims=True)
    seen_mean = seen_ref[pl.ds(0, 1), :] + at_cells(mean, chosen)
    common = (seen_ref[pl.ds(1, 1), :] + at_cells(taken, chosen)) * scale
    innovation = slot_weight * (values - seen_mean)
    for index, block in enumerate(blocks):
        rest = outer_block(index) - mean - doubled(direction_ref[block, :]) * taken
        high, low = pieces(rest, 2)
        high, low = pieces((dot(high, chosen) + dot(low, chosen)) * scale, 2)
        spread_high[block, :] = high + high_in[block, :]
        spread_low[block, :] = low + low_in[block, :]

    high, low = spread_high[...], spread_low[...]
    eye = lax.broadcasted_iota(jnp.int32, (slots, slots), 0) == lax.broadcasted_iota(
        jnp.int32, (slots, slots), 1
    )
    turned = high.T
    cross = dot(turned, low)
    factor[...] = dot(turned, high) + (cross + cross.T) + jnp.where(eye, 1.0, 0.0)
    answer[pl.ds(0, width), :] = product([own_high[...], own_low[...]], [high, low])
    answer[pl.ds(width, 8), :] = jnp.where(
        lax.broadcasted_iota(jnp.int32, (8, slots), 0) == 0, jnp.broadcast_to(common, (8, slots)), 0.0
    )
    half = slots // 2
    upper, lower = pl.ds(0, half), pl.ds(half, half)

    def after(bound):
        return bound * bound / (2.0 - bound * bound)

    def size(matrix):
        return jnp.sum(jnp.sum(matrix * matrix, axis=0, keepdims=True))

    def begin(count):
        parts = pieces(factor[...], count)
        top, bottom = square(parts)
        limit = 1.0001 * jnp.sqrt(jnp.sqrt(size(top) + size(bottom)))
        start = 2.0 / (1.0 + limit)
        bound = 1.0 - start
        gain = 2.0 / (2.0 - bound * bound)
        answer[...] = (gain * start) * (2.0 * answer[...] - start * product(pieces(answer[...], count), parts))
        factor[upper, :] = (gain * start) * (2.0 * factor[upper, :] - start * top)
        factor[lower, :] = (gain * start) * (2.0 * factor[lower, :] - start * bottom)
        return after(bound)

    def refine(bound, count):
        gain = 2.0 / (2.0 - bound * bound)
        parts = pieces(factor[...], count)
        answer[...] = gain * (2.0 * answer[...] - product(pieces(answer[...], count), parts))
        top, bottom = square(parts)
        factor[upper, :] = gain * (2.0 * factor[upper, :] - top)
        factor[lower, :] = gain * (2.0 * factor[lower, :] - bottom)
        return after(bound)

    def close(bound, rest):
        gain = 2.0 / (2.0 - bound * bound)
        answer[...] = gain * (answer[...] + dot(answer[...].astype(BF16), rest))
        return gain

    def finish(bound):
        rest = factor[...].astype(BF16)
        gain = close(bound, rest)
        factor[...] = gain * (dot(rest, rest) - jnp.where(eye, 0.5 * bound * bound, 0.0))
        return after(bound)

    large = size(factor[...]) > LARGE * LARGE
    bound = lax.cond(large, lambda: begin(3), lambda: begin(2))
    bound = lax.while_loop(lambda b: jnp.logical_and(b > COARSE, large), lambda b: refine(b, 3), bound)
    bound = lax.while_loop(lambda b: b > COARSE, lambda b: refine(b, 2), bound)
    factor[...] = jnp.where(eye, 1.0, 0.0) - factor[...]
    bound = lax.while_loop(lambda b: b > DONE, finish, bound)
    close(bound, factor[...].astype(BF16))

    solved = answer[pl.ds(0, width), :]
    alone = answer[pl.ds(width, 1), :]
    share = own_part[:, :1] - jnp.sum(solved * common, axis=1, keepdims=True)
    solved = solved + (share / (1.0 + jnp.sum(common * alone, axis=1, keepdims=True))) * alone
    solved = solved.T
    which = lax.broadcasted_iota(jnp.int32, (8, slots), 0)
    sides = jnp.where(which == 0, innovation * (1.0 / root), jnp.where(which == 1, -0.5 * common, 0.0))
    parts = pieces(solved, 3)
    sides = product(pieces(sides, 3), parts)
    shift, along = sides[0:1], sides[1:2]
    halved = [part * jnp.asarray(-0.5, BF16) for part in pieces(solved, 2)]
    for part, ref, place in ((0, near_ref, 1), (1, far_ref, 0)):
        for chip in range(chips):
            block = blocks[part * chips + chip]
            moved = product([spread_high[block, :], spread_low[block, :]], halved)
            moved = moved + doubled(direction_ref[block, :]) * along
            out_ref[2 * chip + jnp.abs(core - part)] = ref[place, chip] + shift + moved


VMEM = pl.BlockSpec(memory_space=pltpu.VMEM)
SMEM = pl.BlockSpec(memory_space=pltpu.SMEM)


def call(kernel, name, out_shape, args, scratch=(), flops=None, aliases={}, limit=8):
    several = isinstance(out_shape, (list, tuple))
    return pl.pallas_call(
        kernel,
        out_shape=out_shape,
        in_specs=[SMEM] + [VMEM] * (len(args) - 1),
        out_specs=[VMEM] * len(out_shape) if several else VMEM,
        scratch_shapes=scratch,
        input_output_aliases=aliases,
        compiler_params=pltpu.CompilerParams(vmem_limit_bytes=limit * 1024 * 1024),
        cost_estimate=flops and pl.CostEstimate(flops=flops, bytes_accessed=0, transcendentals=0),
        name=name,
    )(*args)


def bfloat(*shape):
    return jax.ShapeDtypeStruct(shape, BF16)


def array(*shape):
    return jax.ShapeDtypeStruct(shape, F32)


def per_device(
    init_field, flow_fields, emission, observed_cell, observed_count, observed_value, observed_scale
):
    step, rows, width = init_field.shape
    slots = observed_cell.shape[1]
    patches, lanes = lax.axis_size("patch"), lax.axis_size("member")
    chips = lanes // 2
    members = lanes * step
    axes = ("patch", "member")
    count = patches * lanes
    patch, lane = lax.axis_index("patch"), lax.axis_index("member")
    info = jnp.stack([lane // 2, lane % 2, patch % 2]).astype(jnp.int32)

    edge = array(STEPS * step + 8, width)
    to_last, to_first = call(pack_kernel, "pack", [edge, edge], [info, init_field, flow_fields])

    def swap(message, start):
        lower = range(start, patches - 1, 2)
        return lax.ppermute(message, "patch", [(p, p + 1) for p in lower] + [(p + 1, p) for p in lower])

    halo_last, halo_first = swap(to_last, 0), swap(to_first, 1)

    mine = jnp.concatenate(
        [
            observed_cell.astype(F32),
            observed_value,
            observed_scale,
            jnp.broadcast_to(observed_count.astype(F32)[:, None], observed_cell.shape),
        ]
        * 2,
        axis=0,
    )

    def between(hops):
        return [(2 * a + core, 2 * b + core) for a, b in hops for core in range(2)]

    pair = array(2, step, width)
    args = [info, init_field, flow_fields, emission[None, :]]
    kept, *inner = call(
        inner_kernel, "inner", [array(4, step, width)] + [pair] * chips, args,
        [pltpu.VMEM((rows, step, width), F32), pltpu.VMEM((rows, 8, width), F32)],
    )
    most = call(
        last_kernel, "last", [pair] * chips, args + [kept, halo_last, *inner],
        [pltpu.VMEM((2, step, width), F32)], aliases={6 + s: s for s in range(chips)},
    )
    order = [s for near in range(chips // 2, 0, -1) for s in sorted({near, chips - near})]
    got_most = {
        s: lax.ppermute(most[s], "member", between([(to - s + chips) % chips, to] for to in range(1, chips)))
        for s in order
    }
    few = call(first_kernel, "first", pair, args + [kept, halo_first])
    got_few = {s: lax.ppermute(few, "member", between([(s, 0)])) for s in range(chips - 1, 0, -1)}
    pieces_in = [most[0]] + [got_most[s] for s in range(1, chips)]
    pieces_in += [few] + [got_few[s] for s in range(1, chips)]
    half_row = array(chips, step, width)
    mine, _ = lax.optimization_barrier((mine, few))
    other = lax.ppermute(
        mine, axes,
        [(p * lanes + i, p * lanes + lanes - 1 - i) for p in range(1, patches, 2) for i in range(lanes)],
    )
    near, first, second, observed = call(
        collect_kernel, "collect", [array(2, chips, step, width), half_row, half_row, array(8, slots)],
        [info, mine, other] + pieces_in,
    )

    def device(p, chip, core):
        return p * lanes + 2 * chip + core

    first_pairs, second_pairs, siblings = [], [], []
    for p in range(patches):
        for chip in range(chips):
            siblings += [(device(p, chip, core), device(p, chip, 1 - core)) for core in range(2)]
            for core, away in ((0, 1), (1, -1)):
                if 0 <= chip + away < chips:
                    to_first, to_second = device(p, chip + away, core), device(p, chip + away, core)
                    to = p
                else:
                    to = p + 1 if (p % 2 == 0) == (away == 1) else p - 1
                    if not 0 <= to < patches:
                        continue
                    to_first = to_second = device(to, chip, 1 - core)
                first_pairs.append((device(p, chip, core), to_first))
                second_pairs.append((device(p, chip, 1 - core), to_second))
    far = lax.ppermute(near, axes, siblings)
    got_first = lax.ppermute(first, axes, first_pairs)
    got_second = lax.ppermute(second, axes, second_pairs)

    split = [pltpu.VMEM((members, slots), BF16)] * 2
    prepared = call(
        prepare_kernel, "prepare",
        [bfloat(members, slots)] * 2 + [bfloat(width, members)] * 2
        + [array(width, width // 2), array(8, slots), array(members, width // 2)],
        [info, observed, near, far],
        [pltpu.VMEM((members, 2 * width), F32)] + [pltpu.VMEM((members, 2 * width), BF16)] * 2,
        flops=8 * members * slots * width, limit=20,
    )
    analysed = call(
        region_kernel, "region", array(lanes, step, width),
        [info, observed, near, far, *prepared, got_first, got_second],
        split + [pltpu.VMEM((slots, slots), F32), pltpu.VMEM((width + 8, slots), F32)],
        limit=24,
    )
    returned = lax.all_to_all(analysed, "member", split_axis=0, concat_axis=0, tiled=True)
    part = step // 4
    return pl.pallas_call(
        unpack_kernel,
        grid=(4,),
        out_shape=array(step, rows, width),
        in_specs=[SMEM, pl.BlockSpec((rows, part, width), lambda i: (0, i, 0))],
        out_specs=pl.BlockSpec((part, rows, width), lambda i: (i, 0, 0)),
        name="unpack",
    )(info, returned)


def solution(mesh):
    return jax.shard_map(
        per_device,
        mesh=mesh,
        in_specs=(
            P("member", "patch", None),
            P(None, "patch", None),
            P("member"),
            P(("patch", "member"), None),
            P(("patch", "member")),
            P(("patch", "member"), None),
            P(("patch", "member"), None),
        ),
        out_specs=P("member", "patch", None),
        check_vma=False,
    )
```

```python
import functools
import math

import jax
import jax.numpy as jnp
from jax import lax
from jax.experimental import pallas as pl
from jax.experimental.pallas import tpu as pltpu
from jax.sharding import PartitionSpec as P

STEPS = 2
COARSE = 0.2
DONE = 0.01
LARGE = 2e4
PART = 256
F32 = jnp.float32
BF16 = jnp.bfloat16


def pack_kernel(field_ref, flow_ref, tail_ref, head_ref):
    members, rows, width = field_ref.shape
    for out_ref, first, edge in ((tail_ref, rows - STEPS, rows - 1), (head_ref, 0, 0)):
        for place in range(STEPS):
            out_ref[pl.ds(place * members, members), :] = field_ref[:, first + place, :]
        out_ref[pl.ds(STEPS * members, 8), :] = jnp.concatenate([flow_ref[:, edge, :]] * 2, axis=0)


def weights_of(flow):
    row_flow, col_flow, kept, source = flow[0:1], flow[1:2], 1.0 - flow[2:3], flow[3:4]
    behind, ahead = jnp.maximum(row_flow, 0.0), -jnp.minimum(row_flow, 0.0)
    left, right = jnp.maximum(col_flow, 0.0), -jnp.minimum(col_flow, 0.0)
    stays = 1.0 - behind - ahead - left - right
    return [kept * stays, kept * behind, kept * ahead, kept * left, kept * right, source]


def advance(weights, emission, behind, field, ahead):
    width = field.shape[1]
    return (
        weights[0] * field
        + weights[1] * behind
        + weights[2] * ahead
        + weights[3] * pltpu.roll(field, 1, 1)
        + weights[4] * pltpu.roll(field, width - 1, 1)
        + emission * weights[5]
    )


def emission_column(emission_ref):
    members = emission_ref.shape[1]
    diagonal = lax.broadcasted_iota(jnp.int32, (members, members), 0) == lax.broadcasted_iota(
        jnp.int32, (members, members), 1
    )
    return jnp.sum(jnp.where(diagonal, emission_ref[...], 0.0), axis=1, keepdims=True)


def second_step(info_ref, target, shift, emission, wide_ref, weight_ref, out_refs):
    rows = weight_ref.shape[0]
    for s, out_ref in enumerate(out_refs):
        chip, wanted = target(s)

        @pl.when(wanted)
        def _():
            for place in range(2):
                position = 2 * chip + place
                row = position + info_ref[2] * (rows - 1 - 2 * position)
                weights = weight_ref[row]
                at = row + shift
                out_ref[place] = advance(
                    [weights[i : i + 1] for i in range(6)],
                    emission, wide_ref[at - 1], wide_ref[at], wide_ref[at + 1],
                )


def store_weights(flow_ref, weight_ref, rows):
    for row in rows:
        for i, weight in enumerate(weights_of(flow_ref[:, row, :])):
            weight_ref[row, pl.ds(i, 1), :] = weight


def inner_kernel(info_ref, field_ref, flow_ref, emission_ref, kept_ref, *refs):
    out_refs, (wide_ref, weight_ref) = refs[:-2], refs[-2:]
    rows = field_ref.shape[1]
    chips = len(out_refs)
    emission = emission_column(emission_ref)
    store_weights(flow_ref, weight_ref, range(2, rows - 2))
    for row in range(1, rows - 1):
        wide_ref[row] = advance(
            weights_of(flow_ref[:, row, :]), emission,
            field_ref[:, row - 1, :], field_ref[:, row, :], field_ref[:, row + 1, :],
        )
    for place, row in enumerate((1, 2, rows - 3, rows - 2)):
        kept_ref[place] = wide_ref[row]

    def target(s):
        chip = lax.rem(info_ref[0] + s, chips)
        return chip, jnp.logical_and(chip > 0, chip < chips - 1)

    second_step(info_ref, target, 0, emission, wide_ref, weight_ref, out_refs)


def edge_kernel(info_ref, field_ref, flow_ref, emission_ref, kept_ref, before_ref, after_ref, *refs):
    out_refs, (wide_ref, weight_ref) = refs[:-2], refs[-2:]
    members, rows, width = field_ref.shape
    chips = len(out_refs)
    emission = emission_column(emission_ref)
    store_weights(flow_ref, weight_ref, (0, 1, rows - 2, rows - 1))

    def flow_row(row):
        if row < 0:
            return before_ref[pl.ds(STEPS * members, 4), :]
        if row >= rows:
            return after_ref[pl.ds(STEPS * members, 4), :]
        return flow_ref[:, row, :]

    def start_row(row):
        if row < 0:
            return before_ref[pl.ds((row + STEPS) * members, members), :]
        if row >= rows:
            return after_ref[pl.ds((row - rows) * members, members), :]
        return field_ref[:, row, :]

    for place, row in enumerate((1, 2, rows - 3, rows - 2)):
        wide_ref[row + 1] = kept_ref[place]
    for row in (-1, 0, rows - 1, rows):
        wide_ref[row + 1] = advance(
            weights_of(flow_row(row)), emission, start_row(row - 1), start_row(row), start_row(row + 1)
        )

    def target(s):
        first, last = info_ref[0] == s, info_ref[0] == chips - 1 - s
        return jnp.where(first, 0, chips - 1), jnp.logical_or(first, last)

    second_step(info_ref, target, 1, emission, wide_ref, weight_ref, out_refs)


def collect_kernel(order, info_ref, mine_ref, other_ref, *refs):
    chips = (len(refs) - 4) // 2
    both_ref, first_ref, second_ref, observed_ref = refs[-4:]
    observed_ref[...] = jnp.where(info_ref[2] == 1, other_ref[...], mine_ref[...])
    chip, core = info_ref[0], info_ref[1]
    at_edge = jnp.logical_or(chip == 0, chip == chips - 1)
    for index, (s, k) in enumerate(order):
        turn, mirror = lax.rem(chip + chips - s, chips), jnp.where(chip == 0, k, chips - 1 - k)
        for ref, here, block in (
            (refs[index], jnp.logical_not(at_edge), turn), (refs[chips + index], at_edge, mirror)
        ):

            @pl.when(here)
            def _():
                other, own = ref[1 - core], ref[core]
                both_ref[0, block] = other
                both_ref[1, block] = own
                first_ref[block] = other
                second_ref[block] = own


def unpack_kernel(rows_ref, out_ref):
    for row in range(rows_ref.shape[0]):
        out_ref[:, row, :] = rows_ref[row]


def pieces(x, count):
    parts = []
    for _ in range(count - 1):
        part = x.astype(BF16)
        parts.append(part)
        x = x - part.astype(F32)
    return parts + [x.astype(BF16)]


def dot(a, b):
    return lax.dot_general(a, b, (((1,), (0,)), ((), ())), preferred_element_type=F32)


def dot_t(a, b):
    return lax.dot_general(a, b, (((0,), (0,)), ((), ())), preferred_element_type=F32)


def product(a, b):
    total = None
    for i, left in enumerate(a):
        for j, right in enumerate(b):
            if i + j < max(len(a), len(b)):
                term = dot(left, right)
                total = term if total is None else total + term
    return total


def observations(info_ref, observed_ref, width, root):
    slots = observed_ref.shape[1]
    cells, values, scales, count = (observed_ref[pl.ds(i, 1), :] for i in range(4))
    cells = cells.astype(jnp.int32)
    offset = sum((cells >= i * width).astype(jnp.int32) for i in (1, 2)) - 1
    column = cells - (offset + 1) * width
    side = offset * jnp.where(info_ref[2] == 1, -1, 1) * (1 - 2 * info_ref[1])
    cells = column + width * jnp.where(side == 0, 2, jnp.where(side < 0, 0, 1))
    active = lax.broadcasted_iota(jnp.int32, (1, slots), 1) < count.astype(jnp.int32)
    slot_weight = jnp.where(active, scales, 0.0)
    return cells, slot_weight, values, slot_weight * (1.0 / root)


def one_hot(cells, first, count):
    return (
        lax.broadcasted_iota(jnp.int32, (count, cells.shape[1]), 0) + first == cells
    ).astype(F32).astype(BF16)


def mean_of(blocks, members):
    total = blocks[0]
    for block in blocks[1:]:
        total = total + block
    return jnp.sum(total, axis=0, keepdims=True) * (1.0 / members)


def at_cells(row, chosen):
    parts = pieces(jnp.broadcast_to(row, (8, row.shape[1])), 3)
    return (dot(parts[0], chosen) + (dot(parts[1], chosen) + dot(parts[2], chosen)))[:1]


def doubled(x):
    return jnp.concatenate([x, x], axis=1)


def prepare_kernel(
    info_ref, observed_ref, near_ref, far_ref,
    spread_high, spread_low, own_high, own_low, own_part, seen_ref, direction_ref,
    anomaly, high_ref, low_ref,
):
    _, chips, step, width = near_ref.shape
    members = 2 * chips * step
    cells, _, _, scale = observations(info_ref, observed_ref, width, math.sqrt(members - 1))
    chosen = one_hot(cells, width, 2 * width)
    blocks = [pl.ds(index * step, step) for index in range(2 * chips)]
    means = []
    for place in range(2):
        columns = pl.ds(place * width, width)
        rows = [near_ref.at[place, chip] for chip in range(chips)] + [far_ref.at[1 - place, chip] for chip in range(chips)]
        means.append(mean_of([row[...] for row in rows], members))
        for block, row in zip(blocks, rows):
            part = row[...] - means[-1]
            anomaly[block, columns] = part
            high_ref[block, columns] = part.astype(BF16)

    def unit(x):
        return x * (1.0 / jnp.maximum(jnp.max(jnp.abs(x)), 1e-30))

    high = high_ref[...]
    along = lax.dot_general(high[:16], high, (((1,), (1,)), ((), ())), preferred_element_type=F32)
    rows = unit(dot(unit(along).astype(BF16), high))
    weight = jnp.sum(rows * rows[:1], axis=1, keepdims=True)
    weight = weight + jnp.where(jnp.max(jnp.abs(weight)) > 0.0, 0.0, 1.0)
    pattern = unit(jnp.sum(rows * weight, axis=0, keepdims=True))
    total = jnp.zeros((1, 1), F32)
    for block in blocks:
        along = jnp.sum(anomaly[block, :] * pattern, axis=1, keepdims=True)
        total = total + jnp.sum(along * along, axis=0, keepdims=True)
        direction_ref[block, :] = jnp.broadcast_to(along, (step, direction_ref.shape[1]))
    length = lax.rsqrt(jnp.maximum(total, 1e-30))
    taken = None
    for block in blocks:
        direction = direction_ref[block, :] * length
        direction_ref[block, :] = direction
        term = anomaly[block, :] * doubled(doubled(direction))
        taken = term if taken is None else taken + term
    taken = jnp.sum(taken, axis=0, keepdims=True)
    own_part[...] = jnp.broadcast_to(taken[:, width:], (own_part.shape[1], width)).T

    for block in blocks:
        rest = anomaly[block, :] - doubled(doubled(direction_ref[block, :])) * taken
        high, low = pieces(rest, 2)
        high_ref[block, :] = high
        low_ref[block, :] = low
        own = rest[:, width:].T
        own_high[:, block], own_low[:, block] = pieces(own, 2)
    seen_ref[pl.ds(0, 1), :] = at_cells(jnp.concatenate(means, axis=1), chosen)
    seen_ref[pl.ds(1, 1), :] = at_cells(taken, chosen)
    for first in range(0, members, PART):
        rows = pl.ds(first, PART)
        spread = (dot(high_ref[rows, :], chosen) + dot(low_ref[rows, :], chosen)) * scale
        high, low = pieces(spread, 2)
        spread_high[rows, :] = high
        spread_low[rows, :] = low


def square(parts):
    half = parts[0].shape[0] // 2
    upper = product([part[:half] for part in parts], parts)
    lower = product([part[half:] for part in parts], [part[:, half:] for part in parts])
    return upper, jnp.concatenate([upper[:, half:].T, lower], axis=1)


def region_kernel(
    info_ref, observed_ref, near_ref, far_ref, high_in, low_in, own_high, own_low, own_part, seen_ref, direction_ref,
    first_ref, second_ref, out_ref, spread_high, spread_low, factor, answer,
):
    _, chips, step, width = near_ref.shape
    members = 2 * chips * step
    slots = observed_ref.shape[1]
    root = math.sqrt(members - 1)
    core = info_ref[1]
    swapped = jnp.logical_or(
        jnp.logical_and(info_ref[0] == 0, core == 0), jnp.logical_and(info_ref[0] == chips - 1, core == 1)
    )
    cells, slot_weight, values, scale = observations(info_ref, observed_ref, width, root)
    chosen = one_hot(cells, 0, width)

    def outer_block(index):
        pair = (first_ref[index % chips], second_ref[index % chips])
        part = index // chips
        return jnp.where(swapped, pair[1 - part], pair[part])

    blocks = [pl.ds(index * step, step) for index in range(2 * chips)]
    mean = mean_of([ref[chip] for ref in (first_ref, second_ref) for chip in range(chips)], members)
    taken = None
    for index, block in enumerate(blocks):
        term = (outer_block(index) - mean) * doubled(direction_ref[block, :])
        taken = term if taken is None else taken + term
    taken = jnp.sum(taken, axis=0, keepdims=True)
    seen_mean = seen_ref[pl.ds(0, 1), :] + at_cells(mean, chosen)
    common = (seen_ref[pl.ds(1, 1), :] + at_cells(taken, chosen)) * scale
    innovation = slot_weight * (values - seen_mean)
    for index, block in enumerate(blocks):
        rest = outer_block(index) - mean - doubled(direction_ref[block, :]) * taken
        high, low = pieces(rest, 2)
        high, low = pieces((dot(high, chosen) + dot(low, chosen)) * scale, 2)
        spread_high[block, :] = high + high_in[block, :]
        spread_low[block, :] = low + low_in[block, :]

    high, low = spread_high[...], spread_low[...]
    eye = lax.broadcasted_iota(jnp.int32, (slots, slots), 0) == lax.broadcasted_iota(
        jnp.int32, (slots, slots), 1
    )
    turned = high.T
    cross = dot(turned, low)
    factor[...] = dot(turned, high) + (cross + cross.T) + jnp.where(eye, 1.0, 0.0)
    answer[pl.ds(0, width), :] = product([own_high[...], own_low[...]], [high, low])
    answer[pl.ds(width, 8), :] = jnp.where(
        lax.broadcasted_iota(jnp.int32, (8, slots), 0) == 0, jnp.broadcast_to(common, (8, slots)), 0.0
    )
    half = slots // 2
    upper, lower = pl.ds(0, half), pl.ds(half, half)

    def after(bound):
        return bound * bound / (2.0 - bound * bound)

    def size(matrix):
        return jnp.sum(jnp.sum(matrix * matrix, axis=0, keepdims=True))

    def begin(count):
        parts = pieces(factor[...], count)
        top, bottom = square(parts)
        limit = 1.0001 * jnp.sqrt(jnp.sqrt(size(top) + size(bottom)))
        start = 2.0 / (1.0 + limit)
        bound = 1.0 - start
        gain = 2.0 / (2.0 - bound * bound)
        answer[...] = (gain * start) * (2.0 * answer[...] - start * product(pieces(answer[...], count), parts))
        factor[upper, :] = (gain * start) * (2.0 * factor[upper, :] - start * top)
        factor[lower, :] = (gain * start) * (2.0 * factor[lower, :] - start * bottom)
        return after(bound)

    def refine(bound, count):
        gain = 2.0 / (2.0 - bound * bound)
        parts = pieces(factor[...], count)
        answer[...] = gain * (2.0 * answer[...] - product(pieces(answer[...], count), parts))
        top, bottom = square(parts)
        factor[upper, :] = gain * (2.0 * factor[upper, :] - top)
        factor[lower, :] = gain * (2.0 * factor[lower, :] - bottom)
        return after(bound)

    def close(bound, rest):
        gain = 2.0 / (2.0 - bound * bound)
        answer[...] = gain * (answer[...] + dot(answer[...].astype(BF16), rest))
        return gain

    def finish(bound):
        rest = factor[...].astype(BF16)
        gain = close(bound, rest)
        factor[...] = gain * (dot(rest, rest) - jnp.where(eye, 0.5 * bound * bound, 0.0))
        return after(bound)

    large = size(factor[...]) > LARGE * LARGE
    bound = lax.cond(large, lambda: begin(3), lambda: begin(2))
    bound = lax.while_loop(lambda b: jnp.logical_and(b > COARSE, large), lambda b: refine(b, 3), bound)
    bound = lax.while_loop(lambda b: b > COARSE, lambda b: refine(b, 2), bound)
    factor[...] = jnp.where(eye, 1.0, 0.0) - factor[...]
    bound = lax.while_loop(lambda b: b > DONE, finish, bound)
    close(bound, factor[...].astype(BF16))

    solved = answer[pl.ds(0, width), :]
    alone = answer[pl.ds(width, 1), :]
    share = own_part[:, :1] - jnp.sum(solved * common, axis=1, keepdims=True)
    solved = solved + (share / (1.0 + jnp.sum(common * alone, axis=1, keepdims=True))) * alone
    solved = solved.T
    which = lax.broadcasted_iota(jnp.int32, (8, slots), 0)
    sides = jnp.where(which == 0, innovation * (1.0 / root), jnp.where(which == 1, -0.5 * common, 0.0))
    parts = pieces(solved, 3)
    sides = product(pieces(sides, 3), parts)
    shift, along = sides[0:1], sides[1:2]
    halved = [part * jnp.asarray(-0.5, BF16) for part in pieces(solved, 2)]
    for part, ref, place in ((0, near_ref, 1), (1, far_ref, 0)):
        for chip in range(chips):
            block = blocks[part * chips + chip]
            moved = product([spread_high[block, :], spread_low[block, :]], halved)
            moved = moved + doubled(direction_ref[block, :]) * along
            lane = 2 * chip + jnp.abs(core - part)
            lane = lane + info_ref[2] * (2 * chips - 1 - 2 * lane)
            out_ref[lane] = ref[place, chip] + shift + moved


VMEM = pl.BlockSpec(memory_space=pltpu.VMEM)
SMEM = pl.BlockSpec(memory_space=pltpu.SMEM)


def call(kernel, name, out_shape, args, scratch=(), flops=None, aliases={}, limit=8):
    several = isinstance(out_shape, (list, tuple))
    return pl.pallas_call(
        kernel,
        out_shape=out_shape,
        in_specs=[SMEM] + [VMEM] * (len(args) - 1),
        out_specs=[VMEM] * len(out_shape) if several else VMEM,
        scratch_shapes=scratch,
        input_output_aliases=aliases,
        compiler_params=pltpu.CompilerParams(vmem_limit_bytes=limit * 1024 * 1024),
        cost_estimate=flops and pl.CostEstimate(flops=flops, bytes_accessed=0, transcendentals=0),
        name=name,
    )(*args)


def bfloat(*shape):
    return jax.ShapeDtypeStruct(shape, BF16)


def array(*shape):
    return jax.ShapeDtypeStruct(shape, F32)


def per_device(
    init_field, flow_fields, emission, observed_cell, observed_count, observed_value, observed_scale
):
    step, rows, width = init_field.shape
    slots = observed_cell.shape[1]
    patches, lanes = lax.axis_size("patch"), lax.axis_size("member")
    chips = lanes // 2
    members = lanes * step
    axes = ("patch", "member")
    count = patches * lanes
    patch, lane = lax.axis_index("patch"), lax.axis_index("member")
    info = jnp.stack([lane // 2, lane % 2, patch % 2]).astype(jnp.int32)

    edge = array(STEPS * step + 8, width)
    tail, head = pl.pallas_call(
        pack_kernel, out_shape=(edge, edge), in_specs=[VMEM] * 2, out_specs=(VMEM, VMEM), name="pack",
    )(init_field, flow_fields)
    before = lax.ppermute(tail, "patch", [(i, i + 1) for i in range(patches - 1)])
    after = lax.ppermute(head, "patch", [(i + 1, i) for i in range(patches - 1)])

    mine = jnp.concatenate(
        [
            observed_cell.astype(F32),
            observed_value,
            observed_scale,
            jnp.broadcast_to(observed_count.astype(F32)[:, None], observed_cell.shape),
        ]
        * 2,
        axis=0,
    )

    def along(piece, s, ends):
        if ends:
            hops = [(s, 0), (chips - 1 - s, chips - 1)]
        else:
            hops = [(chip, (chip + s) % chips) for chip in range(chips)]
            hops = [(chip, to) for chip, to in hops if 0 < to < chips - 1]
        return lax.ppermute(piece, "member", [(2 * a + core, 2 * b + core) for a, b in hops for core in range(2)])

    pair = array(2, step, width)
    wide = [pltpu.VMEM((rows + 2, step, width), F32), pltpu.VMEM((rows, 8, width), F32)]
    args = [info, init_field, flow_fields, emission[None, :]]
    kept, *inner = call(inner_kernel, "inner", [array(4, step, width)] + [pair] * chips, args, wide)
    order = [s for near in range(chips // 2, 0, -1) for s in sorted({near, chips - near})]
    got_inner = {s: along(inner[s], s, False) for s in order}
    outer = call(edge_kernel, "edge", [pair] * chips, args + [kept, before, after], wide)
    mine, _ = lax.optimization_barrier((mine, outer[0]))
    other = lax.ppermute(
        mine, axes,
        [(p * lanes + i, p * lanes + lanes - 1 - i) for p in range(1, patches, 2) for i in range(lanes)],
    )
    got_outer = {s: along(outer[s], s, True) for s in range(chips - 1, 0, -1)}
    got_inner[0], got_outer[0] = inner[0], outer[0]
    order = list(zip(order + [0], range(chips - 1, -1, -1)))
    pieces_in = [got_inner[s] for s, _ in order] + [got_outer[k] for _, k in order]
    half_row = array(chips, step, width)
    near, first, second, observed = call(
        functools.partial(collect_kernel, order), "collect", [array(2, chips, step, width), half_row, half_row, array(8, slots)],
        [info, mine, other] + pieces_in,
    )

    def device(p, chip, core):
        return p * lanes + 2 * chip + core

    first_pairs, second_pairs, siblings = [], [], []
    for p in range(patches):
        for chip in range(chips):
            siblings += [(device(p, chip, core), device(p, chip, 1 - core)) for core in range(2)]
            for core, away in ((0, 1), (1, -1)):
                if 0 <= chip + away < chips:
                    to_first, to_second = device(p, chip + away, core), device(p, chip + away, core)
                    to = p
                else:
                    to = p + 1 if (p % 2 == 0) == (away == 1) else p - 1
                    if not 0 <= to < patches:
                        continue
                    to_first = to_second = device(to, chip, 1 - core)
                first_pairs.append((device(p, chip, core), to_first))
                second_pairs.append((device(p, chip, 1 - core), to_second))
    far = lax.ppermute(near, axes, siblings)
    got_first = lax.ppermute(first, axes, first_pairs)
    got_second = lax.ppermute(second, axes, second_pairs)

    split = [pltpu.VMEM((members, slots), BF16)] * 2
    prepared = call(
        prepare_kernel, "prepare",
        [bfloat(members, slots)] * 2 + [bfloat(width, members)] * 2
        + [array(width, width // 2), array(8, slots), array(members, width // 2)],
        [info, observed, near, far],
        [pltpu.VMEM((members, 2 * width), F32)] + [pltpu.VMEM((members, 2 * width), BF16)] * 2,
        flops=8 * members * slots * width, limit=20,
    )
    analysed = call(
        region_kernel, "region", array(lanes, step, width),
        [info, observed, near, far, *prepared, got_first, got_second],
        split + [pltpu.VMEM((slots, slots), F32), pltpu.VMEM((width + 8, slots), F32)],
        limit=24,
    )
    groups = [[p * lanes + (lanes - 1 - i if p % 2 else i) for i in range(lanes)] for p in range(patches)]
    returned = lax.all_to_all(
        analysed, axes, split_axis=0, concat_axis=0, tiled=True, axis_index_groups=groups
    )
    return pl.pallas_call(
        unpack_kernel, out_shape=array(step, rows, width), in_specs=[VMEM], out_specs=VMEM, name="unpack",
    )(returned)


def solution(mesh):
    return jax.shard_map(
        per_device,
        mesh=mesh,
        in_specs=(
            P("member", "patch", None),
            P(None, "patch", None),
            P("member"),
            P(("patch", "member"), None),
            P(("patch", "member")),
            P(("patch", "member"), None),
            P(("patch", "member"), None),
        ),
        out_specs=P("member", "patch", None),
        check_vma=False,
    )
```

```python
import functools
import math

import jax
import jax.numpy as jnp
from jax import lax
from jax.experimental import pallas as pl
from jax.experimental.pallas import tpu as pltpu
from jax.sharding import PartitionSpec as P

STEPS = 2
COARSE = 0.2
DONE = 0.01
LARGE = 2e4
PART = 256
F32 = jnp.float32
BF16 = jnp.bfloat16


def pack_kernel(field_ref, flow_ref, tail_ref, head_ref):
    members, rows, width = field_ref.shape
    for out_ref, first, edge in ((tail_ref, rows - STEPS, rows - 1), (head_ref, 0, 0)):
        for place in range(STEPS):
            out_ref[pl.ds(place * members, members), :] = field_ref[:, first + place, :]
        out_ref[pl.ds(STEPS * members, 8), :] = jnp.concatenate([flow_ref[:, edge, :]] * 2, axis=0)


def weights_of(flow):
    row_flow, col_flow, kept, source = flow[0:1], flow[1:2], 1.0 - flow[2:3], flow[3:4]
    behind, ahead = jnp.maximum(row_flow, 0.0), -jnp.minimum(row_flow, 0.0)
    left, right = jnp.maximum(col_flow, 0.0), -jnp.minimum(col_flow, 0.0)
    stays = 1.0 - behind - ahead - left - right
    return [kept * stays, kept * behind, kept * ahead, kept * left, kept * right, source]


def advance(weights, emission, behind, field, ahead):
    width = field.shape[1]
    return (
        weights[0] * field
        + weights[1] * behind
        + weights[2] * ahead
        + weights[3] * pltpu.roll(field, 1, 1)
        + weights[4] * pltpu.roll(field, width - 1, 1)
        + emission * weights[5]
    )


def emission_column(emission_ref):
    members = emission_ref.shape[1]
    diagonal = lax.broadcasted_iota(jnp.int32, (members, members), 0) == lax.broadcasted_iota(
        jnp.int32, (members, members), 1
    )
    return jnp.sum(jnp.where(diagonal, emission_ref[...], 0.0), axis=1, keepdims=True)


def second_step(info_ref, target, shift, emission, wide_ref, weight_ref, out_refs):
    rows = weight_ref.shape[0]
    for s, out_ref in enumerate(out_refs):
        chip, wanted = target(s)

        @pl.when(wanted)
        def _():
            for place in range(2):
                position = 2 * chip + jnp.abs(info_ref[1] - 1 + place)
                row = position + info_ref[2] * (rows - 1 - 2 * position)
                weights = weight_ref[row]
                at = row + shift
                out_ref[place] = advance(
                    [weights[i : i + 1] for i in range(6)],
                    emission, wide_ref[at - 1], wide_ref[at], wide_ref[at + 1],
                )


def store_weights(flow_ref, weight_ref, rows):
    for row in rows:
        for i, weight in enumerate(weights_of(flow_ref[:, row, :])):
            weight_ref[row, pl.ds(i, 1), :] = weight


def inner_kernel(info_ref, field_ref, flow_ref, emission_ref, kept_ref, *refs):
    out_refs, (wide_ref, weight_ref) = refs[:-2], refs[-2:]
    rows = field_ref.shape[1]
    chips = len(out_refs)
    emission = emission_column(emission_ref)
    store_weights(flow_ref, weight_ref, range(2, rows - 2))
    for row in range(1, rows - 1):
        wide_ref[row] = advance(
            weights_of(flow_ref[:, row, :]), emission,
            field_ref[:, row - 1, :], field_ref[:, row, :], field_ref[:, row + 1, :],
        )
    for place, row in enumerate((1, 2, rows - 3, rows - 2)):
        kept_ref[place] = wide_ref[row]

    def target(s):
        chip = lax.rem(info_ref[0] + s, chips)
        return chip, jnp.logical_and(chip > 0, chip < chips - 1)

    second_step(info_ref, target, 0, emission, wide_ref, weight_ref, out_refs)


def edge_kernel(info_ref, field_ref, flow_ref, emission_ref, kept_ref, before_ref, after_ref, *refs):
    out_refs, (wide_ref, weight_ref) = refs[:-2], refs[-2:]
    members, rows, width = field_ref.shape
    chips = len(out_refs)
    emission = emission_column(emission_ref)
    store_weights(flow_ref, weight_ref, (0, 1, rows - 2, rows - 1))

    def flow_row(row):
        if row < 0:
            return before_ref[pl.ds(STEPS * members, 4), :]
        if row >= rows:
            return after_ref[pl.ds(STEPS * members, 4), :]
        return flow_ref[:, row, :]

    def start_row(row):
        if row < 0:
            return before_ref[pl.ds((row + STEPS) * members, members), :]
        if row >= rows:
            return after_ref[pl.ds((row - rows) * members, members), :]
        return field_ref[:, row, :]

    for place, row in enumerate((1, 2, rows - 3, rows - 2)):
        wide_ref[row + 1] = kept_ref[place]
    for row in (-1, 0, rows - 1, rows):
        wide_ref[row + 1] = advance(
            weights_of(flow_row(row)), emission, start_row(row - 1), start_row(row), start_row(row + 1)
        )

    def target(s):
        first, last = info_ref[0] == s, info_ref[0] == chips - 1 - s
        return jnp.where(first, 0, chips - 1), jnp.logical_or(first, last)

    second_step(info_ref, target, 1, emission, wide_ref, weight_ref, out_refs)


def source_of(chip, chips, s, k):
    inner = lax.rem(chip + chips - s, chips)
    return jnp.where(chip == 0, k, jnp.where(chip == chips - 1, chips - 1 - k, inner))


def choose_kernel(info_ref, *refs):
    count = (len(refs) - 2) // 2
    other_ref, own_ref = refs[-2:]
    chips = info_ref[3]
    at_edge = jnp.logical_or(info_ref[0] == 0, info_ref[0] == chips - 1)
    for index in range(count):
        for ref, here in ((refs[index], jnp.logical_not(at_edge)), (refs[count + index], at_edge)):

            @pl.when(here)
            def _():
                other_ref[index] = ref[0]
                own_ref[index] = ref[1]


def collect_kernel(order, info_ref, mine_ref, other_ref, *refs):
    chips = len(order)
    both_ref, observed_ref = refs[-2:]
    observed_ref[...] = jnp.where(info_ref[2] == 1, other_ref[...], mine_ref[...])
    chip = info_ref[0]
    at_edge = jnp.logical_or(chip == 0, chip == chips - 1)
    for index, (s, k) in enumerate(order):
        block = source_of(chip, chips, s, k)
        for ref, here in ((refs[index], jnp.logical_not(at_edge)), (refs[chips + index], at_edge)):

            @pl.when(here)
            def _():
                both_ref[0, block] = ref[0]
                both_ref[1, block] = ref[1]


def unpack_kernel(rows_ref, out_ref):
    for row in range(rows_ref.shape[0]):
        out_ref[:, row, :] = rows_ref[row]


def pieces(x, count):
    parts = []
    for _ in range(count - 1):
        part = x.astype(BF16)
        parts.append(part)
        x = x - part.astype(F32)
    return parts + [x.astype(BF16)]


def dot(a, b):
    return lax.dot_general(a, b, (((1,), (0,)), ((), ())), preferred_element_type=F32)


def dot_t(a, b):
    return lax.dot_general(a, b, (((0,), (0,)), ((), ())), preferred_element_type=F32)


def product(a, b):
    total = None
    for i, left in enumerate(a):
        for j, right in enumerate(b):
            if i + j < max(len(a), len(b)):
                term = dot(left, right)
                total = term if total is None else total + term
    return total


def observations(info_ref, observed_ref, width, root):
    slots = observed_ref.shape[1]
    cells, values, scales, count = (observed_ref[pl.ds(i, 1), :] for i in range(4))
    cells = cells.astype(jnp.int32)
    offset = sum((cells >= i * width).astype(jnp.int32) for i in (1, 2)) - 1
    column = cells - (offset + 1) * width
    side = offset * jnp.where(info_ref[2] == 1, -1, 1) * (1 - 2 * info_ref[1])
    cells = column + width * jnp.where(side == 0, 2, jnp.where(side < 0, 0, 1))
    active = lax.broadcasted_iota(jnp.int32, (1, slots), 1) < count.astype(jnp.int32)
    slot_weight = jnp.where(active, scales, 0.0)
    return cells, slot_weight, values, slot_weight * (1.0 / root)


def one_hot(cells, first, count):
    return (
        lax.broadcasted_iota(jnp.int32, (count, cells.shape[1]), 0) + first == cells
    ).astype(F32).astype(BF16)


def mean_of(blocks, members):
    total = blocks[0]
    for block in blocks[1:]:
        total = total + block
    return jnp.sum(total, axis=0, keepdims=True) * (1.0 / members)


def at_cells(row, chosen):
    parts = pieces(jnp.broadcast_to(row, (8, row.shape[1])), 3)
    return (dot(parts[0], chosen) + (dot(parts[1], chosen) + dot(parts[2], chosen)))[:1]


def doubled(x):
    return jnp.concatenate([x, x], axis=1)


def prepare_kernel(
    info_ref, observed_ref, near_ref, far_ref,
    spread_high, spread_low, own_high, own_low, own_part, seen_ref, direction_ref,
    anomaly, high_ref, low_ref,
):
    _, chips, step, width = near_ref.shape
    members = 2 * chips * step
    cells, _, _, scale = observations(info_ref, observed_ref, width, math.sqrt(members - 1))
    chosen = one_hot(cells, width, 2 * width)
    blocks = [pl.ds(index * step, step) for index in range(2 * chips)]
    means = []
    for place in range(2):
        columns = pl.ds(place * width, width)
        rows = [near_ref.at[place, chip] for chip in range(chips)] + [far_ref.at[1 - place, chip] for chip in range(chips)]
        means.append(mean_of([row[...] for row in rows], members))
        for block, row in zip(blocks, rows):
            part = row[...] - means[-1]
            anomaly[block, columns] = part
            high_ref[block, columns] = part.astype(BF16)

    def unit(x):
        return x * (1.0 / jnp.maximum(jnp.max(jnp.abs(x)), 1e-30))

    high = high_ref[...]
    along = lax.dot_general(high[:16], high, (((1,), (1,)), ((), ())), preferred_element_type=F32)
    rows = unit(dot(unit(along).astype(BF16), high))
    weight = jnp.sum(rows * rows[:1], axis=1, keepdims=True)
    weight = weight + jnp.where(jnp.max(jnp.abs(weight)) > 0.0, 0.0, 1.0)
    pattern = unit(jnp.sum(rows * weight, axis=0, keepdims=True))
    total = jnp.zeros((1, 1), F32)
    for block in blocks:
        along = jnp.sum(anomaly[block, :] * pattern, axis=1, keepdims=True)
        total = total + jnp.sum(along * along, axis=0, keepdims=True)
        direction_ref[block, :] = jnp.broadcast_to(along, (step, direction_ref.shape[1]))
    length = lax.rsqrt(jnp.maximum(total, 1e-30))
    taken = None
    for block in blocks:
        direction = direction_ref[block, :] * length
        direction_ref[block, :] = direction
        term = anomaly[block, :] * doubled(doubled(direction))
        taken = term if taken is None else taken + term
    taken = jnp.sum(taken, axis=0, keepdims=True)
    own_part[...] = jnp.broadcast_to(taken[:, width:], (own_part.shape[1], width)).T

    for block in blocks:
        rest = anomaly[block, :] - doubled(doubled(direction_ref[block, :])) * taken
        high, low = pieces(rest, 2)
        high_ref[block, :] = high
        low_ref[block, :] = low
        own = rest[:, width:].T
        own_high[:, block], own_low[:, block] = pieces(own, 2)
    seen_ref[pl.ds(0, 1), :] = at_cells(jnp.concatenate(means, axis=1), chosen)
    seen_ref[pl.ds(1, 1), :] = at_cells(taken, chosen)
    for first in range(0, members, PART):
        rows = pl.ds(first, PART)
        spread = (dot(high_ref[rows, :], chosen) + dot(low_ref[rows, :], chosen)) * scale
        high, low = pieces(spread, 2)
        spread_high[rows, :] = high
        spread_low[rows, :] = low


def square(parts):
    half = parts[0].shape[0] // 2
    upper = product([part[:half] for part in parts], parts)
    lower = product([part[half:] for part in parts], [part[:, half:] for part in parts])
    return upper, jnp.concatenate([upper[:, half:].T, lower], axis=1)


def region_kernel(
    order, groups, info_ref, observed_ref, near_ref, far_ref, high_in, low_in, own_high, own_low, own_part, seen_ref,
    direction_ref, *refs,
):
    outer_refs, (out_ref, spread_high, spread_low, factor, answer) = refs[:-5], refs[-5:]
    _, chips, step, width = near_ref.shape
    members = 2 * chips * step
    slots = observed_ref.shape[1]
    root = math.sqrt(members - 1)
    core = info_ref[1]
    swapped = jnp.logical_or(
        jnp.logical_and(info_ref[0] == 0, core == 0), jnp.logical_and(info_ref[0] == chips - 1, core == 1)
    )
    giver = jnp.where(swapped, info_ref[0], info_ref[0] - 1 + 2 * core)
    cells, slot_weight, values, scale = observations(info_ref, observed_ref, width, root)
    chosen = one_hot(cells, 0, width)

    def outer_block(part, place):
        for pair, group in zip(zip(outer_refs[::2], outer_refs[1::2]), groups):
            if place in group:
                mine, other = pair[part], pair[1 - part]
                at = group.index(place)
                return jnp.where(swapped, other[at], mine[at])

    blocks = [pl.ds(index * step, step) for index in range(2 * chips)]
    arrivals = [
        (part, place, pl.ds(pl.multiple_of((part * chips + source_of(giver, chips, *order[place])) * step, step), step))
        for part in range(2) for place in range(chips)
    ]
    mean = mean_of([outer_block(part, place) for part, place, _ in arrivals], members)
    taken = None
    for part, place, block in arrivals:
        term = (outer_block(part, place) - mean) * doubled(direction_ref[block, :])
        taken = term if taken is None else taken + term
    taken = jnp.sum(taken, axis=0, keepdims=True)
    seen_mean = seen_ref[pl.ds(0, 1), :] + at_cells(mean, chosen)
    common = (seen_ref[pl.ds(1, 1), :] + at_cells(taken, chosen)) * scale
    innovation = slot_weight * (values - seen_mean)
    for part, place, block in arrivals:
        rest = outer_block(part, place) - mean - doubled(direction_ref[block, :]) * taken
        high, low = pieces(rest, 2)
        high, low = pieces((dot(high, chosen) + dot(low, chosen)) * scale, 2)
        spread_high[block, :] = high + high_in[block, :]
        spread_low[block, :] = low + low_in[block, :]

    high, low = spread_high[...], spread_low[...]
    eye = lax.broadcasted_iota(jnp.int32, (slots, slots), 0) == lax.broadcasted_iota(
        jnp.int32, (slots, slots), 1
    )
    turned = high.T
    cross = dot(turned, low)
    factor[...] = dot(turned, high) + (cross + cross.T) + jnp.where(eye, 1.0, 0.0)
    answer[pl.ds(0, width), :] = product([own_high[...], own_low[...]], [high, low])
    answer[pl.ds(width, 8), :] = jnp.where(
        lax.broadcasted_iota(jnp.int32, (8, slots), 0) == 0, jnp.broadcast_to(common, (8, slots)), 0.0
    )
    half = slots // 2
    upper, lower = pl.ds(0, half), pl.ds(half, half)

    def after(bound):
        return bound * bound / (2.0 - bound * bound)

    def size(matrix):
        return jnp.sum(jnp.sum(matrix * matrix, axis=0, keepdims=True))

    def begin(count):
        parts = pieces(factor[...], count)
        top, bottom = square(parts)
        limit = 1.0001 * jnp.sqrt(jnp.sqrt(size(top) + size(bottom)))
        start = 2.0 / (1.0 + limit)
        bound = 1.0 - start
        gain = 2.0 / (2.0 - bound * bound)
        answer[...] = (gain * start) * (2.0 * answer[...] - start * product(pieces(answer[...], count), parts))
        factor[upper, :] = (gain * start) * (2.0 * factor[upper, :] - start * top)
        factor[lower, :] = (gain * start) * (2.0 * factor[lower, :] - start * bottom)
        return after(bound)

    def refine(bound, count):
        gain = 2.0 / (2.0 - bound * bound)
        parts = pieces(factor[...], count)
        answer[...] = gain * (2.0 * answer[...] - product(pieces(answer[...], count), parts))
        top, bottom = square(parts)
        factor[upper, :] = gain * (2.0 * factor[upper, :] - top)
        factor[lower, :] = gain * (2.0 * factor[lower, :] - bottom)
        return after(bound)

    def close(bound, rest):
        gain = 2.0 / (2.0 - bound * bound)
        answer[...] = gain * (answer[...] + dot(answer[...].astype(BF16), rest))
        return gain

    def finish(bound):
        rest = factor[...].astype(BF16)
        gain = close(bound, rest)
        factor[...] = gain * (dot(rest, rest) - jnp.where(eye, 0.5 * bound * bound, 0.0))
        return after(bound)

    large = size(factor[...]) > LARGE * LARGE
    bound = lax.cond(large, lambda: begin(3), lambda: begin(2))
    bound = lax.while_loop(lambda b: jnp.logical_and(b > COARSE, large), lambda b: refine(b, 3), bound)
    bound = lax.while_loop(lambda b: b > COARSE, lambda b: refine(b, 2), bound)
    factor[...] = jnp.where(eye, 1.0, 0.0) - factor[...]
    bound = lax.while_loop(lambda b: b > DONE, finish, bound)
    close(bound, factor[...].astype(BF16))

    solved = answer[pl.ds(0, width), :]
    alone = answer[pl.ds(width, 1), :]
    share = own_part[:, :1] - jnp.sum(solved * common, axis=1, keepdims=True)
    solved = solved + (share / (1.0 + jnp.sum(common * alone, axis=1, keepdims=True))) * alone
    solved = solved.T
    which = lax.broadcasted_iota(jnp.int32, (8, slots), 0)
    sides = jnp.where(which == 0, innovation * (1.0 / root), jnp.where(which == 1, -0.5 * common, 0.0))
    parts = pieces(solved, 3)
    sides = product(pieces(sides, 3), parts)
    shift, along = sides[0:1], sides[1:2]
    halved = [part * jnp.asarray(-0.5, BF16) for part in pieces(solved, 2)]
    for part, ref, place in ((0, near_ref, 1), (1, far_ref, 0)):
        for chip in range(chips):
            block = blocks[part * chips + chip]
            moved = product([spread_high[block, :], spread_low[block, :]], halved)
            moved = moved + doubled(direction_ref[block, :]) * along
            lane = 2 * chip + jnp.abs(core - part)
            lane = lane + info_ref[2] * (2 * chips - 1 - 2 * lane)
            out_ref[lane] = ref[place, chip] + shift + moved


VMEM = pl.BlockSpec(memory_space=pltpu.VMEM)
SMEM = pl.BlockSpec(memory_space=pltpu.SMEM)


def call(kernel, name, out_shape, args, scratch=(), flops=None, aliases={}, limit=8, after=()):
    several = isinstance(out_shape, (list, tuple))
    if after:
        count, inner = len(args), kernel
        args = [*args, *after]
        kernel = lambda *refs: inner(*refs[:count], *refs[len(args) :])
    return pl.pallas_call(
        kernel,
        out_shape=out_shape,
        in_specs=[SMEM] + [VMEM] * (len(args) - 1 - len(after)) + [pl.BlockSpec(memory_space=pl.ANY)] * len(after),
        out_specs=[VMEM] * len(out_shape) if several else VMEM,
        scratch_shapes=scratch,
        input_output_aliases=aliases,
        compiler_params=pltpu.CompilerParams(vmem_limit_bytes=limit * 1024 * 1024),
        cost_estimate=flops and pl.CostEstimate(flops=flops, bytes_accessed=0, transcendentals=0),
        name=name,
    )(*args)


def bfloat(*shape):
    return jax.ShapeDtypeStruct(shape, BF16)


def array(*shape):
    return jax.ShapeDtypeStruct(shape, F32)


def per_device(
    init_field, flow_fields, emission, observed_cell, observed_count, observed_value, observed_scale
):
    step, rows, width = init_field.shape
    slots = observed_cell.shape[1]
    patches, lanes = lax.axis_size("patch"), lax.axis_size("member")
    chips = lanes // 2
    members = lanes * step
    axes = ("patch", "member")
    count = patches * lanes
    patch, lane = lax.axis_index("patch"), lax.axis_index("member")
    info = jnp.stack([lane // 2, lane % 2, patch % 2, jnp.int32(chips)]).astype(jnp.int32)

    edge = array(STEPS * step + 8, width)
    tail, head = pl.pallas_call(
        pack_kernel, out_shape=(edge, edge), in_specs=[VMEM] * 2, out_specs=(VMEM, VMEM), name="pack",
    )(init_field, flow_fields)
    before = lax.ppermute(tail, "patch", [(i, i + 1) for i in range(patches - 1)])
    after = lax.ppermute(head, "patch", [(i + 1, i) for i in range(patches - 1)])

    mine = jnp.concatenate(
        [
            observed_cell.astype(F32),
            observed_value,
            observed_scale,
            jnp.broadcast_to(observed_count.astype(F32)[:, None], observed_cell.shape),
        ]
        * 2,
        axis=0,
    )

    def along(piece, s, ends):
        if ends:
            hops = [(s, 0), (chips - 1 - s, chips - 1)]
        else:
            hops = [(chip, (chip + s) % chips) for chip in range(chips)]
            hops = [(chip, to) for chip, to in hops if 0 < to < chips - 1]
        return lax.ppermute(piece, "member", [(2 * a + core, 2 * b + core) for a, b in hops for core in range(2)])

    pair = array(2, step, width)
    wide = [pltpu.VMEM((rows + 2, step, width), F32), pltpu.VMEM((rows, 8, width), F32)]
    args = [info, init_field, flow_fields, emission[None, :]]
    kept, *inner = call(inner_kernel, "inner", [array(4, step, width)] + [pair] * chips, args, wide)
    order = [s for near in range(chips // 2, 0, -1) for s in sorted({near, chips - near})]
    got_inner = {s: along(inner[s], s, False) for s in order}
    outer = call(edge_kernel, "edge", [pair] * chips, args + [kept, before, after], wide)
    mine, _ = lax.optimization_barrier((mine, outer[0]))
    other = lax.ppermute(
        mine, axes,
        [(p * lanes + i, p * lanes + lanes - 1 - i) for p in range(1, patches, 2) for i in range(lanes)],
    )
    got_outer = {s: along(outer[s], s, True) for s in range(chips - 1, 0, -1)}
    got_inner[0], got_outer[0] = inner[0], outer[0]
    order = list(zip(order + [0], range(chips - 1, -1, -1)))
    pieces_in = [got_inner[s] for s, _ in order] + [got_outer[k] for _, k in order]
    def device(p, chip, core):
        return p * lanes + 2 * chip + core

    first_pairs, second_pairs, siblings = [], [], []
    for p in range(patches):
        for chip in range(chips):
            siblings += [(device(p, chip, core), device(p, chip, 1 - core)) for core in range(2)]
            for core, away in ((0, 1), (1, -1)):
                if 0 <= chip + away < chips:
                    to_first, to_second = device(p, chip + away, core), device(p, chip + away, core)
                    to = p
                else:
                    to = p + 1 if (p % 2 == 0) == (away == 1) else p - 1
                    if not 0 <= to < patches:
                        continue
                    to_first = to_second = device(to, chip, 1 - core)
                first_pairs.append((device(p, chip, core), to_first))
                second_pairs.append((device(p, chip, 1 - core), to_second))
    groups = [[chips - 1, *range(chips - 3)], [chips - 3, chips - 2]]
    outer_rows = []
    for group in groups:
        got = [pieces_in[place] for place in group] + [pieces_in[chips + place] for place in group]
        row = array(len(group), step, width)
        ahead = pieces_in[: chips - 1] if group is groups[0] else ()
        first, second = call(choose_kernel, "choose", [row, row], [info] + got, after=ahead)
        outer_rows += [lax.ppermute(first, axes, first_pairs), lax.ppermute(second, axes, second_pairs)]
    near, observed = call(
        functools.partial(collect_kernel, order), "collect", [array(2, chips, step, width), array(8, slots)],
        [info, mine, other] + pieces_in, after=outer_rows[:2],
    )
    far = lax.ppermute(near, axes, siblings)

    split = [pltpu.VMEM((members, slots), BF16)] * 2
    prepared = call(
        prepare_kernel, "prepare",
        [bfloat(members, slots)] * 2 + [bfloat(width, members)] * 2
        + [array(width, width // 2), array(8, slots), array(members, width // 2)],
        [info, observed, near, far],
        [pltpu.VMEM((members, 2 * width), F32)] + [pltpu.VMEM((members, 2 * width), BF16)] * 2,
        flops=8 * members * slots * width, limit=20,
    )
    analysed = call(
        functools.partial(region_kernel, order, groups), "region", array(lanes, step, width),
        [info, observed, near, far, *prepared, *outer_rows],
        split + [pltpu.VMEM((slots, slots), F32), pltpu.VMEM((width + 8, slots), F32)],
        limit=24,
    )
    lines = [[p * lanes + (lanes - 1 - i if p % 2 else i) for i in range(lanes)] for p in range(patches)]
    returned = lax.all_to_all(
        analysed, axes, split_axis=0, concat_axis=0, tiled=True, axis_index_groups=lines
    )
    return pl.pallas_call(
        unpack_kernel, out_shape=array(step, rows, width), in_specs=[VMEM], out_specs=VMEM, name="unpack",
        compiler_params=pltpu.CompilerParams(vmem_limit_bytes=48 * 1024 * 1024),
    )(returned)


def solution(mesh):
    return jax.shard_map(
        per_device,
        mesh=mesh,
        in_specs=(
            P("member", "patch", None),
            P(None, "patch", None),
            P("member"),
            P(("patch", "member"), None),
            P(("patch", "member")),
            P(("patch", "member"), None),
            P(("patch", "member"), None),
        ),
        out_specs=P("member", "patch", None),
        check_vma=False,
    )
```

```python
import functools
import math

import jax
import jax.numpy as jnp
from jax import lax
from jax.experimental import pallas as pl
from jax.experimental.pallas import tpu as pltpu
from jax.sharding import PartitionSpec as P

STEPS = 2
COARSE = 0.2
DONE = 0.01
LARGE = 2e4
PART = 256
F32 = jnp.float32
BF16 = jnp.bfloat16


def pack_kernel(field_ref, flow_ref, tail_ref, head_ref):
    members, rows, width = field_ref.shape
    for out_ref, first, edge in ((tail_ref, rows - STEPS, rows - 1), (head_ref, 0, 0)):
        for place in range(STEPS):
            out_ref[pl.ds(place * members, members), :] = field_ref[:, first + place, :]
        out_ref[pl.ds(STEPS * members, 8), :] = jnp.concatenate([flow_ref[:, edge, :]] * 2, axis=0)


def weights_of(flow):
    row_flow, col_flow, kept, source = flow[0:1], flow[1:2], 1.0 - flow[2:3], flow[3:4]
    behind, ahead = jnp.maximum(row_flow, 0.0), -jnp.minimum(row_flow, 0.0)
    left, right = jnp.maximum(col_flow, 0.0), -jnp.minimum(col_flow, 0.0)
    stays = 1.0 - behind - ahead - left - right
    return [kept * stays, kept * behind, kept * ahead, kept * left, kept * right, source]


def advance(weights, emission, behind, field, ahead):
    width = field.shape[1]
    return (
        weights[0] * field
        + weights[1] * behind
        + weights[2] * ahead
        + weights[3] * pltpu.roll(field, 1, 1)
        + weights[4] * pltpu.roll(field, width - 1, 1)
        + emission * weights[5]
    )


def emission_column(emission_ref):
    members = emission_ref.shape[1]
    diagonal = lax.broadcasted_iota(jnp.int32, (members, members), 0) == lax.broadcasted_iota(
        jnp.int32, (members, members), 1
    )
    return jnp.sum(jnp.where(diagonal, emission_ref[...], 0.0), axis=1, keepdims=True)


def second_step(info_ref, target, shift, emission, wide_ref, weight_ref, out_refs):
    rows = weight_ref.shape[0]
    for s, out_ref in enumerate(out_refs):
        chip, wanted = target(s)

        @pl.when(wanted)
        def _():
            for place in range(2):
                position = 2 * chip + jnp.abs(info_ref[1] - 1 + place)
                row = position + info_ref[2] * (rows - 1 - 2 * position)
                weights = weight_ref[row]
                at = row + shift
                out_ref[place] = advance(
                    [weights[i : i + 1] for i in range(6)],
                    emission, wide_ref[at - 1], wide_ref[at], wide_ref[at + 1],
                )


def store_weights(flow_ref, weight_ref, rows):
    for row in rows:
        for i, weight in enumerate(weights_of(flow_ref[:, row, :])):
            weight_ref[row, pl.ds(i, 1), :] = weight


def inner_kernel(info_ref, field_ref, flow_ref, emission_ref, kept_ref, *refs):
    out_refs, (wide_ref, weight_ref) = refs[:-2], refs[-2:]
    rows = field_ref.shape[1]
    chips = len(out_refs)
    emission = emission_column(emission_ref)
    store_weights(flow_ref, weight_ref, range(2, rows - 2))
    for row in range(1, rows - 1):
        wide_ref[row] = advance(
            weights_of(flow_ref[:, row, :]), emission,
            field_ref[:, row - 1, :], field_ref[:, row, :], field_ref[:, row + 1, :],
        )
    for place, row in enumerate((1, 2, rows - 3, rows - 2)):
        kept_ref[place] = wide_ref[row]

    def target(s):
        chip = lax.rem(info_ref[0] + s, chips)
        return chip, jnp.logical_and(chip > 0, chip < chips - 1)

    second_step(info_ref, target, 0, emission, wide_ref, weight_ref, out_refs)


def edge_kernel(info_ref, field_ref, flow_ref, emission_ref, kept_ref, before_ref, after_ref, *refs):
    out_refs, (wide_ref, weight_ref) = refs[:-2], refs[-2:]
    members, rows, width = field_ref.shape
    chips = len(out_refs)
    emission = emission_column(emission_ref)
    store_weights(flow_ref, weight_ref, (0, 1, rows - 2, rows - 1))

    def flow_row(row):
        if row < 0:
            return before_ref[pl.ds(STEPS * members, 4), :]
        if row >= rows:
            return after_ref[pl.ds(STEPS * members, 4), :]
        return flow_ref[:, row, :]

    def start_row(row):
        if row < 0:
            return before_ref[pl.ds((row + STEPS) * members, members), :]
        if row >= rows:
            return after_ref[pl.ds((row - rows) * members, members), :]
        return field_ref[:, row, :]

    for place, row in enumerate((1, 2, rows - 3, rows - 2)):
        wide_ref[row + 1] = kept_ref[place]
    for row in (-1, 0, rows - 1, rows):
        wide_ref[row + 1] = advance(
            weights_of(flow_row(row)), emission, start_row(row - 1), start_row(row), start_row(row + 1)
        )

    def target(s):
        first, last = info_ref[0] == s, info_ref[0] == chips - 1 - s
        return jnp.where(first, 0, chips - 1), jnp.logical_or(first, last)

    second_step(info_ref, target, 1, emission, wide_ref, weight_ref, out_refs)


def source_of(chip, chips, s, k):
    inner = lax.rem(chip + chips - s, chips)
    return jnp.where(chip == 0, k, jnp.where(chip == chips - 1, chips - 1 - k, inner))


def choose_kernel(info_ref, *refs):
    count = (len(refs) - 2) // 2
    other_ref, own_ref = refs[-2:]
    chips = info_ref[3]
    at_edge = jnp.logical_or(info_ref[0] == 0, info_ref[0] == chips - 1)
    for index in range(count):
        for ref, here in ((refs[index], jnp.logical_not(at_edge)), (refs[count + index], at_edge)):

            @pl.when(here)
            def _():
                other_ref[index] = ref[0]
                own_ref[index] = ref[1]


def collect_kernel(order, late, info_ref, mine_ref, other_ref, *refs):
    chips = len(order)
    both_ref, late_other, late_own, observed_ref = refs[-4:]
    observed_ref[...] = jnp.where(info_ref[2] == 1, other_ref[...], mine_ref[...])
    chip = info_ref[0]
    at_edge = jnp.logical_or(chip == 0, chip == chips - 1)
    for index, (s, k) in enumerate(order):
        block = source_of(chip, chips, s, k)
        for ref, here in ((refs[index], jnp.logical_not(at_edge)), (refs[chips + index], at_edge)):

            @pl.when(here)
            def _():
                both_ref[0, block] = ref[0]
                both_ref[1, block] = ref[1]
                if index in late:
                    late_other[late.index(index)] = ref[0]
                    late_own[late.index(index)] = ref[1]


def unpack_kernel(rows_ref, out_ref):
    for row in range(rows_ref.shape[0]):
        out_ref[:, row, :] = rows_ref[row]


def pieces(x, count):
    parts = []
    for _ in range(count - 1):
        part = x.astype(BF16)
        parts.append(part)
        x = x - part.astype(F32)
    return parts + [x.astype(BF16)]


def dot(a, b):
    return lax.dot_general(a, b, (((1,), (0,)), ((), ())), preferred_element_type=F32)


def dot_t(a, b):
    return lax.dot_general(a, b, (((0,), (0,)), ((), ())), preferred_element_type=F32)


def product(a, b):
    total = None
    for i, left in enumerate(a):
        for j, right in enumerate(b):
            if i + j < max(len(a), len(b)):
                term = dot(left, right)
                total = term if total is None else total + term
    return total


def observations(info_ref, observed_ref, width, root):
    slots = observed_ref.shape[1]
    cells, values, scales, count = (observed_ref[pl.ds(i, 1), :] for i in range(4))
    cells = cells.astype(jnp.int32)
    offset = sum((cells >= i * width).astype(jnp.int32) for i in (1, 2)) - 1
    column = cells - (offset + 1) * width
    side = offset * jnp.where(info_ref[2] == 1, -1, 1) * (1 - 2 * info_ref[1])
    cells = column + width * jnp.where(side == 0, 2, jnp.where(side < 0, 0, 1))
    active = lax.broadcasted_iota(jnp.int32, (1, slots), 1) < count.astype(jnp.int32)
    slot_weight = jnp.where(active, scales, 0.0)
    return cells, slot_weight, values, slot_weight * (1.0 / root)


def one_hot(cells, first, count):
    return (
        lax.broadcasted_iota(jnp.int32, (count, cells.shape[1]), 0) + first == cells
    ).astype(F32).astype(BF16)


def mean_of(blocks, members):
    total = blocks[0]
    for block in blocks[1:]:
        total = total + block
    return jnp.sum(total, axis=0, keepdims=True) * (1.0 / members)


def at_cells(row, chosen):
    parts = pieces(jnp.broadcast_to(row, (8, row.shape[1])), 3)
    return (dot(parts[0], chosen) + (dot(parts[1], chosen) + dot(parts[2], chosen)))[:1]


def doubled(x):
    return jnp.concatenate([x, x], axis=1)


def prepare_kernel(
    info_ref, observed_ref, near_ref, far_ref,
    spread_high, spread_low, own_high, own_low, own_part, seen_ref, direction_ref,
    anomaly, high_ref, low_ref,
):
    _, chips, step, width = near_ref.shape
    members = 2 * chips * step
    cells, _, _, scale = observations(info_ref, observed_ref, width, math.sqrt(members - 1))
    chosen = one_hot(cells, width, 2 * width)
    blocks = [pl.ds(index * step, step) for index in range(2 * chips)]
    means = []
    for place in range(2):
        columns = pl.ds(place * width, width)
        rows = [near_ref.at[place, chip] for chip in range(chips)] + [far_ref.at[1 - place, chip] for chip in range(chips)]
        means.append(mean_of([row[...] for row in rows], members))
        for block, row in zip(blocks, rows):
            part = row[...] - means[-1]
            anomaly[block, columns] = part
            high_ref[block, columns] = part.astype(BF16)

    def unit(x):
        return x * (1.0 / jnp.maximum(jnp.max(jnp.abs(x)), 1e-30))

    high = high_ref[...]
    along = lax.dot_general(high[:16], high, (((1,), (1,)), ((), ())), preferred_element_type=F32)
    rows = unit(dot(unit(along).astype(BF16), high))
    weight = jnp.sum(rows * rows[:1], axis=1, keepdims=True)
    weight = weight + jnp.where(jnp.max(jnp.abs(weight)) > 0.0, 0.0, 1.0)
    pattern = unit(jnp.sum(rows * weight, axis=0, keepdims=True))
    total = jnp.zeros((1, 1), F32)
    for block in blocks:
        along = jnp.sum(anomaly[block, :] * pattern, axis=1, keepdims=True)
        total = total + jnp.sum(along * along, axis=0, keepdims=True)
        direction_ref[block, :] = jnp.broadcast_to(along, (step, direction_ref.shape[1]))
    length = lax.rsqrt(jnp.maximum(total, 1e-30))
    taken = None
    for block in blocks:
        direction = direction_ref[block, :] * length
        direction_ref[block, :] = direction
        term = anomaly[block, :] * doubled(doubled(direction))
        taken = term if taken is None else taken + term
    taken = jnp.sum(taken, axis=0, keepdims=True)
    own_part[...] = jnp.broadcast_to(taken[:, width:], (own_part.shape[1], width)).T

    for block in blocks:
        rest = anomaly[block, :] - doubled(doubled(direction_ref[block, :])) * taken
        high, low = pieces(rest, 2)
        high_ref[block, :] = high
        low_ref[block, :] = low
        own = rest[:, width:].T
        own_high[:, block], own_low[:, block] = pieces(own, 2)
    seen_ref[pl.ds(0, 1), :] = at_cells(jnp.concatenate(means, axis=1), chosen)
    seen_ref[pl.ds(1, 1), :] = at_cells(taken, chosen)
    for first in range(0, members, PART):
        rows = pl.ds(first, PART)
        spread = (dot(high_ref[rows, :], chosen) + dot(low_ref[rows, :], chosen)) * scale
        high, low = pieces(spread, 2)
        spread_high[rows, :] = high
        spread_low[rows, :] = low


def square(parts):
    half = parts[0].shape[0] // 2
    upper = product([part[:half] for part in parts], parts)
    lower = product([part[half:] for part in parts], [part[:, half:] for part in parts])
    return upper, jnp.concatenate([upper[:, half:].T, lower], axis=1)


def region_kernel(
    order, groups, info_ref, observed_ref, near_ref, far_ref, high_in, low_in, own_high, own_low, own_part, seen_ref,
    direction_ref, *refs,
):
    outer_refs, (out_ref, spread_high, spread_low, factor, answer) = refs[:-5], refs[-5:]
    _, chips, step, width = near_ref.shape
    members = 2 * chips * step
    slots = observed_ref.shape[1]
    root = math.sqrt(members - 1)
    core = info_ref[1]
    swapped = jnp.logical_or(
        jnp.logical_and(info_ref[0] == 0, core == 0), jnp.logical_and(info_ref[0] == chips - 1, core == 1)
    )
    giver = jnp.where(swapped, info_ref[0], info_ref[0] - 1 + 2 * core)
    cells, slot_weight, values, scale = observations(info_ref, observed_ref, width, root)
    chosen = one_hot(cells, 0, width)

    def outer_block(part, place):
        for pair, group in zip(zip(outer_refs[::2], outer_refs[1::2]), groups):
            if place in group:
                mine, other = pair[part], pair[1 - part]
                at = group.index(place)
                return jnp.where(swapped, other[at], mine[at])

    blocks = [pl.ds(index * step, step) for index in range(2 * chips)]
    arrivals = [
        (part, place, pl.ds(pl.multiple_of((part * chips + source_of(giver, chips, *order[place])) * step, step), step))
        for part in range(2) for place in range(chips)
    ]
    mean = mean_of([outer_block(part, place) for part, place, _ in arrivals], members)
    taken = None
    for part, place, block in arrivals:
        term = (outer_block(part, place) - mean) * doubled(direction_ref[block, :])
        taken = term if taken is None else taken + term
    taken = jnp.sum(taken, axis=0, keepdims=True)
    seen_mean = seen_ref[pl.ds(0, 1), :] + at_cells(mean, chosen)
    common = (seen_ref[pl.ds(1, 1), :] + at_cells(taken, chosen)) * scale
    innovation = slot_weight * (values - seen_mean)
    for part, place, block in arrivals:
        rest = outer_block(part, place) - mean - doubled(direction_ref[block, :]) * taken
        high, low = pieces(rest, 2)
        high, low = pieces((dot(high, chosen) + dot(low, chosen)) * scale, 2)
        spread_high[block, :] = high + high_in[block, :]
        spread_low[block, :] = low + low_in[block, :]

    high, low = spread_high[...], spread_low[...]
    eye = lax.broadcasted_iota(jnp.int32, (slots, slots), 0) == lax.broadcasted_iota(
        jnp.int32, (slots, slots), 1
    )
    turned = high.T
    cross = dot(turned, low)
    factor[...] = dot(turned, high) + (cross + cross.T) + jnp.where(eye, 1.0, 0.0)
    answer[pl.ds(0, width), :] = product([own_high[...], own_low[...]], [high, low])
    answer[pl.ds(width, 8), :] = jnp.where(
        lax.broadcasted_iota(jnp.int32, (8, slots), 0) == 0, jnp.broadcast_to(common, (8, slots)), 0.0
    )
    half = slots // 2
    upper, lower = pl.ds(0, half), pl.ds(half, half)

    def after(bound):
        return bound * bound / (2.0 - bound * bound)

    def size(matrix):
        return jnp.sum(jnp.sum(matrix * matrix, axis=0, keepdims=True))

    def begin(count):
        parts = pieces(factor[...], count)
        top, bottom = square(parts)
        limit = 1.0001 * jnp.sqrt(jnp.sqrt(size(top) + size(bottom)))
        start = 2.0 / (1.0 + limit)
        bound = 1.0 - start
        gain = 2.0 / (2.0 - bound * bound)
        answer[...] = (gain * start) * (2.0 * answer[...] - start * product(pieces(answer[...], count), parts))
        factor[upper, :] = (gain * start) * (2.0 * factor[upper, :] - start * top)
        factor[lower, :] = (gain * start) * (2.0 * factor[lower, :] - start * bottom)
        return after(bound)

    def refine(bound, count):
        gain = 2.0 / (2.0 - bound * bound)
        parts = pieces(factor[...], count)
        answer[...] = gain * (2.0 * answer[...] - product(pieces(answer[...], count), parts))
        top, bottom = square(parts)
        factor[upper, :] = gain * (2.0 * factor[upper, :] - top)
        factor[lower, :] = gain * (2.0 * factor[lower, :] - bottom)
        return after(bound)

    def close(bound, rest):
        gain = 2.0 / (2.0 - bound * bound)
        answer[...] = gain * (answer[...] + dot(answer[...].astype(BF16), rest))
        return gain

    def finish(bound):
        rest = factor[...].astype(BF16)
        gain = close(bound, rest)
        factor[...] = gain * (dot(rest, rest) - jnp.where(eye, 0.5 * bound * bound, 0.0))
        return after(bound)

    large = size(factor[...]) > LARGE * LARGE
    bound = lax.cond(large, lambda: begin(3), lambda: begin(2))
    bound = lax.while_loop(lambda b: jnp.logical_and(b > COARSE, large), lambda b: refine(b, 3), bound)
    bound = lax.while_loop(lambda b: b > COARSE, lambda b: refine(b, 2), bound)
    factor[...] = jnp.where(eye, 1.0, 0.0) - factor[...]
    bound = lax.while_loop(lambda b: b > DONE, finish, bound)
    close(bound, factor[...].astype(BF16))

    solved = answer[pl.ds(0, width), :]
    alone = answer[pl.ds(width, 1), :]
    share = own_part[:, :1] - jnp.sum(solved * common, axis=1, keepdims=True)
    solved = solved + (share / (1.0 + jnp.sum(common * alone, axis=1, keepdims=True))) * alone
    solved = solved.T
    which = lax.broadcasted_iota(jnp.int32, (8, slots), 0)
    sides = jnp.where(which == 0, innovation * (1.0 / root), jnp.where(which == 1, -0.5 * common, 0.0))
    parts = pieces(solved, 3)
    sides = product(pieces(sides, 3), parts)
    shift, along = sides[0:1], sides[1:2]
    halved = [part * jnp.asarray(-0.5, BF16) for part in pieces(solved, 2)]
    for part, ref, place in ((0, near_ref, 1), (1, far_ref, 0)):
        for chip in range(chips):
            block = blocks[part * chips + chip]
            moved = product([spread_high[block, :], spread_low[block, :]], halved)
            moved = moved + doubled(direction_ref[block, :]) * along
            lane = 2 * chip + jnp.abs(core - part)
            lane = lane + info_ref[2] * (2 * chips - 1 - 2 * lane)
            out_ref[lane] = ref[place, chip] + shift + moved


VMEM = pl.BlockSpec(memory_space=pltpu.VMEM)
SMEM = pl.BlockSpec(memory_space=pltpu.SMEM)


def call(kernel, name, out_shape, args, scratch=(), flops=None, aliases={}, limit=8, after=()):
    several = isinstance(out_shape, (list, tuple))
    if after:
        count, inner = len(args), kernel
        args = [*args, *after]
        kernel = lambda *refs: inner(*refs[:count], *refs[len(args) :])
    return pl.pallas_call(
        kernel,
        out_shape=out_shape,
        in_specs=[SMEM] + [VMEM] * (len(args) - 1 - len(after)) + [pl.BlockSpec(memory_space=pl.ANY)] * len(after),
        out_specs=[VMEM] * len(out_shape) if several else VMEM,
        scratch_shapes=scratch,
        input_output_aliases=aliases,
        compiler_params=pltpu.CompilerParams(vmem_limit_bytes=limit * 1024 * 1024),
        cost_estimate=flops and pl.CostEstimate(flops=flops, bytes_accessed=0, transcendentals=0),
        name=name,
    )(*args)


def bfloat(*shape):
    return jax.ShapeDtypeStruct(shape, BF16)


def array(*shape):
    return jax.ShapeDtypeStruct(shape, F32)


def per_device(
    init_field, flow_fields, emission, observed_cell, observed_count, observed_value, observed_scale
):
    step, rows, width = init_field.shape
    slots = observed_cell.shape[1]
    patches, lanes = lax.axis_size("patch"), lax.axis_size("member")
    chips = lanes // 2
    members = lanes * step
    axes = ("patch", "member")
    count = patches * lanes
    patch, lane = lax.axis_index("patch"), lax.axis_index("member")
    info = jnp.stack([lane // 2, lane % 2, patch % 2, jnp.int32(chips)]).astype(jnp.int32)

    edge = array(STEPS * step + 8, width)
    tail, head = pl.pallas_call(
        pack_kernel, out_shape=(edge, edge), in_specs=[VMEM] * 2, out_specs=(VMEM, VMEM), name="pack",
    )(init_field, flow_fields)
    before = lax.ppermute(tail, "patch", [(i, i + 1) for i in range(patches - 1)])
    after = lax.ppermute(head, "patch", [(i + 1, i) for i in range(patches - 1)])

    mine = jnp.concatenate(
        [
            observed_cell.astype(F32),
            observed_value,
            observed_scale,
            jnp.broadcast_to(observed_count.astype(F32)[:, None], observed_cell.shape),
        ]
        * 2,
        axis=0,
    )

    def along(piece, s, ends):
        if ends:
            hops = [(s, 0), (chips - 1 - s, chips - 1)]
        else:
            hops = [(chip, (chip + s) % chips) for chip in range(chips)]
            hops = [(chip, to) for chip, to in hops if 0 < to < chips - 1]
        return lax.ppermute(piece, "member", [(2 * a + core, 2 * b + core) for a, b in hops for core in range(2)])

    pair = array(2, step, width)
    wide = [pltpu.VMEM((rows + 2, step, width), F32), pltpu.VMEM((rows, 8, width), F32)]
    args = [info, init_field, flow_fields, emission[None, :]]
    kept, *inner = call(inner_kernel, "inner", [array(4, step, width)] + [pair] * chips, args, wide)
    order = list(range(1, chips))
    got_inner = {s: along(inner[s], s, False) for s in order}
    outer = call(edge_kernel, "edge", [pair] * chips, args + [kept, before, after], wide)
    mine, _ = lax.optimization_barrier((mine, outer[0]))
    other = lax.ppermute(
        mine, axes,
        [(p * lanes + i, p * lanes + lanes - 1 - i) for p in range(1, patches, 2) for i in range(lanes)],
    )
    got_outer = {s: along(outer[s], s, True) for s in order}
    got_inner[0], got_outer[0] = inner[0], outer[0]
    order = [(s, s) for s in range(chips)]
    pieces_in = [got_inner[s] for s, _ in order] + [got_outer[k] for _, k in order]
    def device(p, chip, core):
        return p * lanes + 2 * chip + core

    first_pairs, second_pairs, siblings = [], [], []
    for p in range(patches):
        for chip in range(chips):
            siblings += [(device(p, chip, core), device(p, chip, 1 - core)) for core in range(2)]
            for core, away in ((0, 1), (1, -1)):
                if 0 <= chip + away < chips:
                    to_first, to_second = device(p, chip + away, core), device(p, chip + away, core)
                    to = p
                else:
                    to = p + 1 if (p % 2 == 0) == (away == 1) else p - 1
                    if not 0 <= to < patches:
                        continue
                    to_first = to_second = device(to, chip, 1 - core)
                first_pairs.append((device(p, chip, core), to_first))
                second_pairs.append((device(p, chip, 1 - core), to_second))
    groups = [[0], list(range(1, chips))]
    early, late = groups
    got = [pieces_in[place] for place in early] + [pieces_in[chips + place] for place in early]
    row = array(len(early), step, width)
    early_rows = call(choose_kernel, "choose", [row, row], [info] + got)
    outer_rows = [lax.ppermute(early_rows[0], axes, first_pairs), lax.ppermute(early_rows[1], axes, second_pairs)]
    row = array(len(late), step, width)
    near, *late_rows, observed = call(
        functools.partial(collect_kernel, order, late), "collect",
        [array(2, chips, step, width), row, row, array(8, slots)], [info, mine, other] + pieces_in, after=outer_rows,
    )
    outer_rows += [lax.ppermute(late_rows[0], axes, first_pairs), lax.ppermute(late_rows[1], axes, second_pairs)]
    far = lax.ppermute(near, axes, siblings)

    split = [pltpu.VMEM((members, slots), BF16)] * 2
    prepared = call(
        prepare_kernel, "prepare",
        [bfloat(members, slots)] * 2 + [bfloat(width, members)] * 2
        + [array(width, width // 2), array(8, slots), array(members, width // 2)],
        [info, observed, near, far],
        [pltpu.VMEM((members, 2 * width), F32)] + [pltpu.VMEM((members, 2 * width), BF16)] * 2,
        flops=8 * members * slots * width, limit=20,
    )
    analysed = call(
        functools.partial(region_kernel, order, groups), "region", array(lanes, step, width),
        [info, observed, near, far, *prepared, *outer_rows],
        split + [pltpu.VMEM((slots, slots), F32), pltpu.VMEM((width + 8, slots), F32)],
        limit=24,
    )
    lines = [[p * lanes + (lanes - 1 - i if p % 2 else i) for i in range(lanes)] for p in range(patches)]
    returned = lax.all_to_all(
        analysed, axes, split_axis=0, concat_axis=0, tiled=True, axis_index_groups=lines
    )
    return pl.pallas_call(
        unpack_kernel, out_shape=array(step, rows, width), in_specs=[VMEM], out_specs=VMEM, name="unpack",
        compiler_params=pltpu.CompilerParams(vmem_limit_bytes=48 * 1024 * 1024),
    )(returned)


def solution(mesh):
    return jax.shard_map(
        per_device,
        mesh=mesh,
        in_specs=(
            P("member", "patch", None),
            P(None, "patch", None),
            P("member"),
            P(("patch", "member"), None),
            P(("patch", "member")),
            P(("patch", "member"), None),
            P(("patch", "member"), None),
        ),
        out_specs=P("member", "patch", None),
        check_vma=False,
    )
```

```python
import functools
import math

import jax
import jax.numpy as jnp
from jax import lax
from jax.experimental import pallas as pl
from jax.experimental.pallas import tpu as pltpu
from jax.sharding import PartitionSpec as P

STEPS = 2
COARSE = 0.2
DONE = 0.01
LARGE = 2e4
PART = 256
F32 = jnp.float32
BF16 = jnp.bfloat16


def pack_kernel(info_ref, field_hbm, flow_hbm, emission_hbm, first_ref, second_ref, flow_ref, emission_ref,
                field_ref, member_ref, sems):
    members, rows, width = field_ref.shape
    moves = [
        pltpu.make_async_copy(source, target, sems.at[i])
        for i, (source, target) in enumerate(
            ((field_hbm, field_ref), (flow_hbm, flow_ref), (emission_hbm, member_ref))
        )
    ]
    for move in moves:
        move.start()
    for move in moves[1:]:
        move.wait()
    diagonal = lax.broadcasted_iota(jnp.int32, (members, members), 0) == lax.broadcasted_iota(
        jnp.int32, (members, members), 1
    )
    column = jnp.sum(jnp.where(diagonal, member_ref[...], 0.0), axis=1, keepdims=True)
    emission_ref[...] = jnp.broadcast_to(column, emission_ref.shape)
    moves[0].wait()
    even = info_ref[2] == 0
    for place in range(STEPS):
        tail, head = field_ref[:, rows - STEPS + place, :], field_ref[:, place, :]
        at = pl.ds(place * members, members)
        first_ref[at, :] = jnp.where(even, tail, head)
        second_ref[at, :] = jnp.where(even, head, tail)
    tail, head = flow_ref[:, rows - 1, :], flow_ref[:, 0, :]
    at = pl.ds(STEPS * members, 8)
    first_ref[at, :] = jnp.concatenate([jnp.where(even, tail, head)] * 2, axis=0)
    second_ref[at, :] = jnp.concatenate([jnp.where(even, head, tail)] * 2, axis=0)


def doubled(x):
    return jnp.concatenate([x, x], axis=1)


def weights_of(flow):
    row_flow, col_flow, kept, source = flow[0:1], flow[1:2], 1.0 - flow[2:3], flow[3:4]
    behind, ahead = jnp.maximum(row_flow, 0.0), -jnp.minimum(row_flow, 0.0)
    left, right = jnp.maximum(col_flow, 0.0), -jnp.minimum(col_flow, 0.0)
    stays = 1.0 - behind - ahead - left - right
    return [kept * stays, kept * behind, kept * ahead, kept * left, kept * right, source]


def advance(weights, emission, behind, field, ahead):
    width = field.shape[1]
    return (
        weights[0] * field
        + weights[1] * behind
        + weights[2] * ahead
        + weights[3] * pltpu.roll(field, 1, 1)
        + weights[4] * pltpu.roll(field, width - 1, 1)
        + emission * weights[5]
    )


def inner_kernel(targets, info_ref, field_ref, flow_ref, emission_ref, kept_ref, *refs):
    out_refs, (wide_ref, weight_ref) = refs[:-2], refs[-2:]
    rows = field_ref.shape[1]
    emission = doubled(emission_ref[...])
    for row in range(1, rows - 1):
        weights = weights_of(flow_ref[:, row, :])
        for i, weight in enumerate(weights):
            weight_ref[row, pl.ds(i, 1), :] = weight
        wide_ref[row] = advance(
            weights, emission, field_ref[:, row - 1, :], field_ref[:, row, :], field_ref[:, row + 1, :]
        )
    for place, row in enumerate((1, 2, rows - 3, rows - 2)):
        kept_ref[place] = wide_ref[row]
    for out_ref, hops in zip(out_refs, targets):
        chip = sum(jnp.where(info_ref[0] == source, to, 0) for source, to in hops)

        @pl.when(chip > 0)
        def _():
            for place in range(2):
                position = 2 * chip + jnp.abs(info_ref[1] - 1 + place)
                row = position + info_ref[2] * (rows - 1 - 2 * position)
                weights = weight_ref[row]
                out_ref[place] = advance(
                    [weights[i : i + 1] for i in range(6)],
                    emission, wide_ref[row - 1], wide_ref[row], wide_ref[row + 1],
                )


def end_rows(info_ref, last, field_ref, flow_ref, emission_ref, kept_ref, halo_ref, out_ref):
    members, rows, width = field_ref.shape
    emission = doubled(emission_ref[...])

    def halo_row(place):
        return halo_ref[pl.ds(place * members, members), :]

    halo_weights = weights_of(halo_ref[pl.ds(STEPS * members, 4), :])
    for parity in range(2):

        @pl.when(info_ref[2] == parity)
        def _():
            if parity == last:
                end, near, outside, beyond = 0, 1, halo_row(1), halo_row(0)
                inside, further = kept_ref[0], kept_ref[1]
            else:
                end, near, outside, beyond = rows - 1, rows - 2, halo_row(0), halo_row(1)
                inside, further = kept_ref[3], kept_ref[2]

            def ordered(weights, outer, own, inner):
                behind, ahead = (outer, inner) if end == 0 else (inner, outer)
                return advance(weights, emission, behind, own, ahead)

            end_weights = weights_of(flow_ref[:, end, :])
            end_field = field_ref[:, end, :]
            outer = ordered(halo_weights, beyond, outside, end_field)
            own = ordered(end_weights, outside, end_field, field_ref[:, near, :])
            out_ref[last] = ordered(end_weights, outer, own, inside)
            out_ref[1 - last] = ordered(weights_of(flow_ref[:, near, :]), own, inside, further)


def edge_kernel(info_ref, field_ref, flow_ref, emission_ref, kept_ref, last_ref, first_ref, *refs):
    out_refs, scratch = refs[:-1], refs[-1]
    chips = len(out_refs)
    core = info_ref[1]
    for last, halo_ref in enumerate((first_ref, last_ref)):
        end_rows(info_ref, last, field_ref, flow_ref, emission_ref, kept_ref, halo_ref, scratch)
        for s, out_ref in enumerate(out_refs):

            @pl.when(info_ref[0] == (chips - 1 - s if last else s))
            def _():
                out_ref[0] = scratch[1 - core]
                out_ref[1] = scratch[core]


def source_of(chip, chips, hops, k):
    inner = sum(jnp.where(chip == to, source, 0) for source, to in hops)
    return jnp.where(chip == 0, k, jnp.where(chip == chips - 1, chips - 1 - k, inner))


def choose_kernel(info_ref, *refs):
    count = (len(refs) - 2) // 2
    other_ref, own_ref = refs[-2:]
    chips = info_ref[3]
    at_edge = jnp.logical_or(info_ref[0] == 0, info_ref[0] == chips - 1)
    for index in range(count):
        for ref, here in ((refs[index], jnp.logical_not(at_edge)), (refs[count + index], at_edge)):

            @pl.when(here)
            def _():
                other_ref[index] = ref[0]
                own_ref[index] = ref[1]


def collect_kernel(order, late, info_ref, mine_ref, other_ref, *refs):
    chips = len(order)
    both_ref, late_other, late_own, observed_ref = refs[-4:]
    observed_ref[...] = jnp.where(info_ref[2] == 1, other_ref[...], mine_ref[...])
    chip = info_ref[0]
    at_edge = jnp.logical_or(chip == 0, chip == chips - 1)
    for index, (s, k) in enumerate(order):
        block = source_of(chip, chips, s, k)
        for ref, here in ((refs[index], jnp.logical_not(at_edge)), (refs[chips + index], at_edge)):

            @pl.when(here)
            def _():
                both_ref[0, block] = ref[0]
                both_ref[1, block] = ref[1]
                if index in late:
                    late_other[late.index(index)] = ref[0]
                    late_own[late.index(index)] = ref[1]


def unpack_kernel(rows_ref, out_ref):
    for row in range(rows_ref.shape[0]):
        out_ref[:, row, :] = rows_ref[row]


def pieces(x, count):
    parts = []
    for _ in range(count - 1):
        part = x.astype(BF16)
        parts.append(part)
        x = x - part.astype(F32)
    return parts + [x.astype(BF16)]


def dot(a, b):
    return lax.dot_general(a, b, (((1,), (0,)), ((), ())), preferred_element_type=F32)


def dot_t(a, b):
    return lax.dot_general(a, b, (((0,), (0,)), ((), ())), preferred_element_type=F32)


def product(a, b):
    total = None
    for i, left in enumerate(a):
        for j, right in enumerate(b):
            if i + j < max(len(a), len(b)):
                term = dot(left, right)
                total = term if total is None else total + term
    return total


def observations(info_ref, observed_ref, width, root):
    slots = observed_ref.shape[1]
    cells, values, scales, count = (observed_ref[pl.ds(i, 1), :] for i in range(4))
    cells = cells.astype(jnp.int32)
    offset = sum((cells >= i * width).astype(jnp.int32) for i in (1, 2)) - 1
    column = cells - (offset + 1) * width
    side = offset * jnp.where(info_ref[2] == 1, -1, 1) * (1 - 2 * info_ref[1])
    cells = column + width * jnp.where(side == 0, 2, jnp.where(side < 0, 0, 1))
    active = lax.broadcasted_iota(jnp.int32, (1, slots), 1) < count.astype(jnp.int32)
    slot_weight = jnp.where(active, scales, 0.0)
    return cells, slot_weight, values, slot_weight * (1.0 / root)


def one_hot(cells, first, count):
    return (
        lax.broadcasted_iota(jnp.int32, (count, cells.shape[1]), 0) + first == cells
    ).astype(F32).astype(BF16)


def mean_of(blocks, members):
    total = blocks[0]
    for block in blocks[1:]:
        total = total + block
    return jnp.sum(total, axis=0, keepdims=True) * (1.0 / members)


def at_cells(row, chosen):
    parts = pieces(jnp.broadcast_to(row, (8, row.shape[1])), 3)
    return (dot(parts[0], chosen) + (dot(parts[1], chosen) + dot(parts[2], chosen)))[:1]


def prepare_kernel(
    info_ref, observed_ref, near_ref, far_ref,
    spread_high, spread_low, own_high, own_low, own_part, seen_ref, direction_ref,
    anomaly, high_ref, low_ref,
):
    _, chips, step, width = near_ref.shape
    members = 2 * chips * step
    cells, _, _, scale = observations(info_ref, observed_ref, width, math.sqrt(members - 1))
    chosen = one_hot(cells, width, 2 * width)
    blocks = [pl.ds(index * step, step) for index in range(2 * chips)]
    means = []
    for place in range(2):
        columns = pl.ds(place * width, width)
        rows = [near_ref.at[place, chip] for chip in range(chips)] + [far_ref.at[1 - place, chip] for chip in range(chips)]
        means.append(mean_of([row[...] for row in rows], members))
        for block, row in zip(blocks, rows):
            part = row[...] - means[-1]
            anomaly[block, columns] = part
            high_ref[block, columns] = part.astype(BF16)

    def unit(x):
        return x * (1.0 / jnp.maximum(jnp.max(jnp.abs(x)), 1e-30))

    high = high_ref[...]
    along = lax.dot_general(high[:16], high, (((1,), (1,)), ((), ())), preferred_element_type=F32)
    rows = unit(dot(unit(along).astype(BF16), high))
    weight = jnp.sum(rows * rows[:1], axis=1, keepdims=True)
    weight = weight + jnp.where(jnp.max(jnp.abs(weight)) > 0.0, 0.0, 1.0)
    pattern = unit(jnp.sum(rows * weight, axis=0, keepdims=True))
    total = jnp.zeros((1, 1), F32)
    for block in blocks:
        along = jnp.sum(anomaly[block, :] * pattern, axis=1, keepdims=True)
        total = total + jnp.sum(along * along, axis=0, keepdims=True)
        direction_ref[block, :] = jnp.broadcast_to(along, (step, direction_ref.shape[1]))
    length = lax.rsqrt(jnp.maximum(total, 1e-30))
    taken = None
    for block in blocks:
        direction = direction_ref[block, :] * length
        direction_ref[block, :] = direction
        term = anomaly[block, :] * doubled(doubled(direction))
        taken = term if taken is None else taken + term
    taken = jnp.sum(taken, axis=0, keepdims=True)
    own_part[...] = jnp.broadcast_to(taken[:, width:], (own_part.shape[1], width)).T

    for block in blocks:
        rest = anomaly[block, :] - doubled(doubled(direction_ref[block, :])) * taken
        high, low = pieces(rest, 2)
        high_ref[block, :] = high
        low_ref[block, :] = low
        own = rest[:, width:].T
        own_high[:, block], own_low[:, block] = pieces(own, 2)
    seen_ref[pl.ds(0, 1), :] = at_cells(jnp.concatenate(means, axis=1), chosen)
    seen_ref[pl.ds(1, 1), :] = at_cells(taken, chosen)
    for first in range(0, members, PART):
        rows = pl.ds(first, PART)
        spread = (dot(high_ref[rows, :], chosen) + dot(low_ref[rows, :], chosen)) * scale
        high, low = pieces(spread, 2)
        spread_high[rows, :] = high
        spread_low[rows, :] = low


def square(parts):
    half = parts[0].shape[0] // 2
    upper = product([part[:half] for part in parts], parts)
    lower = product([part[half:] for part in parts], [part[:, half:] for part in parts])
    return upper, jnp.concatenate([upper[:, half:].T, lower], axis=1)


def region_kernel(
    order, groups, info_ref, observed_ref, near_ref, far_ref, high_in, low_in, own_high, own_low, own_part, seen_ref,
    direction_ref, *refs,
):
    outer_refs, (out_ref, spread_high, spread_low, factor, answer) = refs[:-5], refs[-5:]
    _, chips, step, width = near_ref.shape
    members = 2 * chips * step
    slots = observed_ref.shape[1]
    root = math.sqrt(members - 1)
    core = info_ref[1]
    swapped = jnp.logical_or(
        jnp.logical_and(info_ref[0] == 0, core == 0), jnp.logical_and(info_ref[0] == chips - 1, core == 1)
    )
    giver = jnp.where(swapped, info_ref[0], info_ref[0] - 1 + 2 * core)
    cells, slot_weight, values, scale = observations(info_ref, observed_ref, width, root)
    chosen = one_hot(cells, 0, width)

    def outer_block(part, place):
        for pair, group in zip(zip(outer_refs[::2], outer_refs[1::2]), groups):
            if place in group:
                mine, other = pair[part], pair[1 - part]
                at = group.index(place)
                return jnp.where(swapped, other[at], mine[at])

    blocks = [pl.ds(index * step, step) for index in range(2 * chips)]
    arrivals = [
        (part, place, pl.ds(pl.multiple_of((part * chips + source_of(giver, chips, *order[place])) * step, step), step))
        for part in range(2) for place in range(chips)
    ]
    mean = mean_of([outer_block(part, place) for part, place, _ in arrivals], members)
    taken = None
    for part, place, block in arrivals:
        term = (outer_block(part, place) - mean) * doubled(direction_ref[block, :])
        taken = term if taken is None else taken + term
    taken = jnp.sum(taken, axis=0, keepdims=True)
    seen_mean = seen_ref[pl.ds(0, 1), :] + at_cells(mean, chosen)
    common = (seen_ref[pl.ds(1, 1), :] + at_cells(taken, chosen)) * scale
    innovation = slot_weight * (values - seen_mean)
    for part, place, block in arrivals:
        rest = outer_block(part, place) - mean - doubled(direction_ref[block, :]) * taken
        high, low = pieces(rest, 2)
        high, low = pieces((dot(high, chosen) + dot(low, chosen)) * scale, 2)
        spread_high[block, :] = high + high_in[block, :]
        spread_low[block, :] = low + low_in[block, :]

    high, low = spread_high[...], spread_low[...]
    eye = lax.broadcasted_iota(jnp.int32, (slots, slots), 0) == lax.broadcasted_iota(
        jnp.int32, (slots, slots), 1
    )
    turned = high.T
    cross = dot(turned, low)
    factor[...] = dot(turned, high) + (cross + cross.T) + jnp.where(eye, 1.0, 0.0)
    answer[pl.ds(0, width), :] = product([own_high[...], own_low[...]], [high, low])
    answer[pl.ds(width, 8), :] = jnp.where(
        lax.broadcasted_iota(jnp.int32, (8, slots), 0) == 0, jnp.broadcast_to(common, (8, slots)), 0.0
    )
    half = slots // 2
    upper, lower = pl.ds(0, half), pl.ds(half, half)

    def after(bound):
        return bound * bound / (2.0 - bound * bound)

    def size(matrix):
        return jnp.sum(jnp.sum(matrix * matrix, axis=0, keepdims=True))

    def begin(count):
        parts = pieces(factor[...], count)
        top, bottom = square(parts)
        limit = 1.0001 * jnp.sqrt(jnp.sqrt(size(top) + size(bottom)))
        start = 2.0 / (1.0 + limit)
        bound = 1.0 - start
        gain = 2.0 / (2.0 - bound * bound)
        answer[...] = (gain * start) * (2.0 * answer[...] - start * product(pieces(answer[...], count), parts))
        factor[upper, :] = (gain * start) * (2.0 * factor[upper, :] - start * top)
        factor[lower, :] = (gain * start) * (2.0 * factor[lower, :] - start * bottom)
        return after(bound)

    def refine(bound, count):
        gain = 2.0 / (2.0 - bound * bound)
        parts = pieces(factor[...], count)
        answer[...] = gain * (2.0 * answer[...] - product(pieces(answer[...], count), parts))
        top, bottom = square(parts)
        factor[upper, :] = gain * (2.0 * factor[upper, :] - top)
        factor[lower, :] = gain * (2.0 * factor[lower, :] - bottom)
        return after(bound)

    def close(bound, rest):
        gain = 2.0 / (2.0 - bound * bound)
        answer[...] = gain * (answer[...] + dot(answer[...].astype(BF16), rest))
        return gain

    def finish(bound):
        rest = factor[...].astype(BF16)
        gain = close(bound, rest)
        factor[...] = gain * (dot(rest, rest) - jnp.where(eye, 0.5 * bound * bound, 0.0))
        return after(bound)

    large = size(factor[...]) > LARGE * LARGE
    bound = lax.cond(large, lambda: begin(3), lambda: begin(2))
    bound = lax.while_loop(lambda b: jnp.logical_and(b > COARSE, large), lambda b: refine(b, 3), bound)
    bound = lax.while_loop(lambda b: b > COARSE, lambda b: refine(b, 2), bound)
    factor[...] = jnp.where(eye, 1.0, 0.0) - factor[...]
    bound = lax.while_loop(lambda b: b > DONE, finish, bound)
    close(bound, factor[...].astype(BF16))

    solved = answer[pl.ds(0, width), :]
    alone = answer[pl.ds(width, 1), :]
    share = own_part[:, :1] - jnp.sum(solved * common, axis=1, keepdims=True)
    solved = solved + (share / (1.0 + jnp.sum(common * alone, axis=1, keepdims=True))) * alone
    solved = solved.T
    which = lax.broadcasted_iota(jnp.int32, (8, slots), 0)
    sides = jnp.where(which == 0, innovation * (1.0 / root), jnp.where(which == 1, -0.5 * common, 0.0))
    parts = pieces(solved, 3)
    sides = product(pieces(sides, 3), parts)
    shift, along = sides[0:1], sides[1:2]
    halved = [part * jnp.asarray(-0.5, BF16) for part in pieces(solved, 2)]
    for part, ref, place in ((0, near_ref, 1), (1, far_ref, 0)):
        for chip in range(chips):
            block = blocks[part * chips + chip]
            moved = product([spread_high[block, :], spread_low[block, :]], halved)
            moved = moved + doubled(direction_ref[block, :]) * along
            lane = 2 * chip + jnp.abs(core - part)
            lane = lane + info_ref[2] * (2 * chips - 1 - 2 * lane)
            out_ref[lane] = ref[place, chip] + shift + moved


VMEM = pl.BlockSpec(memory_space=pltpu.VMEM)
SMEM = pl.BlockSpec(memory_space=pltpu.SMEM)


def call(kernel, name, out_shape, args, scratch=(), flops=None, aliases={}, limit=8, after=()):
    several = isinstance(out_shape, (list, tuple))
    if after:
        count, inner = len(args), kernel
        args = [*args, *after]
        kernel = lambda *refs: inner(*refs[:count], *refs[len(args) :])
    return pl.pallas_call(
        kernel,
        out_shape=out_shape,
        in_specs=[SMEM] + [VMEM] * (len(args) - 1 - len(after)) + [pl.BlockSpec(memory_space=pl.ANY)] * len(after),
        out_specs=[VMEM] * len(out_shape) if several else VMEM,
        scratch_shapes=scratch,
        input_output_aliases=aliases,
        compiler_params=pltpu.CompilerParams(vmem_limit_bytes=limit * 1024 * 1024),
        cost_estimate=flops and pl.CostEstimate(flops=flops, bytes_accessed=0, transcendentals=0),
        name=name,
    )(*args)


def bfloat(*shape):
    return jax.ShapeDtypeStruct(shape, BF16)


def array(*shape):
    return jax.ShapeDtypeStruct(shape, F32)


def per_device(
    init_field, flow_fields, emission, observed_cell, observed_count, observed_value, observed_scale
):
    step, rows, width = init_field.shape
    slots = observed_cell.shape[1]
    patches, lanes = lax.axis_size("patch"), lax.axis_size("member")
    chips = lanes // 2
    members = lanes * step
    axes = ("patch", "member")
    count = patches * lanes
    patch, lane = lax.axis_index("patch"), lax.axis_index("member")
    info = jnp.stack([lane // 2, lane % 2, patch % 2, jnp.int32(chips)]).astype(jnp.int32)

    edge = array(STEPS * step + 8, width)
    place = pl.BlockSpec(memory_space=pltpu.HBM)
    to_last, to_first, flow, emitted = pl.pallas_call(
        pack_kernel,
        out_shape=[edge, edge, array(*flow_fields.shape), array(step, width // 2)],
        in_specs=[SMEM] + [place] * 3, out_specs=[VMEM] * 4,
        scratch_shapes=[
            pltpu.VMEM((step, rows, width), F32), pltpu.VMEM((1, step), F32), pltpu.SemaphoreType.DMA((3,))
        ],
        compiler_params=pltpu.CompilerParams(vmem_limit_bytes=32 * 1024 * 1024), name="pack",
    )(info, init_field, flow_fields, emission[None, :])

    def swap(message, start):
        lower = range(start, patches - 1, 2)
        return lax.ppermute(message, "patch", [(p, p + 1) for p in lower] + [(p + 1, p) for p in lower])

    halo_last, halo_first = swap(to_last, 0), swap(to_first, 1)

    mine = jnp.concatenate(
        [
            observed_cell.astype(F32),
            observed_value,
            observed_scale,
            jnp.broadcast_to(observed_count.astype(F32)[:, None], observed_cell.shape),
        ]
        * 2,
        axis=0,
    )

    def between(message, hops):
        return lax.ppermute(message, "member", [(2 * a + core, 2 * b + core) for a, b in hops for core in range(2)])

    mirrored = [
        [hop for to in range(1, chips // 2) for hop in (((to + s) % chips, to), (chips - 1 - (to + s) % chips, chips - 1 - to))]
        for s in range(chips)
    ]
    turning = [[((to - s) % chips, to) for to in range(1, chips - 1)] for s in range(chips)]
    single = all(len({source for source, _ in hops}) == len(hops) for hops in mirrored)
    targets = mirrored if single else turning
    pair = array(2, step, width)
    args = [info, init_field, flow, emitted]
    kept, *inner = call(
        functools.partial(inner_kernel, targets), "inner", [array(4, step, width)] + [pair] * chips, args,
        [pltpu.VMEM((rows, step, width), F32), pltpu.VMEM((rows, 8, width), F32)], limit=32,
    )
    got_inner = [inner[0]] + [between(inner[s], targets[s]) for s in range(1, chips)]
    outer = call(
        edge_kernel, "edge", [pair] * chips, args + [kept, halo_last, halo_first],
        [pltpu.VMEM((2, step, width), F32)], limit=32,
    )
    got_outer = [outer[0]] + [
        between(outer[s], [(s, 0), (chips - 1 - s, chips - 1)]) for s in range(1, chips)
    ]
    order = [(targets[s], s) for s in range(chips)]
    pieces_in = got_inner + got_outer
    mine, _ = lax.optimization_barrier((mine, outer[0]))
    other = lax.ppermute(
        mine, axes,
        [(p * lanes + i, p * lanes + lanes - 1 - i) for p in range(1, patches, 2) for i in range(lanes)],
    )

    def device(p, chip, core):
        return p * lanes + 2 * chip + core

    first_pairs, second_pairs, siblings = [], [], []
    for p in range(patches):
        for chip in range(chips):
            siblings += [(device(p, chip, core), device(p, chip, 1 - core)) for core in range(2)]
            for core, away in ((0, 1), (1, -1)):
                if 0 <= chip + away < chips:
                    to_first, to_second = device(p, chip + away, core), device(p, chip + away, core)
                    to = p
                else:
                    to = p + 1 if (p % 2 == 0) == (away == 1) else p - 1
                    if not 0 <= to < patches:
                        continue
                    to_first = to_second = device(to, chip, 1 - core)
                first_pairs.append((device(p, chip, core), to_first))
                second_pairs.append((device(p, chip, 1 - core), to_second))
    groups = [[0], list(range(1, chips))]
    early, late = groups
    got = [pieces_in[place] for place in early] + [pieces_in[chips + place] for place in early]
    row = array(len(early), step, width)
    early_rows = call(choose_kernel, "choose", [row, row], [info] + got)
    outer_rows = [lax.ppermute(early_rows[0], axes, first_pairs), lax.ppermute(early_rows[1], axes, second_pairs)]
    row = array(len(late), step, width)
    near, *late_rows, observed = call(
        functools.partial(collect_kernel, order, late), "collect",
        [array(2, chips, step, width), row, row, array(8, slots)], [info, mine, other] + pieces_in, after=outer_rows,
    )
    outer_rows += [lax.ppermute(late_rows[0], axes, first_pairs), lax.ppermute(late_rows[1], axes, second_pairs)]
    far = lax.ppermute(near, axes, siblings)

    split = [pltpu.VMEM((members, slots), BF16)] * 2
    prepared = call(
        prepare_kernel, "prepare",
        [bfloat(members, slots)] * 2 + [bfloat(width, members)] * 2
        + [array(width, width // 2), array(8, slots), array(members, width // 2)],
        [info, observed, near, far],
        [pltpu.VMEM((members, 2 * width), F32)] + [pltpu.VMEM((members, 2 * width), BF16)] * 2,
        flops=8 * members * slots * width, limit=20,
    )
    analysed = call(
        functools.partial(region_kernel, order, groups), "region", array(lanes, step, width),
        [info, observed, near, far, *prepared, *outer_rows],
        split + [pltpu.VMEM((slots, slots), F32), pltpu.VMEM((width + 8, slots), F32)],
        limit=24,
    )
    lines = [[p * lanes + (lanes - 1 - i if p % 2 else i) for i in range(lanes)] for p in range(patches)]
    returned = lax.all_to_all(
        analysed, axes, split_axis=0, concat_axis=0, tiled=True, axis_index_groups=lines
    )
    return pl.pallas_call(
        unpack_kernel, out_shape=array(step, rows, width), in_specs=[VMEM], out_specs=VMEM, name="unpack",
        compiler_params=pltpu.CompilerParams(vmem_limit_bytes=48 * 1024 * 1024),
    )(returned)


def solution(mesh):
    return jax.shard_map(
        per_device,
        mesh=mesh,
        in_specs=(
            P("member", "patch", None),
            P(None, "patch", None),
            P("member"),
            P(("patch", "member"), None),
            P(("patch", "member")),
            P(("patch", "member"), None),
            P(("patch", "member"), None),
        ),
        out_specs=P("member", "patch", None),
        check_vma=False,
    )
```

```python
import functools
import math

import jax
import jax.numpy as jnp
from jax import lax
from jax.experimental import pallas as pl
from jax.experimental.pallas import tpu as pltpu
from jax.sharding import PartitionSpec as P

STEPS = 2
COARSE = 0.2
DONE = 0.01
LARGE = 2e4
PART = 256
F32 = jnp.float32
BF16 = jnp.bfloat16


def pack_kernel(info_ref, field_hbm, flow_hbm, emission_hbm, first_ref, second_ref, flow_ref, emission_ref,
                field_ref, member_ref, sems):
    members, rows, width = field_ref.shape
    moves = [
        pltpu.make_async_copy(source, target, sems.at[i])
        for i, (source, target) in enumerate(
            ((field_hbm, field_ref), (flow_hbm, flow_ref), (emission_hbm, member_ref))
        )
    ]
    for move in moves:
        move.start()
    for move in moves[1:]:
        move.wait()
    diagonal = lax.broadcasted_iota(jnp.int32, (members, members), 0) == lax.broadcasted_iota(
        jnp.int32, (members, members), 1
    )
    column = jnp.sum(jnp.where(diagonal, member_ref[...], 0.0), axis=1, keepdims=True)
    emission_ref[...] = jnp.broadcast_to(column, emission_ref.shape)
    moves[0].wait()
    even = info_ref[2] == 0
    for place in range(STEPS):
        tail, head = field_ref[:, rows - STEPS + place, :], field_ref[:, place, :]
        at = pl.ds(place * members, members)
        first_ref[at, :] = jnp.where(even, tail, head)
        second_ref[at, :] = jnp.where(even, head, tail)
    tail, head = flow_ref[:, rows - 1, :], flow_ref[:, 0, :]
    at = pl.ds(STEPS * members, 8)
    first_ref[at, :] = jnp.concatenate([jnp.where(even, tail, head)] * 2, axis=0)
    second_ref[at, :] = jnp.concatenate([jnp.where(even, head, tail)] * 2, axis=0)


def doubled(x):
    return jnp.concatenate([x, x], axis=1)


def weights_of(flow):
    row_flow, col_flow, kept, source = flow[0:1], flow[1:2], 1.0 - flow[2:3], flow[3:4]
    behind, ahead = jnp.maximum(row_flow, 0.0), -jnp.minimum(row_flow, 0.0)
    left, right = jnp.maximum(col_flow, 0.0), -jnp.minimum(col_flow, 0.0)
    stays = 1.0 - behind - ahead - left - right
    return [kept * stays, kept * behind, kept * ahead, kept * left, kept * right, source]


def advance(weights, emission, behind, field, ahead):
    width = field.shape[1]
    return (
        weights[0] * field
        + weights[1] * behind
        + weights[2] * ahead
        + weights[3] * pltpu.roll(field, 1, 1)
        + weights[4] * pltpu.roll(field, width - 1, 1)
        + emission * weights[5]
    )


def inner_kernel(targets, info_ref, field_ref, flow_ref, emission_ref, kept_ref, *refs):
    out_refs, (wide_ref, weight_ref) = refs[:-2], refs[-2:]
    rows = field_ref.shape[1]
    emission = doubled(emission_ref[...])
    for row in range(1, rows - 1):
        weights = weights_of(flow_ref[:, row, :])
        for i, weight in enumerate(weights):
            weight_ref[row, pl.ds(i, 1), :] = weight
        wide_ref[row] = advance(
            weights, emission, field_ref[:, row - 1, :], field_ref[:, row, :], field_ref[:, row + 1, :]
        )
    for place, row in enumerate((1, 2, rows - 3, rows - 2)):
        kept_ref[place] = wide_ref[row]
    for out_ref, hops in zip(out_refs, targets):
        chip = sum(jnp.where(info_ref[0] == source, to, 0) for source, to in hops)

        @pl.when(chip > 0)
        def _():
            for place in range(2):
                position = 2 * chip + jnp.abs(info_ref[1] - 1 + place)
                row = position + info_ref[2] * (rows - 1 - 2 * position)
                weights = weight_ref[row]
                out_ref[place] = advance(
                    [weights[i : i + 1] for i in range(6)],
                    emission, wide_ref[row - 1], wide_ref[row], wide_ref[row + 1],
                )


def end_rows(info_ref, last, field_ref, flow_ref, emission_ref, kept_ref, halo_ref, out_ref):
    members, rows, width = field_ref.shape
    emission = doubled(emission_ref[...])

    def halo_row(place):
        return halo_ref[pl.ds(place * members, members), :]

    halo_weights = weights_of(halo_ref[pl.ds(STEPS * members, 4), :])
    for parity in range(2):

        @pl.when(info_ref[2] == parity)
        def _():
            if parity == last:
                end, near, outside, beyond = 0, 1, halo_row(1), halo_row(0)
                inside, further = kept_ref[0], kept_ref[1]
            else:
                end, near, outside, beyond = rows - 1, rows - 2, halo_row(0), halo_row(1)
                inside, further = kept_ref[3], kept_ref[2]

            def ordered(weights, outer, own, inner):
                behind, ahead = (outer, inner) if end == 0 else (inner, outer)
                return advance(weights, emission, behind, own, ahead)

            end_weights = weights_of(flow_ref[:, end, :])
            end_field = field_ref[:, end, :]
            outer = ordered(halo_weights, beyond, outside, end_field)
            own = ordered(end_weights, outside, end_field, field_ref[:, near, :])
            out_ref[last] = ordered(end_weights, outer, own, inside)
            out_ref[1 - last] = ordered(weights_of(flow_ref[:, near, :]), own, inside, further)


def edge_kernel(info_ref, field_ref, flow_ref, emission_ref, kept_ref, last_ref, first_ref, *refs):
    out_refs, scratch = refs[:-1], refs[-1]
    chips = len(out_refs)
    core = info_ref[1]
    for last, halo_ref in enumerate((first_ref, last_ref)):
        end_rows(info_ref, last, field_ref, flow_ref, emission_ref, kept_ref, halo_ref, scratch)
        for s, out_ref in enumerate(out_refs):

            @pl.when(info_ref[0] == (chips - 1 - s if last else s))
            def _():
                out_ref[0] = scratch[1 - core]
                out_ref[1] = scratch[core]


def source_of(chip, chips, hops, k):
    inner = sum(jnp.where(chip == to, source, 0) for source, to in hops)
    return jnp.where(chip == 0, k, jnp.where(chip == chips - 1, chips - 1 - k, inner))


def choose_kernel(info_ref, *refs):
    count = (len(refs) - 2) // 2
    other_ref, own_ref = refs[-2:]
    chips = info_ref[3]
    at_edge = jnp.logical_or(info_ref[0] == 0, info_ref[0] == chips - 1)
    for index in range(count):
        for ref, here in ((refs[index], jnp.logical_not(at_edge)), (refs[count + index], at_edge)):

            @pl.when(here)
            def _():
                other_ref[index] = ref[0]
                own_ref[index] = ref[1]


def collect_kernel(order, late, info_ref, mine_ref, other_ref, *refs):
    chips = len(order)
    both_ref, late_other, late_own, observed_ref = refs[-4:]
    observed_ref[...] = jnp.where(info_ref[2] == 1, other_ref[...], mine_ref[...])
    chip = info_ref[0]
    at_edge = jnp.logical_or(chip == 0, chip == chips - 1)
    for index, (s, k) in enumerate(order):
        block = source_of(chip, chips, s, k)
        for ref, here in ((refs[index], jnp.logical_not(at_edge)), (refs[chips + index], at_edge)):

            @pl.when(here)
            def _():
                both_ref[0, block] = ref[0]
                both_ref[1, block] = ref[1]
                if index in late:
                    late_other[late.index(index)] = ref[0]
                    late_own[late.index(index)] = ref[1]


def unpack_kernel(order, info_ref, *refs):
    row_refs, out_ref, rows_ref = refs[:-2], refs[-2], refs[-1]
    rows = rows_ref.shape[0]
    for x, ref in zip(order, row_refs):
        position = (2 * info_ref[0] + info_ref[1]) ^ x
        rows_ref[position + info_ref[2] * (rows - 1 - 2 * position)] = ref[...]
    for row in range(rows):
        out_ref[:, row, :] = rows_ref[row]


def pieces(x, count):
    parts = []
    for _ in range(count - 1):
        part = x.astype(BF16)
        parts.append(part)
        x = x - part.astype(F32)
    return parts + [x.astype(BF16)]


def dot(a, b):
    return lax.dot_general(a, b, (((1,), (0,)), ((), ())), preferred_element_type=F32)


def dot_t(a, b):
    return lax.dot_general(a, b, (((0,), (0,)), ((), ())), preferred_element_type=F32)


def product(a, b):
    total = None
    for i, left in enumerate(a):
        for j, right in enumerate(b):
            if i + j < max(len(a), len(b)):
                term = dot(left, right)
                total = term if total is None else total + term
    return total


def observations(info_ref, observed_ref, width, root):
    slots = observed_ref.shape[1]
    cells, values, scales, count = (observed_ref[pl.ds(i, 1), :] for i in range(4))
    cells = cells.astype(jnp.int32)
    offset = sum((cells >= i * width).astype(jnp.int32) for i in (1, 2)) - 1
    column = cells - (offset + 1) * width
    side = offset * jnp.where(info_ref[2] == 1, -1, 1) * (1 - 2 * info_ref[1])
    cells = column + width * jnp.where(side == 0, 2, jnp.where(side < 0, 0, 1))
    active = lax.broadcasted_iota(jnp.int32, (1, slots), 1) < count.astype(jnp.int32)
    slot_weight = jnp.where(active, scales, 0.0)
    return cells, slot_weight, values, slot_weight * (1.0 / root)


def one_hot(cells, first, count):
    return (
        lax.broadcasted_iota(jnp.int32, (count, cells.shape[1]), 0) + first == cells
    ).astype(F32).astype(BF16)


def mean_of(blocks, members):
    total = blocks[0]
    for block in blocks[1:]:
        total = total + block
    return jnp.sum(total, axis=0, keepdims=True) * (1.0 / members)


def at_cells(row, chosen):
    parts = pieces(jnp.broadcast_to(row, (8, row.shape[1])), 3)
    return (dot(parts[0], chosen) + (dot(parts[1], chosen) + dot(parts[2], chosen)))[:1]


def prepare_kernel(
    info_ref, observed_ref, near_ref, far_ref,
    spread_high, spread_low, own_high, own_low, own_part, seen_ref, direction_ref,
    anomaly, high_ref, low_ref,
):
    _, chips, step, width = near_ref.shape
    members = 2 * chips * step
    cells, _, _, scale = observations(info_ref, observed_ref, width, math.sqrt(members - 1))
    chosen = one_hot(cells, width, 2 * width)
    blocks = [pl.ds(index * step, step) for index in range(2 * chips)]
    means = []
    for place in range(2):
        columns = pl.ds(place * width, width)
        rows = [near_ref.at[place, chip] for chip in range(chips)] + [far_ref.at[1 - place, chip] for chip in range(chips)]
        means.append(mean_of([row[...] for row in rows], members))
        for block, row in zip(blocks, rows):
            part = row[...] - means[-1]
            anomaly[block, columns] = part
            high_ref[block, columns] = part.astype(BF16)

    def unit(x):
        return x * (1.0 / jnp.maximum(jnp.max(jnp.abs(x)), 1e-30))

    high = high_ref[...]
    along = lax.dot_general(high[:16], high, (((1,), (1,)), ((), ())), preferred_element_type=F32)
    rows = unit(dot(unit(along).astype(BF16), high))
    weight = jnp.sum(rows * rows[:1], axis=1, keepdims=True)
    weight = weight + jnp.where(jnp.max(jnp.abs(weight)) > 0.0, 0.0, 1.0)
    pattern = unit(jnp.sum(rows * weight, axis=0, keepdims=True))
    total = jnp.zeros((1, 1), F32)
    for block in blocks:
        along = jnp.sum(anomaly[block, :] * pattern, axis=1, keepdims=True)
        total = total + jnp.sum(along * along, axis=0, keepdims=True)
        direction_ref[block, :] = jnp.broadcast_to(along, (step, direction_ref.shape[1]))
    length = lax.rsqrt(jnp.maximum(total, 1e-30))
    taken = None
    for block in blocks:
        direction = direction_ref[block, :] * length
        direction_ref[block, :] = direction
        term = anomaly[block, :] * doubled(doubled(direction))
        taken = term if taken is None else taken + term
    taken = jnp.sum(taken, axis=0, keepdims=True)
    own_part[...] = jnp.broadcast_to(taken[:, width:], (own_part.shape[1], width)).T

    for block in blocks:
        rest = anomaly[block, :] - doubled(doubled(direction_ref[block, :])) * taken
        high, low = pieces(rest, 2)
        high_ref[block, :] = high
        low_ref[block, :] = low
        own = rest[:, width:].T
        own_high[:, block], own_low[:, block] = pieces(own, 2)
    seen_ref[pl.ds(0, 1), :] = at_cells(jnp.concatenate(means, axis=1), chosen)
    seen_ref[pl.ds(1, 1), :] = at_cells(taken, chosen)
    for first in range(0, members, PART):
        rows = pl.ds(first, PART)
        spread = (dot(high_ref[rows, :], chosen) + dot(low_ref[rows, :], chosen)) * scale
        high, low = pieces(spread, 2)
        spread_high[rows, :] = high
        spread_low[rows, :] = low


def square(parts):
    half = parts[0].shape[0] // 2
    upper = product([part[:half] for part in parts], parts)
    lower = product([part[half:] for part in parts], [part[:, half:] for part in parts])
    return upper, jnp.concatenate([upper[:, half:].T, lower], axis=1)


def region_kernel(
    order, groups, info_ref, observed_ref, near_ref, far_ref, high_in, low_in, own_high, own_low, own_part, seen_ref,
    direction_ref, *refs,
):
    _, chips, step, width = near_ref.shape
    outer_refs, out_refs = refs[: 2 * len(groups)], refs[2 * len(groups) : -4]
    spread_high, spread_low, factor, answer = refs[-4:]
    members = 2 * chips * step
    slots = observed_ref.shape[1]
    root = math.sqrt(members - 1)
    core = info_ref[1]
    swapped = jnp.logical_or(
        jnp.logical_and(info_ref[0] == 0, core == 0), jnp.logical_and(info_ref[0] == chips - 1, core == 1)
    )
    giver = jnp.where(swapped, info_ref[0], info_ref[0] - 1 + 2 * core)
    cells, slot_weight, values, scale = observations(info_ref, observed_ref, width, root)
    chosen = one_hot(cells, 0, width)

    def outer_block(part, place):
        for pair, group in zip(zip(outer_refs[::2], outer_refs[1::2]), groups):
            if place in group:
                mine, other = pair[part], pair[1 - part]
                at = group.index(place)
                return jnp.where(swapped, other[at], mine[at])

    blocks = [pl.ds(index * step, step) for index in range(2 * chips)]
    arrivals = [
        (part, place, pl.ds(pl.multiple_of((part * chips + source_of(giver, chips, *order[place])) * step, step), step))
        for part in range(2) for place in range(chips)
    ]
    mean = mean_of([outer_block(part, place) for part, place, _ in arrivals], members)
    taken = None
    for part, place, block in arrivals:
        term = (outer_block(part, place) - mean) * doubled(direction_ref[block, :])
        taken = term if taken is None else taken + term
    taken = jnp.sum(taken, axis=0, keepdims=True)
    seen_mean = seen_ref[pl.ds(0, 1), :] + at_cells(mean, chosen)
    common = (seen_ref[pl.ds(1, 1), :] + at_cells(taken, chosen)) * scale
    innovation = slot_weight * (values - seen_mean)
    for part, place, block in arrivals:
        rest = outer_block(part, place) - mean - doubled(direction_ref[block, :]) * taken
        high, low = pieces(rest, 2)
        high, low = pieces((dot(high, chosen) + dot(low, chosen)) * scale, 2)
        spread_high[block, :] = high + high_in[block, :]
        spread_low[block, :] = low + low_in[block, :]

    high, low = spread_high[...], spread_low[...]
    eye = lax.broadcasted_iota(jnp.int32, (slots, slots), 0) == lax.broadcasted_iota(
        jnp.int32, (slots, slots), 1
    )
    turned = high.T
    cross = dot(turned, low)
    factor[...] = dot(turned, high) + (cross + cross.T) + jnp.where(eye, 1.0, 0.0)
    answer[pl.ds(0, width), :] = product([own_high[...], own_low[...]], [high, low])
    answer[pl.ds(width, 8), :] = jnp.where(
        lax.broadcasted_iota(jnp.int32, (8, slots), 0) == 0, jnp.broadcast_to(common, (8, slots)), 0.0
    )
    half = slots // 2
    upper, lower = pl.ds(0, half), pl.ds(half, half)

    def after(bound):
        return bound * bound / (2.0 - bound * bound)

    def size(matrix):
        return jnp.sum(jnp.sum(matrix * matrix, axis=0, keepdims=True))

    def begin(count):
        parts = pieces(factor[...], count)
        top, bottom = square(parts)
        limit = 1.0001 * jnp.sqrt(jnp.sqrt(size(top) + size(bottom)))
        start = 2.0 / (1.0 + limit)
        bound = 1.0 - start
        gain = 2.0 / (2.0 - bound * bound)
        answer[...] = (gain * start) * (2.0 * answer[...] - start * product(pieces(answer[...], count), parts))
        factor[upper, :] = (gain * start) * (2.0 * factor[upper, :] - start * top)
        factor[lower, :] = (gain * start) * (2.0 * factor[lower, :] - start * bottom)
        return after(bound)

    def refine(bound, count):
        gain = 2.0 / (2.0 - bound * bound)
        parts = pieces(factor[...], count)
        answer[...] = gain * (2.0 * answer[...] - product(pieces(answer[...], count), parts))
        top, bottom = square(parts)
        factor[upper, :] = gain * (2.0 * factor[upper, :] - top)
        factor[lower, :] = gain * (2.0 * factor[lower, :] - bottom)
        return after(bound)

    def close(bound, rest):
        gain = 2.0 / (2.0 - bound * bound)
        answer[...] = gain * (answer[...] + dot(answer[...].astype(BF16), rest))
        return gain

    def finish(bound):
        rest = factor[...].astype(BF16)
        gain = close(bound, rest)
        factor[...] = gain * (dot(rest, rest) - jnp.where(eye, 0.5 * bound * bound, 0.0))
        return after(bound)

    large = size(factor[...]) > LARGE * LARGE
    bound = lax.cond(large, lambda: begin(3), lambda: begin(2))
    bound = lax.while_loop(lambda b: jnp.logical_and(b > COARSE, large), lambda b: refine(b, 3), bound)
    bound = lax.while_loop(lambda b: b > COARSE, lambda b: refine(b, 2), bound)
    factor[...] = jnp.where(eye, 1.0, 0.0) - factor[...]
    bound = lax.while_loop(lambda b: b > DONE, finish, bound)
    close(bound, factor[...].astype(BF16))

    solved = answer[pl.ds(0, width), :]
    alone = answer[pl.ds(width, 1), :]
    share = own_part[:, :1] - jnp.sum(solved * common, axis=1, keepdims=True)
    solved = solved + (share / (1.0 + jnp.sum(common * alone, axis=1, keepdims=True))) * alone
    solved = solved.T
    which = lax.broadcasted_iota(jnp.int32, (8, slots), 0)
    sides = jnp.where(which == 0, innovation * (1.0 / root), jnp.where(which == 1, -0.5 * common, 0.0))
    parts = pieces(solved, 3)
    sides = product(pieces(sides, 3), parts)
    shift, along = sides[0:1], sides[1:2]
    halved = [part * jnp.asarray(-0.5, BF16) for part in pieces(solved, 2)]
    for x, out_ref in enumerate(out_refs):
        chip, part = info_ref[0] ^ (x // 2), x % 2
        rows = pl.ds(pl.multiple_of((part * chips + chip) * step, step), step)
        moved = product([spread_high[rows, :], spread_low[rows, :]], halved)
        moved = moved + doubled(direction_ref[rows, :]) * along
        own = far_ref[0, chip] if part else near_ref[1, chip]
        out_ref[...] = own + shift + moved


VMEM = pl.BlockSpec(memory_space=pltpu.VMEM)
SMEM = pl.BlockSpec(memory_space=pltpu.SMEM)


def call(kernel, name, out_shape, args, scratch=(), flops=None, aliases={}, limit=8, after=()):
    several = isinstance(out_shape, (list, tuple))
    if after:
        count, inner = len(args), kernel
        args = [*args, *after]
        kernel = lambda *refs: inner(*refs[:count], *refs[len(args) :])
    return pl.pallas_call(
        kernel,
        out_shape=out_shape,
        in_specs=[SMEM] + [VMEM] * (len(args) - 1 - len(after)) + [pl.BlockSpec(memory_space=pl.ANY)] * len(after),
        out_specs=[VMEM] * len(out_shape) if several else VMEM,
        scratch_shapes=scratch,
        input_output_aliases=aliases,
        compiler_params=pltpu.CompilerParams(vmem_limit_bytes=limit * 1024 * 1024),
        cost_estimate=flops and pl.CostEstimate(flops=flops, bytes_accessed=0, transcendentals=0),
        name=name,
    )(*args)


def bfloat(*shape):
    return jax.ShapeDtypeStruct(shape, BF16)


def array(*shape):
    return jax.ShapeDtypeStruct(shape, F32)


def per_device(
    init_field, flow_fields, emission, observed_cell, observed_count, observed_value, observed_scale
):
    step, rows, width = init_field.shape
    slots = observed_cell.shape[1]
    patches, lanes = lax.axis_size("patch"), lax.axis_size("member")
    chips = lanes // 2
    members = lanes * step
    axes = ("patch", "member")
    count = patches * lanes
    patch, lane = lax.axis_index("patch"), lax.axis_index("member")
    info = jnp.stack([lane // 2, lane % 2, patch % 2, jnp.int32(chips)]).astype(jnp.int32)

    edge = array(STEPS * step + 8, width)
    place = pl.BlockSpec(memory_space=pltpu.HBM)
    to_last, to_first, flow, emitted = pl.pallas_call(
        pack_kernel,
        out_shape=[edge, edge, array(*flow_fields.shape), array(step, width // 2)],
        in_specs=[SMEM] + [place] * 3, out_specs=[VMEM] * 4,
        scratch_shapes=[
            pltpu.VMEM((step, rows, width), F32), pltpu.VMEM((1, step), F32), pltpu.SemaphoreType.DMA((3,))
        ],
        compiler_params=pltpu.CompilerParams(vmem_limit_bytes=32 * 1024 * 1024), name="pack",
    )(info, init_field, flow_fields, emission[None, :])

    def swap(message, start):
        lower = range(start, patches - 1, 2)
        return lax.ppermute(message, "patch", [(p, p + 1) for p in lower] + [(p + 1, p) for p in lower])

    halo_last, halo_first = swap(to_last, 0), swap(to_first, 1)

    mine = jnp.concatenate(
        [
            observed_cell.astype(F32),
            observed_value,
            observed_scale,
            jnp.broadcast_to(observed_count.astype(F32)[:, None], observed_cell.shape),
        ]
        * 2,
        axis=0,
    )

    def between(message, hops):
        return lax.ppermute(message, "member", [(2 * a + core, 2 * b + core) for a, b in hops for core in range(2)])

    mirrored = [
        [hop for to in range(1, chips // 2) for hop in (((to + s) % chips, to), (chips - 1 - (to + s) % chips, chips - 1 - to))]
        for s in range(chips)
    ]
    turning = [[((to - s) % chips, to) for to in range(1, chips - 1)] for s in range(chips)]
    single = all(len({source for source, _ in hops}) == len(hops) for hops in mirrored)
    targets = mirrored if single else turning
    pair = array(2, step, width)
    args = [info, init_field, flow, emitted]
    kept, *inner = call(
        functools.partial(inner_kernel, targets), "inner", [array(4, step, width)] + [pair] * chips, args,
        [pltpu.VMEM((rows, step, width), F32), pltpu.VMEM((rows, 8, width), F32)], limit=32,
    )
    got_inner = [inner[0]] + [between(inner[s], targets[s]) for s in range(1, chips)]
    outer = call(
        edge_kernel, "edge", [pair] * chips, args + [kept, halo_last, halo_first],
        [pltpu.VMEM((2, step, width), F32)], limit=32,
    )
    got_outer = [outer[0]] + [
        between(outer[s], [(s, 0), (chips - 1 - s, chips - 1)]) for s in range(1, chips)
    ]
    order = [(targets[s], s) for s in range(chips)]
    pieces_in = got_inner + got_outer
    mine, _ = lax.optimization_barrier((mine, outer[0]))
    other = lax.ppermute(
        mine, axes,
        [(p * lanes + i, p * lanes + lanes - 1 - i) for p in range(1, patches, 2) for i in range(lanes)],
    )

    def device(p, chip, core):
        return p * lanes + 2 * chip + core

    first_pairs, second_pairs, siblings = [], [], []
    for p in range(patches):
        for chip in range(chips):
            siblings += [(device(p, chip, core), device(p, chip, 1 - core)) for core in range(2)]
            for core, away in ((0, 1), (1, -1)):
                if 0 <= chip + away < chips:
                    to_first, to_second = device(p, chip + away, core), device(p, chip + away, core)
                    to = p
                else:
                    to = p + 1 if (p % 2 == 0) == (away == 1) else p - 1
                    if not 0 <= to < patches:
                        continue
                    to_first = to_second = device(to, chip, 1 - core)
                first_pairs.append((device(p, chip, core), to_first))
                second_pairs.append((device(p, chip, 1 - core), to_second))
    groups = [[0], list(range(1, chips))]
    early, late = groups
    got = [pieces_in[place] for place in early] + [pieces_in[chips + place] for place in early]
    row = array(len(early), step, width)
    early_rows = call(choose_kernel, "choose", [row, row], [info] + got)
    outer_rows = [lax.ppermute(early_rows[0], axes, first_pairs), lax.ppermute(early_rows[1], axes, second_pairs)]
    row = array(len(late), step, width)
    near, *late_rows, observed = call(
        functools.partial(collect_kernel, order, late), "collect",
        [array(2, chips, step, width), row, row, array(8, slots)], [info, mine, other] + pieces_in, after=outer_rows,
    )
    outer_rows += [lax.ppermute(late_rows[0], axes, first_pairs), lax.ppermute(late_rows[1], axes, second_pairs)]
    far = lax.ppermute(near, axes, siblings)

    split = [pltpu.VMEM((members, slots), BF16)] * 2
    prepared = call(
        prepare_kernel, "prepare",
        [bfloat(members, slots)] * 2 + [bfloat(width, members)] * 2
        + [array(width, width // 2), array(8, slots), array(members, width // 2)],
        [info, observed, near, far],
        [pltpu.VMEM((members, 2 * width), F32)] + [pltpu.VMEM((members, 2 * width), BF16)] * 2,
        flops=8 * members * slots * width, limit=20,
    )
    analysed = call(
        functools.partial(region_kernel, order, groups), "region", [array(step, width)] * lanes,
        [info, observed, near, far, *prepared, *outer_rows],
        split + [pltpu.VMEM((slots, slots), F32), pltpu.VMEM((width + 8, slots), F32)],
        limit=24,
    )
    def swapped(x):
        return lax.ppermute(analysed[x], "member", [(i, i ^ x) for i in range(lanes)]) if x else analysed[0]

    order = sorted(range(lanes), key=lambda x: (x.bit_length() != lanes.bit_length() - 1, -x))
    return call(
        functools.partial(unpack_kernel, order), "unpack", array(step, rows, width),
        [info] + [swapped(x) for x in order], [pltpu.VMEM((rows, step, width), F32)], limit=48,
    )


def solution(mesh):
    return jax.shard_map(
        per_device,
        mesh=mesh,
        in_specs=(
            P("member", "patch", None),
            P(None, "patch", None),
            P("member"),
            P(("patch", "member"), None),
            P(("patch", "member")),
            P(("patch", "member"), None),
            P(("patch", "member"), None),
        ),
        out_specs=P("member", "patch", None),
        check_vma=False,
    )
```

```python
import functools
import math

import jax
import jax.numpy as jnp
from jax import lax
from jax.experimental import pallas as pl
from jax.experimental.pallas import tpu as pltpu
from jax.sharding import PartitionSpec as P

STEPS = 2
COARSE = 0.2
DONE = 0.01
LARGE = 2e4
PART = 256
F32 = jnp.float32
BF16 = jnp.bfloat16


def pack_kernel(info_ref, field_hbm, flow_hbm, emission_hbm, first_ref, second_ref, flow_ref, emission_ref,
                field_ref, member_ref, sems):
    members, rows, width = field_ref.shape
    moves = [
        pltpu.make_async_copy(source, target, sems.at[i])
        for i, (source, target) in enumerate(
            ((field_hbm, field_ref), (flow_hbm, flow_ref), (emission_hbm, member_ref))
        )
    ]
    for move in moves:
        move.start()
    for move in moves[1:]:
        move.wait()
    diagonal = lax.broadcasted_iota(jnp.int32, (members, members), 0) == lax.broadcasted_iota(
        jnp.int32, (members, members), 1
    )
    column = jnp.sum(jnp.where(diagonal, member_ref[...], 0.0), axis=1, keepdims=True)
    emission_ref[...] = jnp.broadcast_to(column, emission_ref.shape)
    moves[0].wait()
    even = info_ref[2] == 0
    for place in range(STEPS):
        tail, head = field_ref[:, rows - STEPS + place, :], field_ref[:, place, :]
        at = pl.ds(place * members, members)
        first_ref[at, :] = jnp.where(even, tail, head)
        second_ref[at, :] = jnp.where(even, head, tail)
    tail, head = flow_ref[:, rows - 1, :], flow_ref[:, 0, :]
    at = pl.ds(STEPS * members, 8)
    first_ref[at, :] = jnp.concatenate([jnp.where(even, tail, head)] * 2, axis=0)
    second_ref[at, :] = jnp.concatenate([jnp.where(even, head, tail)] * 2, axis=0)


def doubled(x):
    return jnp.concatenate([x, x], axis=1)


def weights_of(flow):
    row_flow, col_flow, kept, source = flow[0:1], flow[1:2], 1.0 - flow[2:3], flow[3:4]
    behind, ahead = jnp.maximum(row_flow, 0.0), -jnp.minimum(row_flow, 0.0)
    left, right = jnp.maximum(col_flow, 0.0), -jnp.minimum(col_flow, 0.0)
    stays = 1.0 - behind - ahead - left - right
    return [kept * stays, kept * behind, kept * ahead, kept * left, kept * right, source]


def advance(weights, emission, behind, field, ahead):
    width = field.shape[1]
    return (
        weights[0] * field
        + weights[1] * behind
        + weights[2] * ahead
        + weights[3] * pltpu.roll(field, 1, 1)
        + weights[4] * pltpu.roll(field, width - 1, 1)
        + emission * weights[5]
    )


def inner_kernel(targets, info_ref, field_ref, flow_ref, emission_ref, kept_ref, *refs):
    out_refs, (wide_ref, weight_ref) = refs[:-2], refs[-2:]
    rows = field_ref.shape[1]
    emission = doubled(emission_ref[...])
    for row in range(1, rows - 1):
        weights = weights_of(flow_ref[:, row, :])
        for i, weight in enumerate(weights):
            weight_ref[row, pl.ds(i, 1), :] = weight
        wide_ref[row] = advance(
            weights, emission, field_ref[:, row - 1, :], field_ref[:, row, :], field_ref[:, row + 1, :]
        )
    for place, row in enumerate((1, 2, rows - 3, rows - 2)):
        kept_ref[place] = wide_ref[row]
    for out_ref, hops in zip(out_refs, targets):
        chip = sum(jnp.where(info_ref[0] == source, to, 0) for source, to in hops)

        @pl.when(chip > 0)
        def _():
            for place in range(2):
                position = 2 * chip + jnp.abs(info_ref[1] - 1 + place)
                row = position + info_ref[2] * (rows - 1 - 2 * position)
                weights = weight_ref[row]
                out_ref[place] = advance(
                    [weights[i : i + 1] for i in range(6)],
                    emission, wide_ref[row - 1], wide_ref[row], wide_ref[row + 1],
                )


def end_rows(info_ref, last, field_ref, flow_ref, emission_ref, kept_ref, halo_ref, out_ref):
    members, rows, width = field_ref.shape
    emission = doubled(emission_ref[...])

    def halo_row(place):
        return halo_ref[pl.ds(place * members, members), :]

    halo_weights = weights_of(halo_ref[pl.ds(STEPS * members, 4), :])
    for parity in range(2):

        @pl.when(info_ref[2] == parity)
        def _():
            if parity == last:
                end, near, outside, beyond = 0, 1, halo_row(1), halo_row(0)
                inside, further = kept_ref[0], kept_ref[1]
            else:
                end, near, outside, beyond = rows - 1, rows - 2, halo_row(0), halo_row(1)
                inside, further = kept_ref[3], kept_ref[2]

            def ordered(weights, outer, own, inner):
                behind, ahead = (outer, inner) if end == 0 else (inner, outer)
                return advance(weights, emission, behind, own, ahead)

            end_weights = weights_of(flow_ref[:, end, :])
            end_field = field_ref[:, end, :]
            outer = ordered(halo_weights, beyond, outside, end_field)
            own = ordered(end_weights, outside, end_field, field_ref[:, near, :])
            out_ref[last] = ordered(end_weights, outer, own, inside)
            out_ref[1 - last] = ordered(weights_of(flow_ref[:, near, :]), own, inside, further)


def edge_kernel(info_ref, field_ref, flow_ref, emission_ref, kept_ref, last_ref, first_ref, *refs):
    out_refs, scratch = refs[:-1], refs[-1]
    chips = len(out_refs)
    core = info_ref[1]
    for last, halo_ref in enumerate((first_ref, last_ref)):
        end_rows(info_ref, last, field_ref, flow_ref, emission_ref, kept_ref, halo_ref, scratch)
        for s, out_ref in enumerate(out_refs):

            @pl.when(info_ref[0] == (chips - 1 - s if last else s))
            def _():
                out_ref[0] = scratch[1 - core]
                out_ref[1] = scratch[core]


def source_of(chip, chips, hops, k):
    inner = sum(jnp.where(chip == to, source, 0) for source, to in hops)
    return jnp.where(chip == 0, k, jnp.where(chip == chips - 1, chips - 1 - k, inner))


def choose_kernel(info_ref, inner_ref, edge_ref, own_ref):
    at_edge = jnp.logical_or(info_ref[0] == 0, info_ref[0] == info_ref[3] - 1)
    for ref, here in ((inner_ref, jnp.logical_not(at_edge)), (edge_ref, at_edge)):

        @pl.when(here)
        def _():
            own_ref[...] = ref[1]


def collect_kernel(order, info_ref, mine_ref, other_ref, *refs):
    chips = len(order)
    near_other, near_own, late_own, observed_ref = refs[-4:]
    observed_ref[...] = jnp.where(info_ref[2] == 1, other_ref[...], mine_ref[...])
    chip = info_ref[0]
    at_edge = jnp.logical_or(chip == 0, chip == chips - 1)
    for index, (s, k) in enumerate(order):
        block = source_of(chip, chips, s, k)
        for ref, here in ((refs[index], jnp.logical_not(at_edge)), (refs[chips + index], at_edge)):

            @pl.when(here)
            def _():
                near_other[block] = ref[0]
                near_own[block] = ref[1]
                if index:
                    late_own[index - 1] = ref[1]


def unpack_kernel(order, info_ref, *refs):
    row_refs, out_ref, rows_ref = refs[:-2], refs[-2], refs[-1]
    rows = rows_ref.shape[0]
    for x, ref in zip(order, row_refs):
        position = (2 * info_ref[0] + info_ref[1]) ^ x
        rows_ref[position + info_ref[2] * (rows - 1 - 2 * position)] = ref[...]
    for row in range(rows):
        out_ref[:, row, :] = rows_ref[row]


def pieces(x, count):
    parts = []
    for _ in range(count - 1):
        part = x.astype(BF16)
        parts.append(part)
        x = x - part.astype(F32)
    return parts + [x.astype(BF16)]


def dot(a, b):
    return lax.dot_general(a, b, (((1,), (0,)), ((), ())), preferred_element_type=F32)


def dot_t(a, b):
    return lax.dot_general(a, b, (((0,), (0,)), ((), ())), preferred_element_type=F32)


def product(a, b):
    total = None
    for i, left in enumerate(a):
        for j, right in enumerate(b):
            if i + j < max(len(a), len(b)):
                term = dot(left, right)
                total = term if total is None else total + term
    return total


def observations(info_ref, observed_ref, width, root):
    slots = observed_ref.shape[1]
    cells, values, scales, count = (observed_ref[pl.ds(i, 1), :] for i in range(4))
    cells = cells.astype(jnp.int32)
    offset = sum((cells >= i * width).astype(jnp.int32) for i in (1, 2)) - 1
    column = cells - (offset + 1) * width
    side = offset * jnp.where(info_ref[2] == 1, -1, 1) * (1 - 2 * info_ref[1])
    cells = column + width * jnp.where(side == 0, 2, jnp.where(side < 0, 0, 1))
    active = lax.broadcasted_iota(jnp.int32, (1, slots), 1) < count.astype(jnp.int32)
    slot_weight = jnp.where(active, scales, 0.0)
    return cells, slot_weight, values, slot_weight * (1.0 / root)


def one_hot(cells, first, count):
    return (
        lax.broadcasted_iota(jnp.int32, (count, cells.shape[1]), 0) + first == cells
    ).astype(F32).astype(BF16)


def mean_of(blocks, members):
    total = blocks[0]
    for block in blocks[1:]:
        total = total + block
    return jnp.sum(total, axis=0, keepdims=True) * (1.0 / members)


def at_cells(row, chosen):
    parts = pieces(jnp.broadcast_to(row, (8, row.shape[1])), 3)
    return (dot(parts[0], chosen) + (dot(parts[1], chosen) + dot(parts[2], chosen)))[:1]


def prepare_kernel(
    info_ref, observed_ref, near_other, near_own, far_other, far_own,
    spread_high, spread_low, own_high, own_low, own_part, seen_ref, direction_ref,
    anomaly, high_ref, low_ref,
):
    chips, step, width = near_own.shape
    members = 2 * chips * step
    cells, _, _, scale = observations(info_ref, observed_ref, width, math.sqrt(members - 1))
    chosen = one_hot(cells, width, 2 * width)
    blocks = [pl.ds(index * step, step) for index in range(2 * chips)]
    means = []
    for place in range(2):
        columns = pl.ds(place * width, width)
        halves = (near_own, far_own) if place else (near_other, far_other)
        rows = [half.at[chip] for half in halves for chip in range(chips)]
        means.append(mean_of([row[...] for row in rows], members))
        for block, row in zip(blocks, rows):
            part = row[...] - means[-1]
            anomaly[block, columns] = part
            high_ref[block, columns] = part.astype(BF16)

    def unit(x):
        return x * (1.0 / jnp.maximum(jnp.max(jnp.abs(x)), 1e-30))

    high = high_ref[...]
    along = lax.dot_general(high[:16], high, (((1,), (1,)), ((), ())), preferred_element_type=F32)
    rows = unit(dot(unit(along).astype(BF16), high))
    weight = jnp.sum(rows * rows[:1], axis=1, keepdims=True)
    weight = weight + jnp.where(jnp.max(jnp.abs(weight)) > 0.0, 0.0, 1.0)
    pattern = unit(jnp.sum(rows * weight, axis=0, keepdims=True))
    total = jnp.zeros((1, 1), F32)
    for block in blocks:
        along = jnp.sum(anomaly[block, :] * pattern, axis=1, keepdims=True)
        total = total + jnp.sum(along * along, axis=0, keepdims=True)
        direction_ref[block, :] = jnp.broadcast_to(along, (step, direction_ref.shape[1]))
    length = lax.rsqrt(jnp.maximum(total, 1e-30))
    taken = None
    for block in blocks:
        direction = direction_ref[block, :] * length
        direction_ref[block, :] = direction
        term = anomaly[block, :] * doubled(doubled(direction))
        taken = term if taken is None else taken + term
    taken = jnp.sum(taken, axis=0, keepdims=True)
    own_part[...] = jnp.broadcast_to(taken[:, width:], (own_part.shape[1], width)).T

    for block in blocks:
        rest = anomaly[block, :] - doubled(doubled(direction_ref[block, :])) * taken
        high, low = pieces(rest, 2)
        high_ref[block, :] = high
        low_ref[block, :] = low
        own = rest[:, width:].T
        own_high[:, block], own_low[:, block] = pieces(own, 2)
    seen_ref[pl.ds(0, 1), :] = at_cells(jnp.concatenate(means, axis=1), chosen)
    seen_ref[pl.ds(1, 1), :] = at_cells(taken, chosen)
    for first in range(0, members, PART):
        rows = pl.ds(first, PART)
        spread = (dot(high_ref[rows, :], chosen) + dot(low_ref[rows, :], chosen)) * scale
        high, low = pieces(spread, 2)
        spread_high[rows, :] = high
        spread_low[rows, :] = low


def square(parts):
    half = parts[0].shape[0] // 2
    upper = product([part[:half] for part in parts], parts)
    lower = product([part[half:] for part in parts], [part[:, half:] for part in parts])
    return upper, jnp.concatenate([upper[:, half:].T, lower], axis=1)


def region_kernel(
    order, info_ref, observed_ref, near_own, far_own, high_in, low_in, own_high, own_low, own_part, seen_ref,
    direction_ref, early_ref, late_ref, rest_ref, *refs,
):
    chips, step, width = near_own.shape
    out_refs = refs[:-4]
    spread_high, spread_low, factor, answer = refs[-4:]
    members = 2 * chips * step
    slots = observed_ref.shape[1]
    root = math.sqrt(members - 1)
    core = info_ref[1]
    ends = jnp.logical_or(
        jnp.logical_and(info_ref[0] == 0, core == 0), jnp.logical_and(info_ref[0] == chips - 1, core == 1)
    )
    giver = jnp.where(ends, info_ref[0], info_ref[0] - 1 + 2 * core)
    part = jnp.where(ends, 0, 1)
    cells, slot_weight, values, scale = observations(info_ref, observed_ref, width, root)
    chosen = one_hot(cells, 0, width)

    def rows_at(half, chip):
        return pl.ds(pl.multiple_of((half * chips + chip) * step, step), step)

    blocks = [(early_ref, rows_at(part, source_of(giver, chips, *order[0])))]
    blocks += [
        (late_ref.at[place - 1], rows_at(part, source_of(giver, chips, *order[place]))) for place in range(1, chips)
    ]
    blocks += [(rest_ref.at[chip], rows_at(1 - part, chip)) for chip in range(chips)]
    mean = mean_of([ref[...] for ref, _ in blocks], members)
    taken = None
    for ref, block in blocks:
        term = (ref[...] - mean) * doubled(direction_ref[block, :])
        taken = term if taken is None else taken + term
    taken = jnp.sum(taken, axis=0, keepdims=True)
    seen_mean = seen_ref[pl.ds(0, 1), :] + at_cells(mean, chosen)
    common = (seen_ref[pl.ds(1, 1), :] + at_cells(taken, chosen)) * scale
    innovation = slot_weight * (values - seen_mean)
    for ref, block in blocks:
        rest = ref[...] - mean - doubled(direction_ref[block, :]) * taken
        high, low = pieces(rest, 2)
        high, low = pieces((dot(high, chosen) + dot(low, chosen)) * scale, 2)
        spread_high[block, :] = high + high_in[block, :]
        spread_low[block, :] = low + low_in[block, :]

    high, low = spread_high[...], spread_low[...]
    eye = lax.broadcasted_iota(jnp.int32, (slots, slots), 0) == lax.broadcasted_iota(
        jnp.int32, (slots, slots), 1
    )
    turned = high.T
    cross = dot(turned, low)
    factor[...] = dot(turned, high) + (cross + cross.T) + jnp.where(eye, 1.0, 0.0)
    answer[pl.ds(0, width), :] = product([own_high[...], own_low[...]], [high, low])
    answer[pl.ds(width, 8), :] = jnp.where(
        lax.broadcasted_iota(jnp.int32, (8, slots), 0) == 0, jnp.broadcast_to(common, (8, slots)), 0.0
    )
    half = slots // 2
    upper, lower = pl.ds(0, half), pl.ds(half, half)

    def after(bound):
        return bound * bound / (2.0 - bound * bound)

    def size(matrix):
        return jnp.sum(jnp.sum(matrix * matrix, axis=0, keepdims=True))

    def begin(count):
        parts = pieces(factor[...], count)
        top, bottom = square(parts)
        limit = 1.0001 * jnp.sqrt(jnp.sqrt(size(top) + size(bottom)))
        start = 2.0 / (1.0 + limit)
        bound = 1.0 - start
        gain = 2.0 / (2.0 - bound * bound)
        answer[...] = (gain * start) * (2.0 * answer[...] - start * product(pieces(answer[...], count), parts))
        factor[upper, :] = (gain * start) * (2.0 * factor[upper, :] - start * top)
        factor[lower, :] = (gain * start) * (2.0 * factor[lower, :] - start * bottom)
        return after(bound)

    def refine(bound, count):
        gain = 2.0 / (2.0 - bound * bound)
        parts = pieces(factor[...], count)
        answer[...] = gain * (2.0 * answer[...] - product(pieces(answer[...], count), parts))
        top, bottom = square(parts)
        factor[upper, :] = gain * (2.0 * factor[upper, :] - top)
        factor[lower, :] = gain * (2.0 * factor[lower, :] - bottom)
        return after(bound)

    def close(bound, rest):
        gain = 2.0 / (2.0 - bound * bound)
        answer[...] = gain * (answer[...] + dot(answer[...].astype(BF16), rest))
        return gain

    def finish(bound):
        rest = factor[...].astype(BF16)
        gain = close(bound, rest)
        factor[...] = gain * (dot(rest, rest) - jnp.where(eye, 0.5 * bound * bound, 0.0))
        return after(bound)

    large = size(factor[...]) > LARGE * LARGE
    bound = lax.cond(large, lambda: begin(3), lambda: begin(2))
    bound = lax.while_loop(lambda b: jnp.logical_and(b > COARSE, large), lambda b: refine(b, 3), bound)
    bound = lax.while_loop(lambda b: b > COARSE, lambda b: refine(b, 2), bound)
    factor[...] = jnp.where(eye, 1.0, 0.0) - factor[...]
    bound = lax.while_loop(lambda b: b > DONE, finish, bound)
    close(bound, factor[...].astype(BF16))

    solved = answer[pl.ds(0, width), :]
    alone = answer[pl.ds(width, 1), :]
    share = own_part[:, :1] - jnp.sum(solved * common, axis=1, keepdims=True)
    solved = solved + (share / (1.0 + jnp.sum(common * alone, axis=1, keepdims=True))) * alone
    solved = solved.T
    which = lax.broadcasted_iota(jnp.int32, (8, slots), 0)
    sides = jnp.where(which == 0, innovation * (1.0 / root), jnp.where(which == 1, -0.5 * common, 0.0))
    parts = pieces(solved, 3)
    sides = product(pieces(sides, 3), parts)
    shift, along = sides[0:1], sides[1:2]
    halved = [part * jnp.asarray(-0.5, BF16) for part in pieces(solved, 2)]
    for x, out_ref in enumerate(out_refs):
        chip, part = info_ref[0] ^ (x // 2), x % 2
        rows = pl.ds(pl.multiple_of((part * chips + chip) * step, step), step)
        moved = product([spread_high[rows, :], spread_low[rows, :]], halved)
        moved = moved + doubled(direction_ref[rows, :]) * along
        own = (far_own if part else near_own)[chip]
        out_ref[...] = own + shift + moved


VMEM = pl.BlockSpec(memory_space=pltpu.VMEM)
SMEM = pl.BlockSpec(memory_space=pltpu.SMEM)


def call(kernel, name, out_shape, args, scratch=(), flops=None, aliases={}, limit=8, after=()):
    several = isinstance(out_shape, (list, tuple))
    if after:
        count, inner = len(args), kernel
        args = [*args, *after]
        kernel = lambda *refs: inner(*refs[:count], *refs[len(args) :])
    return pl.pallas_call(
        kernel,
        out_shape=out_shape,
        in_specs=[SMEM] + [VMEM] * (len(args) - 1 - len(after)) + [pl.BlockSpec(memory_space=pl.ANY)] * len(after),
        out_specs=[VMEM] * len(out_shape) if several else VMEM,
        scratch_shapes=scratch,
        input_output_aliases=aliases,
        compiler_params=pltpu.CompilerParams(vmem_limit_bytes=limit * 1024 * 1024),
        cost_estimate=flops and pl.CostEstimate(flops=flops, bytes_accessed=0, transcendentals=0),
        name=name,
    )(*args)


def bfloat(*shape):
    return jax.ShapeDtypeStruct(shape, BF16)


def array(*shape):
    return jax.ShapeDtypeStruct(shape, F32)


def per_device(
    init_field, flow_fields, emission, observed_cell, observed_count, observed_value, observed_scale
):
    step, rows, width = init_field.shape
    slots = observed_cell.shape[1]
    patches, lanes = lax.axis_size("patch"), lax.axis_size("member")
    chips = lanes // 2
    members = lanes * step
    axes = ("patch", "member")
    count = patches * lanes
    patch, lane = lax.axis_index("patch"), lax.axis_index("member")
    info = jnp.stack([lane // 2, lane % 2, patch % 2, jnp.int32(chips)]).astype(jnp.int32)

    edge = array(STEPS * step + 8, width)
    place = pl.BlockSpec(memory_space=pltpu.HBM)
    to_last, to_first, flow, emitted = pl.pallas_call(
        pack_kernel,
        out_shape=[edge, edge, array(*flow_fields.shape), array(step, width // 2)],
        in_specs=[SMEM] + [place] * 3, out_specs=[VMEM] * 4,
        scratch_shapes=[
            pltpu.VMEM((step, rows, width), F32), pltpu.VMEM((1, step), F32), pltpu.SemaphoreType.DMA((3,))
        ],
        compiler_params=pltpu.CompilerParams(vmem_limit_bytes=32 * 1024 * 1024), name="pack",
    )(info, init_field, flow_fields, emission[None, :])

    def swap(message, start):
        lower = range(start, patches - 1, 2)
        return lax.ppermute(message, "patch", [(p, p + 1) for p in lower] + [(p + 1, p) for p in lower])

    halo_last, halo_first = swap(to_last, 0), swap(to_first, 1)

    mine = jnp.concatenate(
        [
            observed_cell.astype(F32),
            observed_value,
            observed_scale,
            jnp.broadcast_to(observed_count.astype(F32)[:, None], observed_cell.shape),
        ]
        * 2,
        axis=0,
    )

    def between(message, hops):
        return lax.ppermute(message, "member", [(2 * a + core, 2 * b + core) for a, b in hops for core in range(2)])

    mirrored = [
        [hop for to in range(1, chips // 2) for hop in (((to + s) % chips, to), (chips - 1 - (to + s) % chips, chips - 1 - to))]
        for s in range(chips)
    ]
    turning = [[((to - s) % chips, to) for to in range(1, chips - 1)] for s in range(chips)]
    single = all(len({source for source, _ in hops}) == len(hops) for hops in mirrored)
    targets = mirrored if single else turning
    pair = array(2, step, width)
    args = [info, init_field, flow, emitted]
    kept, *inner = call(
        functools.partial(inner_kernel, targets), "inner", [array(4, step, width)] + [pair] * chips, args,
        [pltpu.VMEM((rows, step, width), F32), pltpu.VMEM((rows, 8, width), F32)], limit=32,
    )
    got_inner = [inner[0]] + [between(inner[s], targets[s]) for s in range(1, chips)]
    outer = call(
        edge_kernel, "edge", [pair] * chips, args + [kept, halo_last, halo_first],
        [pltpu.VMEM((2, step, width), F32)], limit=32,
    )
    got_outer = [outer[0]] + [
        between(outer[s], [(s, 0), (chips - 1 - s, chips - 1)]) for s in range(1, chips)
    ]
    order = [(targets[s], s) for s in range(chips)]
    pieces_in = got_inner + got_outer
    mine, _ = lax.optimization_barrier((mine, outer[0]))
    other = lax.ppermute(
        mine, axes,
        [(p * lanes + i, p * lanes + lanes - 1 - i) for p in range(1, patches, 2) for i in range(lanes)],
    )

    def device(p, chip, core):
        return p * lanes + 2 * chip + core

    borders, siblings = [], []
    for p in range(patches):
        for chip in range(chips):
            for core, away in ((0, -1), (1, 1)):
                siblings.append((device(p, chip, core), device(p, chip, 1 - core)))
                if 0 <= chip + away < chips:
                    borders.append((device(p, chip, core), device(p, chip + away, 1 - core)))
                else:
                    to = p + 1 if (p % 2 == 0) == (away == 1) else p - 1
                    if 0 <= to < patches:
                        borders.append((device(p, chip, core), device(to, chip, core)))

    early = call(choose_kernel, "choose", array(step, width), [info, inner[0], outer[0]])
    got_early = lax.ppermute(early, axes, borders)
    half = array(chips, step, width)
    near_other, near_own, late, observed = call(
        functools.partial(collect_kernel, order), "collect",
        [half, half, array(chips - 1, step, width), array(8, slots)], [info, mine, other] + pieces_in, after=[got_early],
    )
    far_own = lax.ppermute(near_other, axes, siblings)
    got_late = lax.ppermute(late, axes, borders)
    far_other = lax.ppermute(near_own, axes, siblings)
    got_rest = lax.ppermute(far_own, axes, borders)

    split = [pltpu.VMEM((members, slots), BF16)] * 2
    prepared = call(
        prepare_kernel, "prepare",
        [bfloat(members, slots)] * 2 + [bfloat(width, members)] * 2
        + [array(width, width // 2), array(8, slots), array(members, width // 2)],
        [info, observed, near_other, near_own, far_other, far_own],
        [pltpu.VMEM((members, 2 * width), F32)] + [pltpu.VMEM((members, 2 * width), BF16)] * 2,
        flops=8 * members * slots * width, limit=20,
    )
    analysed = call(
        functools.partial(region_kernel, order), "region", [array(step, width)] * lanes,
        [info, observed, near_own, far_own, *prepared, got_early, got_late, got_rest],
        split + [pltpu.VMEM((slots, slots), F32), pltpu.VMEM((width + 8, slots), F32)],
        limit=24,
    )
    def swapped(x):
        return lax.ppermute(analysed[x], "member", [(i, i ^ x) for i in range(lanes)]) if x else analysed[0]

    order = sorted(range(lanes), key=lambda x: (x.bit_length() != lanes.bit_length() - 1, -x))
    return call(
        functools.partial(unpack_kernel, order), "unpack", array(step, rows, width),
        [info] + [swapped(x) for x in order], [pltpu.VMEM((rows, step, width), F32)], limit=48,
    )


def solution(mesh):
    return jax.shard_map(
        per_device,
        mesh=mesh,
        in_specs=(
            P("member", "patch", None),
            P(None, "patch", None),
            P("member"),
            P(("patch", "member"), None),
            P(("patch", "member")),
            P(("patch", "member"), None),
            P(("patch", "member"), None),
        ),
        out_specs=P("member", "patch", None),
        check_vma=False,
    )
```

```python
import functools
import math

import jax
import jax.numpy as jnp
from jax import lax
from jax.experimental import pallas as pl
from jax.experimental.pallas import tpu as pltpu
from jax.sharding import PartitionSpec as P

STEPS = 2
COARSE = 0.2
DONE = 0.01
LARGE = 2e4
PART = 256
PADDING = 8
F32 = jnp.float32
BF16 = jnp.bfloat16


def pack_kernel(info_ref, field_hbm, flow_hbm, emission_hbm, first_ref, second_ref, flow_ref, emission_ref,
                field_ref, member_ref, sems):
    members, rows, width = field_ref.shape
    moves = [
        pltpu.make_async_copy(source, target, sems.at[i])
        for i, (source, target) in enumerate(
            ((field_hbm, field_ref), (flow_hbm, flow_ref), (emission_hbm, member_ref))
        )
    ]
    for move in moves:
        move.start()
    for move in moves[1:]:
        move.wait()
    diagonal = lax.broadcasted_iota(jnp.int32, (members, members), 0) == lax.broadcasted_iota(
        jnp.int32, (members, members), 1
    )
    column = jnp.sum(jnp.where(diagonal, member_ref[...], 0.0), axis=1, keepdims=True)
    emission_ref[...] = jnp.broadcast_to(column, emission_ref.shape)
    moves[0].wait()
    even = info_ref[2] == 0
    for place in range(STEPS):
        tail, head = field_ref[:, rows - STEPS + place, :], field_ref[:, place, :]
        at = pl.ds(place * members, members)
        first_ref[at, :] = jnp.where(even, tail, head)
        second_ref[at, :] = jnp.where(even, head, tail)
    tail, head = flow_ref[:, rows - 1, :], flow_ref[:, 0, :]
    at = pl.ds(STEPS * members, 8)
    first_ref[at, :] = jnp.concatenate([jnp.where(even, tail, head)] * 2, axis=0)
    second_ref[at, :] = jnp.concatenate([jnp.where(even, head, tail)] * 2, axis=0)


def doubled(x):
    return jnp.concatenate([x, x], axis=1)


def weights_of(flow):
    row_flow, col_flow, kept, source = flow[0:1], flow[1:2], 1.0 - flow[2:3], flow[3:4]
    behind, ahead = jnp.maximum(row_flow, 0.0), -jnp.minimum(row_flow, 0.0)
    left, right = jnp.maximum(col_flow, 0.0), -jnp.minimum(col_flow, 0.0)
    stays = 1.0 - behind - ahead - left - right
    return [kept * stays, kept * behind, kept * ahead, kept * left, kept * right, source]


def advance(weights, emission, behind, field, ahead):
    width = field.shape[1]
    return (
        weights[0] * field
        + weights[1] * behind
        + weights[2] * ahead
        + weights[3] * pltpu.roll(field, 1, 1)
        + weights[4] * pltpu.roll(field, width - 1, 1)
        + emission * weights[5]
    )


def inner_kernel(targets, info_ref, field_ref, flow_ref, emission_ref, kept_ref, *refs):
    out_refs, (wide_ref, weight_ref) = refs[:-2], refs[-2:]
    rows = field_ref.shape[1]
    emission = doubled(emission_ref[...])
    for row in range(1, rows - 1):
        weights = weights_of(flow_ref[:, row, :])
        for i, weight in enumerate(weights):
            weight_ref[row, pl.ds(i, 1), :] = weight
        wide_ref[row] = advance(
            weights, emission, field_ref[:, row - 1, :], field_ref[:, row, :], field_ref[:, row + 1, :]
        )
    for place, row in enumerate((1, 2, rows - 3, rows - 2)):
        kept_ref[place] = wide_ref[row]
    for out_ref, hops in zip(out_refs, targets):
        chip = sum(jnp.where(info_ref[0] == source, to, 0) for source, to in hops)

        @pl.when(chip > 0)
        def _():
            for place in range(2):
                position = 2 * chip + jnp.abs(info_ref[1] - 1 + place)
                row = position + info_ref[2] * (rows - 1 - 2 * position)
                weights = weight_ref[row]
                out_ref[place] = advance(
                    [weights[i : i + 1] for i in range(6)],
                    emission, wide_ref[row - 1], wide_ref[row], wide_ref[row + 1],
                )


def end_rows(info_ref, last, field_ref, flow_ref, emission_ref, kept_ref, halo_ref, out_ref):
    members, rows, width = field_ref.shape
    emission = doubled(emission_ref[...])

    def halo_row(place):
        return halo_ref[pl.ds(place * members, members), :]

    halo_weights = weights_of(halo_ref[pl.ds(STEPS * members, 4), :])
    for parity in range(2):

        @pl.when(info_ref[2] == parity)
        def _():
            if parity == last:
                end, near, outside, beyond = 0, 1, halo_row(1), halo_row(0)
                inside, further = kept_ref[0], kept_ref[1]
            else:
                end, near, outside, beyond = rows - 1, rows - 2, halo_row(0), halo_row(1)
                inside, further = kept_ref[3], kept_ref[2]

            def ordered(weights, outer, own, inner):
                behind, ahead = (outer, inner) if end == 0 else (inner, outer)
                return advance(weights, emission, behind, own, ahead)

            end_weights = weights_of(flow_ref[:, end, :])
            end_field = field_ref[:, end, :]
            outer = ordered(halo_weights, beyond, outside, end_field)
            own = ordered(end_weights, outside, end_field, field_ref[:, near, :])
            out_ref[last] = ordered(end_weights, outer, own, inside)
            out_ref[1 - last] = ordered(weights_of(flow_ref[:, near, :]), own, inside, further)


def edge_kernel(info_ref, field_ref, flow_ref, emission_ref, kept_ref, last_ref, first_ref, *refs):
    out_refs, scratch = refs[:-1], refs[-1]
    chips = len(out_refs)
    core = info_ref[1]
    for last, halo_ref in enumerate((first_ref, last_ref)):
        end_rows(info_ref, last, field_ref, flow_ref, emission_ref, kept_ref, halo_ref, scratch)
        for s, out_ref in enumerate(out_refs):

            @pl.when(info_ref[0] == (chips - 1 - s if last else s))
            def _():
                out_ref[0] = scratch[1 - core]
                out_ref[1] = scratch[core]


def source_of(chip, chips, hops, k):
    inner = sum(jnp.where(chip == to, source, 0) for source, to in hops)
    return jnp.where(chip == 0, k, jnp.where(chip == chips - 1, chips - 1 - k, inner))


def collect_kernel(order, info_ref, mine_ref, other_ref, *refs):
    chips = len(order)
    near_other, near_own, observed_ref = refs[-3:]
    step = near_other.shape[1]
    observed_ref[...] = jnp.where(info_ref[2] == 1, other_ref[...], mine_ref[...])
    near_own[pl.ds(chips * step, PADDING), :] = jnp.zeros((PADDING, near_own.shape[1]), F32)
    chip = info_ref[0]
    at_edge = jnp.logical_or(chip == 0, chip == chips - 1)
    for index, (s, k) in enumerate(order):
        block = source_of(chip, chips, s, k)
        rows = pl.ds(pl.multiple_of(block * step, step), step)
        for ref, here in ((refs[index], jnp.logical_not(at_edge)), (refs[chips + index], at_edge)):

            @pl.when(here)
            def _():
                near_other[block] = ref[0]
                near_own[rows, :] = ref[1]


def unpack_kernel(order, info_ref, *refs):
    row_refs, out_ref = refs[:-1], refs[-1]
    rows = out_ref.shape[1]
    for x, ref in zip(order, row_refs):
        position = (2 * info_ref[0] + info_ref[1]) ^ x
        row = position + info_ref[2] * (rows - 1 - 2 * position)
        out_ref[:, pl.ds(row, 1), :] = ref[...][:, None, :]


def pieces(x, count):
    parts = []
    for _ in range(count - 1):
        part = x.astype(BF16)
        parts.append(part)
        x = x - part.astype(F32)
    return parts + [x.astype(BF16)]


def dot(a, b):
    return lax.dot_general(a, b, (((1,), (0,)), ((), ())), preferred_element_type=F32)


def dot_t(a, b):
    return lax.dot_general(a, b, (((0,), (0,)), ((), ())), preferred_element_type=F32)


def product(a, b):
    total = None
    for i, left in enumerate(a):
        for j, right in enumerate(b):
            if i + j < max(len(a), len(b)):
                term = dot(left, right)
                total = term if total is None else total + term
    return total


def observations(info_ref, observed_ref, width, root):
    slots = observed_ref.shape[1]
    cells, values, scales, count = (observed_ref[pl.ds(i, 1), :] for i in range(4))
    cells = cells.astype(jnp.int32)
    offset = sum((cells >= i * width).astype(jnp.int32) for i in (1, 2)) - 1
    column = cells - (offset + 1) * width
    side = offset * jnp.where(info_ref[2] == 1, -1, 1) * (1 - 2 * info_ref[1])
    cells = column + width * jnp.where(side == 0, 2, jnp.where(side < 0, 0, 1))
    active = lax.broadcasted_iota(jnp.int32, (1, slots), 1) < count.astype(jnp.int32)
    slot_weight = jnp.where(active, scales, 0.0)
    return cells, slot_weight, values, slot_weight * (1.0 / root)


def one_hot(cells, first, count):
    return (
        lax.broadcasted_iota(jnp.int32, (count, cells.shape[1]), 0) + first == cells
    ).astype(F32).astype(BF16)


def mean_of(blocks, members):
    total = blocks[0]
    for block in blocks[1:]:
        total = total + block
    return jnp.sum(total, axis=0, keepdims=True) * (1.0 / members)


def at_cells(row, chosen):
    parts = pieces(jnp.broadcast_to(row, (8, row.shape[1])), 3)
    return (dot(parts[0], chosen) + (dot(parts[1], chosen) + dot(parts[2], chosen)))[:1]


def prepare_kernel(
    info_ref, observed_ref, near_other, near_own, far_other, far_own,
    spread_high, spread_low, own_high, own_low, own_part, seen_ref, direction_ref,
    anomaly, high_ref, low_ref,
):
    chips, step, width = near_other.shape
    members = 2 * chips * step
    cells, _, _, scale = observations(info_ref, observed_ref, width, math.sqrt(members - 1))
    chosen = one_hot(cells, width, 2 * width)
    blocks = [pl.ds(index * step, step) for index in range(2 * chips)]
    means = []
    for place in range(2):
        columns = pl.ds(place * width, width)
        if place:
            rows = [near_own.at[block, :] for block in blocks[:chips]] + [far_own.at[chip] for chip in range(chips)]
        else:
            rows = [near_other.at[chip] for chip in range(chips)] + [far_other.at[block, :] for block in blocks[:chips]]
        means.append(mean_of([row[...] for row in rows], members))
        for block, row in zip(blocks, rows):
            part = row[...] - means[-1]
            anomaly[block, columns] = part
            high_ref[block, columns] = part.astype(BF16)

    def unit(x):
        return x * (1.0 / jnp.maximum(jnp.max(jnp.abs(x)), 1e-30))

    high = high_ref[...]
    along = lax.dot_general(high[:16], high, (((1,), (1,)), ((), ())), preferred_element_type=F32)
    rows = unit(dot(unit(along).astype(BF16), high))
    weight = jnp.sum(rows * rows[:1], axis=1, keepdims=True)
    weight = weight + jnp.where(jnp.max(jnp.abs(weight)) > 0.0, 0.0, 1.0)
    pattern = unit(jnp.sum(rows * weight, axis=0, keepdims=True))
    total = jnp.zeros((1, 1), F32)
    for block in blocks:
        along = jnp.sum(anomaly[block, :] * pattern, axis=1, keepdims=True)
        total = total + jnp.sum(along * along, axis=0, keepdims=True)
        direction_ref[block, :] = jnp.broadcast_to(along, (step, direction_ref.shape[1]))
    length = lax.rsqrt(jnp.maximum(total, 1e-30))
    taken = None
    for block in blocks:
        direction = direction_ref[block, :] * length
        direction_ref[block, :] = direction
        term = anomaly[block, :] * doubled(doubled(direction))
        taken = term if taken is None else taken + term
    taken = jnp.sum(taken, axis=0, keepdims=True)
    own_part[...] = jnp.broadcast_to(taken[:, width:], (own_part.shape[1], width)).T

    for block in blocks:
        rest = anomaly[block, :] - doubled(doubled(direction_ref[block, :])) * taken
        high, low = pieces(rest, 2)
        high_ref[block, :] = high
        low_ref[block, :] = low
        own = rest[:, width:].T
        own_high[:, block], own_low[:, block] = pieces(own, 2)
    seen_ref[pl.ds(0, 1), :] = at_cells(jnp.concatenate(means, axis=1), chosen)
    seen_ref[pl.ds(1, 1), :] = at_cells(taken, chosen)
    for first in range(0, members, PART):
        rows = pl.ds(first, PART)
        spread = (dot(high_ref[rows, :], chosen) + dot(low_ref[rows, :], chosen)) * scale
        high, low = pieces(spread, 2)
        spread_high[rows, :] = high
        spread_low[rows, :] = low


def square(parts):
    half = parts[0].shape[0] // 2
    upper = product([part[:half] for part in parts], parts)
    lower = product([part[half:] for part in parts], [part[:, half:] for part in parts])
    return upper, jnp.concatenate([upper[:, half:].T, lower], axis=1)


def region_kernel(
    info_ref, observed_ref, near_own, far_own, high_in, low_in, own_high, own_low, own_part, seen_ref,
    direction_ref, half_ref, rest_ref, *refs,
):
    chips, step, width = far_own.shape
    out_refs = refs[:-4]
    spread_high, spread_low, factor, answer = refs[-4:]
    members = 2 * chips * step
    slots = observed_ref.shape[1]
    root = math.sqrt(members - 1)
    core = info_ref[1]
    ends = jnp.logical_or(
        jnp.logical_and(info_ref[0] == 0, core == 0), jnp.logical_and(info_ref[0] == chips - 1, core == 1)
    )
    part = jnp.where(ends, 0, 1)
    cells, slot_weight, values, scale = observations(info_ref, observed_ref, width, root)
    chosen = one_hot(cells, 0, width)

    def rows_at(half, chip):
        return pl.ds(pl.multiple_of((half * chips + chip) * step, step), step)

    blocks = [(half_ref.at[pl.ds(chip * step, step), :], rows_at(part, chip)) for chip in range(chips)]
    blocks += [(rest_ref.at[chip], rows_at(1 - part, chip)) for chip in range(chips)]
    mean = mean_of([ref[...] for ref, _ in blocks], members)
    taken = None
    for ref, block in blocks:
        term = (ref[...] - mean) * doubled(direction_ref[block, :])
        taken = term if taken is None else taken + term
    taken = jnp.sum(taken, axis=0, keepdims=True)
    seen_mean = seen_ref[pl.ds(0, 1), :] + at_cells(mean, chosen)
    common = (seen_ref[pl.ds(1, 1), :] + at_cells(taken, chosen)) * scale
    innovation = slot_weight * (values - seen_mean)
    for ref, block in blocks:
        rest = ref[...] - mean - doubled(direction_ref[block, :]) * taken
        high, low = pieces(rest, 2)
        high, low = pieces((dot(high, chosen) + dot(low, chosen)) * scale, 2)
        spread_high[block, :] = high + high_in[block, :]
        spread_low[block, :] = low + low_in[block, :]

    high, low = spread_high[...], spread_low[...]
    eye = lax.broadcasted_iota(jnp.int32, (slots, slots), 0) == lax.broadcasted_iota(
        jnp.int32, (slots, slots), 1
    )
    turned = high.T
    cross = dot(turned, low)
    factor[...] = dot(turned, high) + (cross + cross.T) + jnp.where(eye, 1.0, 0.0)
    answer[pl.ds(0, width), :] = product([own_high[...], own_low[...]], [high, low])
    answer[pl.ds(width, 8), :] = jnp.where(
        lax.broadcasted_iota(jnp.int32, (8, slots), 0) == 0, jnp.broadcast_to(common, (8, slots)), 0.0
    )
    half = slots // 2
    upper, lower = pl.ds(0, half), pl.ds(half, half)

    def after(bound):
        return bound * bound / (2.0 - bound * bound)

    def size(matrix):
        return jnp.sum(jnp.sum(matrix * matrix, axis=0, keepdims=True))

    def begin(count):
        parts = pieces(factor[...], count)
        top, bottom = square(parts)
        limit = 1.0001 * jnp.sqrt(jnp.sqrt(size(top) + size(bottom)))
        start = 2.0 / (1.0 + limit)
        bound = 1.0 - start
        gain = 2.0 / (2.0 - bound * bound)
        answer[...] = (gain * start) * (2.0 * answer[...] - start * product(pieces(answer[...], count), parts))
        factor[upper, :] = (gain * start) * (2.0 * factor[upper, :] - start * top)
        factor[lower, :] = (gain * start) * (2.0 * factor[lower, :] - start * bottom)
        return after(bound)

    def refine(bound, count):
        gain = 2.0 / (2.0 - bound * bound)
        parts = pieces(factor[...], count)
        answer[...] = gain * (2.0 * answer[...] - product(pieces(answer[...], count), parts))
        top, bottom = square(parts)
        factor[upper, :] = gain * (2.0 * factor[upper, :] - top)
        factor[lower, :] = gain * (2.0 * factor[lower, :] - bottom)
        return after(bound)

    def close(bound, rest):
        gain = 2.0 / (2.0 - bound * bound)
        answer[...] = gain * (answer[...] + dot(answer[...].astype(BF16), rest))
        return gain

    def finish(bound):
        rest = factor[...].astype(BF16)
        gain = close(bound, rest)
        factor[...] = gain * (dot(rest, rest) - jnp.where(eye, 0.5 * bound * bound, 0.0))
        return after(bound)

    large = size(factor[...]) > LARGE * LARGE
    bound = lax.cond(large, lambda: begin(3), lambda: begin(2))
    bound = lax.while_loop(lambda b: jnp.logical_and(b > COARSE, large), lambda b: refine(b, 3), bound)
    bound = lax.while_loop(lambda b: b > COARSE, lambda b: refine(b, 2), bound)
    factor[...] = jnp.where(eye, 1.0, 0.0) - factor[...]
    bound = lax.while_loop(lambda b: b > DONE, finish, bound)
    close(bound, factor[...].astype(BF16))

    solved = answer[pl.ds(0, width), :]
    alone = answer[pl.ds(width, 1), :]
    share = own_part[:, :1] - jnp.sum(solved * common, axis=1, keepdims=True)
    solved = solved + (share / (1.0 + jnp.sum(common * alone, axis=1, keepdims=True))) * alone
    solved = solved.T
    which = lax.broadcasted_iota(jnp.int32, (8, slots), 0)
    sides = jnp.where(which == 0, innovation * (1.0 / root), jnp.where(which == 1, -0.5 * common, 0.0))
    parts = pieces(solved, 3)
    sides = product(pieces(sides, 3), parts)
    shift, along = sides[0:1], sides[1:2]
    halved = [part * jnp.asarray(-0.5, BF16) for part in pieces(solved, 2)]
    for x, out_ref in enumerate(out_refs):
        chip, part = info_ref[0] ^ (x // 2), x % 2
        rows = pl.ds(pl.multiple_of((part * chips + chip) * step, step), step)
        moved = product([spread_high[rows, :], spread_low[rows, :]], halved)
        moved = moved + doubled(direction_ref[rows, :]) * along
        own = far_own[chip] if part else near_own[rows_at(0, chip), :]
        out_ref[...] = own + shift + moved


VMEM = pl.BlockSpec(memory_space=pltpu.VMEM)
SMEM = pl.BlockSpec(memory_space=pltpu.SMEM)


def call(kernel, name, out_shape, args, scratch=(), flops=None, aliases={}, limit=8, after=()):
    several = isinstance(out_shape, (list, tuple))
    if after:
        count, inner = len(args), kernel
        args = [*args, *after]
        kernel = lambda *refs: inner(*refs[:count], *refs[len(args) :])
    return pl.pallas_call(
        kernel,
        out_shape=out_shape,
        in_specs=[SMEM] + [VMEM] * (len(args) - 1 - len(after)) + [pl.BlockSpec(memory_space=pl.ANY)] * len(after),
        out_specs=[VMEM] * len(out_shape) if several else VMEM,
        scratch_shapes=scratch,
        input_output_aliases=aliases,
        compiler_params=pltpu.CompilerParams(vmem_limit_bytes=limit * 1024 * 1024),
        cost_estimate=flops and pl.CostEstimate(flops=flops, bytes_accessed=0, transcendentals=0),
        name=name,
    )(*args)


def bfloat(*shape):
    return jax.ShapeDtypeStruct(shape, BF16)


def array(*shape):
    return jax.ShapeDtypeStruct(shape, F32)


def per_device(
    init_field, flow_fields, emission, observed_cell, observed_count, observed_value, observed_scale
):
    step, rows, width = init_field.shape
    slots = observed_cell.shape[1]
    patches, lanes = lax.axis_size("patch"), lax.axis_size("member")
    chips = lanes // 2
    members = lanes * step
    axes = ("patch", "member")
    count = patches * lanes
    patch, lane = lax.axis_index("patch"), lax.axis_index("member")
    info = jnp.stack([lane // 2, lane % 2, patch % 2, jnp.int32(chips)]).astype(jnp.int32)

    edge = array(STEPS * step + 8, width)
    place = pl.BlockSpec(memory_space=pltpu.HBM)
    to_last, to_first, flow, emitted = pl.pallas_call(
        pack_kernel,
        out_shape=[edge, edge, array(*flow_fields.shape), array(step, width // 2)],
        in_specs=[SMEM] + [place] * 3, out_specs=[VMEM] * 4,
        scratch_shapes=[
            pltpu.VMEM((step, rows, width), F32), pltpu.VMEM((1, step), F32), pltpu.SemaphoreType.DMA((3,))
        ],
        compiler_params=pltpu.CompilerParams(vmem_limit_bytes=32 * 1024 * 1024), name="pack",
    )(info, init_field, flow_fields, emission[None, :])

    def swap(message, start):
        lower = range(start, patches - 1, 2)
        return lax.ppermute(message, "patch", [(p, p + 1) for p in lower] + [(p + 1, p) for p in lower])

    halo_last, halo_first = swap(to_last, 0), swap(to_first, 1)

    mine = jnp.concatenate(
        [
            observed_cell.astype(F32),
            observed_value,
            observed_scale,
            jnp.broadcast_to(observed_count.astype(F32)[:, None], observed_cell.shape),
        ]
        * 2,
        axis=0,
    )

    def between(message, hops):
        return lax.ppermute(message, "member", [(2 * a + core, 2 * b + core) for a, b in hops for core in range(2)])

    mirrored = [
        [hop for to in range(1, chips // 2) for hop in (((to + s) % chips, to), (chips - 1 - (to + s) % chips, chips - 1 - to))]
        for s in range(chips)
    ]
    turning = [[((to - s) % chips, to) for to in range(1, chips - 1)] for s in range(chips)]
    single = all(len({source for source, _ in hops}) == len(hops) for hops in mirrored)
    targets = mirrored if single else turning
    pair = array(2, step, width)
    args = [info, init_field, flow, emitted]
    kept, *inner = call(
        functools.partial(inner_kernel, targets), "inner", [array(4, step, width)] + [pair] * chips, args,
        [pltpu.VMEM((rows, step, width), F32), pltpu.VMEM((rows, 8, width), F32)], limit=32,
    )
    got_inner = [inner[0]] + [between(inner[s], targets[s]) for s in range(1, chips)]
    outer = call(
        edge_kernel, "edge", [pair] * chips, args + [kept, halo_last, halo_first],
        [pltpu.VMEM((2, step, width), F32)], limit=32,
    )
    got_outer = [outer[0]] + [
        between(outer[s], [(s, 0), (chips - 1 - s, chips - 1)]) for s in range(1, chips)
    ]
    order = [(targets[s], s) for s in range(chips)]
    pieces_in = got_inner + got_outer
    mine, _ = lax.optimization_barrier((mine, outer[0]))
    other = lax.ppermute(
        mine, axes,
        [(p * lanes + i, p * lanes + lanes - 1 - i) for p in range(1, patches, 2) for i in range(lanes)],
    )

    def device(p, chip, core):
        return p * lanes + 2 * chip + core

    borders, siblings = [], []
    for p in range(patches):
        for chip in range(chips):
            for core, away in ((0, -1), (1, 1)):
                siblings.append((device(p, chip, core), device(p, chip, 1 - core)))
                if 0 <= chip + away < chips:
                    borders.append((device(p, chip, core), device(p, chip + away, 1 - core)))
                else:
                    to = p + 1 if (p % 2 == 0) == (away == 1) else p - 1
                    if 0 <= to < patches:
                        borders.append((device(p, chip, core), device(to, chip, core)))

    half = array(chips, step, width)
    near_other, near_own, observed = call(
        functools.partial(collect_kernel, order), "collect",
        [half, array(chips * step + PADDING, width), array(8, slots)], [info, mine, other] + pieces_in,
    )
    far_own = lax.ppermute(near_other, axes, siblings)
    got_half = lax.ppermute(near_own, axes, borders)
    far_other = lax.ppermute(near_own, axes, siblings)
    got_rest = lax.ppermute(far_own, axes, borders)

    split = [pltpu.VMEM((members, slots), BF16)] * 2
    prepared = call(
        prepare_kernel, "prepare",
        [bfloat(members, slots)] * 2 + [bfloat(width, members)] * 2
        + [array(width, width // 2), array(8, slots), array(members, width // 2)],
        [info, observed, near_other, near_own, far_other, far_own],
        [pltpu.VMEM((members, 2 * width), F32)] + [pltpu.VMEM((members, 2 * width), BF16)] * 2,
        flops=8 * members * slots * width, limit=20,
    )
    analysed = call(
        region_kernel, "region", [array(step, width)] * lanes,
        [info, observed, near_own, far_own, *prepared, got_half, got_rest],
        split + [pltpu.VMEM((slots, slots), F32), pltpu.VMEM((width + 8, slots), F32)],
        limit=24,
    )
    def swapped(x):
        return lax.ppermute(analysed[x], "member", [(i, i ^ x) for i in range(lanes)]) if x else analysed[0]

    order = sorted(range(lanes), key=lambda x: (x.bit_length() != lanes.bit_length() - 1, -x))
    return call(
        functools.partial(unpack_kernel, order), "unpack", array(step, rows, width),
        [info] + [swapped(x) for x in order], limit=48,
    )


def solution(mesh):
    return jax.shard_map(
        per_device,
        mesh=mesh,
        in_specs=(
            P("member", "patch", None),
            P(None, "patch", None),
            P("member"),
            P(("patch", "member"), None),
            P(("patch", "member")),
            P(("patch", "member"), None),
            P(("patch", "member"), None),
        ),
        out_specs=P("member", "patch", None),
        check_vma=False,
    )
```

```python
import functools
import math

import jax
import jax.numpy as jnp
from jax import lax
from jax.experimental import pallas as pl
from jax.experimental.pallas import tpu as pltpu
from jax.sharding import PartitionSpec as P

STEPS = 2
COARSE = 0.35
DONE = 0.02
LARGE = 2e4
PART = 256
PADDING = 8
F32 = jnp.float32
BF16 = jnp.bfloat16


def pack_kernel(info_ref, field_hbm, flow_hbm, emission_hbm, first_ref, second_ref, flow_ref, emission_ref,
                field_ref, member_ref, sems):
    members, rows, width = field_ref.shape
    moves = [
        pltpu.make_async_copy(source, target, sems.at[i])
        for i, (source, target) in enumerate(
            ((field_hbm, field_ref), (flow_hbm, flow_ref), (emission_hbm, member_ref))
        )
    ]
    for move in moves:
        move.start()
    for move in moves[1:]:
        move.wait()
    diagonal = lax.broadcasted_iota(jnp.int32, (members, members), 0) == lax.broadcasted_iota(
        jnp.int32, (members, members), 1
    )
    column = jnp.sum(jnp.where(diagonal, member_ref[...], 0.0), axis=1, keepdims=True)
    emission_ref[...] = jnp.broadcast_to(column, emission_ref.shape)
    moves[0].wait()
    even = info_ref[2] == 0
    for place in range(STEPS):
        tail, head = field_ref[:, rows - STEPS + place, :], field_ref[:, place, :]
        at = pl.ds(place * members, members)
        first_ref[at, :] = jnp.where(even, tail, head)
        second_ref[at, :] = jnp.where(even, head, tail)
    tail, head = flow_ref[:, rows - 1, :], flow_ref[:, 0, :]
    at = pl.ds(STEPS * members, 8)
    first_ref[at, :] = jnp.concatenate([jnp.where(even, tail, head)] * 2, axis=0)
    second_ref[at, :] = jnp.concatenate([jnp.where(even, head, tail)] * 2, axis=0)


def doubled(x):
    return jnp.concatenate([x, x], axis=1)


def weights_of(flow):
    row_flow, col_flow, kept, source = flow[0:1], flow[1:2], 1.0 - flow[2:3], flow[3:4]
    behind, ahead = jnp.maximum(row_flow, 0.0), -jnp.minimum(row_flow, 0.0)
    left, right = jnp.maximum(col_flow, 0.0), -jnp.minimum(col_flow, 0.0)
    stays = 1.0 - behind - ahead - left - right
    return [kept * stays, kept * behind, kept * ahead, kept * left, kept * right, source]


def advance(weights, emission, behind, field, ahead):
    width = field.shape[1]
    return (
        weights[0] * field
        + weights[1] * behind
        + weights[2] * ahead
        + weights[3] * pltpu.roll(field, 1, 1)
        + weights[4] * pltpu.roll(field, width - 1, 1)
        + emission * weights[5]
    )


def inner_kernel(targets, info_ref, field_ref, flow_ref, emission_ref, kept_ref, *refs):
    out_refs, (wide_ref, weight_ref) = refs[:-2], refs[-2:]
    rows = field_ref.shape[1]
    emission = doubled(emission_ref[...])
    for row in range(1, rows - 1):
        weights = weights_of(flow_ref[:, row, :])
        for i, weight in enumerate(weights):
            weight_ref[row, pl.ds(i, 1), :] = weight
        wide_ref[row] = advance(
            weights, emission, field_ref[:, row - 1, :], field_ref[:, row, :], field_ref[:, row + 1, :]
        )
    for place, row in enumerate((1, 2, rows - 3, rows - 2)):
        kept_ref[place] = wide_ref[row]
    for out_ref, hops in zip(out_refs, targets):
        chip = sum(jnp.where(info_ref[0] == source, to, 0) for source, to in hops)

        @pl.when(chip > 0)
        def _():
            for place in range(2):
                position = 2 * chip + jnp.abs(info_ref[1] - 1 + place)
                row = position + info_ref[2] * (rows - 1 - 2 * position)
                weights = weight_ref[row]
                out_ref[place] = advance(
                    [weights[i : i + 1] for i in range(6)],
                    emission, wide_ref[row - 1], wide_ref[row], wide_ref[row + 1],
                )


def end_rows(info_ref, last, field_ref, flow_ref, emission_ref, kept_ref, halo_ref, out_ref):
    members, rows, width = field_ref.shape
    emission = doubled(emission_ref[...])

    def halo_row(place):
        return halo_ref[pl.ds(place * members, members), :]

    halo_weights = weights_of(halo_ref[pl.ds(STEPS * members, 4), :])
    for parity in range(2):

        @pl.when(info_ref[2] == parity)
        def _():
            if parity == last:
                end, near, outside, beyond = 0, 1, halo_row(1), halo_row(0)
                inside, further = kept_ref[0], kept_ref[1]
            else:
                end, near, outside, beyond = rows - 1, rows - 2, halo_row(0), halo_row(1)
                inside, further = kept_ref[3], kept_ref[2]

            def ordered(weights, outer, own, inner):
                behind, ahead = (outer, inner) if end == 0 else (inner, outer)
                return advance(weights, emission, behind, own, ahead)

            end_weights = weights_of(flow_ref[:, end, :])
            end_field = field_ref[:, end, :]
            outer = ordered(halo_weights, beyond, outside, end_field)
            own = ordered(end_weights, outside, end_field, field_ref[:, near, :])
            out_ref[last] = ordered(end_weights, outer, own, inside)
            out_ref[1 - last] = ordered(weights_of(flow_ref[:, near, :]), own, inside, further)


def edge_kernel(info_ref, field_ref, flow_ref, emission_ref, kept_ref, first_ref, last_ref, *refs):
    out_refs, scratch = refs[:-1], refs[-1]
    chips = len(out_refs)
    core = info_ref[1]
    for last, halo_ref in enumerate((first_ref, last_ref)):
        end_rows(info_ref, last, field_ref, flow_ref, emission_ref, kept_ref, halo_ref, scratch)
        for s, out_ref in enumerate(out_refs):

            @pl.when(info_ref[0] == (chips - 1 - s if last else s))
            def _():
                out_ref[0] = scratch[1 - core]
                out_ref[1] = scratch[core]


def source_of(chip, chips, hops, k):
    inner = sum(jnp.where(chip == to, source, 0) for source, to in hops)
    return jnp.where(chip == 0, k, jnp.where(chip == chips - 1, chips - 1 - k, inner))


def collect_kernel(order, info_ref, mine_ref, other_ref, *refs):
    chips = len(order)
    near_other, near_own, observed_ref = refs[-3:]
    step = near_other.shape[1]
    observed_ref[...] = jnp.where(info_ref[2] == 1, other_ref[...], mine_ref[...])
    near_own[pl.ds(chips * step, PADDING), :] = jnp.zeros((PADDING, near_own.shape[1]), F32)
    chip = info_ref[0]
    at_edge = jnp.logical_or(chip == 0, chip == chips - 1)
    for index, (s, k) in enumerate(order):
        block = source_of(chip, chips, s, k)
        rows = pl.ds(pl.multiple_of(block * step, step), step)
        for ref, here in ((refs[index], jnp.logical_not(at_edge)), (refs[chips + index], at_edge)):

            @pl.when(here)
            def _():
                near_other[block] = ref[0]
                near_own[rows, :] = ref[1]


def unpack_kernel(order, info_ref, *refs):
    row_refs, out_ref = refs[:-1], refs[-1]
    rows = out_ref.shape[1]
    for x, ref in zip(order, row_refs):
        position = (2 * info_ref[0] + info_ref[1]) ^ x
        row = position + info_ref[2] * (rows - 1 - 2 * position)
        out_ref[:, pl.ds(row, 1), :] = ref[...][:, None, :]


def pieces(x, count):
    parts = []
    for _ in range(count - 1):
        part = x.astype(BF16)
        parts.append(part)
        x = x - part.astype(F32)
    return parts + [x.astype(BF16)]


def dot(a, b):
    return lax.dot_general(a, b, (((1,), (0,)), ((), ())), preferred_element_type=F32)


def dot_t(a, b):
    return lax.dot_general(a, b, (((0,), (0,)), ((), ())), preferred_element_type=F32)


def product(a, b):
    total = None
    for i, left in enumerate(a):
        for j, right in enumerate(b):
            if i + j < max(len(a), len(b)):
                term = dot(left, right)
                total = term if total is None else total + term
    return total


def observations(info_ref, observed_ref, width, root):
    slots = observed_ref.shape[1]
    cells, values, scales, count = (observed_ref[pl.ds(i, 1), :] for i in range(4))
    cells = cells.astype(jnp.int32)
    offset = sum((cells >= i * width).astype(jnp.int32) for i in (1, 2)) - 1
    column = cells - (offset + 1) * width
    side = offset * jnp.where(info_ref[2] == 1, -1, 1) * (1 - 2 * info_ref[1])
    cells = column + width * jnp.where(side == 0, 2, jnp.where(side < 0, 0, 1))
    active = lax.broadcasted_iota(jnp.int32, (1, slots), 1) < count.astype(jnp.int32)
    slot_weight = jnp.where(active, scales, 0.0)
    return cells, slot_weight, values, slot_weight * (1.0 / root)


def one_hot(cells, first, count):
    return (
        lax.broadcasted_iota(jnp.int32, (count, cells.shape[1]), 0) + first == cells
    ).astype(F32).astype(BF16)


def mean_of(blocks, members):
    total = blocks[0]
    for block in blocks[1:]:
        total = total + block
    return jnp.sum(total, axis=0, keepdims=True) * (1.0 / members)


def at_cells(row, chosen):
    parts = pieces(jnp.broadcast_to(row, (8, row.shape[1])), 3)
    return (dot(parts[0], chosen) + (dot(parts[1], chosen) + dot(parts[2], chosen)))[:1]


def prepare_kernel(
    info_ref, observed_ref, near_other, near_own, far_other, far_own,
    spread_high, spread_low, own_high, own_low, own_part, seen_ref, direction_ref,
    anomaly, high_ref, low_ref,
):
    chips, step, width = near_other.shape
    members = 2 * chips * step
    cells, _, _, scale = observations(info_ref, observed_ref, width, math.sqrt(members - 1))
    chosen = one_hot(cells, width, 2 * width)
    blocks = [pl.ds(index * step, step) for index in range(2 * chips)]
    means = []
    for place in range(2):
        columns = pl.ds(place * width, width)
        if place:
            rows = [near_own.at[block, :] for block in blocks[:chips]] + [far_own.at[chip] for chip in range(chips)]
        else:
            rows = [near_other.at[chip] for chip in range(chips)] + [far_other.at[block, :] for block in blocks[:chips]]
        means.append(mean_of([row[...] for row in rows], members))
        for block, row in zip(blocks, rows):
            part = row[...] - means[-1]
            anomaly[block, columns] = part
            high_ref[block, columns] = part.astype(BF16)

    def unit(x):
        return x * (1.0 / jnp.maximum(jnp.max(jnp.abs(x)), 1e-30))

    high = high_ref[...]
    along = lax.dot_general(high[:16], high, (((1,), (1,)), ((), ())), preferred_element_type=F32)
    rows = unit(dot(unit(along).astype(BF16), high))
    weight = jnp.sum(rows * rows[:1], axis=1, keepdims=True)
    weight = weight + jnp.where(jnp.max(jnp.abs(weight)) > 0.0, 0.0, 1.0)
    pattern = unit(jnp.sum(rows * weight, axis=0, keepdims=True))
    total = jnp.zeros((1, 1), F32)
    for block in blocks:
        along = jnp.sum(anomaly[block, :] * pattern, axis=1, keepdims=True)
        total = total + jnp.sum(along * along, axis=0, keepdims=True)
        direction_ref[block, :] = jnp.broadcast_to(along, (step, direction_ref.shape[1]))
    length = lax.rsqrt(jnp.maximum(total, 1e-30))
    taken = None
    for block in blocks:
        direction = direction_ref[block, :] * length
        direction_ref[block, :] = direction
        term = anomaly[block, :] * doubled(doubled(direction))
        taken = term if taken is None else taken + term
    taken = jnp.sum(taken, axis=0, keepdims=True)
    own_part[...] = jnp.broadcast_to(taken[:, width:], (own_part.shape[1], width)).T

    for block in blocks:
        rest = anomaly[block, :] - doubled(doubled(direction_ref[block, :])) * taken
        high, low = pieces(rest, 2)
        high_ref[block, :] = high
        low_ref[block, :] = low
        own = rest[:, width:].T
        own_high[:, block], own_low[:, block] = pieces(own, 2)
    seen_ref[pl.ds(0, 1), :] = at_cells(jnp.concatenate(means, axis=1), chosen)
    seen_ref[pl.ds(1, 1), :] = at_cells(taken, chosen)
    for first in range(0, members, PART):
        rows = pl.ds(first, PART)
        spread = (dot(high_ref[rows, :], chosen) + dot(low_ref[rows, :], chosen)) * scale
        high, low = pieces(spread, 2)
        spread_high[rows, :] = high
        spread_low[rows, :] = low


def square(parts):
    half = parts[0].shape[0] // 2
    upper = product([part[:half] for part in parts], parts)
    lower = product([part[half:] for part in parts], [part[:, half:] for part in parts])
    return upper, jnp.concatenate([upper[:, half:].T, lower], axis=1)


def region_kernel(
    info_ref, observed_ref, near_own, far_own, high_in, low_in, own_high, own_low, own_part, seen_ref,
    direction_ref, half_ref, rest_ref, *refs,
):
    chips, step, width = far_own.shape
    out_refs = refs[:-5]
    spread_high, spread_low, factor, squared, answer = refs[-5:]
    members = 2 * chips * step
    slots = observed_ref.shape[1]
    root = math.sqrt(members - 1)
    core = info_ref[1]
    ends = jnp.logical_or(
        jnp.logical_and(info_ref[0] == 0, core == 0), jnp.logical_and(info_ref[0] == chips - 1, core == 1)
    )
    part = jnp.where(ends, 0, 1)
    cells, slot_weight, values, scale = observations(info_ref, observed_ref, width, root)
    chosen = one_hot(cells, 0, width)

    def rows_at(half, chip):
        return pl.ds(pl.multiple_of((half * chips + chip) * step, step), step)

    blocks = [(half_ref.at[pl.ds(chip * step, step), :], rows_at(part, chip)) for chip in range(chips)]
    blocks += [(rest_ref.at[chip], rows_at(1 - part, chip)) for chip in range(chips)]
    mean = mean_of([ref[...] for ref, _ in blocks], members)
    taken = None
    for ref, block in blocks:
        term = (ref[...] - mean) * doubled(direction_ref[block, :])
        taken = term if taken is None else taken + term
    taken = jnp.sum(taken, axis=0, keepdims=True)
    seen_mean = seen_ref[pl.ds(0, 1), :] + at_cells(mean, chosen)
    common = (seen_ref[pl.ds(1, 1), :] + at_cells(taken, chosen)) * scale
    innovation = slot_weight * (values - seen_mean)
    for ref, block in blocks:
        rest = ref[...] - mean - doubled(direction_ref[block, :]) * taken
        high, low = pieces(rest, 2)
        high, low = pieces((dot(high, chosen) + dot(low, chosen)) * scale, 2)
        spread_high[block, :] = high + high_in[block, :]
        spread_low[block, :] = low + low_in[block, :]

    high, low = spread_high[...], spread_low[...]
    eye = lax.broadcasted_iota(jnp.int32, (slots, slots), 0) == lax.broadcasted_iota(
        jnp.int32, (slots, slots), 1
    )
    turned = high.T
    cross = dot(turned, low)
    factor[...] = dot(turned, high) + (cross + cross.T) + jnp.where(eye, 1.0, 0.0)
    answer[pl.ds(0, width), :] = product([own_high[...], own_low[...]], [high, low])
    answer[pl.ds(width, 8), :] = jnp.where(
        lax.broadcasted_iota(jnp.int32, (8, slots), 0) == 0, jnp.broadcast_to(common, (8, slots)), 0.0
    )
    half = slots // 2
    upper, lower = pl.ds(0, half), pl.ds(half, half)

    def after(bound):
        return bound * bound / (2.0 - bound * bound)

    def size(matrix):
        return jnp.sum(jnp.sum(matrix * matrix, axis=0, keepdims=True))

    def begin(count):
        parts = pieces(factor[...], count)
        if count > 2:
            squared[upper, :], squared[lower, :] = square(parts)
        bound = 1.0 - start
        gain = 2.0 / (2.0 - bound * bound)
        answer[...] = (gain * start) * (2.0 * answer[...] - start * product(pieces(answer[...], count), parts))
        factor[...] = (gain * start) * (2.0 * factor[...] - start * squared[...])
        return after(bound)

    def refine(bound, count):
        gain = 2.0 / (2.0 - bound * bound)
        parts = pieces(factor[...], count)
        answer[...] = gain * (2.0 * answer[...] - product(pieces(answer[...], count), parts))
        top, bottom = square(parts)
        factor[upper, :] = gain * (2.0 * factor[upper, :] - top)
        factor[lower, :] = gain * (2.0 * factor[lower, :] - bottom)
        return after(bound)

    def close(bound, rest):
        gain = 2.0 / (2.0 - bound * bound)
        answer[...] = gain * (answer[...] + dot(answer[...].astype(BF16), rest))
        return gain

    def finish(bound):
        rest = factor[...].astype(BF16)
        gain = close(bound, rest)
        factor[...] = gain * (dot(rest, rest) - jnp.where(eye, 0.5 * bound * bound, 0.0))
        return after(bound)

    top, bottom = square(pieces(factor[...], 2))
    squared[upper, :] = top
    squared[lower, :] = bottom
    limit = 1.0001 * jnp.sqrt(jnp.sqrt(size(top) + size(bottom)))
    start = 2.0 / (1.0 + limit)
    large = limit > LARGE
    bound = lax.cond(large, lambda: begin(3), lambda: begin(2))
    bound = lax.while_loop(lambda b: jnp.logical_and(b > COARSE, large), lambda b: refine(b, 3), bound)
    bound = lax.while_loop(lambda b: b > COARSE, lambda b: refine(b, 2), bound)
    factor[...] = jnp.where(eye, 1.0, 0.0) - factor[...]
    bound = lax.while_loop(lambda b: b > DONE, finish, bound)
    close(bound, factor[...].astype(BF16))

    solved = answer[pl.ds(0, width), :]
    alone = answer[pl.ds(width, 1), :]
    share = own_part[:, :1] - jnp.sum(solved * common, axis=1, keepdims=True)
    solved = solved + (share / (1.0 + jnp.sum(common * alone, axis=1, keepdims=True))) * alone
    solved = solved.T
    which = lax.broadcasted_iota(jnp.int32, (8, slots), 0)
    sides = jnp.where(which == 0, innovation * (1.0 / root), jnp.where(which == 1, -0.5 * common, 0.0))
    parts = pieces(solved, 2)
    sides = product(pieces(sides, 2), parts)
    shift, along = sides[0:1], sides[1:2]
    halved = [part * jnp.asarray(-0.5, BF16) for part in parts]
    for x, out_ref in enumerate(out_refs):
        chip, part = info_ref[0] ^ (x // 2), x % 2
        rows = pl.ds(pl.multiple_of((part * chips + chip) * step, step), step)
        moved = product([spread_high[rows, :], spread_low[rows, :]], halved)
        moved = moved + doubled(direction_ref[rows, :]) * along
        own = far_own[chip] if part else near_own[rows_at(0, chip), :]
        out_ref[...] = own + shift + moved


VMEM = pl.BlockSpec(memory_space=pltpu.VMEM)
SMEM = pl.BlockSpec(memory_space=pltpu.SMEM)


def call(kernel, name, out_shape, args, scratch=(), flops=None, aliases={}, limit=8, after=()):
    several = isinstance(out_shape, (list, tuple))
    if after:
        count, inner = len(args), kernel
        args = [*args, *after]
        kernel = lambda *refs: inner(*refs[:count], *refs[len(args) :])
    return pl.pallas_call(
        kernel,
        out_shape=out_shape,
        in_specs=[SMEM] + [VMEM] * (len(args) - 1 - len(after)) + [pl.BlockSpec(memory_space=pl.ANY)] * len(after),
        out_specs=[VMEM] * len(out_shape) if several else VMEM,
        scratch_shapes=scratch,
        input_output_aliases=aliases,
        compiler_params=pltpu.CompilerParams(vmem_limit_bytes=limit * 1024 * 1024),
        cost_estimate=flops and pl.CostEstimate(flops=flops, bytes_accessed=0, transcendentals=0),
        name=name,
    )(*args)


def bfloat(*shape):
    return jax.ShapeDtypeStruct(shape, BF16)


def array(*shape):
    return jax.ShapeDtypeStruct(shape, F32)


def per_device(
    init_field, flow_fields, emission, observed_cell, observed_count, observed_value, observed_scale
):
    step, rows, width = init_field.shape
    slots = observed_cell.shape[1]
    patches, lanes = lax.axis_size("patch"), lax.axis_size("member")
    chips = lanes // 2
    members = lanes * step
    axes = ("patch", "member")
    count = patches * lanes
    patch, lane = lax.axis_index("patch"), lax.axis_index("member")
    info = jnp.stack([lane // 2, lane % 2, patch % 2, jnp.int32(chips)]).astype(jnp.int32)

    edge = array(STEPS * step + 8, width)
    place = pl.BlockSpec(memory_space=pltpu.HBM)
    to_last, to_first, flow, emitted = pl.pallas_call(
        pack_kernel,
        out_shape=[edge, edge, array(*flow_fields.shape), array(step, width // 2)],
        in_specs=[SMEM] + [place] * 3, out_specs=[VMEM] * 4,
        scratch_shapes=[
            pltpu.VMEM((step, rows, width), F32), pltpu.VMEM((1, step), F32), pltpu.SemaphoreType.DMA((3,))
        ],
        compiler_params=pltpu.CompilerParams(vmem_limit_bytes=32 * 1024 * 1024), name="pack",
    )(info, init_field, flow_fields, emission[None, :])

    def swap(message, start):
        lower = range(start, patches - 1, 2)
        return lax.ppermute(message, "patch", [(p, p + 1) for p in lower] + [(p + 1, p) for p in lower])

    halo_first, halo_last = swap(to_first, 1), swap(to_last, 0)

    mine = jnp.concatenate(
        [
            observed_cell.astype(F32),
            observed_value,
            observed_scale,
            jnp.broadcast_to(observed_count.astype(F32)[:, None], observed_cell.shape),
        ]
        * 2,
        axis=0,
    )

    def between(message, hops):
        return lax.ppermute(message, "member", [(2 * a + core, 2 * b + core) for a, b in hops for core in range(2)])

    mirrored = [
        [hop for to in range(1, chips // 2) for hop in (((to + s) % chips, to), (chips - 1 - (to + s) % chips, chips - 1 - to))]
        for s in range(chips)
    ]
    turning = [[((to - s) % chips, to) for to in range(1, chips - 1)] for s in range(chips)]
    single = all(len({source for source, _ in hops}) == len(hops) for hops in mirrored)
    targets = mirrored if single else turning
    pair = array(2, step, width)
    args = [info, init_field, flow, emitted]
    kept, *inner = call(
        functools.partial(inner_kernel, targets), "inner", [array(4, step, width)] + [pair] * chips, args,
        [pltpu.VMEM((rows, step, width), F32), pltpu.VMEM((rows, 8, width), F32)], limit=32,
    )
    got_inner = [inner[0]] + [between(inner[s], targets[s]) for s in range(1, chips)]
    outer = call(
        edge_kernel, "edge", [pair] * chips, args + [kept, halo_first, halo_last],
        [pltpu.VMEM((2, step, width), F32)], limit=32,
    )
    got_outer = [outer[0]] + [
        between(outer[s], [(s, 0), (chips - 1 - s, chips - 1)]) for s in range(1, chips)
    ]
    order = [(targets[s], s) for s in range(chips)]
    pieces_in = got_inner + got_outer
    mine, _ = lax.optimization_barrier((mine, outer[0]))
    other = lax.ppermute(
        mine, axes,
        [(p * lanes + i, p * lanes + lanes - 1 - i) for p in range(1, patches, 2) for i in range(lanes)],
    )

    def device(p, chip, core):
        return p * lanes + 2 * chip + core

    borders, siblings = [], []
    for p in range(patches):
        for chip in range(chips):
            for core, away in ((0, -1), (1, 1)):
                siblings.append((device(p, chip, core), device(p, chip, 1 - core)))
                if 0 <= chip + away < chips:
                    borders.append((device(p, chip, core), device(p, chip + away, 1 - core)))
                else:
                    to = p + 1 if (p % 2 == 0) == (away == 1) else p - 1
                    if 0 <= to < patches:
                        borders.append((device(p, chip, core), device(to, chip, core)))

    half = array(chips, step, width)
    near_other, near_own, observed = call(
        functools.partial(collect_kernel, order), "collect",
        [half, array(chips * step + PADDING, width), array(8, slots)], [info, mine, other] + pieces_in,
    )
    far_own = lax.ppermute(near_other, axes, siblings)
    got_half = lax.ppermute(near_own, axes, borders)
    far_other = lax.ppermute(near_own, axes, siblings)
    got_rest = lax.ppermute(far_own, axes, borders)

    split = [pltpu.VMEM((members, slots), BF16)] * 2
    prepared = call(
        prepare_kernel, "prepare",
        [bfloat(members, slots)] * 2 + [bfloat(width, members)] * 2
        + [array(width, width // 2), array(8, slots), array(members, width // 2)],
        [info, observed, near_other, near_own, far_other, far_own],
        [pltpu.VMEM((members, 2 * width), F32)] + [pltpu.VMEM((members, 2 * width), BF16)] * 2,
        flops=8 * members * slots * width, limit=20,
    )
    analysed = call(
        region_kernel, "region", [array(step, width)] * lanes,
        [info, observed, near_own, far_own, *prepared, got_half, got_rest],
        split + [pltpu.VMEM((slots, slots), F32)] * 2 + [pltpu.VMEM((width + 8, slots), F32)],
        limit=24,
    )
    def swapped(x):
        return lax.ppermute(analysed[x], "member", [(i, i ^ x) for i in range(lanes)]) if x else analysed[0]

    order = sorted(range(lanes), key=lambda x: (x.bit_length() != lanes.bit_length() - 1, -x))
    return call(
        functools.partial(unpack_kernel, order), "unpack", array(step, rows, width),
        [info] + [swapped(x) for x in order], limit=48,
    )


def solution(mesh):
    return jax.shard_map(
        per_device,
        mesh=mesh,
        in_specs=(
            P("member", "patch", None),
            P(None, "patch", None),
            P("member"),
            P(("patch", "member"), None),
            P(("patch", "member")),
            P(("patch", "member"), None),
            P(("patch", "member"), None),
        ),
        out_specs=P("member", "patch", None),
        check_vma=False,
    )
```

```python
import functools
import math

import jax
import jax.numpy as jnp
from jax import lax
from jax.experimental import pallas as pl
from jax.experimental.pallas import tpu as pltpu
from jax.sharding import PartitionSpec as P

STEPS = 2
COARSE = 0.3
DONE = 0.02
LARGE = 2e4
PART = 256
PADDING = 8
F32 = jnp.float32
BF16 = jnp.bfloat16


def pack_kernel(info_ref, field_hbm, flow_hbm, first_ref, second_ref, field_ref, flow_ref, sems):
    members, rows, width = field_ref.shape
    moves = [
        pltpu.make_async_copy(field_hbm, field_ref, sems.at[0]),
        pltpu.make_async_copy(flow_hbm, flow_ref, sems.at[1]),
    ]
    for move in moves:
        move.start()
    for move in moves:
        move.wait()
    even = info_ref[2] == 0
    for place in range(STEPS):
        tail, head = field_ref[:, rows - STEPS + place, :], field_ref[:, place, :]
        at = pl.ds(place * members, members)
        first_ref[at, :] = jnp.where(even, tail, head)
        second_ref[at, :] = jnp.where(even, head, tail)
    tail, head = flow_ref[:, rows - 1, :], flow_ref[:, 0, :]
    at = pl.ds(STEPS * members, 8)
    first_ref[at, :] = jnp.concatenate([jnp.where(even, tail, head)] * 2, axis=0)
    second_ref[at, :] = jnp.concatenate([jnp.where(even, head, tail)] * 2, axis=0)


def doubled(x):
    return jnp.concatenate([x, x], axis=1)


def weights_of(flow):
    row_flow, col_flow, kept, source = flow[0:1], flow[1:2], 1.0 - flow[2:3], flow[3:4]
    behind, ahead = jnp.maximum(row_flow, 0.0), -jnp.minimum(row_flow, 0.0)
    left, right = jnp.maximum(col_flow, 0.0), -jnp.minimum(col_flow, 0.0)
    stays = 1.0 - behind - ahead - left - right
    return [kept * stays, kept * behind, kept * ahead, kept * left, kept * right, source]


def advance(weights, emission, behind, field, ahead):
    width = field.shape[1]
    return (
        weights[0] * field
        + weights[1] * behind
        + weights[2] * ahead
        + weights[3] * pltpu.roll(field, 1, 1)
        + weights[4] * pltpu.roll(field, width - 1, 1)
        + emission * weights[5]
    )


def emission_column(emission_ref):
    members = emission_ref.shape[1]
    diagonal = lax.broadcasted_iota(jnp.int32, (members, members), 0) == lax.broadcasted_iota(
        jnp.int32, (members, members), 1
    )
    return jnp.sum(jnp.where(diagonal, emission_ref[...], 0.0), axis=1, keepdims=True)


def inner_kernel(targets, info_ref, field_ref, flow_ref, emission_ref, kept_ref, *refs):
    out_refs, (wide_ref, weight_ref) = refs[:-2], refs[-2:]
    rows = field_ref.shape[1]
    emission = emission_column(emission_ref)
    for row in range(1, rows - 1):
        weights = weights_of(flow_ref[:, row, :])
        for i, weight in enumerate(weights):
            weight_ref[row, pl.ds(i, 1), :] = weight
        wide_ref[row] = advance(
            weights, emission, field_ref[:, row - 1, :], field_ref[:, row, :], field_ref[:, row + 1, :]
        )
    for place, row in enumerate((1, 2, rows - 3, rows - 2)):
        kept_ref[place] = wide_ref[row]
    for out_ref, hops in zip(out_refs, targets):
        chip = sum(jnp.where(info_ref[0] == source, to, 0) for source, to in hops)

        @pl.when(chip > 0)
        def _():
            for place in range(2):
                position = 2 * chip + jnp.abs(info_ref[1] - 1 + place)
                row = position + info_ref[2] * (rows - 1 - 2 * position)
                weights = weight_ref[row]
                out_ref[place] = advance(
                    [weights[i : i + 1] for i in range(6)],
                    emission, wide_ref[row - 1], wide_ref[row], wide_ref[row + 1],
                )


def end_rows(info_ref, last, field_ref, flow_ref, emission, kept_ref, halo_ref, out_ref):
    members, rows, width = field_ref.shape

    def halo_row(place):
        return halo_ref[pl.ds(place * members, members), :]

    halo_weights = weights_of(halo_ref[pl.ds(STEPS * members, 4), :])
    for parity in range(2):

        @pl.when(info_ref[2] == parity)
        def _():
            if parity == last:
                end, near, outside, beyond = 0, 1, halo_row(1), halo_row(0)
                inside, further = kept_ref[0], kept_ref[1]
            else:
                end, near, outside, beyond = rows - 1, rows - 2, halo_row(0), halo_row(1)
                inside, further = kept_ref[3], kept_ref[2]

            def ordered(weights, outer, own, inner):
                behind, ahead = (outer, inner) if end == 0 else (inner, outer)
                return advance(weights, emission, behind, own, ahead)

            end_weights = weights_of(flow_ref[:, end, :])
            end_field = field_ref[:, end, :]
            outer = ordered(halo_weights, beyond, outside, end_field)
            own = ordered(end_weights, outside, end_field, field_ref[:, near, :])
            out_ref[last] = ordered(end_weights, outer, own, inside)
            out_ref[1 - last] = ordered(weights_of(flow_ref[:, near, :]), own, inside, further)


def edge_kernel(info_ref, field_ref, flow_ref, emission_ref, kept_ref, last_ref, first_ref, *refs):
    out_refs, scratch = refs[:-1], refs[-1]
    chips = len(out_refs)
    core = info_ref[1]
    emission = emission_column(emission_ref)
    for last, halo_ref in enumerate((first_ref, last_ref)):
        end_rows(info_ref, last, field_ref, flow_ref, emission, kept_ref, halo_ref, scratch)
        for s, out_ref in enumerate(out_refs):

            @pl.when(info_ref[0] == (chips - 1 - s if last else s))
            def _():
                out_ref[0] = scratch[1 - core]
                out_ref[1] = scratch[core]


def source_of(chip, chips, hops, k):
    inner = sum(jnp.where(chip == to, source, 0) for source, to in hops)
    return jnp.where(chip == 0, k, jnp.where(chip == chips - 1, chips - 1 - k, inner))


def collect_kernel(order, info_ref, mine_ref, other_ref, *refs):
    chips = len(order)
    near_other, near_own, observed_ref = refs[-3:]
    step = near_other.shape[1]
    observed_ref[...] = jnp.where(info_ref[2] == 1, other_ref[...], mine_ref[...])
    near_own[pl.ds(chips * step, PADDING), :] = jnp.zeros((PADDING, near_own.shape[1]), F32)
    chip = info_ref[0]
    at_edge = jnp.logical_or(chip == 0, chip == chips - 1)
    for index, (s, k) in enumerate(order):
        block = source_of(chip, chips, s, k)
        rows = pl.ds(pl.multiple_of(block * step, step), step)
        for ref, here in ((refs[index], jnp.logical_not(at_edge)), (refs[chips + index], at_edge)):

            @pl.when(here)
            def _():
                near_other[block] = ref[0]
                near_own[rows, :] = ref[1]


def unpack_kernel(order, info_ref, *refs):
    row_refs, out_ref = refs[:-1], refs[-1]
    rows = out_ref.shape[1]
    for x, ref in zip(order, row_refs):
        position = (2 * info_ref[0] + info_ref[1]) ^ x
        row = position + info_ref[2] * (rows - 1 - 2 * position)
        out_ref[:, pl.ds(row, 1), :] = ref[...][:, None, :]


def pieces(x, count):
    parts = []
    for _ in range(count - 1):
        part = x.astype(BF16)
        parts.append(part)
        x = x - part.astype(F32)
    return parts + [x.astype(BF16)]


def dot(a, b):
    return lax.dot_general(a, b, (((1,), (0,)), ((), ())), preferred_element_type=F32)


def dot_t(a, b):
    return lax.dot_general(a, b, (((0,), (0,)), ((), ())), preferred_element_type=F32)


def product(a, b):
    total = None
    for i, left in enumerate(a):
        for j, right in enumerate(b):
            if i + j < max(len(a), len(b)):
                term = dot(left, right)
                total = term if total is None else total + term
    return total


def observations(info_ref, observed_ref, width, root):
    slots = observed_ref.shape[1]
    cells, values, scales, count = (observed_ref[pl.ds(i, 1), :] for i in range(4))
    cells = cells.astype(jnp.int32)
    offset = sum((cells >= i * width).astype(jnp.int32) for i in (1, 2)) - 1
    column = cells - (offset + 1) * width
    side = offset * jnp.where(info_ref[2] == 1, -1, 1) * (1 - 2 * info_ref[1])
    cells = column + width * jnp.where(side == 0, 2, jnp.where(side < 0, 0, 1))
    active = lax.broadcasted_iota(jnp.int32, (1, slots), 1) < count.astype(jnp.int32)
    slot_weight = jnp.where(active, scales, 0.0)
    return cells, slot_weight, values, slot_weight * (1.0 / root)


def one_hot(cells, first, count):
    return (
        lax.broadcasted_iota(jnp.int32, (count, cells.shape[1]), 0) + first == cells
    ).astype(F32).astype(BF16)


def mean_of(blocks, members):
    total = blocks[0]
    for block in blocks[1:]:
        total = total + block
    return jnp.sum(total, axis=0, keepdims=True) * (1.0 / members)


def at_cells(row, chosen):
    parts = pieces(jnp.broadcast_to(row, (8, row.shape[1])), 3)
    return (dot(parts[0], chosen) + (dot(parts[1], chosen) + dot(parts[2], chosen)))[:1]


def prepare_kernel(
    info_ref, observed_ref, near_other, near_own, far_other, far_own,
    spread_high, spread_low, own_high, own_low, own_part, seen_ref, direction_ref,
    anomaly, high_ref, low_ref,
):
    chips, step, width = near_other.shape
    members = 2 * chips * step
    cells, _, _, scale = observations(info_ref, observed_ref, width, math.sqrt(members - 1))
    chosen = one_hot(cells, width, 2 * width)
    blocks = [pl.ds(index * step, step) for index in range(2 * chips)]
    means = []
    for place in range(2):
        columns = pl.ds(place * width, width)
        if place:
            rows = [near_own.at[block, :] for block in blocks[:chips]] + [far_own.at[chip] for chip in range(chips)]
        else:
            rows = [near_other.at[chip] for chip in range(chips)] + [far_other.at[block, :] for block in blocks[:chips]]
        means.append(mean_of([row[...] for row in rows], members))
        for block, row in zip(blocks, rows):
            part = row[...] - means[-1]
            anomaly[block, columns] = part
            high_ref[block, columns] = part.astype(BF16)

    def unit(x):
        return x * (1.0 / jnp.maximum(jnp.max(jnp.abs(x)), 1e-30))

    high = high_ref[...]
    along = lax.dot_general(high[:16], high, (((1,), (1,)), ((), ())), preferred_element_type=F32)
    rows = unit(dot(unit(along).astype(BF16), high))
    weight = jnp.sum(rows * rows[:1], axis=1, keepdims=True)
    weight = weight + jnp.where(jnp.max(jnp.abs(weight)) > 0.0, 0.0, 1.0)
    pattern = unit(jnp.sum(rows * weight, axis=0, keepdims=True))
    total = jnp.zeros((1, 1), F32)
    for block in blocks:
        along = jnp.sum(anomaly[block, :] * pattern, axis=1, keepdims=True)
        total = total + jnp.sum(along * along, axis=0, keepdims=True)
        direction_ref[block, :] = jnp.broadcast_to(along, (step, direction_ref.shape[1]))
    length = lax.rsqrt(jnp.maximum(total, 1e-30))
    taken = None
    for block in blocks:
        direction = direction_ref[block, :] * length
        direction_ref[block, :] = direction
        term = anomaly[block, :] * doubled(doubled(direction))
        taken = term if taken is None else taken + term
    taken = jnp.sum(taken, axis=0, keepdims=True)
    own_part[...] = jnp.broadcast_to(taken[:, width:], (own_part.shape[1], width)).T

    for block in blocks:
        rest = anomaly[block, :] - doubled(doubled(direction_ref[block, :])) * taken
        high, low = pieces(rest, 2)
        high_ref[block, :] = high
        low_ref[block, :] = low
        own = rest[:, width:].T
        own_high[:, block], own_low[:, block] = pieces(own, 2)
    seen_ref[pl.ds(0, 1), :] = at_cells(jnp.concatenate(means, axis=1), chosen)
    seen_ref[pl.ds(1, 1), :] = at_cells(taken, chosen)
    for first in range(0, members, PART):
        rows = pl.ds(first, PART)
        spread = (dot(high_ref[rows, :], chosen) + dot(low_ref[rows, :], chosen)) * scale
        high, low = pieces(spread, 2)
        spread_high[rows, :] = high
        spread_low[rows, :] = low


def square(parts):
    half = parts[0].shape[0] // 2
    upper = product([part[:half] for part in parts], parts)
    lower = product([part[half:] for part in parts], [part[:, half:] for part in parts])
    return upper, jnp.concatenate([upper[:, half:].T, lower], axis=1)


def region_kernel(
    info_ref, observed_ref, near_own, far_own, high_in, low_in, own_high, own_low, own_part, seen_ref,
    direction_ref, half_ref, rest_ref, *refs,
):
    chips, step, width = far_own.shape
    out_refs = refs[:-5]
    spread_high, spread_low, factor, squared, answer = refs[-5:]
    members = 2 * chips * step
    slots = observed_ref.shape[1]
    root = math.sqrt(members - 1)
    core = info_ref[1]
    ends = jnp.logical_or(
        jnp.logical_and(info_ref[0] == 0, core == 0), jnp.logical_and(info_ref[0] == chips - 1, core == 1)
    )
    part = jnp.where(ends, 0, 1)
    cells, slot_weight, values, scale = observations(info_ref, observed_ref, width, root)
    chosen = one_hot(cells, 0, width)

    def rows_at(half, chip):
        return pl.ds(pl.multiple_of((half * chips + chip) * step, step), step)

    blocks = [(half_ref.at[pl.ds(chip * step, step), :], rows_at(part, chip)) for chip in range(chips)]
    blocks += [(rest_ref.at[chip], rows_at(1 - part, chip)) for chip in range(chips)]
    mean = mean_of([ref[...] for ref, _ in blocks], members)
    taken = None
    for ref, block in blocks:
        term = (ref[...] - mean) * doubled(direction_ref[block, :])
        taken = term if taken is None else taken + term
    taken = jnp.sum(taken, axis=0, keepdims=True)
    seen_mean = seen_ref[pl.ds(0, 1), :] + at_cells(mean, chosen)
    common = (seen_ref[pl.ds(1, 1), :] + at_cells(taken, chosen)) * scale
    innovation = slot_weight * (values - seen_mean)
    for ref, block in blocks:
        rest = ref[...] - mean - doubled(direction_ref[block, :]) * taken
        high, low = pieces(rest, 2)
        high, low = pieces((dot(high, chosen) + dot(low, chosen)) * scale, 2)
        spread_high[block, :] = high + high_in[block, :]
        spread_low[block, :] = low + low_in[block, :]

    high, low = spread_high[...], spread_low[...]
    eye = lax.broadcasted_iota(jnp.int32, (slots, slots), 0) == lax.broadcasted_iota(
        jnp.int32, (slots, slots), 1
    )
    turned = high.T
    cross = dot(turned, low)
    factor[...] = dot(turned, high) + (cross + cross.T) + jnp.where(eye, 1.0, 0.0)
    answer[pl.ds(0, width), :] = product([own_high[...], own_low[...]], [high, low])
    answer[pl.ds(width, 8), :] = jnp.where(
        lax.broadcasted_iota(jnp.int32, (8, slots), 0) == 0, jnp.broadcast_to(common, (8, slots)), 0.0
    )
    half = slots // 2
    upper, lower = pl.ds(0, half), pl.ds(half, half)

    def after(bound):
        return bound * bound / (2.0 - bound * bound)

    def size(matrix):
        return jnp.sum(jnp.sum(matrix * matrix, axis=0, keepdims=True))

    def begin(count):
        parts = pieces(factor[...], count)
        if count > 2:
            squared[upper, :], squared[lower, :] = square(parts)
        bound = 1.0 - start
        gain = 2.0 / (2.0 - bound * bound)
        answer[...] = (gain * start) * (2.0 * answer[...] - start * product(pieces(answer[...], count), parts))
        factor[...] = (gain * start) * (2.0 * factor[...] - start * squared[...])
        return after(bound)

    def refine(bound, count):
        gain = 2.0 / (2.0 - bound * bound)
        parts = pieces(factor[...], count)
        answer[...] = gain * (2.0 * answer[...] - product(pieces(answer[...], count), parts))
        top, bottom = square(parts)
        factor[upper, :] = gain * (2.0 * factor[upper, :] - top)
        factor[lower, :] = gain * (2.0 * factor[lower, :] - bottom)
        return after(bound)

    def close(bound, rest):
        gain = 2.0 / (2.0 - bound * bound)
        answer[...] = gain * (answer[...] + dot(answer[...].astype(BF16), rest))
        return gain

    def finish(bound):
        rest = factor[...].astype(BF16)
        gain = close(bound, rest)
        factor[...] = gain * (dot(rest, rest) - jnp.where(eye, 0.5 * bound * bound, 0.0))
        return after(bound)

    top, bottom = square(pieces(factor[...], 2))
    squared[upper, :] = top
    squared[lower, :] = bottom
    limit = 1.0001 * jnp.sqrt(jnp.sqrt(size(top) + size(bottom)))
    start = 2.0 / (1.0 + limit)
    large = limit > LARGE
    bound = lax.cond(large, lambda: begin(3), lambda: begin(2))
    bound = lax.while_loop(lambda b: jnp.logical_and(b > COARSE, large), lambda b: refine(b, 3), bound)
    bound = lax.while_loop(lambda b: b > COARSE, lambda b: refine(b, 2), bound)
    factor[...] = jnp.where(eye, 1.0, 0.0) - factor[...]
    bound = lax.while_loop(lambda b: b > DONE, finish, bound)
    close(bound, factor[...].astype(BF16))

    solved = answer[pl.ds(0, width), :]
    alone = answer[pl.ds(width, 1), :]
    share = own_part[:, :1] - jnp.sum(solved * common, axis=1, keepdims=True)
    solved = solved + (share / (1.0 + jnp.sum(common * alone, axis=1, keepdims=True))) * alone
    solved = solved.T
    which = lax.broadcasted_iota(jnp.int32, (8, slots), 0)
    sides = jnp.where(which == 0, innovation * (1.0 / root), jnp.where(which == 1, -0.5 * common, 0.0))
    parts = pieces(solved, 2)
    sides = product(pieces(sides, 2), parts)
    shift, along = sides[0:1], sides[1:2]
    halved = [part * jnp.asarray(-0.5, BF16) for part in parts]
    for x, out_ref in enumerate(out_refs):
        chip, part = info_ref[0] ^ (x // 2), x % 2
        rows = pl.ds(pl.multiple_of((part * chips + chip) * step, step), step)
        moved = product([spread_high[rows, :], spread_low[rows, :]], halved)
        moved = moved + doubled(direction_ref[rows, :]) * along
        own = far_own[chip] if part else near_own[rows_at(0, chip), :]
        out_ref[...] = own + shift + moved


VMEM = pl.BlockSpec(memory_space=pltpu.VMEM)
SMEM = pl.BlockSpec(memory_space=pltpu.SMEM)


def call(kernel, name, out_shape, args, scratch=(), flops=None, aliases={}, limit=8, after=()):
    several = isinstance(out_shape, (list, tuple))
    if after:
        count, inner = len(args), kernel
        args = [*args, *after]
        kernel = lambda *refs: inner(*refs[:count], *refs[len(args) :])
    return pl.pallas_call(
        kernel,
        out_shape=out_shape,
        in_specs=[SMEM] + [VMEM] * (len(args) - 1 - len(after)) + [pl.BlockSpec(memory_space=pl.ANY)] * len(after),
        out_specs=[VMEM] * len(out_shape) if several else VMEM,
        scratch_shapes=scratch,
        input_output_aliases=aliases,
        compiler_params=pltpu.CompilerParams(vmem_limit_bytes=limit * 1024 * 1024),
        cost_estimate=flops and pl.CostEstimate(flops=flops, bytes_accessed=0, transcendentals=0),
        name=name,
    )(*args)


def bfloat(*shape):
    return jax.ShapeDtypeStruct(shape, BF16)


def array(*shape):
    return jax.ShapeDtypeStruct(shape, F32)


def per_device(
    init_field, flow_fields, emission, observed_cell, observed_count, observed_value, observed_scale
):
    step, rows, width = init_field.shape
    slots = observed_cell.shape[1]
    patches, lanes = lax.axis_size("patch"), lax.axis_size("member")
    chips = lanes // 2
    members = lanes * step
    axes = ("patch", "member")
    count = patches * lanes
    patch, lane = lax.axis_index("patch"), lax.axis_index("member")
    info = jnp.stack([lane // 2, lane % 2, patch % 2, jnp.int32(chips)]).astype(jnp.int32)

    edge = array(STEPS * step + 8, width)
    place = pl.BlockSpec(memory_space=pl.ANY)
    to_last, to_first = pl.pallas_call(
        pack_kernel,
        out_shape=[edge, edge],
        in_specs=[SMEM] + [place] * 2, out_specs=[VMEM] * 2,
        scratch_shapes=[
            pltpu.VMEM((step, rows, width), F32), pltpu.VMEM(flow_fields.shape, F32), pltpu.SemaphoreType.DMA((2,))
        ],
        compiler_params=pltpu.CompilerParams(vmem_limit_bytes=60 * 1024 * 1024), name="pack",
    )(info, init_field, flow_fields)

    def swap(message, start):
        lower = range(start, patches - 1, 2)
        return lax.ppermute(message, "patch", [(p, p + 1) for p in lower] + [(p + 1, p) for p in lower])

    halo_last, halo_first = swap(to_last, 0), swap(to_first, 1)

    mine = jnp.concatenate(
        [
            observed_cell.astype(F32),
            observed_value,
            observed_scale,
            jnp.broadcast_to(observed_count.astype(F32)[:, None], observed_cell.shape),
        ]
        * 2,
        axis=0,
    )

    def between(message, hops):
        return lax.ppermute(message, "member", [(2 * a + core, 2 * b + core) for a, b in hops for core in range(2)])

    mirrored = [
        [hop for to in range(1, chips // 2) for hop in (((to + s) % chips, to), (chips - 1 - (to + s) % chips, chips - 1 - to))]
        for s in range(chips)
    ]
    turning = [[((to - s) % chips, to) for to in range(1, chips - 1)] for s in range(chips)]
    single = all(len({source for source, _ in hops}) == len(hops) for hops in mirrored)
    targets = mirrored if single else turning
    pair = array(2, step, width)
    args = [info, init_field, flow_fields, emission[None, :]]
    kept, *inner = call(
        functools.partial(inner_kernel, targets), "inner", [array(4, step, width)] + [pair] * chips, args,
        [pltpu.VMEM((rows, step, width), F32), pltpu.VMEM((rows, 8, width), F32)], limit=32,
    )
    got_inner = [inner[0]] + [between(inner[s], targets[s]) for s in range(1, chips)]
    outer = call(
        edge_kernel, "edge", [pair] * chips, args + [kept, halo_last, halo_first],
        [pltpu.VMEM((2, step, width), F32)], limit=32,
    )
    got_outer = [outer[0]] + [
        between(outer[s], [(s, 0), (chips - 1 - s, chips - 1)]) for s in range(1, chips)
    ]
    order = [(targets[s], s) for s in range(chips)]
    pieces_in = got_inner + got_outer
    mine, _ = lax.optimization_barrier((mine, outer[0]))
    other = lax.ppermute(
        mine, axes,
        [(p * lanes + i, p * lanes + lanes - 1 - i) for p in range(1, patches, 2) for i in range(lanes)],
    )

    def device(p, chip, core):
        return p * lanes + 2 * chip + core

    borders, siblings = [], []
    for p in range(patches):
        for chip in range(chips):
            for core, away in ((0, -1), (1, 1)):
                siblings.append((device(p, chip, core), device(p, chip, 1 - core)))
                if 0 <= chip + away < chips:
                    borders.append((device(p, chip, core), device(p, chip + away, 1 - core)))
                else:
                    to = p + 1 if (p % 2 == 0) == (away == 1) else p - 1
                    if 0 <= to < patches:
                        borders.append((device(p, chip, core), device(to, chip, core)))

    half = array(chips, step, width)
    near_other, near_own, observed = call(
        functools.partial(collect_kernel, order), "collect",
        [half, array(chips * step + PADDING, width), array(8, slots)], [info, mine, other] + pieces_in,
    )
    far_own = lax.ppermute(near_other, axes, siblings)
    got_half = lax.ppermute(near_own, axes, borders)
    far_other = lax.ppermute(near_own, axes, siblings)
    got_rest = lax.ppermute(far_own, axes, borders)

    split = [pltpu.VMEM((members, slots), BF16)] * 2
    prepared = call(
        prepare_kernel, "prepare",
        [bfloat(members, slots)] * 2 + [bfloat(width, members)] * 2
        + [array(width, width // 2), array(8, slots), array(members, width // 2)],
        [info, observed, near_other, near_own, far_other, far_own],
        [pltpu.VMEM((members, 2 * width), F32)] + [pltpu.VMEM((members, 2 * width), BF16)] * 2,
        flops=8 * members * slots * width, limit=20,
    )
    analysed = call(
        region_kernel, "region", [array(step, width)] * lanes,
        [info, observed, near_own, far_own, *prepared, got_half, got_rest],
        split + [pltpu.VMEM((slots, slots), F32)] * 2 + [pltpu.VMEM((width + 8, slots), F32)],
        limit=24,
    )
    def swapped(x):
        return lax.ppermute(analysed[x], "member", [(i, i ^ x) for i in range(lanes)]) if x else analysed[0]

    order = sorted(range(lanes), key=lambda x: (x.bit_length() != lanes.bit_length() - 1, -x))
    return call(
        functools.partial(unpack_kernel, order), "unpack", array(step, rows, width),
        [info] + [swapped(x) for x in order], limit=48,
    )


def solution(mesh):
    return jax.shard_map(
        per_device,
        mesh=mesh,
        in_specs=(
            P("member", "patch", None),
            P(None, "patch", None),
            P("member"),
            P(("patch", "member"), None),
            P(("patch", "member")),
            P(("patch", "member"), None),
            P(("patch", "member"), None),
        ),
        out_specs=P("member", "patch", None),
        check_vma=False,
    )
```

```python
import functools
import math

import jax
import jax.numpy as jnp
from jax import lax
from jax.experimental import pallas as pl
from jax.experimental.pallas import tpu as pltpu
from jax.sharding import PartitionSpec as P

STEPS = 2
COARSE = 0.35
DONE = 0.02
LARGE = 2e4
PART = 256
PADDING = 8
F32 = jnp.float32
BF16 = jnp.bfloat16


def pack_kernel(info_ref, field_ref, flow_ref, member_ref, first_ref, second_ref, emission_ref):
    members, rows, width = field_ref.shape
    diagonal = lax.broadcasted_iota(jnp.int32, (members, members), 0) == lax.broadcasted_iota(
        jnp.int32, (members, members), 1
    )
    column = jnp.sum(jnp.where(diagonal, member_ref[...], 0.0), axis=1, keepdims=True)
    emission_ref[...] = jnp.broadcast_to(column, emission_ref.shape)
    even = info_ref[2] == 0
    for place in range(STEPS):
        tail, head = field_ref[:, rows - STEPS + place, :], field_ref[:, place, :]
        at = pl.ds(place * members, members)
        first_ref[at, :] = jnp.where(even, tail, head)
        second_ref[at, :] = jnp.where(even, head, tail)
    tail, head = flow_ref[:, rows - 1, :], flow_ref[:, 0, :]
    at = pl.ds(STEPS * members, 8)
    first_ref[at, :] = jnp.concatenate([jnp.where(even, tail, head)] * 2, axis=0)
    second_ref[at, :] = jnp.concatenate([jnp.where(even, head, tail)] * 2, axis=0)


def doubled(x):
    return jnp.concatenate([x, x], axis=1)


def weights_of(flow):
    row_flow, col_flow, kept, source = flow[0:1], flow[1:2], 1.0 - flow[2:3], flow[3:4]
    behind, ahead = jnp.maximum(row_flow, 0.0), -jnp.minimum(row_flow, 0.0)
    left, right = jnp.maximum(col_flow, 0.0), -jnp.minimum(col_flow, 0.0)
    stays = 1.0 - behind - ahead - left - right
    return [kept * stays, kept * behind, kept * ahead, kept * left, kept * right, source]


def advance(weights, emission, behind, field, ahead):
    width = field.shape[1]
    return (
        weights[0] * field
        + weights[1] * behind
        + weights[2] * ahead
        + weights[3] * pltpu.roll(field, 1, 1)
        + weights[4] * pltpu.roll(field, width - 1, 1)
        + emission * weights[5]
    )


def inner_kernel(targets, info_ref, field_ref, flow_ref, emission_ref, kept_ref, *refs):
    out_refs, (wide_ref, weight_ref) = refs[:-2], refs[-2:]
    rows = field_ref.shape[1]
    emission = doubled(emission_ref[...])
    for row in range(1, rows - 1):
        weights = weights_of(flow_ref[:, row, :])
        for i, weight in enumerate(weights):
            weight_ref[row, pl.ds(i, 1), :] = weight
        wide_ref[row] = advance(
            weights, emission, field_ref[:, row - 1, :], field_ref[:, row, :], field_ref[:, row + 1, :]
        )
    for place, row in enumerate((1, 2, rows - 3, rows - 2)):
        kept_ref[place] = wide_ref[row]
    for out_ref, hops in zip(out_refs, targets):
        chip = sum(jnp.where(info_ref[0] == source, to, 0) for source, to in hops)

        @pl.when(chip > 0)
        def _():
            for place in range(2):
                position = 2 * chip + jnp.abs(info_ref[1] - 1 + place)
                row = position + info_ref[2] * (rows - 1 - 2 * position)
                weights = weight_ref[row]
                out_ref[place] = advance(
                    [weights[i : i + 1] for i in range(6)],
                    emission, wide_ref[row - 1], wide_ref[row], wide_ref[row + 1],
                )


def end_rows(info_ref, last, field_ref, flow_ref, emission_ref, kept_ref, halo_ref, out_ref):
    members, rows, width = field_ref.shape
    emission = doubled(emission_ref[...])

    def halo_row(place):
        return halo_ref[pl.ds(place * members, members), :]

    halo_weights = weights_of(halo_ref[pl.ds(STEPS * members, 4), :])
    for parity in range(2):

        @pl.when(info_ref[2] == parity)
        def _():
            if parity == last:
                end, near, outside, beyond = 0, 1, halo_row(1), halo_row(0)
                inside, further = kept_ref[0], kept_ref[1]
            else:
                end, near, outside, beyond = rows - 1, rows - 2, halo_row(0), halo_row(1)
                inside, further = kept_ref[3], kept_ref[2]

            def ordered(weights, outer, own, inner):
                behind, ahead = (outer, inner) if end == 0 else (inner, outer)
                return advance(weights, emission, behind, own, ahead)

            end_weights = weights_of(flow_ref[:, end, :])
            end_field = field_ref[:, end, :]
            outer = ordered(halo_weights, beyond, outside, end_field)
            own = ordered(end_weights, outside, end_field, field_ref[:, near, :])
            out_ref[last] = ordered(end_weights, outer, own, inside)
            out_ref[1 - last] = ordered(weights_of(flow_ref[:, near, :]), own, inside, further)


def edge_kernel(info_ref, field_ref, flow_ref, emission_ref, kept_ref, last_ref, first_ref, *refs):
    out_refs, scratch = refs[:-1], refs[-1]
    chips = len(out_refs)
    core = info_ref[1]
    for last, halo_ref in enumerate((first_ref, last_ref)):
        end_rows(info_ref, last, field_ref, flow_ref, emission_ref, kept_ref, halo_ref, scratch)
        for s, out_ref in enumerate(out_refs):

            @pl.when(info_ref[0] == (chips - 1 - s if last else s))
            def _():
                out_ref[0] = scratch[1 - core]
                out_ref[1] = scratch[core]


def source_of(chip, chips, hops, k):
    inner = sum(jnp.where(chip == to, source, 0) for source, to in hops)
    return jnp.where(chip == 0, k, jnp.where(chip == chips - 1, chips - 1 - k, inner))


def collect_kernel(order, info_ref, mine_ref, other_ref, *refs):
    chips = len(order)
    near_other, near_own, observed_ref = refs[-3:]
    step = near_other.shape[1]
    observed_ref[...] = jnp.where(info_ref[2] == 1, other_ref[...], mine_ref[...])
    near_own[pl.ds(chips * step, PADDING), :] = jnp.zeros((PADDING, near_own.shape[1]), F32)
    chip = info_ref[0]
    at_edge = jnp.logical_or(chip == 0, chip == chips - 1)
    for index, (s, k) in enumerate(order):
        block = source_of(chip, chips, s, k)
        rows = pl.ds(pl.multiple_of(block * step, step), step)
        for ref, here in ((refs[index], jnp.logical_not(at_edge)), (refs[chips + index], at_edge)):

            @pl.when(here)
            def _():
                near_other[block] = ref[0]
                near_own[rows, :] = ref[1]


def unpack_kernel(order, info_ref, *refs):
    row_refs, out_ref = refs[:-1], refs[-1]
    rows = out_ref.shape[1]
    for x, ref in zip(order, row_refs):
        position = (2 * info_ref[0] + info_ref[1]) ^ x
        row = position + info_ref[2] * (rows - 1 - 2 * position)
        out_ref[:, pl.ds(row, 1), :] = ref[...][:, None, :]


def pieces(x, count):
    parts = []
    for _ in range(count - 1):
        part = x.astype(BF16)
        parts.append(part)
        x = x - part.astype(F32)
    return parts + [x.astype(BF16)]


def dot(a, b):
    return lax.dot_general(a, b, (((1,), (0,)), ((), ())), preferred_element_type=F32)


def dot_t(a, b):
    return lax.dot_general(a, b, (((0,), (0,)), ((), ())), preferred_element_type=F32)


def product(a, b):
    total = None
    for i, left in enumerate(a):
        for j, right in enumerate(b):
            if i + j < max(len(a), len(b)):
                term = dot(left, right)
                total = term if total is None else total + term
    return total


def observations(info_ref, observed_ref, width, root):
    slots = observed_ref.shape[1]
    cells, values, scales, count = (observed_ref[pl.ds(i, 1), :] for i in range(4))
    cells = cells.astype(jnp.int32)
    offset = sum((cells >= i * width).astype(jnp.int32) for i in (1, 2)) - 1
    column = cells - (offset + 1) * width
    side = offset * jnp.where(info_ref[2] == 1, -1, 1) * (1 - 2 * info_ref[1])
    cells = column + width * jnp.where(side == 0, 2, jnp.where(side < 0, 0, 1))
    active = lax.broadcasted_iota(jnp.int32, (1, slots), 1) < count.astype(jnp.int32)
    slot_weight = jnp.where(active, scales, 0.0)
    return cells, slot_weight, values, slot_weight * (1.0 / root)


def one_hot(cells, first, count):
    return (
        lax.broadcasted_iota(jnp.int32, (count, cells.shape[1]), 0) + first == cells
    ).astype(F32).astype(BF16)


def mean_of(blocks, members):
    total = blocks[0]
    for block in blocks[1:]:
        total = total + block
    return jnp.sum(total, axis=0, keepdims=True) * (1.0 / members)


def at_cells(row, chosen):
    parts = pieces(jnp.broadcast_to(row, (8, row.shape[1])), 3)
    return (dot(parts[0], chosen) + (dot(parts[1], chosen) + dot(parts[2], chosen)))[:1]


def prepare_kernel(
    info_ref, observed_ref, near_other, near_own, far_other, far_own,
    spread_high, spread_low, own_high, own_low, own_part, seen_ref, direction_ref,
    anomaly, high_ref, low_ref,
):
    chips, step, width = near_other.shape
    members = 2 * chips * step
    cells, _, _, scale = observations(info_ref, observed_ref, width, math.sqrt(members - 1))
    chosen = one_hot(cells, width, 2 * width)
    blocks = [pl.ds(index * step, step) for index in range(2 * chips)]
    means = []
    for place in range(2):
        columns = pl.ds(place * width, width)
        if place:
            rows = [near_own.at[block, :] for block in blocks[:chips]] + [far_own.at[chip] for chip in range(chips)]
        else:
            rows = [near_other.at[chip] for chip in range(chips)] + [far_other.at[block, :] for block in blocks[:chips]]
        means.append(mean_of([row[...] for row in rows], members))
        for block, row in zip(blocks, rows):
            part = row[...] - means[-1]
            anomaly[block, columns] = part
            high_ref[block, columns] = part.astype(BF16)

    def unit(x):
        return x * (1.0 / jnp.maximum(jnp.max(jnp.abs(x)), 1e-30))

    high = high_ref[...]
    along = lax.dot_general(high[:16], high, (((1,), (1,)), ((), ())), preferred_element_type=F32)
    rows = unit(dot(unit(along).astype(BF16), high))
    weight = jnp.sum(rows * rows[:1], axis=1, keepdims=True)
    weight = weight + jnp.where(jnp.max(jnp.abs(weight)) > 0.0, 0.0, 1.0)
    pattern = unit(jnp.sum(rows * weight, axis=0, keepdims=True))
    total = jnp.zeros((1, 1), F32)
    for block in blocks:
        along = jnp.sum(anomaly[block, :] * pattern, axis=1, keepdims=True)
        total = total + jnp.sum(along * along, axis=0, keepdims=True)
        direction_ref[block, :] = jnp.broadcast_to(along, (step, direction_ref.shape[1]))
    length = lax.rsqrt(jnp.maximum(total, 1e-30))
    taken = None
    for block in blocks:
        direction = direction_ref[block, :] * length
        direction_ref[block, :] = direction
        term = anomaly[block, :] * doubled(doubled(direction))
        taken = term if taken is None else taken + term
    taken = jnp.sum(taken, axis=0, keepdims=True)
    own_part[...] = jnp.broadcast_to(taken[:, width:], (own_part.shape[1], width)).T

    for block in blocks:
        rest = anomaly[block, :] - doubled(doubled(direction_ref[block, :])) * taken
        high, low = pieces(rest, 2)
        high_ref[block, :] = high
        low_ref[block, :] = low
        own = rest[:, width:].T
        own_high[:, block], own_low[:, block] = pieces(own, 2)
    seen_ref[pl.ds(0, 1), :] = at_cells(jnp.concatenate(means, axis=1), chosen)
    seen_ref[pl.ds(1, 1), :] = at_cells(taken, chosen)
    for first in range(0, members, PART):
        rows = pl.ds(first, PART)
        spread = (dot(high_ref[rows, :], chosen) + dot(low_ref[rows, :], chosen)) * scale
        high, low = pieces(spread, 2)
        spread_high[rows, :] = high
        spread_low[rows, :] = low


def square(parts):
    half = parts[0].shape[0] // 2
    upper = product([part[:half] for part in parts], parts)
    lower = product([part[half:] for part in parts], [part[:, half:] for part in parts])
    return upper, jnp.concatenate([upper[:, half:].T, lower], axis=1)


def region_kernel(
    info_ref, observed_ref, near_own, far_own, high_in, low_in, own_high, own_low, own_part, seen_ref,
    direction_ref, half_ref, rest_ref, *refs,
):
    chips, step, width = far_own.shape
    out_refs = refs[:-5]
    spread_high, spread_low, factor, squared, answer = refs[-5:]
    members = 2 * chips * step
    slots = observed_ref.shape[1]
    root = math.sqrt(members - 1)
    core = info_ref[1]
    ends = jnp.logical_or(
        jnp.logical_and(info_ref[0] == 0, core == 0), jnp.logical_and(info_ref[0] == chips - 1, core == 1)
    )
    part = jnp.where(ends, 0, 1)
    cells, slot_weight, values, scale = observations(info_ref, observed_ref, width, root)
    chosen = one_hot(cells, 0, width)

    def rows_at(half, chip):
        return pl.ds(pl.multiple_of((half * chips + chip) * step, step), step)

    blocks = [(half_ref.at[pl.ds(chip * step, step), :], rows_at(part, chip)) for chip in range(chips)]
    blocks += [(rest_ref.at[chip], rows_at(1 - part, chip)) for chip in range(chips)]
    mean = mean_of([ref[...] for ref, _ in blocks], members)
    taken = None
    for ref, block in blocks:
        term = (ref[...] - mean) * doubled(direction_ref[block, :])
        taken = term if taken is None else taken + term
    taken = jnp.sum(taken, axis=0, keepdims=True)
    seen_mean = seen_ref[pl.ds(0, 1), :] + at_cells(mean, chosen)
    common = (seen_ref[pl.ds(1, 1), :] + at_cells(taken, chosen)) * scale
    innovation = slot_weight * (values - seen_mean)
    for ref, block in blocks:
        rest = ref[...] - mean - doubled(direction_ref[block, :]) * taken
        high, low = pieces(rest, 2)
        high, low = pieces((dot(high, chosen) + dot(low, chosen)) * scale, 2)
        spread_high[block, :] = high + high_in[block, :]
        spread_low[block, :] = low + low_in[block, :]

    high, low = spread_high[...], spread_low[...]
    eye = lax.broadcasted_iota(jnp.int32, (slots, slots), 0) == lax.broadcasted_iota(
        jnp.int32, (slots, slots), 1
    )
    turned = high.T
    cross = dot(turned, low)
    factor[...] = dot(turned, high) + (cross + cross.T) + jnp.where(eye, 1.0, 0.0)
    answer[pl.ds(0, width), :] = product([own_high[...], own_low[...]], [high, low])
    answer[pl.ds(width, 8), :] = jnp.where(
        lax.broadcasted_iota(jnp.int32, (8, slots), 0) == 0, jnp.broadcast_to(common, (8, slots)), 0.0
    )
    half = slots // 2
    upper, lower = pl.ds(0, half), pl.ds(half, half)

    def after(bound):
        return bound * bound / (2.0 - bound * bound)

    def size(matrix):
        return jnp.sum(jnp.sum(matrix * matrix, axis=0, keepdims=True))

    def begin(count):
        parts = pieces(factor[...], count)
        if count > 2:
            squared[upper, :], squared[lower, :] = square(parts)
        bound = 1.0 - start
        gain = 2.0 / (2.0 - bound * bound)
        answer[...] = (gain * start) * (2.0 * answer[...] - start * product(pieces(answer[...], count), parts))
        factor[...] = (gain * start) * (2.0 * factor[...] - start * squared[...])
        return after(bound)

    def refine(bound, count):
        gain = 2.0 / (2.0 - bound * bound)
        parts = pieces(factor[...], count)
        answer[...] = gain * (2.0 * answer[...] - product(pieces(answer[...], count), parts))
        top, bottom = square(parts)
        factor[upper, :] = gain * (2.0 * factor[upper, :] - top)
        factor[lower, :] = gain * (2.0 * factor[lower, :] - bottom)
        return after(bound)

    def close(bound, rest):
        gain = 2.0 / (2.0 - bound * bound)
        answer[...] = gain * (answer[...] + dot(answer[...].astype(BF16), rest))
        return gain

    def finish(bound):
        rest = factor[...].astype(BF16)
        gain = close(bound, rest)
        factor[...] = gain * (dot(rest, rest) - jnp.where(eye, 0.5 * bound * bound, 0.0))
        return after(bound)

    top, bottom = square(pieces(factor[...], 2))
    squared[upper, :] = top
    squared[lower, :] = bottom
    limit = 1.0001 * jnp.sqrt(jnp.sqrt(size(top) + size(bottom)))
    start = 2.0 / (1.0 + limit)
    large = limit > LARGE
    bound = lax.cond(large, lambda: begin(3), lambda: begin(2))
    bound = lax.while_loop(lambda b: jnp.logical_and(b > COARSE, large), lambda b: refine(b, 3), bound)
    bound = lax.while_loop(lambda b: b > COARSE, lambda b: refine(b, 2), bound)
    factor[...] = jnp.where(eye, 1.0, 0.0) - factor[...]
    bound = lax.while_loop(lambda b: b > DONE, finish, bound)
    close(bound, factor[...].astype(BF16))

    solved = answer[pl.ds(0, width), :]
    alone = answer[pl.ds(width, 1), :]
    share = own_part[:, :1] - jnp.sum(solved * common, axis=1, keepdims=True)
    solved = solved + (share / (1.0 + jnp.sum(common * alone, axis=1, keepdims=True))) * alone
    solved = solved.T
    which = lax.broadcasted_iota(jnp.int32, (8, slots), 0)
    sides = jnp.where(which == 0, innovation * (1.0 / root), jnp.where(which == 1, -0.5 * common, 0.0))
    parts = pieces(solved, 2)
    sides = product(pieces(sides, 2), parts)
    shift, along = sides[0:1], sides[1:2]
    halved = [part * jnp.asarray(-0.5, BF16) for part in parts]
    for x, out_ref in enumerate(out_refs):
        chip, part = info_ref[0] ^ (x // 2), x % 2
        rows = pl.ds(pl.multiple_of((part * chips + chip) * step, step), step)
        moved = product([spread_high[rows, :], spread_low[rows, :]], halved)
        moved = moved + doubled(direction_ref[rows, :]) * along
        own = far_own[chip] if part else near_own[rows_at(0, chip), :]
        out_ref[...] = own + shift + moved


VMEM = pl.BlockSpec(memory_space=pltpu.VMEM)
SMEM = pl.BlockSpec(memory_space=pltpu.SMEM)


def call(kernel, name, out_shape, args, scratch=(), flops=None, aliases={}, limit=8, after=()):
    several = isinstance(out_shape, (list, tuple))
    if after:
        count, inner = len(args), kernel
        args = [*args, *after]
        kernel = lambda *refs: inner(*refs[:count], *refs[len(args) :])
    return pl.pallas_call(
        kernel,
        out_shape=out_shape,
        in_specs=[SMEM] + [VMEM] * (len(args) - 1 - len(after)) + [pl.BlockSpec(memory_space=pl.ANY)] * len(after),
        out_specs=[VMEM] * len(out_shape) if several else VMEM,
        scratch_shapes=scratch,
        input_output_aliases=aliases,
        compiler_params=pltpu.CompilerParams(vmem_limit_bytes=limit * 1024 * 1024),
        cost_estimate=flops and pl.CostEstimate(flops=flops, bytes_accessed=0, transcendentals=0),
        name=name,
    )(*args)


def bfloat(*shape):
    return jax.ShapeDtypeStruct(shape, BF16)


def array(*shape):
    return jax.ShapeDtypeStruct(shape, F32)


def per_device(
    init_field, flow_fields, emission, observed_cell, observed_count, observed_value, observed_scale
):
    step, rows, width = init_field.shape
    slots = observed_cell.shape[1]
    patches, lanes = lax.axis_size("patch"), lax.axis_size("member")
    chips = lanes // 2
    members = lanes * step
    axes = ("patch", "member")
    count = patches * lanes
    patch, lane = lax.axis_index("patch"), lax.axis_index("member")
    info = jnp.stack([lane // 2, lane % 2, patch % 2, jnp.int32(chips)]).astype(jnp.int32)

    edge = array(STEPS * step + 8, width)
    to_last, to_first, emitted = call(
        pack_kernel, "pack", [edge, edge, array(step, width // 2)],
        [info, init_field, flow_fields, emission[None, :]], limit=32,
    )

    def swap(message, start):
        lower = range(start, patches - 1, 2)
        return lax.ppermute(message, "patch", [(p, p + 1) for p in lower] + [(p + 1, p) for p in lower])

    halo_last, halo_first = swap(to_last, 0), swap(to_first, 1)

    mine = jnp.concatenate(
        [
            observed_cell.astype(F32),
            observed_value,
            observed_scale,
            jnp.broadcast_to(observed_count.astype(F32)[:, None], observed_cell.shape),
        ]
        * 2,
        axis=0,
    )

    def between(message, hops):
        return lax.ppermute(message, "member", [(2 * a + core, 2 * b + core) for a, b in hops for core in range(2)])

    mirrored = [
        [hop for to in range(1, chips // 2) for hop in (((to + s) % chips, to), (chips - 1 - (to + s) % chips, chips - 1 - to))]
        for s in range(chips)
    ]
    turning = [[((to - s) % chips, to) for to in range(1, chips - 1)] for s in range(chips)]
    single = all(len({source for source, _ in hops}) == len(hops) for hops in mirrored)
    targets = mirrored if single else turning
    pair = array(2, step, width)
    args = [info, init_field, flow_fields, emitted]
    kept, *inner = call(
        functools.partial(inner_kernel, targets), "inner", [array(4, step, width)] + [pair] * chips, args,
        [pltpu.VMEM((rows, step, width), F32), pltpu.VMEM((rows, 8, width), F32)], limit=32,
    )
    got_inner = [inner[0]] + [between(inner[s], targets[s]) for s in range(1, chips)]
    outer = call(
        edge_kernel, "edge", [pair] * chips, args + [kept, halo_last, halo_first],
        [pltpu.VMEM((2, step, width), F32)], limit=32,
    )
    got_outer = [outer[0]] + [
        between(outer[s], [(s, 0), (chips - 1 - s, chips - 1)]) for s in range(1, chips)
    ]
    order = [(targets[s], s) for s in range(chips)]
    pieces_in = got_inner + got_outer
    mine, _ = lax.optimization_barrier((mine, outer[0]))
    other = lax.ppermute(
        mine, axes,
        [(p * lanes + i, p * lanes + lanes - 1 - i) for p in range(1, patches, 2) for i in range(lanes)],
    )

    def device(p, chip, core):
        return p * lanes + 2 * chip + core

    borders, siblings = [], []
    for p in range(patches):
        for chip in range(chips):
            for core, away in ((0, -1), (1, 1)):
                siblings.append((device(p, chip, core), device(p, chip, 1 - core)))
                if 0 <= chip + away < chips:
                    borders.append((device(p, chip, core), device(p, chip + away, 1 - core)))
                else:
                    to = p + 1 if (p % 2 == 0) == (away == 1) else p - 1
                    if 0 <= to < patches:
                        borders.append((device(p, chip, core), device(to, chip, core)))

    half = array(chips, step, width)
    near_other, near_own, observed = call(
        functools.partial(collect_kernel, order), "collect",
        [half, array(chips * step + PADDING, width), array(8, slots)], [info, mine, other] + pieces_in,
    )
    far_own = lax.ppermute(near_other, axes, siblings)
    got_half = lax.ppermute(near_own, axes, borders)
    far_other = lax.ppermute(near_own, axes, siblings)
    got_rest = lax.ppermute(far_own, axes, borders)

    split = [pltpu.VMEM((members, slots), BF16)] * 2
    prepared = call(
        prepare_kernel, "prepare",
        [bfloat(members, slots)] * 2 + [bfloat(width, members)] * 2
        + [array(width, width // 2), array(8, slots), array(members, width // 2)],
        [info, observed, near_other, near_own, far_other, far_own],
        [pltpu.VMEM((members, 2 * width), F32)] + [pltpu.VMEM((members, 2 * width), BF16)] * 2,
        flops=8 * members * slots * width, limit=20,
    )
    analysed = call(
        region_kernel, "region", [array(step, width)] * lanes,
        [info, observed, near_own, far_own, *prepared, got_half, got_rest],
        split + [pltpu.VMEM((slots, slots), F32)] * 2 + [pltpu.VMEM((width + 8, slots), F32)],
        limit=24,
    )
    def swapped(x):
        return lax.ppermute(analysed[x], "member", [(i, i ^ x) for i in range(lanes)]) if x else analysed[0]

    order = sorted(range(lanes), key=lambda x: (x.bit_length() != lanes.bit_length() - 1, -x))
    return call(
        functools.partial(unpack_kernel, order), "unpack", array(step, rows, width),
        [info] + [swapped(x) for x in order], limit=48,
    )


def solution(mesh):
    return jax.shard_map(
        per_device,
        mesh=mesh,
        in_specs=(
            P("member", "patch", None),
            P(None, "patch", None),
            P("member"),
            P(("patch", "member"), None),
            P(("patch", "member")),
            P(("patch", "member"), None),
            P(("patch", "member"), None),
        ),
        out_specs=P("member", "patch", None),
        check_vma=False,
    )
```

```python
import functools
import math

import jax
import jax.numpy as jnp
from jax import lax
from jax.experimental import pallas as pl
from jax.experimental.pallas import tpu as pltpu
from jax.sharding import PartitionSpec as P

STEPS = 2
COARSE = 0.35
DONE = 0.02
LARGE = 2e4
PART = 256
PADDING = 8
F32 = jnp.float32
BF16 = jnp.bfloat16


def pack_kernel(info, field_ref, flow_ref, member_ref, first_ref, second_ref, emission_ref):
    members, rows, width = field_ref.shape
    diagonal = lax.broadcasted_iota(jnp.int32, (members, members), 0) == lax.broadcasted_iota(
        jnp.int32, (members, members), 1
    )
    column = jnp.sum(jnp.where(diagonal, member_ref[...], 0.0), axis=1, keepdims=True)
    emission_ref[...] = jnp.broadcast_to(column, emission_ref.shape)
    even = info[2] == 0
    for place in range(STEPS):
        tail, head = field_ref[:, rows - STEPS + place, :], field_ref[:, place, :]
        at = pl.ds(place * members, members)
        first_ref[at, :] = jnp.where(even, tail, head)
        second_ref[at, :] = jnp.where(even, head, tail)
    tail, head = flow_ref[:, rows - 1, :], flow_ref[:, 0, :]
    at = pl.ds(STEPS * members, 8)
    first_ref[at, :] = jnp.concatenate([jnp.where(even, tail, head)] * 2, axis=0)
    second_ref[at, :] = jnp.concatenate([jnp.where(even, head, tail)] * 2, axis=0)


def doubled(x):
    return jnp.concatenate([x, x], axis=1)


def weights_of(flow):
    row_flow, col_flow, kept, source = flow[0:1], flow[1:2], 1.0 - flow[2:3], flow[3:4]
    behind, ahead = jnp.maximum(row_flow, 0.0), -jnp.minimum(row_flow, 0.0)
    left, right = jnp.maximum(col_flow, 0.0), -jnp.minimum(col_flow, 0.0)
    stays = 1.0 - behind - ahead - left - right
    return [kept * stays, kept * behind, kept * ahead, kept * left, kept * right, source]


def advance(weights, emission, behind, field, ahead):
    width = field.shape[1]
    return (
        weights[0] * field
        + weights[1] * behind
        + weights[2] * ahead
        + weights[3] * pltpu.roll(field, 1, 1)
        + weights[4] * pltpu.roll(field, width - 1, 1)
        + emission * weights[5]
    )


def inner_kernel(targets, info, field_ref, flow_ref, emission_ref, kept_ref, *refs):
    out_refs, (wide_ref, weight_ref) = refs[:-2], refs[-2:]
    rows = field_ref.shape[1]
    emission = doubled(emission_ref[...])
    for row in range(1, rows - 1):
        weights = weights_of(flow_ref[:, row, :])
        for i, weight in enumerate(weights):
            weight_ref[row, pl.ds(i, 1), :] = weight
        wide_ref[row] = advance(
            weights, emission, field_ref[:, row - 1, :], field_ref[:, row, :], field_ref[:, row + 1, :]
        )
    for place, row in enumerate((1, 2, rows - 3, rows - 2)):
        kept_ref[place] = wide_ref[row]
    for out_ref, hops in zip(out_refs, targets):
        chip = sum(jnp.where(info[0] == source, to, 0) for source, to in hops)

        @pl.when(chip > 0)
        def _():
            for place in range(2):
                position = 2 * chip + jnp.abs(info[1] - 1 + place)
                row = position + info[2] * (rows - 1 - 2 * position)
                weights = weight_ref[row]
                out_ref[place] = advance(
                    [weights[i : i + 1] for i in range(6)],
                    emission, wide_ref[row - 1], wide_ref[row], wide_ref[row + 1],
                )


def end_rows(info, last, field_ref, flow_ref, emission_ref, kept_ref, halo_ref, out_ref):
    members, rows, width = field_ref.shape
    emission = doubled(emission_ref[...])

    def halo_row(place):
        return halo_ref[pl.ds(place * members, members), :]

    halo_weights = weights_of(halo_ref[pl.ds(STEPS * members, 4), :])
    for parity in range(2):

        @pl.when(info[2] == parity)
        def _():
            if parity == last:
                end, near, outside, beyond = 0, 1, halo_row(1), halo_row(0)
                inside, further = kept_ref[0], kept_ref[1]
            else:
                end, near, outside, beyond = rows - 1, rows - 2, halo_row(0), halo_row(1)
                inside, further = kept_ref[3], kept_ref[2]

            def ordered(weights, outer, own, inner):
                behind, ahead = (outer, inner) if end == 0 else (inner, outer)
                return advance(weights, emission, behind, own, ahead)

            end_weights = weights_of(flow_ref[:, end, :])
            end_field = field_ref[:, end, :]
            outer = ordered(halo_weights, beyond, outside, end_field)
            own = ordered(end_weights, outside, end_field, field_ref[:, near, :])
            out_ref[last] = ordered(end_weights, outer, own, inside)
            out_ref[1 - last] = ordered(weights_of(flow_ref[:, near, :]), own, inside, further)


def edge_kernel(info, field_ref, flow_ref, emission_ref, kept_ref, last_ref, first_ref, *refs):
    out_refs, scratch = refs[:-1], refs[-1]
    chips = len(out_refs)
    core = info[1]
    for last, halo_ref in enumerate((first_ref, last_ref)):
        end_rows(info, last, field_ref, flow_ref, emission_ref, kept_ref, halo_ref, scratch)
        for s, out_ref in enumerate(out_refs):

            @pl.when(info[0] == (chips - 1 - s if last else s))
            def _():
                out_ref[0] = scratch[1 - core]
                out_ref[1] = scratch[core]


def source_of(chip, chips, hops, k):
    inner = sum(jnp.where(chip == to, source, 0) for source, to in hops)
    return jnp.where(chip == 0, k, jnp.where(chip == chips - 1, chips - 1 - k, inner))


def collect_kernel(order, info, mine_ref, other_ref, *refs):
    chips = len(order)
    near_other, near_own, observed_ref = refs[-3:]
    step = near_other.shape[1]
    observed_ref[...] = jnp.where(info[2] == 1, other_ref[...], mine_ref[...])
    near_own[pl.ds(chips * step, PADDING), :] = jnp.zeros((PADDING, near_own.shape[1]), F32)
    chip = info[0]
    at_edge = jnp.logical_or(chip == 0, chip == chips - 1)
    for index, (s, k) in enumerate(order):
        block = source_of(chip, chips, s, k)
        rows = pl.ds(pl.multiple_of(block * step, step), step)
        for ref, here in ((refs[index], jnp.logical_not(at_edge)), (refs[chips + index], at_edge)):

            @pl.when(here)
            def _():
                near_other[block] = ref[0]
                near_own[rows, :] = ref[1]


def unpack_kernel(order, info, *refs):
    row_refs, out_ref = refs[:-1], refs[-1]
    rows = out_ref.shape[1]
    for x, ref in zip(order, row_refs):
        position = (2 * info[0] + info[1]) ^ x
        row = position + info[2] * (rows - 1 - 2 * position)
        out_ref[:, pl.ds(row, 1), :] = ref[...][:, None, :]


def pieces(x, count):
    parts = []
    for _ in range(count - 1):
        part = x.astype(BF16)
        parts.append(part)
        x = x - part.astype(F32)
    return parts + [x.astype(BF16)]


def dot(a, b):
    return lax.dot_general(a, b, (((1,), (0,)), ((), ())), preferred_element_type=F32)


def dot_t(a, b):
    return lax.dot_general(a, b, (((0,), (0,)), ((), ())), preferred_element_type=F32)


def product(a, b):
    total = None
    for i, left in enumerate(a):
        for j, right in enumerate(b):
            if i + j < max(len(a), len(b)):
                term = dot(left, right)
                total = term if total is None else total + term
    return total


def observations(info, observed_ref, width, root):
    slots = observed_ref.shape[1]
    cells, values, scales, count = (observed_ref[pl.ds(i, 1), :] for i in range(4))
    cells = cells.astype(jnp.int32)
    offset = sum((cells >= i * width).astype(jnp.int32) for i in (1, 2)) - 1
    column = cells - (offset + 1) * width
    side = offset * jnp.where(info[2] == 1, -1, 1) * (1 - 2 * info[1])
    cells = column + width * jnp.where(side == 0, 2, jnp.where(side < 0, 0, 1))
    active = lax.broadcasted_iota(jnp.int32, (1, slots), 1) < count.astype(jnp.int32)
    slot_weight = jnp.where(active, scales, 0.0)
    return cells, slot_weight, values, slot_weight * (1.0 / root)


def one_hot(cells, first, count):
    return (
        lax.broadcasted_iota(jnp.int32, (count, cells.shape[1]), 0) + first == cells
    ).astype(F32).astype(BF16)


def mean_of(blocks, members):
    total = blocks[0]
    for block in blocks[1:]:
        total = total + block
    return jnp.sum(total, axis=0, keepdims=True) * (1.0 / members)


def at_cells(row, chosen):
    parts = pieces(jnp.broadcast_to(row, (8, row.shape[1])), 3)
    return (dot(parts[0], chosen) + (dot(parts[1], chosen) + dot(parts[2], chosen)))[:1]


def prepare_kernel(
    info, observed_ref, near_other, near_own, far_other, far_own,
    spread_high, spread_low, own_high, own_low, own_part, seen_ref, direction_ref,
    anomaly, high_ref, low_ref,
):
    chips, step, width = near_other.shape
    members = 2 * chips * step
    cells, _, _, scale = observations(info, observed_ref, width, math.sqrt(members - 1))
    chosen = one_hot(cells, width, 2 * width)
    blocks = [pl.ds(index * step, step) for index in range(2 * chips)]
    means = []
    for place in range(2):
        columns = pl.ds(place * width, width)
        if place:
            rows = [near_own.at[block, :] for block in blocks[:chips]] + [far_own.at[chip] for chip in range(chips)]
        else:
            rows = [near_other.at[chip] for chip in range(chips)] + [far_other.at[block, :] for block in blocks[:chips]]
        means.append(mean_of([row[...] for row in rows], members))
        for block, row in zip(blocks, rows):
            part = row[...] - means[-1]
            anomaly[block, columns] = part
            high_ref[block, columns] = part.astype(BF16)

    def unit(x):
        return x * (1.0 / jnp.maximum(jnp.max(jnp.abs(x)), 1e-30))

    high = high_ref[...]
    along = lax.dot_general(high[:16], high, (((1,), (1,)), ((), ())), preferred_element_type=F32)
    rows = unit(dot(unit(along).astype(BF16), high))
    weight = jnp.sum(rows * rows[:1], axis=1, keepdims=True)
    weight = weight + jnp.where(jnp.max(jnp.abs(weight)) > 0.0, 0.0, 1.0)
    pattern = unit(jnp.sum(rows * weight, axis=0, keepdims=True))
    total = jnp.zeros((1, 1), F32)
    for block in blocks:
        along = jnp.sum(anomaly[block, :] * pattern, axis=1, keepdims=True)
        total = total + jnp.sum(along * along, axis=0, keepdims=True)
        direction_ref[block, :] = jnp.broadcast_to(along, (step, direction_ref.shape[1]))
    length = lax.rsqrt(jnp.maximum(total, 1e-30))
    taken = None
    for block in blocks:
        direction = direction_ref[block, :] * length
        direction_ref[block, :] = direction
        term = anomaly[block, :] * doubled(doubled(direction))
        taken = term if taken is None else taken + term
    taken = jnp.sum(taken, axis=0, keepdims=True)
    own_part[...] = jnp.broadcast_to(taken[:, width:], (own_part.shape[1], width)).T

    for block in blocks:
        rest = anomaly[block, :] - doubled(doubled(direction_ref[block, :])) * taken
        high, low = pieces(rest, 2)
        high_ref[block, :] = high
        low_ref[block, :] = low
        own = rest[:, width:].T
        own_high[:, block], own_low[:, block] = pieces(own, 2)
    seen_ref[pl.ds(0, 1), :] = at_cells(jnp.concatenate(means, axis=1), chosen)
    seen_ref[pl.ds(1, 1), :] = at_cells(taken, chosen)
    for first in range(0, members, PART):
        rows = pl.ds(first, PART)
        spread = (dot(high_ref[rows, :], chosen) + dot(low_ref[rows, :], chosen)) * scale
        high, low = pieces(spread, 2)
        spread_high[rows, :] = high
        spread_low[rows, :] = low


def square(parts):
    half = parts[0].shape[0] // 2
    upper = product([part[:half] for part in parts], parts)
    lower = product([part[half:] for part in parts], [part[:, half:] for part in parts])
    return upper, jnp.concatenate([upper[:, half:].T, lower], axis=1)


def region_kernel(
    info, observed_ref, near_own, far_own, high_in, low_in, own_high, own_low, own_part, seen_ref,
    direction_ref, half_ref, rest_ref, *refs,
):
    chips, step, width = far_own.shape
    out_refs = refs[:-5]
    spread_high, spread_low, factor, squared, answer = refs[-5:]
    members = 2 * chips * step
    slots = observed_ref.shape[1]
    root = math.sqrt(members - 1)
    core = info[1]
    ends = jnp.logical_or(
        jnp.logical_and(info[0] == 0, core == 0), jnp.logical_and(info[0] == chips - 1, core == 1)
    )
    part = jnp.where(ends, 0, 1)
    cells, slot_weight, values, scale = observations(info, observed_ref, width, root)
    chosen = one_hot(cells, 0, width)

    def rows_at(half, chip):
        return pl.ds(pl.multiple_of((half * chips + chip) * step, step), step)

    blocks = [(half_ref.at[pl.ds(chip * step, step), :], rows_at(part, chip)) for chip in range(chips)]
    blocks += [(rest_ref.at[chip], rows_at(1 - part, chip)) for chip in range(chips)]
    mean = mean_of([ref[...] for ref, _ in blocks], members)
    taken = None
    for ref, block in blocks:
        term = (ref[...] - mean) * doubled(direction_ref[block, :])
        taken = term if taken is None else taken + term
    taken = jnp.sum(taken, axis=0, keepdims=True)
    seen_mean = seen_ref[pl.ds(0, 1), :] + at_cells(mean, chosen)
    common = (seen_ref[pl.ds(1, 1), :] + at_cells(taken, chosen)) * scale
    innovation = slot_weight * (values - seen_mean)
    for ref, block in blocks:
        rest = ref[...] - mean - doubled(direction_ref[block, :]) * taken
        high, low = pieces(rest, 2)
        high, low = pieces((dot(high, chosen) + dot(low, chosen)) * scale, 2)
        spread_high[block, :] = high + high_in[block, :]
        spread_low[block, :] = low + low_in[block, :]

    high, low = spread_high[...], spread_low[...]
    eye = lax.broadcasted_iota(jnp.int32, (slots, slots), 0) == lax.broadcasted_iota(
        jnp.int32, (slots, slots), 1
    )
    turned = high.T
    cross = dot(turned, low)
    factor[...] = dot(turned, high) + (cross + cross.T) + jnp.where(eye, 1.0, 0.0)
    answer[pl.ds(0, width), :] = product([own_high[...], own_low[...]], [high, low])
    answer[pl.ds(width, 8), :] = jnp.where(
        lax.broadcasted_iota(jnp.int32, (8, slots), 0) == 0, jnp.broadcast_to(common, (8, slots)), 0.0
    )
    half = slots // 2
    upper, lower = pl.ds(0, half), pl.ds(half, half)

    def after(bound):
        return bound * bound / (2.0 - bound * bound)

    def size(matrix):
        return jnp.sum(jnp.sum(matrix * matrix, axis=0, keepdims=True))

    def begin(count):
        parts = pieces(factor[...], count)
        if count > 2:
            squared[upper, :], squared[lower, :] = square(parts)
        bound = 1.0 - start
        gain = 2.0 / (2.0 - bound * bound)
        answer[...] = (gain * start) * (2.0 * answer[...] - start * product(pieces(answer[...], count), parts))
        factor[...] = (gain * start) * (2.0 * factor[...] - start * squared[...])
        return after(bound)

    def refine(bound, count):
        gain = 2.0 / (2.0 - bound * bound)
        parts = pieces(factor[...], count)
        answer[...] = gain * (2.0 * answer[...] - product(pieces(answer[...], count), parts))
        top, bottom = square(parts)
        factor[upper, :] = gain * (2.0 * factor[upper, :] - top)
        factor[lower, :] = gain * (2.0 * factor[lower, :] - bottom)
        return after(bound)

    def close(bound, rest):
        gain = 2.0 / (2.0 - bound * bound)
        answer[...] = gain * (answer[...] + dot(answer[...].astype(BF16), rest))
        return gain

    def finish(bound):
        rest = factor[...].astype(BF16)
        gain = close(bound, rest)
        factor[...] = gain * (dot(rest, rest) - jnp.where(eye, 0.5 * bound * bound, 0.0))
        return after(bound)

    top, bottom = square(pieces(factor[...], 2))
    squared[upper, :] = top
    squared[lower, :] = bottom
    limit = 1.0001 * jnp.sqrt(jnp.sqrt(size(top) + size(bottom)))
    start = 2.0 / (1.0 + limit)
    large = limit > LARGE
    bound = lax.cond(large, lambda: begin(3), lambda: begin(2))
    bound = lax.while_loop(lambda b: jnp.logical_and(b > COARSE, large), lambda b: refine(b, 3), bound)
    bound = lax.while_loop(lambda b: b > COARSE, lambda b: refine(b, 2), bound)
    factor[...] = jnp.where(eye, 1.0, 0.0) - factor[...]
    bound = lax.while_loop(lambda b: b > DONE, finish, bound)
    close(bound, factor[...].astype(BF16))

    solved = answer[pl.ds(0, width), :]
    alone = answer[pl.ds(width, 1), :]
    share = own_part[:, :1] - jnp.sum(solved * common, axis=1, keepdims=True)
    solved = solved + (share / (1.0 + jnp.sum(common * alone, axis=1, keepdims=True))) * alone
    solved = solved.T
    which = lax.broadcasted_iota(jnp.int32, (8, slots), 0)
    sides = jnp.where(which == 0, innovation * (1.0 / root), jnp.where(which == 1, -0.5 * common, 0.0))
    parts = pieces(solved, 2)
    sides = product(pieces(sides, 2), parts)
    shift, along = sides[0:1], sides[1:2]
    halved = [part * jnp.asarray(-0.5, BF16) for part in parts]
    for x, out_ref in enumerate(out_refs):
        chip, part = info[0] ^ (x // 2), x % 2
        rows = pl.ds(pl.multiple_of((part * chips + chip) * step, step), step)
        moved = product([spread_high[rows, :], spread_low[rows, :]], halved)
        moved = moved + doubled(direction_ref[rows, :]) * along
        own = far_own[chip] if part else near_own[rows_at(0, chip), :]
        out_ref[...] = own + shift + moved


VMEM = pl.BlockSpec(memory_space=pltpu.VMEM)


def position():
    lane, patch = lax.axis_index("member"), lax.axis_index("patch")
    return lax.div(lane, 2), lax.rem(lane, 2), lax.rem(patch, 2), lax.axis_size("member") // 2


def call(kernel, name, out_shape, args, scratch=(), flops=None, limit=8):
    several = isinstance(out_shape, (list, tuple))
    return pl.pallas_call(
        lambda *refs: kernel(position(), *refs),
        out_shape=out_shape,
        in_specs=[VMEM] * len(args),
        out_specs=[VMEM] * len(out_shape) if several else VMEM,
        scratch_shapes=scratch,
        compiler_params=pltpu.CompilerParams(vmem_limit_bytes=limit * 1024 * 1024),
        cost_estimate=flops and pl.CostEstimate(flops=flops, bytes_accessed=0, transcendentals=0),
        name=name,
    )(*args)


def bfloat(*shape):
    return jax.ShapeDtypeStruct(shape, BF16)


def array(*shape):
    return jax.ShapeDtypeStruct(shape, F32)


def per_device(
    init_field, flow_fields, emission, observed_cell, observed_count, observed_value, observed_scale
):
    step, rows, width = init_field.shape
    slots = observed_cell.shape[1]
    patches, lanes = lax.axis_size("patch"), lax.axis_size("member")
    chips = lanes // 2
    members = lanes * step
    axes = ("patch", "member")
    count = patches * lanes

    edge = array(STEPS * step + 8, width)
    to_last, to_first, emitted = call(
        pack_kernel, "pack", [edge, edge, array(step, width // 2)],
        [init_field, flow_fields, emission[None, :]], limit=32,
    )

    def swap(message, start):
        lower = range(start, patches - 1, 2)
        return lax.ppermute(message, "patch", [(p, p + 1) for p in lower] + [(p + 1, p) for p in lower])

    halo_last, halo_first = swap(to_last, 0), swap(to_first, 1)

    mine = jnp.concatenate(
        [
            observed_cell.astype(F32),
            observed_value,
            observed_scale,
            jnp.broadcast_to(observed_count.astype(F32)[:, None], observed_cell.shape),
        ]
        * 2,
        axis=0,
    )

    def between(message, hops):
        return lax.ppermute(message, "member", [(2 * a + core, 2 * b + core) for a, b in hops for core in range(2)])

    mirrored = [
        [hop for to in range(1, chips // 2) for hop in (((to + s) % chips, to), (chips - 1 - (to + s) % chips, chips - 1 - to))]
        for s in range(chips)
    ]
    turning = [[((to - s) % chips, to) for to in range(1, chips - 1)] for s in range(chips)]
    single = all(len({source for source, _ in hops}) == len(hops) for hops in mirrored)
    targets = mirrored if single else turning
    pair = array(2, step, width)
    args = [init_field, flow_fields, emitted]
    kept, *inner = call(
        functools.partial(inner_kernel, targets), "inner", [array(4, step, width)] + [pair] * chips, args,
        [pltpu.VMEM((rows, step, width), F32), pltpu.VMEM((rows, 8, width), F32)], limit=32,
    )
    got_inner = [inner[0]] + [between(inner[s], targets[s]) for s in range(1, chips)]
    outer = call(
        edge_kernel, "edge", [pair] * chips, args + [kept, halo_last, halo_first],
        [pltpu.VMEM((2, step, width), F32)], limit=32,
    )
    got_outer = [outer[0]] + [
        between(outer[s], [(s, 0), (chips - 1 - s, chips - 1)]) for s in range(1, chips)
    ]
    order = [(targets[s], s) for s in range(chips)]
    pieces_in = got_inner + got_outer
    mine, _ = lax.optimization_barrier((mine, outer[0]))
    other = lax.ppermute(
        mine, axes,
        [(p * lanes + i, p * lanes + lanes - 1 - i) for p in range(1, patches, 2) for i in range(lanes)],
    )

    def device(p, chip, core):
        return p * lanes + 2 * chip + core

    borders, siblings = [], []
    for p in range(patches):
        for chip in range(chips):
            for core, away in ((0, -1), (1, 1)):
                siblings.append((device(p, chip, core), device(p, chip, 1 - core)))
                if 0 <= chip + away < chips:
                    borders.append((device(p, chip, core), device(p, chip + away, 1 - core)))
                else:
                    to = p + 1 if (p % 2 == 0) == (away == 1) else p - 1
                    if 0 <= to < patches:
                        borders.append((device(p, chip, core), device(to, chip, core)))

    half = array(chips, step, width)
    near_other, near_own, observed = call(
        functools.partial(collect_kernel, order), "collect",
        [half, array(chips * step + PADDING, width), array(8, slots)], [mine, other] + pieces_in,
    )
    far_own = lax.ppermute(near_other, axes, siblings)
    got_half = lax.ppermute(near_own, axes, borders)
    far_other = lax.ppermute(near_own, axes, siblings)
    got_rest = lax.ppermute(far_own, axes, borders)

    split = [pltpu.VMEM((members, slots), BF16)] * 2
    prepared = call(
        prepare_kernel, "prepare",
        [bfloat(members, slots)] * 2 + [bfloat(width, members)] * 2
        + [array(width, width // 2), array(8, slots), array(members, width // 2)],
        [observed, near_other, near_own, far_other, far_own],
        [pltpu.VMEM((members, 2 * width), F32)] + [pltpu.VMEM((members, 2 * width), BF16)] * 2,
        flops=8 * members * slots * width, limit=20,
    )
    analysed = call(
        region_kernel, "region", [array(step, width)] * lanes,
        [observed, near_own, far_own, *prepared, got_half, got_rest],
        split + [pltpu.VMEM((slots, slots), F32)] * 2 + [pltpu.VMEM((width + 8, slots), F32)],
        limit=24,
    )
    def swapped(x):
        return lax.ppermute(analysed[x], "member", [(i, i ^ x) for i in range(lanes)]) if x else analysed[0]

    order = sorted(range(lanes), key=lambda x: (x.bit_length() != lanes.bit_length() - 1, -x))
    return call(
        functools.partial(unpack_kernel, order), "unpack", array(step, rows, width),
        [swapped(x) for x in order], limit=48,
    )


def solution(mesh):
    return jax.shard_map(
        per_device,
        mesh=mesh,
        in_specs=(
            P("member", "patch", None),
            P(None, "patch", None),
            P("member"),
            P(("patch", "member"), None),
            P(("patch", "member")),
            P(("patch", "member"), None),
            P(("patch", "member"), None),
        ),
        out_specs=P("member", "patch", None),
        check_vma=False,
    )
```

```python
import functools
import math

import jax
import jax.numpy as jnp
from jax import lax
from jax.experimental import pallas as pl
from jax.experimental.pallas import tpu as pltpu
from jax.sharding import PartitionSpec as P

STEPS = 2
COARSE = 0.35
DONE = 0.02
LARGE = 2e4
PART = 256
PADDING = 8
F32 = jnp.float32
BF16 = jnp.bfloat16


def pack_kernel(info, field_ref, flow_ref, first_ref, second_ref):
    members, rows, width = field_ref.shape
    even = info[2] == 0
    for place in range(STEPS):
        tail, head = field_ref[:, rows - STEPS + place, :], field_ref[:, place, :]
        at = pl.ds(place * members, members)
        first_ref[at, :] = jnp.where(even, tail, head)
        second_ref[at, :] = jnp.where(even, head, tail)
    tail, head = flow_ref[:, rows - 1, :], flow_ref[:, 0, :]
    at = pl.ds(STEPS * members, 8)
    first_ref[at, :] = jnp.concatenate([jnp.where(even, tail, head)] * 2, axis=0)
    second_ref[at, :] = jnp.concatenate([jnp.where(even, head, tail)] * 2, axis=0)


def doubled(x):
    return jnp.concatenate([x, x], axis=1)


def weights_of(flow):
    row_flow, col_flow, kept, source = flow[0:1], flow[1:2], 1.0 - flow[2:3], flow[3:4]
    behind, ahead = jnp.maximum(row_flow, 0.0), -jnp.minimum(row_flow, 0.0)
    left, right = jnp.maximum(col_flow, 0.0), -jnp.minimum(col_flow, 0.0)
    stays = 1.0 - behind - ahead - left - right
    return [kept * stays, kept * behind, kept * ahead, kept * left, kept * right, source]


def advance(weights, emission, behind, field, ahead):
    width = field.shape[1]
    return (
        weights[0] * field
        + weights[1] * behind
        + weights[2] * ahead
        + weights[3] * pltpu.roll(field, 1, 1)
        + weights[4] * pltpu.roll(field, width - 1, 1)
        + emission * weights[5]
    )


def inner_kernel(targets, info, field_ref, flow_ref, member_ref, kept_ref, emission_ref, *refs):
    out_refs, (wide_ref, weight_ref) = refs[:-2], refs[-2:]
    members, rows, _ = field_ref.shape
    diagonal = lax.broadcasted_iota(jnp.int32, (members, members), 0) == lax.broadcasted_iota(
        jnp.int32, (members, members), 1
    )
    column = jnp.sum(jnp.where(diagonal, member_ref[...], 0.0), axis=1, keepdims=True)
    emission_ref[...] = jnp.broadcast_to(column, emission_ref.shape)
    emission = doubled(emission_ref[...])
    for row in range(1, rows - 1):
        weights = weights_of(flow_ref[:, row, :])
        for i, weight in enumerate(weights):
            weight_ref[row, pl.ds(i, 1), :] = weight
        wide_ref[row] = advance(
            weights, emission, field_ref[:, row - 1, :], field_ref[:, row, :], field_ref[:, row + 1, :]
        )
    for place, row in enumerate((1, 2, rows - 3, rows - 2)):
        kept_ref[place] = wide_ref[row]
    for out_ref, hops in zip(out_refs, targets):
        chip = sum(jnp.where(info[0] == source, to, 0) for source, to in hops)

        @pl.when(chip > 0)
        def _():
            for place in range(2):
                position = 2 * chip + jnp.abs(info[1] - 1 + place)
                row = position + info[2] * (rows - 1 - 2 * position)
                weights = weight_ref[row]
                out_ref[place] = advance(
                    [weights[i : i + 1] for i in range(6)],
                    emission, wide_ref[row - 1], wide_ref[row], wide_ref[row + 1],
                )


def end_rows(info, last, field_ref, flow_ref, emission_ref, kept_ref, halo_ref, out_ref):
    members, rows, width = field_ref.shape
    emission = doubled(emission_ref[...])

    def halo_row(place):
        return halo_ref[pl.ds(place * members, members), :]

    halo_weights = weights_of(halo_ref[pl.ds(STEPS * members, 4), :])
    for parity in range(2):

        @pl.when(info[2] == parity)
        def _():
            if parity == last:
                end, near, outside, beyond = 0, 1, halo_row(1), halo_row(0)
                inside, further = kept_ref[0], kept_ref[1]
            else:
                end, near, outside, beyond = rows - 1, rows - 2, halo_row(0), halo_row(1)
                inside, further = kept_ref[3], kept_ref[2]

            def ordered(weights, outer, own, inner):
                behind, ahead = (outer, inner) if end == 0 else (inner, outer)
                return advance(weights, emission, behind, own, ahead)

            end_weights = weights_of(flow_ref[:, end, :])
            end_field = field_ref[:, end, :]
            outer = ordered(halo_weights, beyond, outside, end_field)
            own = ordered(end_weights, outside, end_field, field_ref[:, near, :])
            out_ref[last] = ordered(end_weights, outer, own, inside)
            out_ref[1 - last] = ordered(weights_of(flow_ref[:, near, :]), own, inside, further)


def edge_kernel(info, field_ref, flow_ref, emission_ref, kept_ref, last_ref, first_ref, *refs):
    out_refs, scratch = refs[:-1], refs[-1]
    chips = len(out_refs)
    core = info[1]
    for last, halo_ref in enumerate((first_ref, last_ref)):
        end_rows(info, last, field_ref, flow_ref, emission_ref, kept_ref, halo_ref, scratch)
        for s, out_ref in enumerate(out_refs):

            @pl.when(info[0] == (chips - 1 - s if last else s))
            def _():
                out_ref[0] = scratch[1 - core]
                out_ref[1] = scratch[core]


def source_of(chip, chips, hops, k):
    inner = sum(jnp.where(chip == to, source, 0) for source, to in hops)
    return jnp.where(chip == 0, k, jnp.where(chip == chips - 1, chips - 1 - k, inner))


def collect_kernel(order, info, mine_ref, other_ref, *refs):
    chips = len(order)
    near_other, near_own, observed_ref = refs[-3:]
    step = near_other.shape[1]
    observed_ref[...] = jnp.where(info[2] == 1, other_ref[...], mine_ref[...])
    near_own[pl.ds(chips * step, PADDING), :] = jnp.zeros((PADDING, near_own.shape[1]), F32)
    chip = info[0]
    at_edge = jnp.logical_or(chip == 0, chip == chips - 1)
    for index, (s, k) in enumerate(order):
        block = source_of(chip, chips, s, k)
        rows = pl.ds(pl.multiple_of(block * step, step), step)
        for ref, here in ((refs[index], jnp.logical_not(at_edge)), (refs[chips + index], at_edge)):

            @pl.when(here)
            def _():
                near_other[block] = ref[0]
                near_own[rows, :] = ref[1]


def unpack_kernel(order, info, *refs):
    row_refs, (out_hbm, out_ref, sems) = refs[:-3], refs[-3:]
    members, rows, _ = out_ref.shape
    part = members // 4
    moves = []
    for index in range(4):
        some = pl.ds(index * part, part)
        for x, ref in zip(order, row_refs):
            position = (2 * info[0] + info[1]) ^ x
            row = position + info[2] * (rows - 1 - 2 * position)
            out_ref[some, pl.ds(row, 1), :] = ref[some, :][:, None, :]
        moves.append(pltpu.make_async_copy(out_ref.at[some], out_hbm.at[some], sems.at[index]))
        moves[-1].start()
    for move in moves:
        move.wait()


def pieces(x, count):
    parts = []
    for _ in range(count - 1):
        part = x.astype(BF16)
        parts.append(part)
        x = x - part.astype(F32)
    return parts + [x.astype(BF16)]


def dot(a, b):
    return lax.dot_general(a, b, (((1,), (0,)), ((), ())), preferred_element_type=F32)


def dot_t(a, b):
    return lax.dot_general(a, b, (((0,), (0,)), ((), ())), preferred_element_type=F32)


def product(a, b):
    total = None
    for i, left in enumerate(a):
        for j, right in enumerate(b):
            if i + j < max(len(a), len(b)):
                term = dot(left, right)
                total = term if total is None else total + term
    return total


def observations(info, observed_ref, width, root):
    slots = observed_ref.shape[1]
    cells, values, scales, count = (observed_ref[pl.ds(i, 1), :] for i in range(4))
    cells = cells.astype(jnp.int32)
    offset = sum((cells >= i * width).astype(jnp.int32) for i in (1, 2)) - 1
    column = cells - (offset + 1) * width
    side = offset * jnp.where(info[2] == 1, -1, 1) * (1 - 2 * info[1])
    cells = column + width * jnp.where(side == 0, 2, jnp.where(side < 0, 0, 1))
    active = lax.broadcasted_iota(jnp.int32, (1, slots), 1) < count.astype(jnp.int32)
    slot_weight = jnp.where(active, scales, 0.0)
    return cells, slot_weight, values, slot_weight * (1.0 / root)


def one_hot(cells, first, count):
    return (
        lax.broadcasted_iota(jnp.int32, (count, cells.shape[1]), 0) + first == cells
    ).astype(F32).astype(BF16)


def mean_of(blocks, members):
    total = blocks[0]
    for block in blocks[1:]:
        total = total + block
    return jnp.sum(total, axis=0, keepdims=True) * (1.0 / members)


def at_cells(row, chosen):
    parts = pieces(jnp.broadcast_to(row, (8, row.shape[1])), 3)
    return (dot(parts[0], chosen) + (dot(parts[1], chosen) + dot(parts[2], chosen)))[:1]


def prepare_kernel(
    info, observed_ref, near_other, near_own, far_other, far_own,
    spread_high, spread_low, own_high, own_low, own_part, seen_ref, direction_ref,
    anomaly, high_ref, low_ref,
):
    chips, step, width = near_other.shape
    members = 2 * chips * step
    cells, _, _, scale = observations(info, observed_ref, width, math.sqrt(members - 1))
    chosen = one_hot(cells, width, 2 * width)
    blocks = [pl.ds(index * step, step) for index in range(2 * chips)]
    means = []
    for place in range(2):
        columns = pl.ds(place * width, width)
        if place:
            rows = [near_own.at[block, :] for block in blocks[:chips]] + [far_own.at[chip] for chip in range(chips)]
        else:
            rows = [near_other.at[chip] for chip in range(chips)] + [far_other.at[block, :] for block in blocks[:chips]]
        means.append(mean_of([row[...] for row in rows], members))
        for block, row in zip(blocks, rows):
            part = row[...] - means[-1]
            anomaly[block, columns] = part
            high_ref[block, columns] = part.astype(BF16)

    def unit(x):
        return x * (1.0 / jnp.maximum(jnp.max(jnp.abs(x)), 1e-30))

    high = high_ref[...]
    along = lax.dot_general(high[:16], high, (((1,), (1,)), ((), ())), preferred_element_type=F32)
    rows = unit(dot(unit(along).astype(BF16), high))
    weight = jnp.sum(rows * rows[:1], axis=1, keepdims=True)
    weight = weight + jnp.where(jnp.max(jnp.abs(weight)) > 0.0, 0.0, 1.0)
    pattern = unit(jnp.sum(rows * weight, axis=0, keepdims=True))
    total = jnp.zeros((1, 1), F32)
    for block in blocks:
        along = jnp.sum(anomaly[block, :] * pattern, axis=1, keepdims=True)
        total = total + jnp.sum(along * along, axis=0, keepdims=True)
        direction_ref[block, :] = jnp.broadcast_to(along, (step, direction_ref.shape[1]))
    length = lax.rsqrt(jnp.maximum(total, 1e-30))
    taken = None
    for block in blocks:
        direction = direction_ref[block, :] * length
        direction_ref[block, :] = direction
        term = anomaly[block, :] * doubled(doubled(direction))
        taken = term if taken is None else taken + term
    taken = jnp.sum(taken, axis=0, keepdims=True)
    own_part[...] = jnp.broadcast_to(taken[:, width:], (own_part.shape[1], width)).T

    for block in blocks:
        rest = anomaly[block, :] - doubled(doubled(direction_ref[block, :])) * taken
        high, low = pieces(rest, 2)
        high_ref[block, :] = high
        low_ref[block, :] = low
        own = rest[:, width:].T
        own_high[:, block], own_low[:, block] = pieces(own, 2)
    seen_ref[pl.ds(0, 1), :] = at_cells(jnp.concatenate(means, axis=1), chosen)
    seen_ref[pl.ds(1, 1), :] = at_cells(taken, chosen)
    for first in range(0, members, PART):
        rows = pl.ds(first, PART)
        spread = (dot(high_ref[rows, :], chosen) + dot(low_ref[rows, :], chosen)) * scale
        high, low = pieces(spread, 2)
        spread_high[rows, :] = high
        spread_low[rows, :] = low


def square(parts):
    half = parts[0].shape[0] // 2
    upper = product([part[:half] for part in parts], parts)
    lower = product([part[half:] for part in parts], [part[:, half:] for part in parts])
    return upper, jnp.concatenate([upper[:, half:].T, lower], axis=1)


def region_kernel(
    info, observed_ref, near_own, far_own, high_in, low_in, own_high, own_low, own_part, seen_ref,
    direction_ref, half_ref, rest_ref, *refs,
):
    chips, step, width = far_own.shape
    out_refs = refs[:-5]
    spread_high, spread_low, factor, squared, answer = refs[-5:]
    members = 2 * chips * step
    slots = observed_ref.shape[1]
    root = math.sqrt(members - 1)
    core = info[1]
    ends = jnp.logical_or(
        jnp.logical_and(info[0] == 0, core == 0), jnp.logical_and(info[0] == chips - 1, core == 1)
    )
    part = jnp.where(ends, 0, 1)
    cells, slot_weight, values, scale = observations(info, observed_ref, width, root)
    chosen = one_hot(cells, 0, width)

    def rows_at(half, chip):
        return pl.ds(pl.multiple_of((half * chips + chip) * step, step), step)

    blocks = [(half_ref.at[pl.ds(chip * step, step), :], rows_at(part, chip)) for chip in range(chips)]
    blocks += [(rest_ref.at[chip], rows_at(1 - part, chip)) for chip in range(chips)]
    mean = mean_of([ref[...] for ref, _ in blocks], members)
    taken = None
    for ref, block in blocks:
        term = (ref[...] - mean) * doubled(direction_ref[block, :])
        taken = term if taken is None else taken + term
    taken = jnp.sum(taken, axis=0, keepdims=True)
    seen_mean = seen_ref[pl.ds(0, 1), :] + at_cells(mean, chosen)
    common = (seen_ref[pl.ds(1, 1), :] + at_cells(taken, chosen)) * scale
    innovation = slot_weight * (values - seen_mean)
    for ref, block in blocks:
        rest = ref[...] - mean - doubled(direction_ref[block, :]) * taken
        high, low = pieces(rest, 2)
        high, low = pieces((dot(high, chosen) + dot(low, chosen)) * scale, 2)
        spread_high[block, :] = high + high_in[block, :]
        spread_low[block, :] = low + low_in[block, :]

    high, low = spread_high[...], spread_low[...]
    eye = lax.broadcasted_iota(jnp.int32, (slots, slots), 0) == lax.broadcasted_iota(
        jnp.int32, (slots, slots), 1
    )
    turned = high.T
    cross = dot(turned, low)
    factor[...] = dot(turned, high) + (cross + cross.T) + jnp.where(eye, 1.0, 0.0)
    answer[pl.ds(0, width), :] = product([own_high[...], own_low[...]], [high, low])
    answer[pl.ds(width, 8), :] = jnp.where(
        lax.broadcasted_iota(jnp.int32, (8, slots), 0) == 0, jnp.broadcast_to(common, (8, slots)), 0.0
    )
    half = slots // 2
    upper, lower = pl.ds(0, half), pl.ds(half, half)

    def after(bound):
        return bound * bound / (2.0 - bound * bound)

    def size(matrix):
        return jnp.sum(jnp.sum(matrix * matrix, axis=0, keepdims=True))

    def begin(count):
        parts = pieces(factor[...], count)
        if count > 2:
            squared[upper, :], squared[lower, :] = square(parts)
        bound = 1.0 - start
        gain = 2.0 / (2.0 - bound * bound)
        answer[...] = (gain * start) * (2.0 * answer[...] - start * product(pieces(answer[...], count), parts))
        factor[...] = (gain * start) * (2.0 * factor[...] - start * squared[...])
        return after(bound)

    def refine(bound, count):
        gain = 2.0 / (2.0 - bound * bound)
        parts = pieces(factor[...], count)
        answer[...] = gain * (2.0 * answer[...] - product(pieces(answer[...], count), parts))
        top, bottom = square(parts)
        factor[upper, :] = gain * (2.0 * factor[upper, :] - top)
        factor[lower, :] = gain * (2.0 * factor[lower, :] - bottom)
        return after(bound)

    def close(bound, rest):
        gain = 2.0 / (2.0 - bound * bound)
        answer[...] = gain * (answer[...] + dot(answer[...].astype(BF16), rest))
        return gain

    def finish(bound):
        rest = factor[...].astype(BF16)
        gain = close(bound, rest)
        factor[...] = gain * (dot(rest, rest) - jnp.where(eye, 0.5 * bound * bound, 0.0))
        return after(bound)

    top, bottom = square(pieces(factor[...], 2))
    squared[upper, :] = top
    squared[lower, :] = bottom
    limit = 1.0001 * jnp.sqrt(jnp.sqrt(size(top) + size(bottom)))
    start = 2.0 / (1.0 + limit)
    large = limit > LARGE
    bound = lax.cond(large, lambda: begin(3), lambda: begin(2))
    bound = lax.while_loop(lambda b: jnp.logical_and(b > COARSE, large), lambda b: refine(b, 3), bound)
    bound = lax.while_loop(lambda b: b > COARSE, lambda b: refine(b, 2), bound)
    factor[...] = jnp.where(eye, 1.0, 0.0) - factor[...]
    bound = lax.while_loop(lambda b: b > DONE, finish, bound)
    close(bound, factor[...].astype(BF16))

    solved = answer[pl.ds(0, width), :]
    alone = answer[pl.ds(width, 1), :]
    share = own_part[:, :1] - jnp.sum(solved * common, axis=1, keepdims=True)
    solved = solved + (share / (1.0 + jnp.sum(common * alone, axis=1, keepdims=True))) * alone
    solved = solved.T
    which = lax.broadcasted_iota(jnp.int32, (8, slots), 0)
    sides = jnp.where(which == 0, innovation * (1.0 / root), jnp.where(which == 1, -0.5 * common, 0.0))
    parts = pieces(solved, 2)
    sides = product(pieces(sides, 2), parts)
    shift, along = sides[0:1], sides[1:2]
    halved = [part * jnp.asarray(-0.5, BF16) for part in parts]
    for x, out_ref in enumerate(out_refs):
        chip, part = info[0] ^ (x // 2), x % 2
        rows = pl.ds(pl.multiple_of((part * chips + chip) * step, step), step)
        moved = product([spread_high[rows, :], spread_low[rows, :]], halved)
        moved = moved + doubled(direction_ref[rows, :]) * along
        own = far_own[chip] if part else near_own[rows_at(0, chip), :]
        out_ref[...] = own + shift + moved


VMEM = pl.BlockSpec(memory_space=pltpu.VMEM)


def position():
    lane, patch = lax.axis_index("member"), lax.axis_index("patch")
    return lax.div(lane, 2), lax.rem(lane, 2), lax.rem(patch, 2), lax.axis_size("member") // 2


def call(kernel, name, out_shape, args, scratch=(), flops=None, limit=8, out=VMEM):
    several = isinstance(out_shape, (list, tuple))
    return pl.pallas_call(
        lambda *refs: kernel(position(), *refs),
        out_shape=out_shape,
        in_specs=[VMEM] * len(args),
        out_specs=[out] * len(out_shape) if several else out,
        scratch_shapes=scratch,
        compiler_params=pltpu.CompilerParams(vmem_limit_bytes=limit * 1024 * 1024),
        cost_estimate=flops and pl.CostEstimate(flops=flops, bytes_accessed=0, transcendentals=0),
        name=name,
    )(*args)


def bfloat(*shape):
    return jax.ShapeDtypeStruct(shape, BF16)


def array(*shape):
    return jax.ShapeDtypeStruct(shape, F32)


def per_device(
    init_field, flow_fields, emission, observed_cell, observed_count, observed_value, observed_scale
):
    step, rows, width = init_field.shape
    slots = observed_cell.shape[1]
    patches, lanes = lax.axis_size("patch"), lax.axis_size("member")
    chips = lanes // 2
    members = lanes * step
    axes = ("patch", "member")
    count = patches * lanes

    edge = array(STEPS * step + 8, width)
    to_last, to_first = call(pack_kernel, "pack", [edge, edge], [init_field, flow_fields], limit=32)

    def swap(message, start):
        lower = range(start, patches - 1, 2)
        return lax.ppermute(message, "patch", [(p, p + 1) for p in lower] + [(p + 1, p) for p in lower])

    halo_last, halo_first = swap(to_last, 0), swap(to_first, 1)

    mine = jnp.concatenate(
        [
            observed_cell.astype(F32),
            observed_value,
            observed_scale,
            jnp.broadcast_to(observed_count.astype(F32)[:, None], observed_cell.shape),
        ]
        * 2,
        axis=0,
    )

    def between(message, hops):
        return lax.ppermute(message, "member", [(2 * a + core, 2 * b + core) for a, b in hops for core in range(2)])

    mirrored = [
        [hop for to in range(1, chips // 2) for hop in (((to + s) % chips, to), (chips - 1 - (to + s) % chips, chips - 1 - to))]
        for s in range(chips)
    ]
    turning = [[((to - s) % chips, to) for to in range(1, chips - 1)] for s in range(chips)]
    single = all(len({source for source, _ in hops}) == len(hops) for hops in mirrored)
    targets = mirrored if single else turning
    pair = array(2, step, width)
    kept, emitted, *inner = call(
        functools.partial(inner_kernel, targets), "inner",
        [array(4, step, width), array(step, width // 2)] + [pair] * chips,
        [init_field, flow_fields, emission[None, :]],
        [pltpu.VMEM((rows, step, width), F32), pltpu.VMEM((rows, 8, width), F32)], limit=32,
    )
    got_inner = [inner[0]] + [between(inner[s], targets[s]) for s in range(1, chips)]
    outer = call(
        edge_kernel, "edge", [pair] * chips, [init_field, flow_fields, emitted, kept, halo_last, halo_first],
        [pltpu.VMEM((2, step, width), F32)], limit=32,
    )
    got_outer = [outer[0]] + [
        between(outer[s], [(s, 0), (chips - 1 - s, chips - 1)]) for s in range(1, chips)
    ]
    order = [(targets[s], s) for s in range(chips)]
    pieces_in = got_inner + got_outer
    mine, _ = lax.optimization_barrier((mine, outer[0]))
    other = lax.ppermute(
        mine, axes,
        [(p * lanes + i, p * lanes + lanes - 1 - i) for p in range(1, patches, 2) for i in range(lanes)],
    )

    def device(p, chip, core):
        return p * lanes + 2 * chip + core

    borders, siblings = [], []
    for p in range(patches):
        for chip in range(chips):
            for core, away in ((0, -1), (1, 1)):
                siblings.append((device(p, chip, core), device(p, chip, 1 - core)))
                if 0 <= chip + away < chips:
                    borders.append((device(p, chip, core), device(p, chip + away, 1 - core)))
                else:
                    to = p + 1 if (p % 2 == 0) == (away == 1) else p - 1
                    if 0 <= to < patches:
                        borders.append((device(p, chip, core), device(to, chip, core)))

    half = array(chips, step, width)
    near_other, near_own, observed = call(
        functools.partial(collect_kernel, order), "collect",
        [half, array(chips * step + PADDING, width), array(8, slots)], [mine, other] + pieces_in,
    )
    far_own = lax.ppermute(near_other, axes, siblings)
    got_half = lax.ppermute(near_own, axes, borders)
    far_other = lax.ppermute(near_own, axes, siblings)
    got_rest = lax.ppermute(far_own, axes, borders)

    split = [pltpu.VMEM((members, slots), BF16)] * 2
    prepared = call(
        prepare_kernel, "prepare",
        [bfloat(members, slots)] * 2 + [bfloat(width, members)] * 2
        + [array(width, width // 2), array(8, slots), array(members, width // 2)],
        [observed, near_other, near_own, far_other, far_own],
        [pltpu.VMEM((members, 2 * width), F32)] + [pltpu.VMEM((members, 2 * width), BF16)] * 2,
        flops=8 * members * slots * width, limit=20,
    )
    analysed = call(
        region_kernel, "region", [array(step, width)] * lanes,
        [observed, near_own, far_own, *prepared, got_half, got_rest],
        split + [pltpu.VMEM((slots, slots), F32)] * 2 + [pltpu.VMEM((width + 8, slots), F32)],
        limit=24,
    )
    def swapped(x):
        return lax.ppermute(analysed[x], "member", [(i, i ^ x) for i in range(lanes)]) if x else analysed[0]

    order = sorted(range(lanes), key=lambda x: (x.bit_length() != lanes.bit_length() - 1, -x))
    return call(
        functools.partial(unpack_kernel, order), "unpack", array(step, rows, width),
        [swapped(x) for x in order], [pltpu.VMEM((step, rows, width), F32), pltpu.SemaphoreType.DMA((4,))],
        limit=48, out=pl.BlockSpec(memory_space=pltpu.HBM),
    )


def solution(mesh):
    return jax.shard_map(
        per_device,
        mesh=mesh,
        in_specs=(
            P("member", "patch", None),
            P(None, "patch", None),
            P("member"),
            P(("patch", "member"), None),
            P(("patch", "member")),
            P(("patch", "member"), None),
            P(("patch", "member"), None),
        ),
        out_specs=P("member", "patch", None),
        check_vma=False,
    )
```

```python
import functools
import math

import jax
import jax.numpy as jnp
from jax import lax
from jax.experimental import pallas as pl
from jax.experimental.pallas import tpu as pltpu
from jax.sharding import PartitionSpec as P

STEPS = 2
COARSE = 0.35
DONE = 0.02
LARGE = 2e4
PART = 256
PADDING = 8
F32 = jnp.float32
BF16 = jnp.bfloat16


def pack_kernel(info, field_ref, flow_ref, first_ref, second_ref):
    members, rows, width = field_ref.shape
    even = info[2] == 0
    for place in range(STEPS):
        tail, head = field_ref[:, rows - STEPS + place, :], field_ref[:, place, :]
        at = pl.ds(place * members, members)
        first_ref[at, :] = jnp.where(even, tail, head)
        second_ref[at, :] = jnp.where(even, head, tail)
    tail, head = flow_ref[:, rows - 1, :], flow_ref[:, 0, :]
    at = pl.ds(STEPS * members, 8)
    first_ref[at, :] = jnp.concatenate([jnp.where(even, tail, head)] * 2, axis=0)
    second_ref[at, :] = jnp.concatenate([jnp.where(even, head, tail)] * 2, axis=0)


def doubled(x):
    return jnp.concatenate([x, x], axis=1)


def weights_of(flow):
    row_flow, col_flow, kept, source = flow[0:1], flow[1:2], 1.0 - flow[2:3], flow[3:4]
    behind, ahead = jnp.maximum(row_flow, 0.0), -jnp.minimum(row_flow, 0.0)
    left, right = jnp.maximum(col_flow, 0.0), -jnp.minimum(col_flow, 0.0)
    stays = 1.0 - behind - ahead - left - right
    return [kept * stays, kept * behind, kept * ahead, kept * left, kept * right, source]


def advance(weights, emission, behind, field, ahead):
    width = field.shape[1]
    return (
        weights[0] * field
        + weights[1] * behind
        + weights[2] * ahead
        + weights[3] * pltpu.roll(field, 1, 1)
        + weights[4] * pltpu.roll(field, width - 1, 1)
        + emission * weights[5]
    )


def inner_kernel(targets, info, field_ref, flow_ref, member_ref, kept_ref, emission_ref, *refs):
    out_refs, (wide_ref, weight_ref) = refs[:-2], refs[-2:]
    members, rows, _ = field_ref.shape
    diagonal = lax.broadcasted_iota(jnp.int32, (members, members), 0) == lax.broadcasted_iota(
        jnp.int32, (members, members), 1
    )
    column = jnp.sum(jnp.where(diagonal, member_ref[...], 0.0), axis=1, keepdims=True)
    emission_ref[...] = jnp.broadcast_to(column, emission_ref.shape)
    emission = doubled(emission_ref[...])
    for row in range(1, rows - 1):
        weights = weights_of(flow_ref[:, row, :])
        for i, weight in enumerate(weights):
            weight_ref[row, pl.ds(i, 1), :] = weight
        wide_ref[row] = advance(
            weights, emission, field_ref[:, row - 1, :], field_ref[:, row, :], field_ref[:, row + 1, :]
        )
    for place, row in enumerate((1, 2, rows - 3, rows - 2)):
        kept_ref[place] = wide_ref[row]
    for out_ref, hops in zip(out_refs, targets):
        chip = sum(jnp.where(info[0] == source, to, 0) for source, to in hops)

        @pl.when(chip > 0)
        def _():
            for place in range(2):
                position = 2 * chip + jnp.abs(info[1] - 1 + place)
                row = position + info[2] * (rows - 1 - 2 * position)
                weights = weight_ref[row]
                out_ref[place] = advance(
                    [weights[i : i + 1] for i in range(6)],
                    emission, wide_ref[row - 1], wide_ref[row], wide_ref[row + 1],
                )


def end_rows(info, last, field_ref, flow_ref, emission_ref, kept_ref, halo_ref, out_ref):
    members, rows, width = field_ref.shape
    emission = doubled(emission_ref[...])

    def halo_row(place):
        return halo_ref[pl.ds(place * members, members), :]

    halo_weights = weights_of(halo_ref[pl.ds(STEPS * members, 4), :])
    for parity in range(2):

        @pl.when(info[2] == parity)
        def _():
            if parity == last:
                end, near, outside, beyond = 0, 1, halo_row(1), halo_row(0)
                inside, further = kept_ref[0], kept_ref[1]
            else:
                end, near, outside, beyond = rows - 1, rows - 2, halo_row(0), halo_row(1)
                inside, further = kept_ref[3], kept_ref[2]

            def ordered(weights, outer, own, inner):
                behind, ahead = (outer, inner) if end == 0 else (inner, outer)
                return advance(weights, emission, behind, own, ahead)

            end_weights = weights_of(flow_ref[:, end, :])
            end_field = field_ref[:, end, :]
            outer = ordered(halo_weights, beyond, outside, end_field)
            own = ordered(end_weights, outside, end_field, field_ref[:, near, :])
            out_ref[last] = ordered(end_weights, outer, own, inside)
            out_ref[1 - last] = ordered(weights_of(flow_ref[:, near, :]), own, inside, further)


def edge_kernel(info, field_ref, flow_ref, emission_ref, kept_ref, last_ref, first_ref, *refs):
    out_refs, scratch = refs[:-1], refs[-1]
    chips = len(out_refs)
    core = info[1]
    for last, halo_ref in enumerate((first_ref, last_ref)):
        end_rows(info, last, field_ref, flow_ref, emission_ref, kept_ref, halo_ref, scratch)
        for s, out_ref in enumerate(out_refs):

            @pl.when(info[0] == (chips - 1 - s if last else s))
            def _():
                out_ref[0] = scratch[1 - core]
                out_ref[1] = scratch[core]


def source_of(chip, chips, hops, k):
    inner = sum(jnp.where(chip == to, source, 0) for source, to in hops)
    return jnp.where(chip == 0, k, jnp.where(chip == chips - 1, chips - 1 - k, inner))


def collect_kernel(order, info, mine_ref, other_ref, *refs):
    chips = len(order)
    near_other, near_own, observed_ref = refs[-3:]
    step = near_other.shape[1]
    observed_ref[...] = jnp.where(info[2] == 1, other_ref[...], mine_ref[...])
    near_own[pl.ds(chips * step, PADDING), :] = jnp.zeros((PADDING, near_own.shape[1]), F32)
    chip = info[0]
    at_edge = jnp.logical_or(chip == 0, chip == chips - 1)
    for index, (s, k) in enumerate(order):
        block = source_of(chip, chips, s, k)
        rows = pl.ds(pl.multiple_of(block * step, step), step)
        for ref, here in ((refs[index], jnp.logical_not(at_edge)), (refs[chips + index], at_edge)):

            @pl.when(here)
            def _():
                near_other[block] = ref[0]
                near_own[rows, :] = ref[1]


def unpack_kernel(order, info, *refs):
    row_refs, (out_hbm, out_ref, sems) = refs[:-3], refs[-3:]
    members, rows, _ = out_ref.shape
    part = members // 4
    moves = []
    for index in range(4):
        some = pl.ds(index * part, part)
        for x, ref in zip(order, row_refs):
            position = (2 * info[0] + info[1]) ^ x
            row = position + info[2] * (rows - 1 - 2 * position)
            out_ref[some, pl.ds(row, 1), :] = ref[some, :][:, None, :]
        moves.append(pltpu.make_async_copy(out_ref.at[some], out_hbm.at[some], sems.at[index]))
        moves[-1].start()
    for move in moves:
        move.wait()


def pieces(x, count):
    parts = []
    for _ in range(count - 1):
        part = x.astype(BF16)
        parts.append(part)
        x = x - part.astype(F32)
    return parts + [x.astype(BF16)]


def dot(a, b):
    return lax.dot_general(a, b, (((1,), (0,)), ((), ())), preferred_element_type=F32)


def dot_t(a, b):
    return lax.dot_general(a, b, (((0,), (0,)), ((), ())), preferred_element_type=F32)


def product(a, b):
    total = None
    for i, left in enumerate(a):
        for j, right in enumerate(b):
            if i + j < max(len(a), len(b)):
                term = dot(left, right)
                total = term if total is None else total + term
    return total


def observations(info, observed_ref, width, root):
    slots = observed_ref.shape[1]
    cells, values, scales, count = (observed_ref[pl.ds(i, 1), :] for i in range(4))
    cells = cells.astype(jnp.int32)
    offset = sum((cells >= i * width).astype(jnp.int32) for i in (1, 2)) - 1
    column = cells - (offset + 1) * width
    side = offset * jnp.where(info[2] == 1, -1, 1) * (1 - 2 * info[1])
    cells = column + width * jnp.where(side == 0, 2, jnp.where(side < 0, 0, 1))
    active = lax.broadcasted_iota(jnp.int32, (1, slots), 1) < count.astype(jnp.int32)
    slot_weight = jnp.where(active, scales, 0.0)
    return cells, slot_weight, values, slot_weight * (1.0 / root)


def one_hot(cells, first, count):
    return (
        lax.broadcasted_iota(jnp.int32, (count, cells.shape[1]), 0) + first == cells
    ).astype(F32).astype(BF16)


def mean_of(blocks, members):
    total = blocks[0]
    for block in blocks[1:]:
        total = total + block
    return jnp.sum(total, axis=0, keepdims=True) * (1.0 / members)


def at_cells(row, chosen):
    parts = pieces(jnp.broadcast_to(row, (8, row.shape[1])), 3)
    return (dot(parts[0], chosen) + (dot(parts[1], chosen) + dot(parts[2], chosen)))[:1]


def prepare_kernel(
    info, observed_ref, near_other, near_own, far_other, far_own,
    spread_high, spread_low, own_high, own_low, own_part, seen_ref, direction_ref,
    anomaly, high_ref, low_ref,
):
    chips, step, width = near_other.shape
    members = 2 * chips * step
    cells, _, _, scale = observations(info, observed_ref, width, math.sqrt(members - 1))
    chosen = one_hot(cells, width, 2 * width)
    blocks = [pl.ds(index * step, step) for index in range(2 * chips)]
    means = []
    for place in range(2):
        columns = pl.ds(place * width, width)
        if place:
            rows = [near_own.at[block, :] for block in blocks[:chips]] + [far_own.at[chip] for chip in range(chips)]
        else:
            rows = [near_other.at[chip] for chip in range(chips)] + [far_other.at[block, :] for block in blocks[:chips]]
        means.append(mean_of([row[...] for row in rows], members))
        for block, row in zip(blocks, rows):
            part = row[...] - means[-1]
            anomaly[block, columns] = part
            high_ref[block, columns] = part.astype(BF16)

    def unit(x):
        return x * (1.0 / jnp.maximum(jnp.max(jnp.abs(x)), 1e-30))

    high = high_ref[...]
    along = lax.dot_general(high[:16], high, (((1,), (1,)), ((), ())), preferred_element_type=F32)
    rows = unit(dot(unit(along).astype(BF16), high))
    weight = jnp.sum(rows * rows[:1], axis=1, keepdims=True)
    weight = weight + jnp.where(jnp.max(jnp.abs(weight)) > 0.0, 0.0, 1.0)
    pattern = unit(jnp.sum(rows * weight, axis=0, keepdims=True))
    total = jnp.zeros((1, 1), F32)
    for block in blocks:
        along = jnp.sum(anomaly[block, :] * pattern, axis=1, keepdims=True)
        total = total + jnp.sum(along * along, axis=0, keepdims=True)
        direction_ref[block, :] = jnp.broadcast_to(along, (step, direction_ref.shape[1]))
    length = lax.rsqrt(jnp.maximum(total, 1e-30))
    taken = None
    for block in blocks:
        direction = direction_ref[block, :] * length
        direction_ref[block, :] = direction
        term = anomaly[block, :] * doubled(doubled(direction))
        taken = term if taken is None else taken + term
    taken = jnp.sum(taken, axis=0, keepdims=True)
    own_part[...] = jnp.broadcast_to(taken[:, width:], (own_part.shape[1], width)).T

    for block in blocks:
        rest = anomaly[block, :] - doubled(doubled(direction_ref[block, :])) * taken
        high, low = pieces(rest, 2)
        high_ref[block, :] = high
        low_ref[block, :] = low
        own = rest[:, width:].T
        own_high[:, block], own_low[:, block] = pieces(own, 2)
    seen_ref[pl.ds(0, 1), :] = at_cells(jnp.concatenate(means, axis=1), chosen)
    seen_ref[pl.ds(1, 1), :] = at_cells(taken, chosen)
    for first in range(0, members, PART):
        rows = pl.ds(first, PART)
        spread = (dot(high_ref[rows, :], chosen) + dot(low_ref[rows, :], chosen)) * scale
        high, low = pieces(spread, 2)
        spread_high[rows, :] = high
        spread_low[rows, :] = low


def square(parts):
    half = parts[0].shape[0] // 2
    upper = product([part[:half] for part in parts], parts)
    lower = product([part[half:] for part in parts], [part[:, half:] for part in parts])
    return upper, jnp.concatenate([upper[:, half:].T, lower], axis=1)


def at_border(info):
    chip, core, _, chips = info
    ends = jnp.logical_or(jnp.logical_and(chip == 0, core == 0), jnp.logical_and(chip == chips - 1, core == 1))
    return jnp.where(ends, 0, 1)


def shifted_spread(rows, blocks, direction_ref, shift, along, chosen, scale, high_in, low_in, high_out, low_out):
    total, taken = None, None
    step = rows[0].shape[0]
    for index, (row, block) in enumerate(zip(rows, blocks)):
        here = pl.ds(index * step, step)
        direction = doubled(direction_ref[block, :])
        rest = row[...] - shift - direction * along
        total = rest if total is None else total + rest
        taken = direction * rest if taken is None else taken + direction * rest
        high, low = pieces(rest, 2)
        high, low = pieces((dot(high, chosen) + dot(low, chosen)) * scale, 2)
        high_out[here, :] = high + high_in[block, :]
        low_out[here, :] = low + low_in[block, :]
    return jnp.sum(total, axis=0, keepdims=True), jnp.sum(taken, axis=0, keepdims=True)


def gram(high, low):
    turned = high.T
    cross = dot(turned, low)
    return dot(turned, high) + (cross + cross.T)


def middle_kernel(
    info, observed_ref, high_in, low_in, own_high, own_low, direction_ref, half_ref,
    high_ref, low_ref, gram_ref, right_ref, known_ref,
):
    chips = info[3]
    count, slots = high_ref.shape
    step = count // chips
    width = half_ref.shape[1]
    first = at_border(info) * count
    cells, _, _, scale = observations(info, observed_ref, width, math.sqrt(2 * count - 1))
    chosen = one_hot(cells, 0, width)
    rows = [half_ref.at[pl.ds(chip * step, step), :] for chip in range(chips)]
    blocks = [pl.ds(pl.multiple_of(first + chip * step, step), step) for chip in range(chips)]
    mean = mean_of([row[...] for row in rows], count)
    along, weight = None, None
    for row, block in zip(rows, blocks):
        direction = direction_ref[block, :]
        term = (row[...] - mean) * doubled(direction)
        along = term if along is None else along + term
        weight = direction * direction if weight is None else weight + direction * direction
    weight = doubled(jnp.sum(weight, axis=0, keepdims=True))
    along = jnp.sum(along, axis=0, keepdims=True) / jnp.maximum(weight, 0.1)
    total, taken = shifted_spread(
        rows, blocks, direction_ref, mean, along, chosen, scale, high_in, low_in, high_ref, low_ref
    )
    for index, known in enumerate((mean, along, total, taken)):
        known_ref[pl.ds(index, 1), :] = known
    high, low = high_ref[...], low_ref[...]
    gram_ref[...] = gram(high, low)
    members = pl.ds(pl.multiple_of(first, count), count)
    right_ref[...] = product([own_high[:, members], own_low[:, members]], [high, low])


def region_kernel(
    info, observed_ref, near_own, far_own, high_in, low_in, own_high, own_low, own_part, seen_ref,
    direction_ref, high_half, low_half, gram_half, right_half, known_ref, rest_ref, *refs,
):
    chips, step, width = far_own.shape
    out_refs = refs[:-5]
    high_rest, low_rest, factor, squared, answer = refs[-5:]
    count = chips * step
    members = 2 * count
    slots = observed_ref.shape[1]
    root = math.sqrt(members - 1)
    part = at_border(info)
    first = (1 - part) * count
    cells, slot_weight, values, scale = observations(info, observed_ref, width, root)
    chosen = one_hot(cells, 0, width)
    shift, along, total, taken = (known_ref[pl.ds(index, 1), :] for index in range(4))
    more, further = shifted_spread(
        [rest_ref.at[chip] for chip in range(chips)],
        [pl.ds(pl.multiple_of(first + chip * step, step), step) for chip in range(chips)],
        direction_ref, shift, along, chosen, scale, high_in, low_in, high_rest, low_rest,
    )
    left = (total + more) * (1.0 / members)
    taken = taken + further
    seen_mean = seen_ref[pl.ds(0, 1), :] + at_cells(shift + left, chosen)
    left, taken_here = at_cells(left, chosen) * scale, at_cells(taken, chosen) * scale
    common = (seen_ref[pl.ds(1, 1), :] + at_cells(along + taken, chosen)) * scale
    innovation = slot_weight * (values - seen_mean)
    place = lax.broadcasted_iota(jnp.int32, (8, slots), 0)
    excess = jnp.where(place == 0, left * math.sqrt(members), jnp.where(place == 1, taken_here, 0.0))
    excess = pieces(excess, 2)

    eye = lax.broadcasted_iota(jnp.int32, (slots, slots), 0) == lax.broadcasted_iota(
        jnp.int32, (slots, slots), 1
    )
    high, low = high_rest[...], low_rest[...]
    over = dot_t(excess[0], excess[0]) + (dot_t(excess[0], excess[1]) + dot_t(excess[1], excess[0]))
    factor[...] = gram(high, low) + (gram_half[...] - over) + jnp.where(eye, 1.0, 0.0)
    rows = pl.ds(pl.multiple_of(first, count), count)
    answer[pl.ds(0, width), :] = right_half[...] + product([own_high[:, rows], own_low[:, rows]], [high, low])
    answer[pl.ds(width, 8), :] = jnp.where(
        lax.broadcasted_iota(jnp.int32, (8, slots), 0) == 0, jnp.broadcast_to(common, (8, slots)), 0.0
    )
    half = slots // 2
    upper, lower = pl.ds(0, half), pl.ds(half, half)

    def after(bound):
        return bound * bound / (2.0 - bound * bound)

    def size(matrix):
        return jnp.sum(jnp.sum(matrix * matrix, axis=0, keepdims=True))

    def begin(count):
        parts = pieces(factor[...], count)
        if count > 2:
            squared[upper, :], squared[lower, :] = square(parts)
        bound = 1.0 - start
        gain = 2.0 / (2.0 - bound * bound)
        answer[...] = (gain * start) * (2.0 * answer[...] - start * product(pieces(answer[...], count), parts))
        factor[...] = (gain * start) * (2.0 * factor[...] - start * squared[...])
        return after(bound)

    def refine(bound, count):
        gain = 2.0 / (2.0 - bound * bound)
        parts = pieces(factor[...], count)
        answer[...] = gain * (2.0 * answer[...] - product(pieces(answer[...], count), parts))
        top, bottom = square(parts)
        factor[upper, :] = gain * (2.0 * factor[upper, :] - top)
        factor[lower, :] = gain * (2.0 * factor[lower, :] - bottom)
        return after(bound)

    def close(bound, rest):
        gain = 2.0 / (2.0 - bound * bound)
        answer[...] = gain * (answer[...] + dot(answer[...].astype(BF16), rest))
        return gain

    def finish(bound):
        rest = factor[...].astype(BF16)
        gain = close(bound, rest)
        factor[...] = gain * (dot(rest, rest) - jnp.where(eye, 0.5 * bound * bound, 0.0))
        return after(bound)

    top, bottom = square(pieces(factor[...], 2))
    squared[upper, :] = top
    squared[lower, :] = bottom
    limit = 1.0001 * jnp.sqrt(jnp.sqrt(size(top) + size(bottom)))
    start = 2.0 / (1.0 + limit)
    large = limit > LARGE
    bound = lax.cond(large, lambda: begin(3), lambda: begin(2))
    bound = lax.while_loop(lambda b: jnp.logical_and(b > COARSE, large), lambda b: refine(b, 3), bound)
    bound = lax.while_loop(lambda b: b > COARSE, lambda b: refine(b, 2), bound)
    factor[...] = jnp.where(eye, 1.0, 0.0) - factor[...]
    bound = lax.while_loop(lambda b: b > DONE, finish, bound)
    close(bound, factor[...].astype(BF16))

    solved = answer[pl.ds(0, width), :]
    alone = answer[pl.ds(width, 1), :]
    share = own_part[:, :1] - jnp.sum(solved * common, axis=1, keepdims=True)
    solved = solved + (share / (1.0 + jnp.sum(common * alone, axis=1, keepdims=True))) * alone
    solved = solved.T
    which = lax.broadcasted_iota(jnp.int32, (8, slots), 0)
    sides = jnp.where(
        which == 0, innovation * (1.0 / root) + 0.5 * left, jnp.where(which == 1, 0.5 * (taken_here - common), 0.0)
    )
    parts = pieces(solved, 2)
    sides = product(pieces(sides, 2), parts)
    shift, along = sides[0:1], sides[1:2]
    halved = [part * jnp.asarray(-0.5, BF16) for part in parts]
    for x, out_ref in enumerate(out_refs):
        chip, mine = info[0] ^ (x // 2), x % 2
        rows = pl.ds(pl.multiple_of(chip * step, step), step)
        spread = [
            jnp.where(part == mine, half[rows, :], rest[rows, :])
            for half, rest in ((high_half, high_rest), (low_half, low_rest))
        ]
        block = pl.ds(pl.multiple_of((mine * chips + chip) * step, step), step)
        moved = product(spread, halved) + doubled(direction_ref[block, :]) * along
        own = far_own[chip] if mine else near_own[rows, :]
        out_ref[...] = own + shift + moved


VMEM = pl.BlockSpec(memory_space=pltpu.VMEM)


def position():
    lane, patch = lax.axis_index("member"), lax.axis_index("patch")
    return lax.div(lane, 2), lax.rem(lane, 2), lax.rem(patch, 2), lax.axis_size("member") // 2


def call(kernel, name, out_shape, args, scratch=(), flops=None, limit=8, out=VMEM):
    several = isinstance(out_shape, (list, tuple))
    return pl.pallas_call(
        lambda *refs: kernel(position(), *refs),
        out_shape=out_shape,
        in_specs=[VMEM] * len(args),
        out_specs=[out] * len(out_shape) if several else out,
        scratch_shapes=scratch,
        compiler_params=pltpu.CompilerParams(vmem_limit_bytes=limit * 1024 * 1024),
        cost_estimate=flops and pl.CostEstimate(flops=flops, bytes_accessed=0, transcendentals=0),
        name=name,
    )(*args)


def bfloat(*shape):
    return jax.ShapeDtypeStruct(shape, BF16)


def array(*shape):
    return jax.ShapeDtypeStruct(shape, F32)


def per_device(
    init_field, flow_fields, emission, observed_cell, observed_count, observed_value, observed_scale
):
    step, rows, width = init_field.shape
    slots = observed_cell.shape[1]
    patches, lanes = lax.axis_size("patch"), lax.axis_size("member")
    chips = lanes // 2
    members = lanes * step
    axes = ("patch", "member")
    count = patches * lanes

    edge = array(STEPS * step + 8, width)
    to_last, to_first = call(pack_kernel, "pack", [edge, edge], [init_field, flow_fields], limit=32)

    def swap(message, start):
        lower = range(start, patches - 1, 2)
        return lax.ppermute(message, "patch", [(p, p + 1) for p in lower] + [(p + 1, p) for p in lower])

    halo_last, halo_first = swap(to_last, 0), swap(to_first, 1)

    mine = jnp.concatenate(
        [
            observed_cell.astype(F32),
            observed_value,
            observed_scale,
            jnp.broadcast_to(observed_count.astype(F32)[:, None], observed_cell.shape),
        ]
        * 2,
        axis=0,
    )

    def between(message, hops):
        return lax.ppermute(message, "member", [(2 * a + core, 2 * b + core) for a, b in hops for core in range(2)])

    mirrored = [
        [hop for to in range(1, chips // 2) for hop in (((to + s) % chips, to), (chips - 1 - (to + s) % chips, chips - 1 - to))]
        for s in range(chips)
    ]
    turning = [[((to - s) % chips, to) for to in range(1, chips - 1)] for s in range(chips)]
    single = all(len({source for source, _ in hops}) == len(hops) for hops in mirrored)
    targets = mirrored if single else turning
    pair = array(2, step, width)
    kept, emitted, *inner = call(
        functools.partial(inner_kernel, targets), "inner",
        [array(4, step, width), array(step, width // 2)] + [pair] * chips,
        [init_field, flow_fields, emission[None, :]],
        [pltpu.VMEM((rows, step, width), F32), pltpu.VMEM((rows, 8, width), F32)], limit=32,
    )
    got_inner = [inner[0]] + [between(inner[s], targets[s]) for s in range(1, chips)]
    outer = call(
        edge_kernel, "edge", [pair] * chips, [init_field, flow_fields, emitted, kept, halo_last, halo_first],
        [pltpu.VMEM((2, step, width), F32)], limit=32,
    )
    got_outer = [outer[0]] + [
        between(outer[s], [(s, 0), (chips - 1 - s, chips - 1)]) for s in range(1, chips)
    ]
    order = [(targets[s], s) for s in range(chips)]
    pieces_in = got_inner + got_outer
    mine, _ = lax.optimization_barrier((mine, outer[0]))
    other = lax.ppermute(
        mine, axes,
        [(p * lanes + i, p * lanes + lanes - 1 - i) for p in range(1, patches, 2) for i in range(lanes)],
    )

    def device(p, chip, core):
        return p * lanes + 2 * chip + core

    borders, siblings = [], []
    for p in range(patches):
        for chip in range(chips):
            for core, away in ((0, -1), (1, 1)):
                siblings.append((device(p, chip, core), device(p, chip, 1 - core)))
                if 0 <= chip + away < chips:
                    borders.append((device(p, chip, core), device(p, chip + away, 1 - core)))
                else:
                    to = p + 1 if (p % 2 == 0) == (away == 1) else p - 1
                    if 0 <= to < patches:
                        borders.append((device(p, chip, core), device(to, chip, core)))

    half = array(chips, step, width)
    near_other, near_own, observed = call(
        functools.partial(collect_kernel, order), "collect",
        [half, array(chips * step + PADDING, width), array(8, slots)], [mine, other] + pieces_in,
    )
    far_own = lax.ppermute(near_other, axes, siblings)
    got_half = lax.ppermute(near_own, axes, borders)
    far_other = lax.ppermute(near_own, axes, siblings)
    got_rest = lax.ppermute(far_own, axes, borders)

    split = [pltpu.VMEM((members // 2, slots), BF16)] * 2
    prepared = call(
        prepare_kernel, "prepare",
        [bfloat(members, slots)] * 2 + [bfloat(width, members)] * 2
        + [array(width, width // 2), array(8, slots), array(members, width // 2)],
        [observed, near_other, near_own, far_other, far_own],
        [pltpu.VMEM((members, 2 * width), F32)] + [pltpu.VMEM((members, 2 * width), BF16)] * 2,
        flops=8 * members * slots * width, limit=20,
    )
    halves = members // 2
    middle = call(
        middle_kernel, "middle",
        [bfloat(halves, slots)] * 2 + [array(slots, slots), array(width, slots), array(8, width)],
        [observed, *prepared[:4], prepared[6], got_half],
        flops=10 * halves * slots * slots, limit=20,
    )
    analysed = call(
        region_kernel, "region", [array(step, width)] * lanes,
        [observed, near_own, far_own, *prepared, *middle, got_rest],
        split + [pltpu.VMEM((slots, slots), F32)] * 2 + [pltpu.VMEM((width + 8, slots), F32)],
        limit=24,
    )

    def swapped(x):
        return lax.ppermute(analysed[x], "member", [(i, i ^ x) for i in range(lanes)]) if x else analysed[0]

    order = sorted(range(lanes), key=lambda x: (x.bit_length() != lanes.bit_length() - 1, -x))
    return call(
        functools.partial(unpack_kernel, order), "unpack", array(step, rows, width),
        [swapped(x) for x in order], [pltpu.VMEM((step, rows, width), F32), pltpu.SemaphoreType.DMA((4,))],
        limit=48, out=pl.BlockSpec(memory_space=pltpu.HBM),
    )


def solution(mesh):
    return jax.shard_map(
        per_device,
        mesh=mesh,
        in_specs=(
            P("member", "patch", None),
            P(None, "patch", None),
            P("member"),
            P(("patch", "member"), None),
            P(("patch", "member")),
            P(("patch", "member"), None),
            P(("patch", "member"), None),
        ),
        out_specs=P("member", "patch", None),
        check_vma=False,
    )
```

```python
import functools
import math

import jax
import jax.numpy as jnp
from jax import lax
from jax.experimental import pallas as pl
from jax.experimental.pallas import tpu as pltpu
from jax.sharding import PartitionSpec as P

STEPS = 2
COARSE = 0.35
DONE = 0.02
LARGE = 2e4
PART = 256
PADDING = 8
F32 = jnp.float32
BF16 = jnp.bfloat16


def pack_kernel(info, field_ref, flow_ref, first_ref, second_ref):
    members, rows, width = field_ref.shape
    even = info[2] == 0
    for place in range(STEPS):
        tail, head = field_ref[:, rows - STEPS + place, :], field_ref[:, place, :]
        at = pl.ds(place * members, members)
        first_ref[at, :] = jnp.where(even, tail, head)
        second_ref[at, :] = jnp.where(even, head, tail)
    tail, head = flow_ref[:, rows - 1, :], flow_ref[:, 0, :]
    at = pl.ds(STEPS * members, 8)
    first_ref[at, :] = jnp.concatenate([jnp.where(even, tail, head)] * 2, axis=0)
    second_ref[at, :] = jnp.concatenate([jnp.where(even, head, tail)] * 2, axis=0)


def doubled(x):
    return jnp.concatenate([x, x], axis=1)


def weights_of(flow):
    row_flow, col_flow, kept, source = flow[0:1], flow[1:2], 1.0 - flow[2:3], flow[3:4]
    behind, ahead = jnp.maximum(row_flow, 0.0), -jnp.minimum(row_flow, 0.0)
    left, right = jnp.maximum(col_flow, 0.0), -jnp.minimum(col_flow, 0.0)
    stays = 1.0 - behind - ahead - left - right
    return [kept * stays, kept * behind, kept * ahead, kept * left, kept * right, source]


def advance(weights, emission, behind, field, ahead):
    width = field.shape[1]
    return (
        weights[0] * field
        + weights[1] * behind
        + weights[2] * ahead
        + weights[3] * pltpu.roll(field, 1, 1)
        + weights[4] * pltpu.roll(field, width - 1, 1)
        + emission * weights[5]
    )


def inner_kernel(targets, info, field_ref, flow_ref, member_ref, kept_ref, emission_ref, *refs):
    out_refs, (wide_ref, weight_ref) = refs[:-2], refs[-2:]
    members, rows, _ = field_ref.shape
    diagonal = lax.broadcasted_iota(jnp.int32, (members, members), 0) == lax.broadcasted_iota(
        jnp.int32, (members, members), 1
    )
    column = jnp.sum(jnp.where(diagonal, member_ref[...], 0.0), axis=1, keepdims=True)
    emission_ref[...] = jnp.broadcast_to(column, emission_ref.shape)
    emission = doubled(emission_ref[...])
    for row in range(1, rows - 1):
        weights = weights_of(flow_ref[:, row, :])
        for i, weight in enumerate(weights):
            weight_ref[row, pl.ds(i, 1), :] = weight
        wide_ref[row] = advance(
            weights, emission, field_ref[:, row - 1, :], field_ref[:, row, :], field_ref[:, row + 1, :]
        )
    for place, row in enumerate((1, 2, rows - 3, rows - 2)):
        kept_ref[place] = wide_ref[row]
    for out_ref, hops in zip(out_refs, targets):
        chip = sum(jnp.where(info[0] == source, to, 0) for source, to in hops)

        @pl.when(chip > 0)
        def _():
            for place in range(2):
                position = 2 * chip + jnp.abs(info[1] - 1 + place)
                row = position + info[2] * (rows - 1 - 2 * position)
                weights = weight_ref[row]
                out_ref[place] = advance(
                    [weights[i : i + 1] for i in range(6)],
                    emission, wide_ref[row - 1], wide_ref[row], wide_ref[row + 1],
                )


def end_rows(info, last, field_ref, flow_ref, emission_ref, kept_ref, halo_ref, out_ref):
    members, rows, width = field_ref.shape
    emission = doubled(emission_ref[...])

    def halo_row(place):
        return halo_ref[pl.ds(place * members, members), :]

    halo_weights = weights_of(halo_ref[pl.ds(STEPS * members, 4), :])
    for parity in range(2):

        @pl.when(info[2] == parity)
        def _():
            if parity == last:
                end, near, outside, beyond = 0, 1, halo_row(1), halo_row(0)
                inside, further = kept_ref[0], kept_ref[1]
            else:
                end, near, outside, beyond = rows - 1, rows - 2, halo_row(0), halo_row(1)
                inside, further = kept_ref[3], kept_ref[2]

            def ordered(weights, outer, own, inner):
                behind, ahead = (outer, inner) if end == 0 else (inner, outer)
                return advance(weights, emission, behind, own, ahead)

            end_weights = weights_of(flow_ref[:, end, :])
            end_field = field_ref[:, end, :]
            outer = ordered(halo_weights, beyond, outside, end_field)
            own = ordered(end_weights, outside, end_field, field_ref[:, near, :])
            out_ref[last] = ordered(end_weights, outer, own, inside)
            out_ref[1 - last] = ordered(weights_of(flow_ref[:, near, :]), own, inside, further)


def edge_kernel(info, field_ref, flow_ref, emission_ref, kept_ref, last_ref, first_ref, *refs):
    out_refs, scratch = refs[:-1], refs[-1]
    chips = len(out_refs)
    core = info[1]
    for last, halo_ref in enumerate((first_ref, last_ref)):
        end_rows(info, last, field_ref, flow_ref, emission_ref, kept_ref, halo_ref, scratch)
        for s, out_ref in enumerate(out_refs):

            @pl.when(info[0] == (chips - 1 - s if last else s))
            def _():
                out_ref[0] = scratch[1 - core]
                out_ref[1] = scratch[core]


def source_of(chip, chips, hops, k):
    inner = sum(jnp.where(chip == to, source, 0) for source, to in hops)
    return jnp.where(chip == 0, k, jnp.where(chip == chips - 1, chips - 1 - k, inner))


def collect_kernel(order, info, mine_ref, other_ref, *refs):
    chips = len(order)
    near_other, near_own, observed_ref = refs[-3:]
    step = near_other.shape[1]
    observed_ref[...] = jnp.where(info[2] == 1, other_ref[...], mine_ref[...])
    near_own[pl.ds(chips * step, PADDING), :] = jnp.zeros((PADDING, near_own.shape[1]), F32)
    chip = info[0]
    at_edge = jnp.logical_or(chip == 0, chip == chips - 1)
    for index, (s, k) in enumerate(order):
        block = source_of(chip, chips, s, k)
        rows = pl.ds(pl.multiple_of(block * step, step), step)
        for ref, here in ((refs[index], jnp.logical_not(at_edge)), (refs[chips + index], at_edge)):

            @pl.when(here)
            def _():
                near_other[block] = ref[0]
                near_own[rows, :] = ref[1]


def unpack_kernel(order, info, *refs):
    row_refs, (out_hbm, out_ref, sems) = refs[:-3], refs[-3:]
    members, rows, _ = out_ref.shape
    part = members // 4
    moves = []
    for index in range(4):
        some = pl.ds(index * part, part)
        for x, ref in zip(order, row_refs):
            position = (2 * info[0] + info[1]) ^ x
            row = position + info[2] * (rows - 1 - 2 * position)
            out_ref[some, pl.ds(row, 1), :] = ref[some, :][:, None, :]
        moves.append(pltpu.make_async_copy(out_ref.at[some], out_hbm.at[some], sems.at[index]))
        moves[-1].start()
    for move in moves:
        move.wait()


def pieces(x, count):
    parts = []
    for _ in range(count - 1):
        part = x.astype(BF16)
        parts.append(part)
        x = x - part.astype(F32)
    return parts + [x.astype(BF16)]


def dot(a, b):
    return lax.dot_general(a, b, (((1,), (0,)), ((), ())), preferred_element_type=F32)


def dot_t(a, b):
    return lax.dot_general(a, b, (((0,), (0,)), ((), ())), preferred_element_type=F32)


def product(a, b):
    total = None
    for i, left in enumerate(a):
        for j, right in enumerate(b):
            if i + j < max(len(a), len(b)):
                term = dot(left, right)
                total = term if total is None else total + term
    return total


def observations(info, observed_ref, width, root):
    slots = observed_ref.shape[1]
    cells, values, scales, count = (observed_ref[pl.ds(i, 1), :] for i in range(4))
    cells = cells.astype(jnp.int32)
    offset = sum((cells >= i * width).astype(jnp.int32) for i in (1, 2)) - 1
    column = cells - (offset + 1) * width
    side = offset * jnp.where(info[2] == 1, -1, 1) * (1 - 2 * info[1])
    cells = column + width * jnp.where(side == 0, 2, jnp.where(side < 0, 0, 1))
    active = lax.broadcasted_iota(jnp.int32, (1, slots), 1) < count.astype(jnp.int32)
    slot_weight = jnp.where(active, scales, 0.0)
    return cells, slot_weight, values, slot_weight * (1.0 / root)


def one_hot(cells, first, count):
    return (
        lax.broadcasted_iota(jnp.int32, (count, cells.shape[1]), 0) + first == cells
    ).astype(F32).astype(BF16)


def mean_of(blocks, members):
    total = blocks[0]
    for block in blocks[1:]:
        total = total + block
    return jnp.sum(total, axis=0, keepdims=True) * (1.0 / members)


def at_cells(row, chosen):
    parts = pieces(jnp.broadcast_to(row, (8, row.shape[1])), 3)
    return (dot(parts[0], chosen) + (dot(parts[1], chosen) + dot(parts[2], chosen)))[:1]


def prepare_kernel(
    info, observed_ref, near_other, near_own, far_other, far_own,
    spread_high, spread_low, own_high, own_low, own_part, seen_ref, direction_ref,
    anomaly, high_ref, low_ref,
):
    chips, step, width = near_other.shape
    members = 2 * chips * step
    cells, _, _, scale = observations(info, observed_ref, width, math.sqrt(members - 1))
    chosen = one_hot(cells, width, 2 * width)
    blocks = [pl.ds(index * step, step) for index in range(2 * chips)]
    means = []
    for place in range(2):
        columns = pl.ds(place * width, width)
        if place:
            rows = [near_own.at[block, :] for block in blocks[:chips]] + [far_own.at[chip] for chip in range(chips)]
        else:
            rows = [near_other.at[chip] for chip in range(chips)] + [far_other.at[block, :] for block in blocks[:chips]]
        means.append(mean_of([row[...] for row in rows], members))
        for block, row in zip(blocks, rows):
            part = row[...] - means[-1]
            anomaly[block, columns] = part
            high_ref[block, columns] = part.astype(BF16)

    def unit(x):
        return x * (1.0 / jnp.maximum(jnp.max(jnp.abs(x)), 1e-30))

    high = high_ref[...]
    along = lax.dot_general(high[:16], high, (((1,), (1,)), ((), ())), preferred_element_type=F32)
    rows = unit(dot(unit(along).astype(BF16), high))
    weight = jnp.sum(rows * rows[:1], axis=1, keepdims=True)
    weight = weight + jnp.where(jnp.max(jnp.abs(weight)) > 0.0, 0.0, 1.0)
    pattern = unit(jnp.sum(rows * weight, axis=0, keepdims=True))
    total = jnp.zeros((1, 1), F32)
    for block in blocks:
        along = jnp.sum(anomaly[block, :] * pattern, axis=1, keepdims=True)
        total = total + jnp.sum(along * along, axis=0, keepdims=True)
        direction_ref[block, :] = jnp.broadcast_to(along, (step, direction_ref.shape[1]))
    length = lax.rsqrt(jnp.maximum(total, 1e-30))
    taken = None
    for block in blocks:
        direction = direction_ref[block, :] * length
        direction_ref[block, :] = direction
        term = anomaly[block, :] * doubled(doubled(direction))
        taken = term if taken is None else taken + term
    taken = jnp.sum(taken, axis=0, keepdims=True)
    own_part[...] = jnp.broadcast_to(taken[:, width:], (own_part.shape[1], width)).T

    for block in blocks:
        rest = anomaly[block, :] - doubled(doubled(direction_ref[block, :])) * taken
        high, low = pieces(rest, 2)
        high_ref[block, :] = high
        low_ref[block, :] = low
        own = rest[:, width:].T
        own_high[:, block], own_low[:, block] = pieces(own, 2)
    seen_ref[pl.ds(0, 1), :] = at_cells(jnp.concatenate(means, axis=1), chosen)
    seen_ref[pl.ds(1, 1), :] = at_cells(taken, chosen)
    for first in range(0, members, PART):
        rows = pl.ds(first, PART)
        spread = (dot(high_ref[rows, :], chosen) + dot(low_ref[rows, :], chosen)) * scale
        high, low = pieces(spread, 2)
        spread_high[rows, :] = high
        spread_low[rows, :] = low


def square(parts):
    half = parts[0].shape[0] // 2
    upper = product([part[:half] for part in parts], parts)
    lower = product([part[half:] for part in parts], [part[:, half:] for part in parts])
    return upper, jnp.concatenate([upper[:, half:].T, lower], axis=1)


def at_border(info):
    chip, core, _, chips = info
    ends = jnp.logical_or(jnp.logical_and(chip == 0, core == 0), jnp.logical_and(chip == chips - 1, core == 1))
    return jnp.where(ends, 0, 1)


def shifted_spread(rows, blocks, direction_ref, shift, along, chosen, scale, high_in, low_in, high_out, low_out):
    total, taken = None, None
    step = rows[0].shape[0]
    for index, (row, block) in enumerate(zip(rows, blocks)):
        here = pl.ds(index * step, step)
        direction = doubled(direction_ref[block, :])
        rest = row[...] - shift - direction * along
        total = rest if total is None else total + rest
        taken = direction * rest if taken is None else taken + direction * rest
        high, low = pieces(rest, 2)
        high, low = pieces((dot(high, chosen) + dot(low, chosen)) * scale, 2)
        high_out[here, :] = high + high_in[block, :]
        low_out[here, :] = low + low_in[block, :]
    return jnp.sum(total, axis=0, keepdims=True), jnp.sum(taken, axis=0, keepdims=True)


def gram(high, low):
    turned = high.T
    cross = dot(turned, low)
    return dot(turned, high) + (cross + cross.T)


def middle_kernel(
    info, observed_ref, high_in, low_in, own_high, own_low, direction_ref, half_ref,
    high_ref, low_ref, gram_ref, right_ref, known_ref,
):
    chips = info[3]
    count, slots = high_ref.shape
    step = count // chips
    width = half_ref.shape[1]
    first = at_border(info) * count
    cells, _, _, scale = observations(info, observed_ref, width, math.sqrt(2 * count - 1))
    chosen = one_hot(cells, 0, width)
    rows = [half_ref.at[pl.ds(chip * step, step), :] for chip in range(chips)]
    blocks = [pl.ds(pl.multiple_of(first + chip * step, step), step) for chip in range(chips)]
    mean = mean_of([row[...] for row in rows], count)
    along, weight = None, None
    for row, block in zip(rows, blocks):
        direction = direction_ref[block, :]
        term = (row[...] - mean) * doubled(direction)
        along = term if along is None else along + term
        weight = direction * direction if weight is None else weight + direction * direction
    weight = doubled(jnp.sum(weight, axis=0, keepdims=True))
    along = jnp.sum(along, axis=0, keepdims=True) / jnp.maximum(weight, 0.1)
    total, taken = shifted_spread(
        rows, blocks, direction_ref, mean, along, chosen, scale, high_in, low_in, high_ref, low_ref
    )
    for index, known in enumerate((mean, along, total, taken)):
        known_ref[pl.ds(index, 1), :] = known
    high, low = high_ref[...], low_ref[...]
    gram_ref[...] = gram(high, low)
    members = pl.ds(pl.multiple_of(first, count), count)
    right_ref[...] = product([own_high[:, members], own_low[:, members]], [high, low])


def analysed_row(info, x, near_own, far_own, direction_ref, halves, rests, parts, sides):
    chips, step, _ = far_own.shape
    chip, mine = info[0] ^ (x // 2), x % 2
    rows = pl.ds(pl.multiple_of(chip * step, step), step)
    spread = [
        jnp.where(at_border(info) == mine, half[rows, :], rest[rows, :]) for half, rest in zip(halves, rests)
    ]
    block = pl.ds(pl.multiple_of((mine * chips + chip) * step, step), step)
    own = far_own[chip] if mine else near_own[rows, :]
    return own + sides[0:1] + product(spread, parts) + doubled(direction_ref[block, :]) * sides[1:2]


def others_kernel(
    order, info, near_own, far_own, direction_ref, high_half, low_half, high_rest, low_rest,
    solved_high, solved_low, sides_ref, *out_refs,
):
    parts = [solved_high[...], solved_low[...]]
    for x, out_ref in zip(order, out_refs):
        out_ref[...] = analysed_row(
            info, x, near_own, far_own, direction_ref, (high_half, low_half), (high_rest, low_rest), parts, sides_ref[...]
        )


def region_kernel(
    order, info, observed_ref, near_own, far_own, high_in, low_in, own_high, own_low, own_part, seen_ref,
    direction_ref, high_half, low_half, gram_half, right_half, known_ref, rest_ref, *refs,
):
    chips, step, width = far_own.shape
    high_rest, low_rest, solved_high, solved_low, sides_ref = refs[:5]
    out_refs, (factor, squared, answer) = refs[5:-3], refs[-3:]
    count = chips * step
    members = 2 * count
    slots = observed_ref.shape[1]
    root = math.sqrt(members - 1)
    part = at_border(info)
    first = (1 - part) * count
    cells, slot_weight, values, scale = observations(info, observed_ref, width, root)
    chosen = one_hot(cells, 0, width)
    shift, along, total, taken = (known_ref[pl.ds(index, 1), :] for index in range(4))
    more, further = shifted_spread(
        [rest_ref.at[chip] for chip in range(chips)],
        [pl.ds(pl.multiple_of(first + chip * step, step), step) for chip in range(chips)],
        direction_ref, shift, along, chosen, scale, high_in, low_in, high_rest, low_rest,
    )
    left = (total + more) * (1.0 / members)
    taken = taken + further
    seen_mean = seen_ref[pl.ds(0, 1), :] + at_cells(shift + left, chosen)
    left, taken_here = at_cells(left, chosen) * scale, at_cells(taken, chosen) * scale
    common = (seen_ref[pl.ds(1, 1), :] + at_cells(along + taken, chosen)) * scale
    innovation = slot_weight * (values - seen_mean)
    place = lax.broadcasted_iota(jnp.int32, (8, slots), 0)
    excess = jnp.where(place == 0, left * math.sqrt(members), jnp.where(place == 1, taken_here, 0.0))
    excess = pieces(excess, 2)

    eye = lax.broadcasted_iota(jnp.int32, (slots, slots), 0) == lax.broadcasted_iota(
        jnp.int32, (slots, slots), 1
    )
    high, low = high_rest[...], low_rest[...]
    over = dot_t(excess[0], excess[0]) + (dot_t(excess[0], excess[1]) + dot_t(excess[1], excess[0]))
    factor[...] = gram(high, low) + (gram_half[...] - over) + jnp.where(eye, 1.0, 0.0)
    rows = pl.ds(pl.multiple_of(first, count), count)
    answer[pl.ds(0, width), :] = right_half[...] + product([own_high[:, rows], own_low[:, rows]], [high, low])
    answer[pl.ds(width, 8), :] = jnp.where(
        lax.broadcasted_iota(jnp.int32, (8, slots), 0) == 0, jnp.broadcast_to(common, (8, slots)), 0.0
    )
    half = slots // 2
    upper, lower = pl.ds(0, half), pl.ds(half, half)

    def after(bound):
        return bound * bound / (2.0 - bound * bound)

    def size(matrix):
        return jnp.sum(jnp.sum(matrix * matrix, axis=0, keepdims=True))

    def begin(count):
        parts = pieces(factor[...], count)
        if count > 2:
            squared[upper, :], squared[lower, :] = square(parts)
        bound = 1.0 - start
        gain = 2.0 / (2.0 - bound * bound)
        answer[...] = (gain * start) * (2.0 * answer[...] - start * product(pieces(answer[...], count), parts))
        factor[...] = (gain * start) * (2.0 * factor[...] - start * squared[...])
        return after(bound)

    def refine(bound, count):
        gain = 2.0 / (2.0 - bound * bound)
        parts = pieces(factor[...], count)
        answer[...] = gain * (2.0 * answer[...] - product(pieces(answer[...], count), parts))
        top, bottom = square(parts)
        factor[upper, :] = gain * (2.0 * factor[upper, :] - top)
        factor[lower, :] = gain * (2.0 * factor[lower, :] - bottom)
        return after(bound)

    def close(bound, rest):
        gain = 2.0 / (2.0 - bound * bound)
        answer[...] = gain * (answer[...] + dot(answer[...].astype(BF16), rest))
        return gain

    def finish(bound):
        rest = factor[...].astype(BF16)
        gain = close(bound, rest)
        factor[...] = gain * (dot(rest, rest) - jnp.where(eye, 0.5 * bound * bound, 0.0))
        return after(bound)

    top, bottom = square(pieces(factor[...], 2))
    squared[upper, :] = top
    squared[lower, :] = bottom
    limit = 1.0001 * jnp.sqrt(jnp.sqrt(size(top) + size(bottom)))
    start = 2.0 / (1.0 + limit)
    large = limit > LARGE
    bound = lax.cond(large, lambda: begin(3), lambda: begin(2))
    bound = lax.while_loop(lambda b: jnp.logical_and(b > COARSE, large), lambda b: refine(b, 3), bound)
    bound = lax.while_loop(lambda b: b > COARSE, lambda b: refine(b, 2), bound)
    factor[...] = jnp.where(eye, 1.0, 0.0) - factor[...]
    bound = lax.while_loop(lambda b: b > DONE, finish, bound)
    close(bound, factor[...].astype(BF16))

    solved = answer[pl.ds(0, width), :]
    alone = answer[pl.ds(width, 1), :]
    share = own_part[:, :1] - jnp.sum(solved * common, axis=1, keepdims=True)
    solved = solved + (share / (1.0 + jnp.sum(common * alone, axis=1, keepdims=True))) * alone
    solved = solved.T
    which = lax.broadcasted_iota(jnp.int32, (8, slots), 0)
    sides = jnp.where(
        which == 0, innovation * (1.0 / root) + 0.5 * left, jnp.where(which == 1, 0.5 * (taken_here - common), 0.0)
    )
    parts = pieces(solved, 2)
    sides = product(pieces(sides, 2), parts)
    parts = [part * jnp.asarray(-0.5, BF16) for part in parts]
    sides_ref[...] = sides
    solved_high[...], solved_low[...] = parts
    for x, out_ref in zip(order, out_refs):
        out_ref[...] = analysed_row(
            info, x, near_own, far_own, direction_ref, (high_half, low_half), (high_rest, low_rest), parts, sides
        )


VMEM = pl.BlockSpec(memory_space=pltpu.VMEM)


def position():
    lane, patch = lax.axis_index("member"), lax.axis_index("patch")
    return lax.div(lane, 2), lax.rem(lane, 2), lax.rem(patch, 2), lax.axis_size("member") // 2


def call(kernel, name, out_shape, args, scratch=(), flops=None, limit=8, out=VMEM):
    several = isinstance(out_shape, (list, tuple))
    return pl.pallas_call(
        lambda *refs: kernel(position(), *refs),
        out_shape=out_shape,
        in_specs=[VMEM] * len(args),
        out_specs=[out] * len(out_shape) if several else out,
        scratch_shapes=scratch,
        compiler_params=pltpu.CompilerParams(vmem_limit_bytes=limit * 1024 * 1024),
        cost_estimate=flops and pl.CostEstimate(flops=flops, bytes_accessed=0, transcendentals=0),
        name=name,
    )(*args)


def bfloat(*shape):
    return jax.ShapeDtypeStruct(shape, BF16)


def array(*shape):
    return jax.ShapeDtypeStruct(shape, F32)


def per_device(
    init_field, flow_fields, emission, observed_cell, observed_count, observed_value, observed_scale
):
    step, rows, width = init_field.shape
    slots = observed_cell.shape[1]
    patches, lanes = lax.axis_size("patch"), lax.axis_size("member")
    chips = lanes // 2
    members = lanes * step
    axes = ("patch", "member")
    count = patches * lanes

    edge = array(STEPS * step + 8, width)
    to_last, to_first = call(pack_kernel, "pack", [edge, edge], [init_field, flow_fields], limit=32)

    def swap(message, start):
        lower = range(start, patches - 1, 2)
        return lax.ppermute(message, "patch", [(p, p + 1) for p in lower] + [(p + 1, p) for p in lower])

    halo_last, halo_first = swap(to_last, 0), swap(to_first, 1)

    mine = jnp.concatenate(
        [
            observed_cell.astype(F32),
            observed_value,
            observed_scale,
            jnp.broadcast_to(observed_count.astype(F32)[:, None], observed_cell.shape),
        ]
        * 2,
        axis=0,
    )

    def between(message, hops):
        return lax.ppermute(message, "member", [(2 * a + core, 2 * b + core) for a, b in hops for core in range(2)])

    mirrored = [
        [hop for to in range(1, chips // 2) for hop in (((to + s) % chips, to), (chips - 1 - (to + s) % chips, chips - 1 - to))]
        for s in range(chips)
    ]
    turning = [[((to - s) % chips, to) for to in range(1, chips - 1)] for s in range(chips)]
    single = all(len({source for source, _ in hops}) == len(hops) for hops in mirrored)
    targets = mirrored if single else turning
    pair = array(2, step, width)
    kept, emitted, *inner = call(
        functools.partial(inner_kernel, targets), "inner",
        [array(4, step, width), array(step, width // 2)] + [pair] * chips,
        [init_field, flow_fields, emission[None, :]],
        [pltpu.VMEM((rows, step, width), F32), pltpu.VMEM((rows, 8, width), F32)], limit=32,
    )
    got_inner = [inner[0]] + [between(inner[s], targets[s]) for s in range(1, chips)]
    outer = call(
        edge_kernel, "edge", [pair] * chips, [init_field, flow_fields, emitted, kept, halo_last, halo_first],
        [pltpu.VMEM((2, step, width), F32)], limit=32,
    )
    got_outer = [outer[0]] + [
        between(outer[s], [(s, 0), (chips - 1 - s, chips - 1)]) for s in range(1, chips)
    ]
    order = [(targets[s], s) for s in range(chips)]
    pieces_in = got_inner + got_outer
    mine, _ = lax.optimization_barrier((mine, outer[0]))
    other = lax.ppermute(
        mine, axes,
        [(p * lanes + i, p * lanes + lanes - 1 - i) for p in range(1, patches, 2) for i in range(lanes)],
    )

    def device(p, chip, core):
        return p * lanes + 2 * chip + core

    borders, siblings = [], []
    for p in range(patches):
        for chip in range(chips):
            for core, away in ((0, -1), (1, 1)):
                siblings.append((device(p, chip, core), device(p, chip, 1 - core)))
                if 0 <= chip + away < chips:
                    borders.append((device(p, chip, core), device(p, chip + away, 1 - core)))
                else:
                    to = p + 1 if (p % 2 == 0) == (away == 1) else p - 1
                    if 0 <= to < patches:
                        borders.append((device(p, chip, core), device(to, chip, core)))

    half = array(chips, step, width)
    near_other, near_own, observed = call(
        functools.partial(collect_kernel, order), "collect",
        [half, array(chips * step + PADDING, width), array(8, slots)], [mine, other] + pieces_in,
    )
    far_own = lax.ppermute(near_other, axes, siblings)
    got_half = lax.ppermute(near_own, axes, borders)
    far_other = lax.ppermute(near_own, axes, siblings)
    got_rest = lax.ppermute(far_own, axes, borders)

    prepared = call(
        prepare_kernel, "prepare",
        [bfloat(members, slots)] * 2 + [bfloat(width, members)] * 2
        + [array(width, width // 2), array(8, slots), array(members, width // 2)],
        [observed, near_other, near_own, far_other, far_own],
        [pltpu.VMEM((members, 2 * width), F32)] + [pltpu.VMEM((members, 2 * width), BF16)] * 2,
        flops=8 * members * slots * width, limit=20,
    )
    halves = members // 2
    middle = call(
        middle_kernel, "middle",
        [bfloat(halves, slots)] * 2 + [array(slots, slots), array(width, slots), array(8, width)],
        [observed, *prepared[:4], prepared[6], got_half],
        flops=10 * halves * slots * slots, limit=20,
    )
    order = sorted(range(lanes), key=lambda x: (x.bit_length() != lanes.bit_length() - 1, -x))
    row = array(step, width)
    *shared, first, second = call(
        functools.partial(region_kernel, order[:2]), "region",
        [bfloat(halves, slots)] * 2 + [bfloat(slots, width)] * 2 + [array(8, width)] + [row] * 2,
        [observed, near_own, far_own, *prepared, *middle, got_rest],
        [pltpu.VMEM((slots, slots), F32)] * 2 + [pltpu.VMEM((width + 8, slots), F32)],
        limit=24,
    )
    others = call(
        functools.partial(others_kernel, order[2:]), "others", [row] * (lanes - 2),
        [near_own, far_own, prepared[6], *middle[:2], *shared],
        flops=6 * members * slots * width, limit=16,
    )
    analysed = dict(zip(order, [first, second, *others]))

    def swapped(x):
        return lax.ppermute(analysed[x], "member", [(i, i ^ x) for i in range(lanes)]) if x else analysed[0]

    return call(
        functools.partial(unpack_kernel, order), "unpack", array(step, rows, width),
        [swapped(x) for x in order], [pltpu.VMEM((step, rows, width), F32), pltpu.SemaphoreType.DMA((4,))],
        limit=48, out=pl.BlockSpec(memory_space=pltpu.HBM),
    )


def solution(mesh):
    return jax.shard_map(
        per_device,
        mesh=mesh,
        in_specs=(
            P("member", "patch", None),
            P(None, "patch", None),
            P("member"),
            P(("patch", "member"), None),
            P(("patch", "member")),
            P(("patch", "member"), None),
            P(("patch", "member"), None),
        ),
        out_specs=P("member", "patch", None),
        check_vma=False,
    )
```

```python
import functools
import math

import jax
import jax.numpy as jnp
from jax import lax
from jax.experimental import pallas as pl
from jax.experimental.pallas import tpu as pltpu
from jax.sharding import PartitionSpec as P

STEPS = 2
COARSE = 0.35
DONE = 0.02
LARGE = 2e4
PART = 256
PADDING = 8
F32 = jnp.float32
BF16 = jnp.bfloat16


def pack_kernel(info, field_ref, flow_ref, first_ref, second_ref):
    members, rows, width = field_ref.shape
    even = info[2] == 0
    for place in range(STEPS):
        tail, head = field_ref[:, rows - STEPS + place, :], field_ref[:, place, :]
        at = pl.ds(place * members, members)
        first_ref[at, :] = jnp.where(even, tail, head)
        second_ref[at, :] = jnp.where(even, head, tail)
    tail, head = flow_ref[:, rows - 1, :], flow_ref[:, 0, :]
    at = pl.ds(STEPS * members, 8)
    first_ref[at, :] = jnp.concatenate([jnp.where(even, tail, head)] * 2, axis=0)
    second_ref[at, :] = jnp.concatenate([jnp.where(even, head, tail)] * 2, axis=0)


def doubled(x):
    return jnp.concatenate([x, x], axis=1)


def weights_of(flow):
    row_flow, col_flow, kept, source = flow[0:1], flow[1:2], 1.0 - flow[2:3], flow[3:4]
    behind, ahead = jnp.maximum(row_flow, 0.0), -jnp.minimum(row_flow, 0.0)
    left, right = jnp.maximum(col_flow, 0.0), -jnp.minimum(col_flow, 0.0)
    stays = 1.0 - behind - ahead - left - right
    return [kept * stays, kept * behind, kept * ahead, kept * left, kept * right, source]


def advance(weights, emission, behind, field, ahead):
    width = field.shape[1]
    return (
        weights[0] * field
        + weights[1] * behind
        + weights[2] * ahead
        + weights[3] * pltpu.roll(field, 1, 1)
        + weights[4] * pltpu.roll(field, width - 1, 1)
        + emission * weights[5]
    )


def inner_kernel(targets, info, field_ref, flow_ref, member_ref, kept_ref, emission_ref, *refs):
    out_refs, (wide_ref, weight_ref) = refs[:-2], refs[-2:]
    members, rows, _ = field_ref.shape
    diagonal = lax.broadcasted_iota(jnp.int32, (members, members), 0) == lax.broadcasted_iota(
        jnp.int32, (members, members), 1
    )
    column = jnp.sum(jnp.where(diagonal, member_ref[...], 0.0), axis=1, keepdims=True)
    emission_ref[...] = jnp.broadcast_to(column, emission_ref.shape)
    emission = doubled(emission_ref[...])
    for row in range(1, rows - 1):
        weights = weights_of(flow_ref[:, row, :])
        for i, weight in enumerate(weights):
            weight_ref[row, pl.ds(i, 1), :] = weight
        wide_ref[row] = advance(
            weights, emission, field_ref[:, row - 1, :], field_ref[:, row, :], field_ref[:, row + 1, :]
        )
    for place, row in enumerate((1, 2, rows - 3, rows - 2)):
        kept_ref[place] = wide_ref[row]
    for out_ref, hops in zip(out_refs, targets):
        chip = sum(jnp.where(info[0] == source, to, 0) for source, to in hops)

        @pl.when(chip > 0)
        def _():
            for place in range(2):
                position = 2 * chip + jnp.abs(info[1] - 1 + place)
                row = position + info[2] * (rows - 1 - 2 * position)
                weights = weight_ref[row]
                out_ref[place] = advance(
                    [weights[i : i + 1] for i in range(6)],
                    emission, wide_ref[row - 1], wide_ref[row], wide_ref[row + 1],
                )


def end_rows(info, last, field_ref, flow_ref, emission_ref, kept_ref, halo_ref, out_ref):
    members, rows, width = field_ref.shape
    emission = doubled(emission_ref[...])

    def halo_row(place):
        return halo_ref[pl.ds(place * members, members), :]

    halo_weights = weights_of(halo_ref[pl.ds(STEPS * members, 4), :])
    for parity in range(2):

        @pl.when(info[2] == parity)
        def _():
            if parity == last:
                end, near, outside, beyond = 0, 1, halo_row(1), halo_row(0)
                inside, further = kept_ref[0], kept_ref[1]
            else:
                end, near, outside, beyond = rows - 1, rows - 2, halo_row(0), halo_row(1)
                inside, further = kept_ref[3], kept_ref[2]

            def ordered(weights, outer, own, inner):
                behind, ahead = (outer, inner) if end == 0 else (inner, outer)
                return advance(weights, emission, behind, own, ahead)

            end_weights = weights_of(flow_ref[:, end, :])
            end_field = field_ref[:, end, :]
            outer = ordered(halo_weights, beyond, outside, end_field)
            own = ordered(end_weights, outside, end_field, field_ref[:, near, :])
            out_ref[last] = ordered(end_weights, outer, own, inside)
            out_ref[1 - last] = ordered(weights_of(flow_ref[:, near, :]), own, inside, further)


def edge_kernel(info, field_ref, flow_ref, emission_ref, kept_ref, last_ref, first_ref, *refs):
    out_refs, scratch = refs[:-1], refs[-1]
    chips = len(out_refs)
    core = info[1]
    for last, halo_ref in enumerate((first_ref, last_ref)):
        end_rows(info, last, field_ref, flow_ref, emission_ref, kept_ref, halo_ref, scratch)
        for s, out_ref in enumerate(out_refs):

            @pl.when(info[0] == (chips - 1 - s if last else s))
            def _():
                out_ref[0] = scratch[1 - core]
                out_ref[1] = scratch[core]


def source_of(chip, chips, hops, k):
    inner = sum(jnp.where(chip == to, source, 0) for source, to in hops)
    return jnp.where(chip == 0, k, jnp.where(chip == chips - 1, chips - 1 - k, inner))


def collect_kernel(order, info, mine_ref, other_ref, *refs):
    chips = len(order)
    *near_others, near_own, observed_ref = refs[-4:]
    portion, step, _ = near_others[0].shape
    observed_ref[...] = jnp.where(info[2] == 1, other_ref[...], mine_ref[...])
    near_own[pl.ds(chips * step, PADDING), :] = jnp.zeros((PADDING, near_own.shape[1]), F32)
    chip = info[0]
    at_edge = jnp.logical_or(chip == 0, chip == chips - 1)
    for index, (s, k) in enumerate(order):
        block = source_of(chip, chips, s, k)
        rows = pl.ds(pl.multiple_of(block * step, step), step)
        for ref, here in ((refs[index], jnp.logical_not(at_edge)), (refs[chips + index], at_edge)):

            @pl.when(here)
            def _():
                near_own[rows, :] = ref[1]
                for index, near_other in enumerate(near_others):

                    @pl.when(lax.div(block, portion) == index)
                    def _():
                        near_other[lax.rem(block, portion)] = ref[0]


def unpack_kernel(order, info, *refs):
    row_refs, (out_hbm, out_ref, sems) = refs[:-3], refs[-3:]
    members, rows, _ = out_ref.shape
    part = members // 4
    moves = []
    for index in range(4):
        some = pl.ds(index * part, part)
        for x, ref in zip(order, row_refs):
            position = (2 * info[0] + info[1]) ^ x
            row = position + info[2] * (rows - 1 - 2 * position)
            out_ref[some, pl.ds(row, 1), :] = ref[some, :][:, None, :]
        moves.append(pltpu.make_async_copy(out_ref.at[some], out_hbm.at[some], sems.at[index]))
        moves[-1].start()
    for move in moves:
        move.wait()


def pieces(x, count):
    parts = []
    for _ in range(count - 1):
        part = x.astype(BF16)
        parts.append(part)
        x = x - part.astype(F32)
    return parts + [x.astype(BF16)]


def dot(a, b):
    return lax.dot_general(a, b, (((1,), (0,)), ((), ())), preferred_element_type=F32)


def dot_t(a, b):
    return lax.dot_general(a, b, (((0,), (0,)), ((), ())), preferred_element_type=F32)


def product(a, b):
    total = None
    for i, left in enumerate(a):
        for j, right in enumerate(b):
            if i + j < max(len(a), len(b)):
                term = dot(left, right)
                total = term if total is None else total + term
    return total


def observations(info, observed_ref, width, root):
    slots = observed_ref.shape[1]
    cells, values, scales, count = (observed_ref[pl.ds(i, 1), :] for i in range(4))
    cells = cells.astype(jnp.int32)
    offset = sum((cells >= i * width).astype(jnp.int32) for i in (1, 2)) - 1
    column = cells - (offset + 1) * width
    side = offset * jnp.where(info[2] == 1, -1, 1) * (1 - 2 * info[1])
    cells = column + width * jnp.where(side == 0, 2, jnp.where(side < 0, 0, 1))
    active = lax.broadcasted_iota(jnp.int32, (1, slots), 1) < count.astype(jnp.int32)
    slot_weight = jnp.where(active, scales, 0.0)
    return cells, slot_weight, values, slot_weight * (1.0 / root)


def one_hot(cells, first, count):
    return (
        lax.broadcasted_iota(jnp.int32, (count, cells.shape[1]), 0) + first == cells
    ).astype(F32).astype(BF16)


def mean_of(blocks, members):
    total = blocks[0]
    for block in blocks[1:]:
        total = total + block
    return jnp.sum(total, axis=0, keepdims=True) * (1.0 / members)


def at_cells(row, chosen):
    parts = pieces(jnp.broadcast_to(row, (8, row.shape[1])), 3)
    return (dot(parts[0], chosen) + (dot(parts[1], chosen) + dot(parts[2], chosen)))[:1]


def each(*refs):
    return [ref.at[index] for ref in refs for index in range(ref.shape[0])]


def prepare_kernel(
    info, observed_ref, near_first, near_second, near_own, far_other, far_first, far_second,
    spread_high, spread_low, own_high, own_low, own_part, seen_ref, direction_ref,
    anomaly, high_ref, low_ref,
):
    chips, (_, step, width) = info[3], near_first.shape
    members = 2 * chips * step
    cells, _, _, scale = observations(info, observed_ref, width, math.sqrt(members - 1))
    chosen = one_hot(cells, width, 2 * width)
    blocks = [pl.ds(index * step, step) for index in range(2 * chips)]
    means = []
    for place in range(2):
        columns = pl.ds(place * width, width)
        if place:
            rows = [near_own.at[block, :] for block in blocks[:chips]] + each(far_first, far_second)
        else:
            rows = each(near_first, near_second) + [far_other.at[block, :] for block in blocks[:chips]]
        means.append(mean_of([row[...] for row in rows], members))
        for block, row in zip(blocks, rows):
            part = row[...] - means[-1]
            anomaly[block, columns] = part
            high_ref[block, columns] = part.astype(BF16)

    def unit(x):
        return x * (1.0 / jnp.maximum(jnp.max(jnp.abs(x)), 1e-30))

    high = high_ref[...]
    along = lax.dot_general(high[:16], high, (((1,), (1,)), ((), ())), preferred_element_type=F32)
    rows = unit(dot(unit(along).astype(BF16), high))
    weight = jnp.sum(rows * rows[:1], axis=1, keepdims=True)
    weight = weight + jnp.where(jnp.max(jnp.abs(weight)) > 0.0, 0.0, 1.0)
    pattern = unit(jnp.sum(rows * weight, axis=0, keepdims=True))
    total = jnp.zeros((1, 1), F32)
    for block in blocks:
        along = jnp.sum(anomaly[block, :] * pattern, axis=1, keepdims=True)
        total = total + jnp.sum(along * along, axis=0, keepdims=True)
        direction_ref[block, :] = jnp.broadcast_to(along, (step, direction_ref.shape[1]))
    length = lax.rsqrt(jnp.maximum(total, 1e-30))
    taken = None
    for block in blocks:
        direction = direction_ref[block, :] * length
        direction_ref[block, :] = direction
        term = anomaly[block, :] * doubled(doubled(direction))
        taken = term if taken is None else taken + term
    taken = jnp.sum(taken, axis=0, keepdims=True)
    own_part[...] = jnp.broadcast_to(taken[:, width:], (own_part.shape[1], width)).T

    for block in blocks:
        rest = anomaly[block, :] - doubled(doubled(direction_ref[block, :])) * taken
        high, low = pieces(rest, 2)
        high_ref[block, :] = high
        low_ref[block, :] = low
        own = rest[:, width:].T
        own_high[:, block], own_low[:, block] = pieces(own, 2)
    seen_ref[pl.ds(0, 1), :] = at_cells(jnp.concatenate(means, axis=1), chosen)
    seen_ref[pl.ds(1, 1), :] = at_cells(taken, chosen)
    for first in range(0, members, PART):
        rows = pl.ds(first, PART)
        spread = (dot(high_ref[rows, :], chosen) + dot(low_ref[rows, :], chosen)) * scale
        high, low = pieces(spread, 2)
        spread_high[rows, :] = high
        spread_low[rows, :] = low


def square(parts):
    half = parts[0].shape[0] // 2
    upper = product([part[:half] for part in parts], parts)
    lower = product([part[half:] for part in parts], [part[:, half:] for part in parts])
    return upper, jnp.concatenate([upper[:, half:].T, lower], axis=1)


def at_border(info):
    chip, core, _, chips = info
    ends = jnp.logical_or(jnp.logical_and(chip == 0, core == 0), jnp.logical_and(chip == chips - 1, core == 1))
    return jnp.where(ends, 0, 1)


def shifted_spread(rows, blocks, direction_ref, shift, along, chosen, scale, high_in, low_in, high_out, low_out):
    total, taken = None, None
    step = rows[0].shape[0]
    for index, (row, block) in enumerate(zip(rows, blocks)):
        here = pl.ds(index * step, step)
        direction = doubled(direction_ref[block, :])
        rest = row[...] - shift - direction * along
        total = rest if total is None else total + rest
        taken = direction * rest if taken is None else taken + direction * rest
        high, low = pieces(rest, 2)
        high, low = pieces((dot(high, chosen) + dot(low, chosen)) * scale, 2)
        high_out[here, :] = high + high_in[block, :]
        low_out[here, :] = low + low_in[block, :]
    return jnp.sum(total, axis=0, keepdims=True), jnp.sum(taken, axis=0, keepdims=True)


def gram(high, low):
    turned = high.T
    cross = dot(turned, low)
    return dot(turned, high) + (cross + cross.T)


def middle_kernel(
    info, observed_ref, high_in, low_in, own_high, own_low, direction_ref, half_ref,
    high_ref, low_ref, gram_ref, right_ref, known_ref,
):
    chips = info[3]
    count, slots = high_ref.shape
    step = count // chips
    width = half_ref.shape[1]
    first = at_border(info) * count
    cells, _, _, scale = observations(info, observed_ref, width, math.sqrt(2 * count - 1))
    chosen = one_hot(cells, 0, width)
    rows = [half_ref.at[pl.ds(chip * step, step), :] for chip in range(chips)]
    blocks = [pl.ds(pl.multiple_of(first + chip * step, step), step) for chip in range(chips)]
    mean = mean_of([row[...] for row in rows], count)
    along, weight = None, None
    for row, block in zip(rows, blocks):
        direction = direction_ref[block, :]
        term = (row[...] - mean) * doubled(direction)
        along = term if along is None else along + term
        weight = direction * direction if weight is None else weight + direction * direction
    weight = doubled(jnp.sum(weight, axis=0, keepdims=True))
    along = jnp.sum(along, axis=0, keepdims=True) / jnp.maximum(weight, 0.1)
    total, taken = shifted_spread(
        rows, blocks, direction_ref, mean, along, chosen, scale, high_in, low_in, high_ref, low_ref
    )
    for index, known in enumerate((mean, along, total, taken)):
        known_ref[pl.ds(index, 1), :] = known
    high, low = high_ref[...], low_ref[...]
    gram_ref[...] = gram(high, low)
    members = pl.ds(pl.multiple_of(first, count), count)
    right_ref[...] = product([own_high[:, members], own_low[:, members]], [high, low])


def more_kernel(
    info, observed_ref, high_in, low_in, own_high, own_low, direction_ref, gram_half, right_half, known_half, rest_ref,
    high_ref, low_ref, gram_ref, right_ref, known_ref,
):
    portion, step, width = rest_ref.shape
    count = info[3] * step
    first = (1 - at_border(info)) * count
    cells, _, _, scale = observations(info, observed_ref, width, math.sqrt(2 * count - 1))
    shift, along, total, taken = (known_half[pl.ds(index, 1), :] for index in range(4))
    more, further = shifted_spread(
        each(rest_ref),
        [pl.ds(pl.multiple_of(first + index * step, step), step) for index in range(portion)],
        direction_ref, shift, along, one_hot(cells, 0, width), scale, high_in, low_in, high_ref, low_ref,
    )
    for index, known in enumerate((shift, along, total + more, taken + further)):
        known_ref[pl.ds(index, 1), :] = known
    high, low = high_ref[...], low_ref[...]
    gram_ref[...] = gram_half[...] + gram(high, low)
    members = pl.ds(pl.multiple_of(first, portion * step), portion * step)
    right_ref[...] = right_half[...] + product([own_high[:, members], own_low[:, members]], [high, low])


def analysed_row(info, x, near_own, far_owns, direction_ref, spreads, parts, sides):
    portion, step, _ = far_owns[0].shape
    chip, mine = info[0] ^ (x // 2), x % 2
    early = chip < portion
    rows = pl.ds(pl.multiple_of(chip * step, step), step)
    place = lax.rem(chip, portion)
    within = pl.ds(pl.multiple_of(place * step, step), step)
    spread = [
        jnp.where(at_border(info) == mine, half[rows, :], jnp.where(early, first[within, :], second[within, :]))
        for half, first, second in spreads
    ]
    block = pl.ds(pl.multiple_of((mine * info[3] + chip) * step, step), step)
    own = jnp.where(early, far_owns[0][place], far_owns[1][place]) if mine else near_own[rows, :]
    return own + sides[0:1] + product(spread, parts) + doubled(direction_ref[block, :]) * sides[1:2]


def others_kernel(
    order, info, near_own, far_first, far_second, direction_ref, high_half, low_half, high_first, low_first,
    high_second, low_second, solved_high, solved_low, sides_ref, *out_refs,
):
    parts = [solved_high[...], solved_low[...]]
    spreads = ((high_half, high_first, high_second), (low_half, low_first, low_second))
    for x, out_ref in zip(order, out_refs):
        out_ref[...] = analysed_row(
            info, x, near_own, (far_first, far_second), direction_ref, spreads, parts, sides_ref[...]
        )


def region_kernel(
    order, info, observed_ref, near_own, far_first, far_second, high_in, low_in, own_high, own_low, own_part, seen_ref,
    direction_ref, high_half, low_half, high_first, low_first, gram_half, right_half, known_ref, rest_ref, *refs,
):
    chips, (portion, step, width) = info[3], rest_ref.shape
    high_rest, low_rest, solved_high, solved_low, sides_ref = refs[:5]
    out_refs, (factor, squared, answer) = refs[5:-3], refs[-3:]
    count = chips * step
    members = 2 * count
    slots = observed_ref.shape[1]
    root = math.sqrt(members - 1)
    first = (1 - at_border(info)) * count + (chips - portion) * step
    cells, slot_weight, values, scale = observations(info, observed_ref, width, root)
    chosen = one_hot(cells, 0, width)
    shift, along, total, taken = (known_ref[pl.ds(index, 1), :] for index in range(4))
    more, further = shifted_spread(
        each(rest_ref),
        [pl.ds(pl.multiple_of(first + index * step, step), step) for index in range(portion)],
        direction_ref, shift, along, chosen, scale, high_in, low_in, high_rest, low_rest,
    )
    left = (total + more) * (1.0 / members)
    taken = taken + further
    seen_mean = seen_ref[pl.ds(0, 1), :] + at_cells(shift + left, chosen)
    left, taken_here = at_cells(left, chosen) * scale, at_cells(taken, chosen) * scale
    common = (seen_ref[pl.ds(1, 1), :] + at_cells(along + taken, chosen)) * scale
    innovation = slot_weight * (values - seen_mean)
    place = lax.broadcasted_iota(jnp.int32, (8, slots), 0)
    excess = jnp.where(place == 0, left * math.sqrt(members), jnp.where(place == 1, taken_here, 0.0))
    excess = pieces(excess, 2)

    eye = lax.broadcasted_iota(jnp.int32, (slots, slots), 0) == lax.broadcasted_iota(
        jnp.int32, (slots, slots), 1
    )
    high, low = high_rest[...], low_rest[...]
    over = dot_t(excess[0], excess[0]) + (dot_t(excess[0], excess[1]) + dot_t(excess[1], excess[0]))
    factor[...] = gram(high, low) + (gram_half[...] - over) + jnp.where(eye, 1.0, 0.0)
    rows = pl.ds(pl.multiple_of(first, portion * step), portion * step)
    answer[pl.ds(0, width), :] = right_half[...] + product([own_high[:, rows], own_low[:, rows]], [high, low])
    answer[pl.ds(width, 8), :] = jnp.where(
        lax.broadcasted_iota(jnp.int32, (8, slots), 0) == 0, jnp.broadcast_to(common, (8, slots)), 0.0
    )
    half = slots // 2
    upper, lower = pl.ds(0, half), pl.ds(half, half)

    def after(bound):
        return bound * bound / (2.0 - bound * bound)

    def size(matrix):
        return jnp.sum(jnp.sum(matrix * matrix, axis=0, keepdims=True))

    def begin(count):
        parts = pieces(factor[...], count)
        if count > 2:
            squared[upper, :], squared[lower, :] = square(parts)
        bound = 1.0 - start
        gain = 2.0 / (2.0 - bound * bound)
        answer[...] = (gain * start) * (2.0 * answer[...] - start * product(pieces(answer[...], count), parts))
        factor[...] = (gain * start) * (2.0 * factor[...] - start * squared[...])
        return after(bound)

    def refine(bound, count):
        gain = 2.0 / (2.0 - bound * bound)
        parts = pieces(factor[...], count)
        answer[...] = gain * (2.0 * answer[...] - product(pieces(answer[...], count), parts))
        top, bottom = square(parts)
        factor[upper, :] = gain * (2.0 * factor[upper, :] - top)
        factor[lower, :] = gain * (2.0 * factor[lower, :] - bottom)
        return after(bound)

    def close(bound, rest):
        gain = 2.0 / (2.0 - bound * bound)
        answer[...] = gain * (answer[...] + dot(answer[...].astype(BF16), rest))
        return gain

    def finish(bound):
        rest = factor[...].astype(BF16)
        gain = close(bound, rest)
        factor[...] = gain * (dot(rest, rest) - jnp.where(eye, 0.5 * bound * bound, 0.0))
        return after(bound)

    top, bottom = square(pieces(factor[...], 2))
    squared[upper, :] = top
    squared[lower, :] = bottom
    limit = 1.0001 * jnp.sqrt(jnp.sqrt(size(top) + size(bottom)))
    start = 2.0 / (1.0 + limit)
    large = limit > LARGE
    bound = lax.cond(large, lambda: begin(3), lambda: begin(2))
    bound = lax.while_loop(lambda b: jnp.logical_and(b > COARSE, large), lambda b: refine(b, 3), bound)
    bound = lax.while_loop(lambda b: b > COARSE, lambda b: refine(b, 2), bound)
    factor[...] = jnp.where(eye, 1.0, 0.0) - factor[...]
    bound = lax.while_loop(lambda b: b > DONE, finish, bound)
    close(bound, factor[...].astype(BF16))

    solved = answer[pl.ds(0, width), :]
    alone = answer[pl.ds(width, 1), :]
    share = own_part[:, :1] - jnp.sum(solved * common, axis=1, keepdims=True)
    solved = solved + (share / (1.0 + jnp.sum(common * alone, axis=1, keepdims=True))) * alone
    solved = solved.T
    which = lax.broadcasted_iota(jnp.int32, (8, slots), 0)
    sides = jnp.where(
        which == 0, innovation * (1.0 / root) + 0.5 * left, jnp.where(which == 1, 0.5 * (taken_here - common), 0.0)
    )
    parts = pieces(solved, 2)
    sides = product(pieces(sides, 2), parts)
    parts = [part * jnp.asarray(-0.5, BF16) for part in parts]
    sides_ref[...] = sides
    solved_high[...], solved_low[...] = parts
    spreads = ((high_half, high_first, high_rest), (low_half, low_first, low_rest))
    for x, out_ref in zip(order, out_refs):
        out_ref[...] = analysed_row(
            info, x, near_own, (far_first, far_second), direction_ref, spreads, parts, sides
        )


VMEM = pl.BlockSpec(memory_space=pltpu.VMEM)


def position():
    lane, patch = lax.axis_index("member"), lax.axis_index("patch")
    return lax.div(lane, 2), lax.rem(lane, 2), lax.rem(patch, 2), lax.axis_size("member") // 2


def call(kernel, name, out_shape, args, scratch=(), flops=None, limit=8, out=VMEM):
    several = isinstance(out_shape, (list, tuple))
    return pl.pallas_call(
        lambda *refs: kernel(position(), *refs),
        out_shape=out_shape,
        in_specs=[VMEM] * len(args),
        out_specs=[out] * len(out_shape) if several else out,
        scratch_shapes=scratch,
        compiler_params=pltpu.CompilerParams(vmem_limit_bytes=limit * 1024 * 1024),
        cost_estimate=flops and pl.CostEstimate(flops=flops, bytes_accessed=0, transcendentals=0),
        name=name,
    )(*args)


def bfloat(*shape):
    return jax.ShapeDtypeStruct(shape, BF16)


def array(*shape):
    return jax.ShapeDtypeStruct(shape, F32)


def per_device(
    init_field, flow_fields, emission, observed_cell, observed_count, observed_value, observed_scale
):
    step, rows, width = init_field.shape
    slots = observed_cell.shape[1]
    patches, lanes = lax.axis_size("patch"), lax.axis_size("member")
    chips = lanes // 2
    members = lanes * step
    axes = ("patch", "member")
    count = patches * lanes

    edge = array(STEPS * step + 8, width)
    to_last, to_first = call(pack_kernel, "pack", [edge, edge], [init_field, flow_fields], limit=32)

    def swap(message, start):
        lower = range(start, patches - 1, 2)
        return lax.ppermute(message, "patch", [(p, p + 1) for p in lower] + [(p + 1, p) for p in lower])

    halo_last, halo_first = swap(to_last, 0), swap(to_first, 1)

    mine = jnp.concatenate(
        [
            observed_cell.astype(F32),
            observed_value,
            observed_scale,
            jnp.broadcast_to(observed_count.astype(F32)[:, None], observed_cell.shape),
        ]
        * 2,
        axis=0,
    )

    def between(message, hops):
        return lax.ppermute(message, "member", [(2 * a + core, 2 * b + core) for a, b in hops for core in range(2)])

    mirrored = [
        [hop for to in range(1, chips // 2) for hop in (((to + s) % chips, to), (chips - 1 - (to + s) % chips, chips - 1 - to))]
        for s in range(chips)
    ]
    turning = [[((to - s) % chips, to) for to in range(1, chips - 1)] for s in range(chips)]
    single = all(len({source for source, _ in hops}) == len(hops) for hops in mirrored)
    targets = mirrored if single else turning
    pair = array(2, step, width)
    kept, emitted, *inner = call(
        functools.partial(inner_kernel, targets), "inner",
        [array(4, step, width), array(step, width // 2)] + [pair] * chips,
        [init_field, flow_fields, emission[None, :]],
        [pltpu.VMEM((rows, step, width), F32), pltpu.VMEM((rows, 8, width), F32)], limit=32,
    )
    got_inner = [inner[0]] + [between(inner[s], targets[s]) for s in range(1, chips)]
    outer = call(
        edge_kernel, "edge", [pair] * chips, [init_field, flow_fields, emitted, kept, halo_last, halo_first],
        [pltpu.VMEM((2, step, width), F32)], limit=32,
    )
    got_outer = [outer[0]] + [
        between(outer[s], [(s, 0), (chips - 1 - s, chips - 1)]) for s in range(1, chips)
    ]
    order = [(targets[s], s) for s in range(chips)]
    pieces_in = got_inner + got_outer
    mine, _ = lax.optimization_barrier((mine, outer[0]))
    other = lax.ppermute(
        mine, axes,
        [(p * lanes + i, p * lanes + lanes - 1 - i) for p in range(1, patches, 2) for i in range(lanes)],
    )

    def device(p, chip, core):
        return p * lanes + 2 * chip + core

    borders, siblings = [], []
    for p in range(patches):
        for chip in range(chips):
            for core, away in ((0, -1), (1, 1)):
                siblings.append((device(p, chip, core), device(p, chip, 1 - core)))
                if 0 <= chip + away < chips:
                    borders.append((device(p, chip, core), device(p, chip + away, 1 - core)))
                else:
                    to = p + 1 if (p % 2 == 0) == (away == 1) else p - 1
                    if 0 <= to < patches:
                        borders.append((device(p, chip, core), device(to, chip, core)))

    portion = array(chips // 2, step, width)
    near_first, near_second, near_own, observed = call(
        functools.partial(collect_kernel, order), "collect",
        [portion, portion, array(chips * step + PADDING, width), array(8, slots)], [mine, other] + pieces_in,
    )
    far_first, far_second = (lax.ppermute(near, axes, siblings) for near in (near_first, near_second))
    got_half = lax.ppermute(near_own, axes, borders)
    far_other = lax.ppermute(near_own, axes, siblings)
    got_first, got_second = (lax.ppermute(far, axes, borders) for far in (far_first, far_second))

    prepared = call(
        prepare_kernel, "prepare",
        [bfloat(members, slots)] * 2 + [bfloat(width, members)] * 2
        + [array(width, width // 2), array(8, slots), array(members, width // 2)],
        [observed, near_first, near_second, near_own, far_other, far_first, far_second],
        [pltpu.VMEM((members, 2 * width), F32)] + [pltpu.VMEM((members, 2 * width), BF16)] * 2,
        flops=8 * members * slots * width, limit=20,
    )
    halves = members // 2
    middle = call(
        middle_kernel, "middle",
        [bfloat(halves, slots)] * 2 + [array(slots, slots), array(width, slots), array(8, width)],
        [observed, *prepared[:4], prepared[6], got_half],
        flops=10 * halves * slots * slots, limit=20,
    )
    quarter = members // 4
    more = call(
        more_kernel, "more",
        [bfloat(quarter, slots)] * 2 + [array(slots, slots), array(width, slots), array(8, width)],
        [observed, *prepared[:4], prepared[6], *middle[2:], got_first],
        flops=5 * halves * slots * slots, limit=20,
    )
    order = sorted(range(lanes), key=lambda x: (x.bit_length() != lanes.bit_length() - 1, -x))
    row = array(step, width)
    *shared, first, second = call(
        functools.partial(region_kernel, order[:2]), "region",
        [bfloat(quarter, slots)] * 2 + [bfloat(slots, width)] * 2 + [array(8, width)] + [row] * 2,
        [observed, near_own, far_first, far_second, *prepared, *middle[:2], *more, got_second],
        [pltpu.VMEM((slots, slots), F32)] * 2 + [pltpu.VMEM((width + 8, slots), F32)],
        limit=24,
    )
    others = call(
        functools.partial(others_kernel, order[2:]), "others", [row] * (lanes - 2),
        [near_own, far_first, far_second, prepared[6], *middle[:2], *more[:2], *shared],
        flops=6 * members * slots * width, limit=16,
    )
    analysed = dict(zip(order, [first, second, *others]))

    def swapped(x):
        return lax.ppermute(analysed[x], "member", [(i, i ^ x) for i in range(lanes)]) if x else analysed[0]

    return call(
        functools.partial(unpack_kernel, order), "unpack", array(step, rows, width),
        [swapped(x) for x in order], [pltpu.VMEM((step, rows, width), F32), pltpu.SemaphoreType.DMA((4,))],
        limit=48, out=pl.BlockSpec(memory_space=pltpu.HBM),
    )


def solution(mesh):
    return jax.shard_map(
        per_device,
        mesh=mesh,
        in_specs=(
            P("member", "patch", None),
            P(None, "patch", None),
            P("member"),
            P(("patch", "member"), None),
            P(("patch", "member")),
            P(("patch", "member"), None),
            P(("patch", "member"), None),
        ),
        out_specs=P("member", "patch", None),
        check_vma=False,
    )
```

```python
import functools
import math

import jax
import jax.numpy as jnp
from jax import lax
from jax.experimental import pallas as pl
from jax.experimental.pallas import tpu as pltpu
from jax.sharding import PartitionSpec as P

STEPS = 2
COARSE = 0.35
DONE = 0.02
LARGE = 2e4
PART = 256
PADDING = 8
F32 = jnp.float32
BF16 = jnp.bfloat16


def pack_kernel(info, field_ref, flow_ref, first_ref, second_ref):
    members, rows, width = field_ref.shape
    even = info[2] == 0
    for place in range(STEPS):
        tail, head = field_ref[:, rows - STEPS + place, :], field_ref[:, place, :]
        at = pl.ds(place * members, members)
        first_ref[at, :] = jnp.where(even, tail, head)
        second_ref[at, :] = jnp.where(even, head, tail)
    head, tail = flow_ref[0], flow_ref[1]
    at = pl.ds(STEPS * members, 8)
    first_ref[at, :] = jnp.concatenate([jnp.where(even, tail, head)] * 2, axis=0)
    second_ref[at, :] = jnp.concatenate([jnp.where(even, head, tail)] * 2, axis=0)


def doubled(x):
    return jnp.concatenate([x, x], axis=1)


def weights_of(flow):
    row_flow, col_flow, kept, source = flow[0:1], flow[1:2], 1.0 - flow[2:3], flow[3:4]
    behind, ahead = jnp.maximum(row_flow, 0.0), -jnp.minimum(row_flow, 0.0)
    left, right = jnp.maximum(col_flow, 0.0), -jnp.minimum(col_flow, 0.0)
    stays = 1.0 - behind - ahead - left - right
    return [kept * stays, kept * behind, kept * ahead, kept * left, kept * right, source]


def advance(weights, emission, behind, field, ahead):
    width = field.shape[1]
    return (
        weights[0] * field
        + weights[1] * behind
        + weights[2] * ahead
        + weights[3] * pltpu.roll(field, 1, 1)
        + weights[4] * pltpu.roll(field, width - 1, 1)
        + emission * weights[5]
    )


def inner_kernel(targets, info, field_ref, flow_ref, member_ref, kept_ref, emission_ref, *refs):
    out_refs, (wide_ref, weight_ref) = refs[:-2], refs[-2:]
    members, rows, _ = field_ref.shape
    diagonal = lax.broadcasted_iota(jnp.int32, (members, members), 0) == lax.broadcasted_iota(
        jnp.int32, (members, members), 1
    )
    column = jnp.sum(jnp.where(diagonal, member_ref[...], 0.0), axis=1, keepdims=True)
    emission_ref[...] = jnp.broadcast_to(column, emission_ref.shape)
    emission = doubled(emission_ref[...])
    for row in range(1, rows - 1):
        weights = weights_of(flow_ref[:, row, :])
        for i, weight in enumerate(weights):
            weight_ref[row, pl.ds(i, 1), :] = weight
        wide_ref[row] = advance(
            weights, emission, field_ref[:, row - 1, :], field_ref[:, row, :], field_ref[:, row + 1, :]
        )
    for place, row in enumerate((1, 2, rows - 3, rows - 2)):
        kept_ref[place] = wide_ref[row]
    for out_ref, hops in zip(out_refs, targets):
        chip = sum(jnp.where(info[0] == source, to, 0) for source, to in hops)

        @pl.when(chip > 0)
        def _():
            for place in range(2):
                position = 2 * chip + jnp.abs(info[1] - 1 + place)
                row = position + info[2] * (rows - 1 - 2 * position)
                weights = weight_ref[row]
                out_ref[place] = advance(
                    [weights[i : i + 1] for i in range(6)],
                    emission, wide_ref[row - 1], wide_ref[row], wide_ref[row + 1],
                )


def end_rows(info, last, field_ref, flow_ref, emission_ref, kept_ref, halo_ref, out_ref):
    members, rows, width = field_ref.shape
    emission = doubled(emission_ref[...])

    def halo_row(place):
        return halo_ref[pl.ds(place * members, members), :]

    halo_weights = weights_of(halo_ref[pl.ds(STEPS * members, 4), :])
    for parity in range(2):

        @pl.when(info[2] == parity)
        def _():
            if parity == last:
                end, near, outside, beyond = 0, 1, halo_row(1), halo_row(0)
                inside, further = kept_ref[0], kept_ref[1]
            else:
                end, near, outside, beyond = rows - 1, rows - 2, halo_row(0), halo_row(1)
                inside, further = kept_ref[3], kept_ref[2]

            def ordered(weights, outer, own, inner):
                behind, ahead = (outer, inner) if end == 0 else (inner, outer)
                return advance(weights, emission, behind, own, ahead)

            end_weights = weights_of(flow_ref[:, end, :])
            end_field = field_ref[:, end, :]
            outer = ordered(halo_weights, beyond, outside, end_field)
            own = ordered(end_weights, outside, end_field, field_ref[:, near, :])
            out_ref[last] = ordered(end_weights, outer, own, inside)
            out_ref[1 - last] = ordered(weights_of(flow_ref[:, near, :]), own, inside, further)


def edge_kernel(info, field_ref, flow_ref, emission_ref, kept_ref, last_ref, first_ref, *refs):
    out_refs, scratch = refs[:-1], refs[-1]
    chips = len(out_refs)
    core = info[1]
    for last, halo_ref in enumerate((first_ref, last_ref)):
        end_rows(info, last, field_ref, flow_ref, emission_ref, kept_ref, halo_ref, scratch)
        for s, out_ref in enumerate(out_refs):

            @pl.when(info[0] == (chips - 1 - s if last else s))
            def _():
                out_ref[0] = scratch[1 - core]
                out_ref[1] = scratch[core]


def source_of(chip, chips, hops, k):
    inner = sum(jnp.where(chip == to, source, 0) for source, to in hops)
    return jnp.where(chip == 0, k, jnp.where(chip == chips - 1, chips - 1 - k, inner))


def collect_kernel(order, info, mine_ref, other_ref, *refs):
    chips = len(order)
    near_other, near_own, observed_ref = refs[-3:]
    step = near_other.shape[1]
    observed_ref[...] = jnp.where(info[2] == 1, other_ref[...], mine_ref[...])
    near_own[pl.ds(chips * step, PADDING), :] = jnp.zeros((PADDING, near_own.shape[1]), F32)
    chip = info[0]
    at_edge = jnp.logical_or(chip == 0, chip == chips - 1)
    for index, (s, k) in enumerate(order):
        block = source_of(chip, chips, s, k)
        rows = pl.ds(pl.multiple_of(block * step, step), step)
        for ref, here in ((refs[index], jnp.logical_not(at_edge)), (refs[chips + index], at_edge)):

            @pl.when(here)
            def _():
                near_other[block] = ref[0]
                near_own[rows, :] = ref[1]


def unpack_kernel(order, info, *refs):
    row_refs, (out_hbm, out_ref, sems) = refs[:-3], refs[-3:]
    members, rows, _ = out_ref.shape
    part = members // 4
    moves = []
    for index in range(4):
        some = pl.ds(index * part, part)
        for x, ref in zip(order, row_refs):
            position = (2 * info[0] + info[1]) ^ x
            row = position + info[2] * (rows - 1 - 2 * position)
            out_ref[some, pl.ds(row, 1), :] = ref[some, :][:, None, :]
        moves.append(pltpu.make_async_copy(out_ref.at[some], out_hbm.at[some], sems.at[index]))
        moves[-1].start()
    for move in moves:
        move.wait()


def pieces(x, count):
    parts = []
    for _ in range(count - 1):
        part = x.astype(BF16)
        parts.append(part)
        x = x - part.astype(F32)
    return parts + [x.astype(BF16)]


def dot(a, b):
    return lax.dot_general(a, b, (((1,), (0,)), ((), ())), preferred_element_type=F32)


def dot_t(a, b):
    return lax.dot_general(a, b, (((0,), (0,)), ((), ())), preferred_element_type=F32)


def product(a, b):
    total = None
    for i, left in enumerate(a):
        for j, right in enumerate(b):
            if i + j < max(len(a), len(b)):
                term = dot(left, right)
                total = term if total is None else total + term
    return total


def observations(info, observed_ref, width, root):
    slots = observed_ref.shape[1]
    cells, values, scales, count = (observed_ref[pl.ds(i, 1), :] for i in range(4))
    cells = cells.astype(jnp.int32)
    offset = sum((cells >= i * width).astype(jnp.int32) for i in (1, 2)) - 1
    column = cells - (offset + 1) * width
    side = offset * jnp.where(info[2] == 1, -1, 1) * (1 - 2 * info[1])
    cells = column + width * jnp.where(side == 0, 2, jnp.where(side < 0, 0, 1))
    active = lax.broadcasted_iota(jnp.int32, (1, slots), 1) < count.astype(jnp.int32)
    slot_weight = jnp.where(active, scales, 0.0)
    return cells, slot_weight, values, slot_weight * (1.0 / root)


def one_hot(cells, first, count):
    return (
        lax.broadcasted_iota(jnp.int32, (count, cells.shape[1]), 0) + first == cells
    ).astype(F32).astype(BF16)


def mean_of(blocks, members):
    total = blocks[0]
    for block in blocks[1:]:
        total = total + block
    return jnp.sum(total, axis=0, keepdims=True) * (1.0 / members)


def at_cells(row, chosen):
    parts = pieces(jnp.broadcast_to(row, (8, row.shape[1])), 3)
    return (dot(parts[0], chosen) + (dot(parts[1], chosen) + dot(parts[2], chosen)))[:1]


def prepare_kernel(
    info, observed_ref, near_other, near_own, far_other, far_own,
    spread_high, spread_low, own_high, own_low, own_part, seen_ref, direction_ref,
    anomaly, high_ref, low_ref,
):
    chips, step, width = near_other.shape
    members = 2 * chips * step
    cells, _, _, scale = observations(info, observed_ref, width, math.sqrt(members - 1))
    chosen = one_hot(cells, width, 2 * width)
    blocks = [pl.ds(index * step, step) for index in range(2 * chips)]
    means = []
    for place in range(2):
        columns = pl.ds(place * width, width)
        if place:
            rows = [near_own.at[block, :] for block in blocks[:chips]] + [far_own.at[chip] for chip in range(chips)]
        else:
            rows = [near_other.at[chip] for chip in range(chips)] + [far_other.at[block, :] for block in blocks[:chips]]
        means.append(mean_of([row[...] for row in rows], members))
        for block, row in zip(blocks, rows):
            part = row[...] - means[-1]
            anomaly[block, columns] = part
            high_ref[block, columns] = part.astype(BF16)

    def unit(x):
        return x * (1.0 / jnp.maximum(jnp.max(jnp.abs(x)), 1e-30))

    high = high_ref[...]
    along = lax.dot_general(high[:16], high, (((1,), (1,)), ((), ())), preferred_element_type=F32)
    rows = unit(dot(unit(along).astype(BF16), high))
    weight = jnp.sum(rows * rows[:1], axis=1, keepdims=True)
    weight = weight + jnp.where(jnp.max(jnp.abs(weight)) > 0.0, 0.0, 1.0)
    pattern = unit(jnp.sum(rows * weight, axis=0, keepdims=True))
    total = jnp.zeros((1, 1), F32)
    for block in blocks:
        along = jnp.sum(anomaly[block, :] * pattern, axis=1, keepdims=True)
        total = total + jnp.sum(along * along, axis=0, keepdims=True)
        direction_ref[block, :] = jnp.broadcast_to(along, (step, direction_ref.shape[1]))
    length = lax.rsqrt(jnp.maximum(total, 1e-30))
    taken = None
    for block in blocks:
        direction = direction_ref[block, :] * length
        direction_ref[block, :] = direction
        term = anomaly[block, :] * doubled(doubled(direction))
        taken = term if taken is None else taken + term
    taken = jnp.sum(taken, axis=0, keepdims=True)
    own_part[...] = jnp.broadcast_to(taken[:, width:], (own_part.shape[1], width)).T

    for block in blocks:
        rest = anomaly[block, :] - doubled(doubled(direction_ref[block, :])) * taken
        high, low = pieces(rest, 2)
        high_ref[block, :] = high
        low_ref[block, :] = low
        own = rest[:, width:].T
        own_high[:, block], own_low[:, block] = pieces(own, 2)
    seen_ref[pl.ds(0, 1), :] = at_cells(jnp.concatenate(means, axis=1), chosen)
    seen_ref[pl.ds(1, 1), :] = at_cells(taken, chosen)
    for first in range(0, members, PART):
        rows = pl.ds(first, PART)
        spread = (dot(high_ref[rows, :], chosen) + dot(low_ref[rows, :], chosen)) * scale
        high, low = pieces(spread, 2)
        spread_high[rows, :] = high
        spread_low[rows, :] = low


def square(parts):
    half = parts[0].shape[0] // 2
    upper = product([part[:half] for part in parts], parts)
    lower = product([part[half:] for part in parts], [part[:, half:] for part in parts])
    return upper, jnp.concatenate([upper[:, half:].T, lower], axis=1)


def at_border(info):
    chip, core, _, chips = info
    ends = jnp.logical_or(jnp.logical_and(chip == 0, core == 0), jnp.logical_and(chip == chips - 1, core == 1))
    return jnp.where(ends, 0, 1)


def shifted_spread(rows, blocks, direction_ref, shift, along, chosen, scale, high_in, low_in, high_out, low_out):
    total, taken = None, None
    step = rows[0].shape[0]
    for index, (row, block) in enumerate(zip(rows, blocks)):
        here = pl.ds(index * step, step)
        direction = doubled(direction_ref[block, :])
        rest = row[...] - shift - direction * along
        total = rest if total is None else total + rest
        taken = direction * rest if taken is None else taken + direction * rest
        high, low = pieces(rest, 2)
        high, low = pieces((dot(high, chosen) + dot(low, chosen)) * scale, 2)
        high_out[here, :] = high + high_in[block, :]
        low_out[here, :] = low + low_in[block, :]
    return jnp.sum(total, axis=0, keepdims=True), jnp.sum(taken, axis=0, keepdims=True)


def gram(high, low):
    turned = high.T
    cross = dot(turned, low)
    return dot(turned, high) + (cross + cross.T)


def middle_kernel(
    info, observed_ref, high_in, low_in, own_high, own_low, direction_ref, half_ref,
    high_ref, low_ref, gram_ref, right_ref, known_ref,
):
    chips = info[3]
    count, slots = high_ref.shape
    step = count // chips
    width = half_ref.shape[1]
    first = at_border(info) * count
    cells, _, _, scale = observations(info, observed_ref, width, math.sqrt(2 * count - 1))
    chosen = one_hot(cells, 0, width)
    rows = [half_ref.at[pl.ds(chip * step, step), :] for chip in range(chips)]
    blocks = [pl.ds(pl.multiple_of(first + chip * step, step), step) for chip in range(chips)]
    mean = mean_of([row[...] for row in rows], count)
    along, weight = None, None
    for row, block in zip(rows, blocks):
        direction = direction_ref[block, :]
        term = (row[...] - mean) * doubled(direction)
        along = term if along is None else along + term
        weight = direction * direction if weight is None else weight + direction * direction
    weight = doubled(jnp.sum(weight, axis=0, keepdims=True))
    along = jnp.sum(along, axis=0, keepdims=True) / jnp.maximum(weight, 0.1)
    total, taken = shifted_spread(
        rows, blocks, direction_ref, mean, along, chosen, scale, high_in, low_in, high_ref, low_ref
    )
    for index, known in enumerate((mean, along, total, taken)):
        known_ref[pl.ds(index, 1), :] = known
    high, low = high_ref[...], low_ref[...]
    gram_ref[...] = gram(high, low)
    members = pl.ds(pl.multiple_of(first, count), count)
    right_ref[...] = product([own_high[:, members], own_low[:, members]], [high, low])


def analysed_row(info, x, near_own, far_own, direction_ref, halves, rests, parts, sides):
    chips, step, _ = far_own.shape
    chip, mine = info[0] ^ (x // 2), x % 2
    rows = pl.ds(pl.multiple_of(chip * step, step), step)
    spread = [
        jnp.where(at_border(info) == mine, half[rows, :], rest[rows, :]) for half, rest in zip(halves, rests)
    ]
    block = pl.ds(pl.multiple_of((mine * chips + chip) * step, step), step)
    own = far_own[chip] if mine else near_own[rows, :]
    return own + sides[0:1] + product(spread, parts) + doubled(direction_ref[block, :]) * sides[1:2]


def others_kernel(
    order, info, near_own, far_own, direction_ref, high_half, low_half, high_rest, low_rest,
    solved_high, solved_low, sides_ref, *out_refs,
):
    parts = [solved_high[...], solved_low[...]]
    for x, out_ref in zip(order, out_refs):
        out_ref[...] = analysed_row(
            info, x, near_own, far_own, direction_ref, (high_half, low_half), (high_rest, low_rest), parts, sides_ref[...]
        )


def region_kernel(
    order, info, observed_ref, near_own, far_own, high_in, low_in, own_high, own_low, own_part, seen_ref,
    direction_ref, high_half, low_half, gram_half, right_half, known_ref, rest_ref, *refs,
):
    chips, step, width = far_own.shape
    high_rest, low_rest, solved_high, solved_low, sides_ref = refs[:5]
    out_refs, (factor, squared, answer) = refs[5:-3], refs[-3:]
    count = chips * step
    members = 2 * count
    slots = observed_ref.shape[1]
    root = math.sqrt(members - 1)
    part = at_border(info)
    first = (1 - part) * count
    cells, slot_weight, values, scale = observations(info, observed_ref, width, root)
    chosen = one_hot(cells, 0, width)
    shift, along, total, taken = (known_ref[pl.ds(index, 1), :] for index in range(4))
    more, further = shifted_spread(
        [rest_ref.at[chip] for chip in range(chips)],
        [pl.ds(pl.multiple_of(first + chip * step, step), step) for chip in range(chips)],
        direction_ref, shift, along, chosen, scale, high_in, low_in, high_rest, low_rest,
    )
    left = (total + more) * (1.0 / members)
    taken = taken + further
    seen_mean = seen_ref[pl.ds(0, 1), :] + at_cells(shift + left, chosen)
    left, taken_here = at_cells(left, chosen) * scale, at_cells(taken, chosen) * scale
    common = (seen_ref[pl.ds(1, 1), :] + at_cells(along + taken, chosen)) * scale
    innovation = slot_weight * (values - seen_mean)
    place = lax.broadcasted_iota(jnp.int32, (8, slots), 0)
    excess = jnp.where(place == 0, left * math.sqrt(members), jnp.where(place == 1, taken_here, 0.0))
    excess = pieces(excess, 2)

    eye = lax.broadcasted_iota(jnp.int32, (slots, slots), 0) == lax.broadcasted_iota(
        jnp.int32, (slots, slots), 1
    )
    high, low = high_rest[...], low_rest[...]
    over = dot_t(excess[0], excess[0]) + (dot_t(excess[0], excess[1]) + dot_t(excess[1], excess[0]))
    factor[...] = gram(high, low) + (gram_half[...] - over) + jnp.where(eye, 1.0, 0.0)
    rows = pl.ds(pl.multiple_of(first, count), count)
    answer[pl.ds(0, width), :] = right_half[...] + product([own_high[:, rows], own_low[:, rows]], [high, low])
    answer[pl.ds(width, 8), :] = jnp.where(
        lax.broadcasted_iota(jnp.int32, (8, slots), 0) == 0, jnp.broadcast_to(common, (8, slots)), 0.0
    )
    half = slots // 2
    upper, lower = pl.ds(0, half), pl.ds(half, half)

    def after(bound):
        return bound * bound / (2.0 - bound * bound)

    def size(matrix):
        return jnp.sum(jnp.sum(matrix * matrix, axis=0, keepdims=True))

    def begin(count):
        parts = pieces(factor[...], count)
        if count > 2:
            squared[upper, :], squared[lower, :] = square(parts)
        bound = 1.0 - start
        gain = 2.0 / (2.0 - bound * bound)
        answer[...] = (gain * start) * (2.0 * answer[...] - start * product(pieces(answer[...], count), parts))
        factor[...] = (gain * start) * (2.0 * factor[...] - start * squared[...])
        return after(bound)

    def refine(bound, count):
        gain = 2.0 / (2.0 - bound * bound)
        parts = pieces(factor[...], count)
        answer[...] = gain * (2.0 * answer[...] - product(pieces(answer[...], count), parts))
        top, bottom = square(parts)
        factor[upper, :] = gain * (2.0 * factor[upper, :] - top)
        factor[lower, :] = gain * (2.0 * factor[lower, :] - bottom)
        return after(bound)

    def close(bound, rest):
        gain = 2.0 / (2.0 - bound * bound)
        answer[...] = gain * (answer[...] + dot(answer[...].astype(BF16), rest))
        return gain

    def finish(bound):
        rest = factor[...].astype(BF16)
        gain = close(bound, rest)
        factor[...] = gain * (dot(rest, rest) - jnp.where(eye, 0.5 * bound * bound, 0.0))
        return after(bound)

    top, bottom = square(pieces(factor[...], 2))
    squared[upper, :] = top
    squared[lower, :] = bottom
    limit = 1.0001 * jnp.sqrt(jnp.sqrt(size(top) + size(bottom)))
    start = 2.0 / (1.0 + limit)
    large = limit > LARGE
    bound = lax.cond(large, lambda: begin(3), lambda: begin(2))
    bound = lax.while_loop(lambda b: jnp.logical_and(b > COARSE, large), lambda b: refine(b, 3), bound)
    bound = lax.while_loop(lambda b: b > COARSE, lambda b: refine(b, 2), bound)
    factor[...] = jnp.where(eye, 1.0, 0.0) - factor[...]
    bound = lax.while_loop(lambda b: b > DONE, finish, bound)
    close(bound, factor[...].astype(BF16))

    solved = answer[pl.ds(0, width), :]
    alone = answer[pl.ds(width, 1), :]
    share = own_part[:, :1] - jnp.sum(solved * common, axis=1, keepdims=True)
    solved = solved + (share / (1.0 + jnp.sum(common * alone, axis=1, keepdims=True))) * alone
    solved = solved.T
    which = lax.broadcasted_iota(jnp.int32, (8, slots), 0)
    sides = jnp.where(
        which == 0, innovation * (1.0 / root) + 0.5 * left, jnp.where(which == 1, 0.5 * (taken_here - common), 0.0)
    )
    parts = pieces(solved, 2)
    sides = product(pieces(sides, 2), parts)
    parts = [part * jnp.asarray(-0.5, BF16) for part in parts]
    sides_ref[...] = sides
    solved_high[...], solved_low[...] = parts
    for x, out_ref in zip(order, out_refs):
        out_ref[...] = analysed_row(
            info, x, near_own, far_own, direction_ref, (high_half, low_half), (high_rest, low_rest), parts, sides
        )


VMEM = pl.BlockSpec(memory_space=pltpu.VMEM)


def position():
    lane, patch = lax.axis_index("member"), lax.axis_index("patch")
    return lax.div(lane, 2), lax.rem(lane, 2), lax.rem(patch, 2), lax.axis_size("member") // 2


def call(kernel, name, out_shape, args, scratch=(), flops=None, limit=8, out=VMEM):
    several = isinstance(out_shape, (list, tuple))
    return pl.pallas_call(
        lambda *refs: kernel(position(), *refs),
        out_shape=out_shape,
        in_specs=[VMEM] * len(args),
        out_specs=[out] * len(out_shape) if several else out,
        scratch_shapes=scratch,
        compiler_params=pltpu.CompilerParams(vmem_limit_bytes=limit * 1024 * 1024),
        cost_estimate=flops and pl.CostEstimate(flops=flops, bytes_accessed=0, transcendentals=0),
        name=name,
    )(*args)


def bfloat(*shape):
    return jax.ShapeDtypeStruct(shape, BF16)


def array(*shape):
    return jax.ShapeDtypeStruct(shape, F32)


def per_device(
    init_field, flow_fields, emission, observed_cell, observed_count, observed_value, observed_scale
):
    step, rows, width = init_field.shape
    slots = observed_cell.shape[1]
    patches, lanes = lax.axis_size("patch"), lax.axis_size("member")
    chips = lanes // 2
    members = lanes * step
    axes = ("patch", "member")
    count = patches * lanes

    edge = array(STEPS * step + 8, width)
    flow_edges = jnp.stack([flow_fields[:, 0], flow_fields[:, rows - 1]]) * 1.0
    to_last, to_first = call(pack_kernel, "pack", [edge, edge], [init_field, flow_edges], limit=32)

    def swap(message, start):
        lower = range(start, patches - 1, 2)
        return lax.ppermute(message, "patch", [(p, p + 1) for p in lower] + [(p + 1, p) for p in lower])

    halo_last, halo_first = swap(to_last, 0), swap(to_first, 1)

    mine = jnp.concatenate(
        [
            observed_cell.astype(F32),
            observed_value,
            observed_scale,
            jnp.broadcast_to(observed_count.astype(F32)[:, None], observed_cell.shape),
        ]
        * 2,
        axis=0,
    )

    def between(message, hops):
        return lax.ppermute(message, "member", [(2 * a + core, 2 * b + core) for a, b in hops for core in range(2)])

    mirrored = [
        [hop for to in range(1, chips // 2) for hop in (((to + s) % chips, to), (chips - 1 - (to + s) % chips, chips - 1 - to))]
        for s in range(chips)
    ]
    turning = [[((to - s) % chips, to) for to in range(1, chips - 1)] for s in range(chips)]
    single = all(len({source for source, _ in hops}) == len(hops) for hops in mirrored)
    targets = mirrored if single else turning
    pair = array(2, step, width)
    kept, emitted, *inner = call(
        functools.partial(inner_kernel, targets), "inner",
        [array(4, step, width), array(step, width // 2)] + [pair] * chips,
        [init_field, flow_fields, emission[None, :]],
        [pltpu.VMEM((rows, step, width), F32), pltpu.VMEM((rows, 8, width), F32)], limit=32,
    )
    got_inner = [inner[0]] + [between(inner[s], targets[s]) for s in range(1, chips)]
    outer = call(
        edge_kernel, "edge", [pair] * chips, [init_field, flow_fields, emitted, kept, halo_last, halo_first],
        [pltpu.VMEM((2, step, width), F32)], limit=32,
    )
    got_outer = [outer[0]] + [
        between(outer[s], [(s, 0), (chips - 1 - s, chips - 1)]) for s in range(1, chips)
    ]
    order = [(targets[s], s) for s in range(chips)]
    pieces_in = got_inner + got_outer
    mine, _ = lax.optimization_barrier((mine, outer[0]))
    other = lax.ppermute(
        mine, axes,
        [(p * lanes + i, p * lanes + lanes - 1 - i) for p in range(1, patches, 2) for i in range(lanes)],
    )

    def device(p, chip, core):
        return p * lanes + 2 * chip + core

    borders, siblings = [], []
    for p in range(patches):
        for chip in range(chips):
            for core, away in ((0, -1), (1, 1)):
                siblings.append((device(p, chip, core), device(p, chip, 1 - core)))
                if 0 <= chip + away < chips:
                    borders.append((device(p, chip, core), device(p, chip + away, 1 - core)))
                else:
                    to = p + 1 if (p % 2 == 0) == (away == 1) else p - 1
                    if 0 <= to < patches:
                        borders.append((device(p, chip, core), device(to, chip, core)))

    half = array(chips, step, width)
    near_other, near_own, observed = call(
        functools.partial(collect_kernel, order), "collect",
        [half, array(chips * step + PADDING, width), array(8, slots)], [mine, other] + pieces_in,
    )
    far_own = lax.ppermute(near_other, axes, siblings)
    got_half = lax.ppermute(near_own, axes, borders)
    far_other = lax.ppermute(near_own, axes, siblings)
    got_rest = lax.ppermute(far_own, axes, borders)

    prepared = call(
        prepare_kernel, "prepare",
        [bfloat(members, slots)] * 2 + [bfloat(width, members)] * 2
        + [array(width, width // 2), array(8, slots), array(members, width // 2)],
        [observed, near_other, near_own, far_other, far_own],
        [pltpu.VMEM((members, 2 * width), F32)] + [pltpu.VMEM((members, 2 * width), BF16)] * 2,
        flops=8 * members * slots * width, limit=20,
    )
    halves = members // 2
    middle = call(
        middle_kernel, "middle",
        [bfloat(halves, slots)] * 2 + [array(slots, slots), array(width, slots), array(8, width)],
        [observed, *prepared[:4], prepared[6], got_half],
        flops=10 * halves * slots * slots, limit=20,
    )
    order = sorted(range(lanes), key=lambda x: (x.bit_length() != lanes.bit_length() - 1, -x))
    row = array(step, width)
    *shared, first, second = call(
        functools.partial(region_kernel, order[:2]), "region",
        [bfloat(halves, slots)] * 2 + [bfloat(slots, width)] * 2 + [array(8, width)] + [row] * 2,
        [observed, near_own, far_own, *prepared, *middle, got_rest],
        [pltpu.VMEM((slots, slots), F32)] * 2 + [pltpu.VMEM((width + 8, slots), F32)],
        limit=24,
    )
    others = call(
        functools.partial(others_kernel, order[2:]), "others", [row] * (lanes - 2),
        [near_own, far_own, prepared[6], *middle[:2], *shared],
        flops=6 * members * slots * width, limit=16,
    )
    analysed = dict(zip(order, [first, second, *others]))

    def swapped(x):
        return lax.ppermute(analysed[x], "member", [(i, i ^ x) for i in range(lanes)]) if x else analysed[0]

    return call(
        functools.partial(unpack_kernel, order), "unpack", array(step, rows, width),
        [swapped(x) for x in order], [pltpu.VMEM((step, rows, width), F32), pltpu.SemaphoreType.DMA((4,))],
        limit=48, out=pl.BlockSpec(memory_space=pltpu.HBM),
    )


def solution(mesh):
    return jax.shard_map(
        per_device,
        mesh=mesh,
        in_specs=(
            P("member", "patch", None),
            P(None, "patch", None),
            P("member"),
            P(("patch", "member"), None),
            P(("patch", "member")),
            P(("patch", "member"), None),
            P(("patch", "member"), None),
        ),
        out_specs=P("member", "patch", None),
        check_vma=False,
    )
```

```python
import functools
import math

import jax
import jax.numpy as jnp
from jax import lax
from jax.experimental import pallas as pl
from jax.experimental.pallas import tpu as pltpu
from jax.sharding import PartitionSpec as P

STEPS = 2
COARSE = 0.35
DONE = 0.03
LARGE = 2e4
PART = 256
PADDING = 8
F32 = jnp.float32
BF16 = jnp.bfloat16


def pack_kernel(info, field_ref, flow_ref, first_ref, second_ref):
    members, rows, width = field_ref.shape
    even = info[2] == 0
    for place in range(STEPS):
        tail, head = field_ref[:, rows - STEPS + place, :], field_ref[:, place, :]
        at = pl.ds(place * members, members)
        first_ref[at, :] = jnp.where(even, tail, head)
        second_ref[at, :] = jnp.where(even, head, tail)
    tail, head = flow_ref[:, rows - 1, :], flow_ref[:, 0, :]
    at = pl.ds(STEPS * members, 8)
    first_ref[at, :] = jnp.concatenate([jnp.where(even, tail, head)] * 2, axis=0)
    second_ref[at, :] = jnp.concatenate([jnp.where(even, head, tail)] * 2, axis=0)


def doubled(x):
    return jnp.concatenate([x, x], axis=1)


def weights_of(flow):
    row_flow, col_flow, kept, source = flow[0:1], flow[1:2], 1.0 - flow[2:3], flow[3:4]
    behind, ahead = jnp.maximum(row_flow, 0.0), -jnp.minimum(row_flow, 0.0)
    left, right = jnp.maximum(col_flow, 0.0), -jnp.minimum(col_flow, 0.0)
    stays = 1.0 - behind - ahead - left - right
    return [kept * stays, kept * behind, kept * ahead, kept * left, kept * right, source]


def advance(weights, emission, behind, field, ahead):
    width = field.shape[1]
    return (
        weights[0] * field
        + weights[1] * behind
        + weights[2] * ahead
        + weights[3] * pltpu.roll(field, 1, 1)
        + weights[4] * pltpu.roll(field, width - 1, 1)
        + emission * weights[5]
    )


def inner_kernel(targets, info, field_ref, flow_ref, member_ref, kept_ref, emission_ref, *refs):
    out_refs, (wide_ref, weight_ref) = refs[:-2], refs[-2:]
    members, rows, _ = field_ref.shape
    diagonal = lax.broadcasted_iota(jnp.int32, (members, members), 0) == lax.broadcasted_iota(
        jnp.int32, (members, members), 1
    )
    column = jnp.sum(jnp.where(diagonal, member_ref[...], 0.0), axis=1, keepdims=True)
    emission_ref[...] = jnp.broadcast_to(column, emission_ref.shape)
    emission = doubled(emission_ref[...])
    for row in range(1, rows - 1):
        weights = weights_of(flow_ref[:, row, :])
        for i, weight in enumerate(weights):
            weight_ref[row, pl.ds(i, 1), :] = weight
        wide_ref[row] = advance(
            weights, emission, field_ref[:, row - 1, :], field_ref[:, row, :], field_ref[:, row + 1, :]
        )
    for place, row in enumerate((1, 2, rows - 3, rows - 2)):
        kept_ref[place] = wide_ref[row]
    for out_ref, hops in zip(out_refs, targets):
        chip = sum(jnp.where(info[0] == source, to, 0) for source, to in hops)

        @pl.when(chip > 0)
        def _():
            for place in range(2):
                position = 2 * chip + jnp.abs(info[1] - 1 + place)
                row = position + info[2] * (rows - 1 - 2 * position)
                weights = weight_ref[row]
                out_ref[place] = advance(
                    [weights[i : i + 1] for i in range(6)],
                    emission, wide_ref[row - 1], wide_ref[row], wide_ref[row + 1],
                )


def end_rows(info, last, field_ref, flow_ref, emission_ref, kept_ref, halo_ref, out_ref):
    members, rows, width = field_ref.shape
    emission = doubled(emission_ref[...])

    def halo_row(place):
        return halo_ref[pl.ds(place * members, members), :]

    halo_weights = weights_of(halo_ref[pl.ds(STEPS * members, 4), :])
    for parity in range(2):

        @pl.when(info[2] == parity)
        def _():
            if parity == last:
                end, near, outside, beyond = 0, 1, halo_row(1), halo_row(0)
                inside, further = kept_ref[0], kept_ref[1]
            else:
                end, near, outside, beyond = rows - 1, rows - 2, halo_row(0), halo_row(1)
                inside, further = kept_ref[3], kept_ref[2]

            def ordered(weights, outer, own, inner):
                behind, ahead = (outer, inner) if end == 0 else (inner, outer)
                return advance(weights, emission, behind, own, ahead)

            end_weights = weights_of(flow_ref[:, end, :])
            end_field = field_ref[:, end, :]
            outer = ordered(halo_weights, beyond, outside, end_field)
            own = ordered(end_weights, outside, end_field, field_ref[:, near, :])
            out_ref[last] = ordered(end_weights, outer, own, inside)
            out_ref[1 - last] = ordered(weights_of(flow_ref[:, near, :]), own, inside, further)


def edge_kernel(info, field_ref, flow_ref, emission_ref, kept_ref, last_ref, first_ref, *refs):
    out_refs, scratch = refs[:-1], refs[-1]
    chips = len(out_refs)
    core = info[1]
    for last, halo_ref in enumerate((first_ref, last_ref)):
        end_rows(info, last, field_ref, flow_ref, emission_ref, kept_ref, halo_ref, scratch)
        for s, out_ref in enumerate(out_refs):

            @pl.when(info[0] == (chips - 1 - s if last else s))
            def _():
                out_ref[0] = scratch[1 - core]
                out_ref[1] = scratch[core]


def source_of(chip, chips, hops, k):
    inner = sum(jnp.where(chip == to, source, 0) for source, to in hops)
    return jnp.where(chip == 0, k, jnp.where(chip == chips - 1, chips - 1 - k, inner))


def collect_kernel(order, info, mine_ref, other_ref, *refs):
    chips = len(order)
    near_other, near_own, observed_ref = refs[-3:]
    step = near_other.shape[1]
    observed_ref[...] = jnp.where(info[2] == 1, other_ref[...], mine_ref[...])
    near_own[pl.ds(chips * step, PADDING), :] = jnp.zeros((PADDING, near_own.shape[1]), F32)
    chip = info[0]
    at_edge = jnp.logical_or(chip == 0, chip == chips - 1)
    for index, (s, k) in enumerate(order):
        block = source_of(chip, chips, s, k)
        rows = pl.ds(pl.multiple_of(block * step, step), step)
        for ref, here in ((refs[index], jnp.logical_not(at_edge)), (refs[chips + index], at_edge)):

            @pl.when(here)
            def _():
                near_other[block] = ref[0]
                near_own[rows, :] = ref[1]


def unpack_kernel(order, info, *refs):
    row_refs, (out_hbm, out_ref, sems) = refs[:-3], refs[-3:]
    members, rows, _ = out_ref.shape
    part = members // 4
    moves = []
    for index in range(4):
        some = pl.ds(index * part, part)
        for x, ref in zip(order, row_refs):
            position = (2 * info[0] + info[1]) ^ x
            row = position + info[2] * (rows - 1 - 2 * position)
            out_ref[some, pl.ds(row, 1), :] = ref[some, :][:, None, :]
        moves.append(pltpu.make_async_copy(out_ref.at[some], out_hbm.at[some], sems.at[index]))
        moves[-1].start()
    for move in moves:
        move.wait()


def pieces(x, count):
    parts = []
    for _ in range(count - 1):
        part = x.astype(BF16)
        parts.append(part)
        x = x - part.astype(F32)
    return parts + [x.astype(BF16)]


def dot(a, b):
    return lax.dot_general(a, b, (((1,), (0,)), ((), ())), preferred_element_type=F32)


def dot_t(a, b):
    return lax.dot_general(a, b, (((0,), (0,)), ((), ())), preferred_element_type=F32)


def product(a, b):
    total = None
    for i, left in enumerate(a):
        for j, right in enumerate(b):
            if i + j < max(len(a), len(b)):
                term = dot(left, right)
                total = term if total is None else total + term
    return total


def observations(info, observed_ref, width, root):
    slots = observed_ref.shape[1]
    cells, values, scales, count = (observed_ref[pl.ds(i, 1), :] for i in range(4))
    cells = cells.astype(jnp.int32)
    offset = sum((cells >= i * width).astype(jnp.int32) for i in (1, 2)) - 1
    column = cells - (offset + 1) * width
    side = offset * jnp.where(info[2] == 1, -1, 1) * (1 - 2 * info[1])
    cells = column + width * jnp.where(side == 0, 2, jnp.where(side < 0, 0, 1))
    active = lax.broadcasted_iota(jnp.int32, (1, slots), 1) < count.astype(jnp.int32)
    slot_weight = jnp.where(active, scales, 0.0)
    return cells, slot_weight, values, slot_weight * (1.0 / root)


def one_hot(cells, first, count):
    return (
        lax.broadcasted_iota(jnp.int32, (count, cells.shape[1]), 0) + first == cells
    ).astype(F32).astype(BF16)


def mean_of(blocks, members):
    total = blocks[0]
    for block in blocks[1:]:
        total = total + block
    return jnp.sum(total, axis=0, keepdims=True) * (1.0 / members)


def at_cells(row, chosen):
    parts = pieces(jnp.broadcast_to(row, (8, row.shape[1])), 3)
    return (dot(parts[0], chosen) + (dot(parts[1], chosen) + dot(parts[2], chosen)))[:1]


def prepare_kernel(
    info, observed_ref, near_other, near_own, far_other, far_own,
    spread_high, spread_low, own_high, own_low, own_part, seen_ref, direction_ref,
    anomaly, high_ref, low_ref,
):
    chips, step, width = near_other.shape
    members = 2 * chips * step
    cells, _, _, scale = observations(info, observed_ref, width, math.sqrt(members - 1))
    chosen = one_hot(cells, width, 2 * width)
    blocks = [pl.ds(index * step, step) for index in range(2 * chips)]
    means = []
    for place in range(2):
        columns = pl.ds(place * width, width)
        if place:
            rows = [near_own.at[block, :] for block in blocks[:chips]] + [far_own.at[chip] for chip in range(chips)]
        else:
            rows = [near_other.at[chip] for chip in range(chips)] + [far_other.at[block, :] for block in blocks[:chips]]
        means.append(mean_of([row[...] for row in rows], members))
        for block, row in zip(blocks, rows):
            part = row[...] - means[-1]
            anomaly[block, columns] = part
            high_ref[block, columns] = part.astype(BF16)

    def unit(x):
        return x * (1.0 / jnp.maximum(jnp.max(jnp.abs(x)), 1e-30))

    high = high_ref[...]
    along = lax.dot_general(high[:16], high, (((1,), (1,)), ((), ())), preferred_element_type=F32)
    rows = unit(dot(unit(along).astype(BF16), high))
    weight = jnp.sum(rows * rows[:1], axis=1, keepdims=True)
    weight = weight + jnp.where(jnp.max(jnp.abs(weight)) > 0.0, 0.0, 1.0)
    pattern = unit(jnp.sum(rows * weight, axis=0, keepdims=True))
    total = jnp.zeros((1, 1), F32)
    for block in blocks:
        along = jnp.sum(anomaly[block, :] * pattern, axis=1, keepdims=True)
        total = total + jnp.sum(along * along, axis=0, keepdims=True)
        direction_ref[block, :] = jnp.broadcast_to(along, (step, direction_ref.shape[1]))
    length = lax.rsqrt(jnp.maximum(total, 1e-30))
    taken = None
    for block in blocks:
        direction = direction_ref[block, :] * length
        direction_ref[block, :] = direction
        term = anomaly[block, :] * doubled(doubled(direction))
        taken = term if taken is None else taken + term
    taken = jnp.sum(taken, axis=0, keepdims=True)
    own_part[...] = jnp.broadcast_to(taken[:, width:], (own_part.shape[1], width)).T

    for block in blocks:
        rest = anomaly[block, :] - doubled(doubled(direction_ref[block, :])) * taken
        high, low = pieces(rest, 2)
        high_ref[block, :] = high
        low_ref[block, :] = low
        own = rest[:, width:].T
        own_high[:, block], own_low[:, block] = pieces(own, 2)
    seen_ref[pl.ds(0, 1), :] = at_cells(jnp.concatenate(means, axis=1), chosen)
    seen_ref[pl.ds(1, 1), :] = at_cells(taken, chosen)
    for first in range(0, members, PART):
        rows = pl.ds(first, PART)
        spread = (dot(high_ref[rows, :], chosen) + dot(low_ref[rows, :], chosen)) * scale
        high, low = pieces(spread, 2)
        spread_high[rows, :] = high
        spread_low[rows, :] = low


def square(parts):
    half = parts[0].shape[0] // 2
    upper = product([part[:half] for part in parts], parts)
    lower = product([part[half:] for part in parts], [part[:, half:] for part in parts])
    return upper, jnp.concatenate([upper[:, half:].T, lower], axis=1)


def at_border(info):
    chip, core, _, chips = info
    ends = jnp.logical_or(jnp.logical_and(chip == 0, core == 0), jnp.logical_and(chip == chips - 1, core == 1))
    return jnp.where(ends, 0, 1)


def shifted_spread(rows, blocks, direction_ref, shift, along, chosen, scale, high_in, low_in, high_out, low_out):
    total, taken = None, None
    step = rows[0].shape[0]
    for index, (row, block) in enumerate(zip(rows, blocks)):
        here = pl.ds(index * step, step)
        direction = doubled(direction_ref[block, :])
        rest = row[...] - shift - direction * along
        total = rest if total is None else total + rest
        taken = direction * rest if taken is None else taken + direction * rest
        high, low = pieces(rest, 2)
        high, low = pieces((dot(high, chosen) + dot(low, chosen)) * scale, 2)
        high_out[here, :] = high + high_in[block, :]
        low_out[here, :] = low + low_in[block, :]
    return jnp.sum(total, axis=0, keepdims=True), jnp.sum(taken, axis=0, keepdims=True)


def gram(high, low):
    turned = high.T
    cross = dot(turned, low)
    return dot(turned, high) + (cross + cross.T)


def middle_kernel(
    info, observed_ref, high_in, low_in, own_high, own_low, direction_ref, half_ref,
    high_ref, low_ref, gram_ref, right_ref, known_ref,
):
    chips = info[3]
    count, slots = high_ref.shape
    step = count // chips
    width = half_ref.shape[1]
    first = at_border(info) * count
    cells, _, _, scale = observations(info, observed_ref, width, math.sqrt(2 * count - 1))
    chosen = one_hot(cells, 0, width)
    rows = [half_ref.at[pl.ds(chip * step, step), :] for chip in range(chips)]
    blocks = [pl.ds(pl.multiple_of(first + chip * step, step), step) for chip in range(chips)]
    mean = mean_of([row[...] for row in rows], count)
    along, weight = None, None
    for row, block in zip(rows, blocks):
        direction = direction_ref[block, :]
        term = (row[...] - mean) * doubled(direction)
        along = term if along is None else along + term
        weight = direction * direction if weight is None else weight + direction * direction
    weight = doubled(jnp.sum(weight, axis=0, keepdims=True))
    along = jnp.sum(along, axis=0, keepdims=True) / jnp.maximum(weight, 0.1)
    total, taken = shifted_spread(
        rows, blocks, direction_ref, mean, along, chosen, scale, high_in, low_in, high_ref, low_ref
    )
    for index, known in enumerate((mean, along, total, taken)):
        known_ref[pl.ds(index, 1), :] = known
    high, low = high_ref[...], low_ref[...]
    gram_ref[...] = gram(high, low)
    members = pl.ds(pl.multiple_of(first, count), count)
    right_ref[...] = product([own_high[:, members], own_low[:, members]], [high, low])


def analysed_row(info, x, near_own, far_own, direction_ref, halves, rests, parts, sides):
    chips, step, _ = far_own.shape
    chip, mine = info[0] ^ (x // 2), x % 2
    rows = pl.ds(pl.multiple_of(chip * step, step), step)
    spread = [
        jnp.where(at_border(info) == mine, half[rows, :], rest[rows, :]) for half, rest in zip(halves, rests)
    ]
    block = pl.ds(pl.multiple_of((mine * chips + chip) * step, step), step)
    own = far_own[chip] if mine else near_own[rows, :]
    return own + sides[0:1] + product(spread, parts) + doubled(direction_ref[block, :]) * sides[1:2]


def others_kernel(
    order, info, near_own, far_own, direction_ref, high_half, low_half, high_rest, low_rest,
    solved_high, solved_low, sides_ref, *out_refs,
):
    parts = [solved_high[...], solved_low[...]]
    for x, out_ref in zip(order, out_refs):
        out_ref[...] = analysed_row(
            info, x, near_own, far_own, direction_ref, (high_half, low_half), (high_rest, low_rest), parts, sides_ref[...]
        )


def region_kernel(
    order, info, observed_ref, near_own, far_own, high_in, low_in, own_high, own_low, own_part, seen_ref,
    direction_ref, high_half, low_half, gram_half, right_half, known_ref, rest_ref, *refs,
):
    chips, step, width = far_own.shape
    high_rest, low_rest, solved_high, solved_low, sides_ref = refs[:5]
    out_refs, (factor, squared, answer) = refs[5:-3], refs[-3:]
    count = chips * step
    members = 2 * count
    slots = observed_ref.shape[1]
    root = math.sqrt(members - 1)
    part = at_border(info)
    first = (1 - part) * count
    cells, slot_weight, values, scale = observations(info, observed_ref, width, root)
    chosen = one_hot(cells, 0, width)
    shift, along, total, taken = (known_ref[pl.ds(index, 1), :] for index in range(4))
    more, further = shifted_spread(
        [rest_ref.at[chip] for chip in range(chips)],
        [pl.ds(pl.multiple_of(first + chip * step, step), step) for chip in range(chips)],
        direction_ref, shift, along, chosen, scale, high_in, low_in, high_rest, low_rest,
    )
    left = (total + more) * (1.0 / members)
    taken = taken + further
    seen_mean = seen_ref[pl.ds(0, 1), :] + at_cells(shift + left, chosen)
    left, taken_here = at_cells(left, chosen) * scale, at_cells(taken, chosen) * scale
    common = (seen_ref[pl.ds(1, 1), :] + at_cells(along + taken, chosen)) * scale
    innovation = slot_weight * (values - seen_mean)
    place = lax.broadcasted_iota(jnp.int32, (8, slots), 0)
    excess = jnp.where(place == 0, left * math.sqrt(members), jnp.where(place == 1, taken_here, 0.0))
    excess = pieces(excess, 2)

    eye = lax.broadcasted_iota(jnp.int32, (slots, slots), 0) == lax.broadcasted_iota(
        jnp.int32, (slots, slots), 1
    )
    high, low = high_rest[...], low_rest[...]
    over = dot_t(excess[0], excess[0]) + (dot_t(excess[0], excess[1]) + dot_t(excess[1], excess[0]))
    factor[...] = gram(high, low) + (gram_half[...] - over) + jnp.where(eye, 1.0, 0.0)
    rows = pl.ds(pl.multiple_of(first, count), count)
    answer[pl.ds(0, width), :] = right_half[...] + product([own_high[:, rows], own_low[:, rows]], [high, low])
    answer[pl.ds(width, 8), :] = jnp.where(
        lax.broadcasted_iota(jnp.int32, (8, slots), 0) == 0, jnp.broadcast_to(common, (8, slots)), 0.0
    )
    half = slots // 2
    upper, lower = pl.ds(0, half), pl.ds(half, half)

    def after(bound):
        return bound * bound / (2.0 - bound * bound)

    def size(matrix):
        return jnp.sum(jnp.sum(matrix * matrix, axis=0, keepdims=True))

    def begin(parts, count):
        if count > 2:
            squared[upper, :], squared[lower, :] = square(parts)
        bound = 1.0 - start
        gain = 2.0 / (2.0 - bound * bound)
        answer[...] = (gain * start) * (2.0 * answer[...] - start * product(pieces(answer[...], count), parts))
        factor[...] = (gain * start) * (2.0 * factor[...] - start * squared[...])
        return after(bound)

    def refine(bound, count):
        gain = 2.0 / (2.0 - bound * bound)
        parts = pieces(factor[...], count)
        answer[...] = gain * (2.0 * answer[...] - product(pieces(answer[...], count), parts))
        top, bottom = square(parts)
        factor[upper, :] = gain * (2.0 * factor[upper, :] - top)
        factor[lower, :] = gain * (2.0 * factor[lower, :] - bottom)
        return after(bound)

    def close(bound, rest):
        gain = 2.0 / (2.0 - bound * bound)
        answer[...] = gain * (answer[...] + dot(answer[...].astype(BF16), rest))
        return gain

    def finish(bound):
        rest = factor[...].astype(BF16)
        gain = close(bound, rest)
        factor[...] = gain * (dot(rest, rest) - jnp.where(eye, 0.5 * bound * bound, 0.0))
        return after(bound)

    parts = pieces(factor[...], 2)
    top, bottom = square(parts)
    squared[upper, :] = top
    squared[lower, :] = bottom
    limit = 1.0001 * jnp.sqrt(jnp.sqrt(size(top) + size(bottom)))
    start = 2.0 / (1.0 + limit)
    large = limit > LARGE
    bound = lax.cond(large, lambda: begin(pieces(factor[...], 3), 3), lambda: begin(parts, 2))
    bound = lax.while_loop(lambda b: jnp.logical_and(b > COARSE, large), lambda b: refine(b, 3), bound)
    bound = lax.while_loop(lambda b: b > COARSE, lambda b: refine(b, 2), bound)
    factor[...] = jnp.where(eye, 1.0, 0.0) - factor[...]
    bound = lax.while_loop(lambda b: b > DONE, finish, bound)
    close(bound, factor[...].astype(BF16))

    solved = answer[pl.ds(0, width), :]
    alone = answer[pl.ds(width, 1), :]
    share = own_part[:, :1] - jnp.sum(solved * common, axis=1, keepdims=True)
    solved = solved + (share / (1.0 + jnp.sum(common * alone, axis=1, keepdims=True))) * alone
    solved = solved.T
    which = lax.broadcasted_iota(jnp.int32, (8, slots), 0)
    sides = jnp.where(
        which == 0, innovation * (1.0 / root) + 0.5 * left, jnp.where(which == 1, 0.5 * (taken_here - common), 0.0)
    )
    parts = pieces(solved, 2)
    sides = product(pieces(sides, 2), parts)
    parts = [part * jnp.asarray(-0.5, BF16) for part in parts]
    sides_ref[...] = sides
    solved_high[...], solved_low[...] = parts
    for x, out_ref in zip(order, out_refs):
        out_ref[...] = analysed_row(
            info, x, near_own, far_own, direction_ref, (high_half, low_half), (high_rest, low_rest), parts, sides
        )


VMEM = pl.BlockSpec(memory_space=pltpu.VMEM)


def position():
    lane, patch = lax.axis_index("member"), lax.axis_index("patch")
    return lax.div(lane, 2), lax.rem(lane, 2), lax.rem(patch, 2), lax.axis_size("member") // 2


def call(kernel, name, out_shape, args, scratch=(), flops=None, limit=8, out=VMEM):
    several = isinstance(out_shape, (list, tuple))
    return pl.pallas_call(
        lambda *refs: kernel(position(), *refs),
        out_shape=out_shape,
        in_specs=[VMEM] * len(args),
        out_specs=[out] * len(out_shape) if several else out,
        scratch_shapes=scratch,
        compiler_params=pltpu.CompilerParams(vmem_limit_bytes=limit * 1024 * 1024),
        cost_estimate=flops and pl.CostEstimate(flops=flops, bytes_accessed=0, transcendentals=0),
        name=name,
    )(*args)


def bfloat(*shape):
    return jax.ShapeDtypeStruct(shape, BF16)


def array(*shape):
    return jax.ShapeDtypeStruct(shape, F32)


def per_device(
    init_field, flow_fields, emission, observed_cell, observed_count, observed_value, observed_scale
):
    step, rows, width = init_field.shape
    slots = observed_cell.shape[1]
    patches, lanes = lax.axis_size("patch"), lax.axis_size("member")
    chips = lanes // 2
    members = lanes * step
    axes = ("patch", "member")
    count = patches * lanes

    edge = array(STEPS * step + 8, width)
    to_last, to_first = call(pack_kernel, "pack", [edge, edge], [init_field, flow_fields], limit=32)

    def swap(message, start):
        lower = range(start, patches - 1, 2)
        return lax.ppermute(message, "patch", [(p, p + 1) for p in lower] + [(p + 1, p) for p in lower])

    halo_last, halo_first = swap(to_last, 0), swap(to_first, 1)

    mine = jnp.concatenate(
        [
            observed_cell.astype(F32),
            observed_value,
            observed_scale,
            jnp.broadcast_to(observed_count.astype(F32)[:, None], observed_cell.shape),
        ]
        * 2,
        axis=0,
    )

    def between(message, hops):
        return lax.ppermute(message, "member", [(2 * a + core, 2 * b + core) for a, b in hops for core in range(2)])

    mirrored = [
        [hop for to in range(1, chips // 2) for hop in (((to + s) % chips, to), (chips - 1 - (to + s) % chips, chips - 1 - to))]
        for s in range(chips)
    ]
    turning = [[((to - s) % chips, to) for to in range(1, chips - 1)] for s in range(chips)]
    single = all(len({source for source, _ in hops}) == len(hops) for hops in mirrored)
    targets = mirrored if single else turning
    pair = array(2, step, width)
    kept, emitted, *inner = call(
        functools.partial(inner_kernel, targets), "inner",
        [array(4, step, width), array(step, width // 2)] + [pair] * chips,
        [init_field, flow_fields, emission[None, :]],
        [pltpu.VMEM((rows, step, width), F32), pltpu.VMEM((rows, 8, width), F32)], limit=32,
    )
    got_inner = [inner[0]] + [between(inner[s], targets[s]) for s in range(1, chips)]
    outer = call(
        edge_kernel, "edge", [pair] * chips, [init_field, flow_fields, emitted, kept, halo_last, halo_first],
        [pltpu.VMEM((2, step, width), F32)], limit=32,
    )
    got_outer = [outer[0]] + [
        between(outer[s], [(s, 0), (chips - 1 - s, chips - 1)]) for s in range(1, chips)
    ]
    order = [(targets[s], s) for s in range(chips)]
    pieces_in = got_inner + got_outer
    mine, _ = lax.optimization_barrier((mine, outer[0]))
    other = lax.ppermute(
        mine, axes,
        [(p * lanes + i, p * lanes + lanes - 1 - i) for p in range(1, patches, 2) for i in range(lanes)],
    )

    def device(p, chip, core):
        return p * lanes + 2 * chip + core

    borders, siblings = [], []
    for p in range(patches):
        for chip in range(chips):
            for core, away in ((0, -1), (1, 1)):
                siblings.append((device(p, chip, core), device(p, chip, 1 - core)))
                if 0 <= chip + away < chips:
                    borders.append((device(p, chip, core), device(p, chip + away, 1 - core)))
                else:
                    to = p + 1 if (p % 2 == 0) == (away == 1) else p - 1
                    if 0 <= to < patches:
                        borders.append((device(p, chip, core), device(to, chip, core)))

    half = array(chips, step, width)
    near_other, near_own, observed = call(
        functools.partial(collect_kernel, order), "collect",
        [half, array(chips * step + PADDING, width), array(8, slots)], [mine, other] + pieces_in,
    )
    far_own = lax.ppermute(near_other, axes, siblings)
    got_half = lax.ppermute(near_own, axes, borders)
    far_other = lax.ppermute(near_own, axes, siblings)
    got_rest = lax.ppermute(far_own, axes, borders)

    prepared = call(
        prepare_kernel, "prepare",
        [bfloat(members, slots)] * 2 + [bfloat(width, members)] * 2
        + [array(width, width // 2), array(8, slots), array(members, width // 2)],
        [observed, near_other, near_own, far_other, far_own],
        [pltpu.VMEM((members, 2 * width), F32)] + [pltpu.VMEM((members, 2 * width), BF16)] * 2,
        flops=8 * members * slots * width, limit=20,
    )
    halves = members // 2
    middle = call(
        middle_kernel, "middle",
        [bfloat(halves, slots)] * 2 + [array(slots, slots), array(width, slots), array(8, width)],
        [observed, *prepared[:4], prepared[6], got_half],
        flops=10 * halves * slots * slots, limit=20,
    )
    order = sorted(range(lanes), key=lambda x: (x.bit_length() != lanes.bit_length() - 1, -x))
    row = array(step, width)
    *shared, first, second = call(
        functools.partial(region_kernel, order[:2]), "region",
        [bfloat(halves, slots)] * 2 + [bfloat(slots, width)] * 2 + [array(8, width)] + [row] * 2,
        [observed, near_own, far_own, *prepared, *middle, got_rest],
        [pltpu.VMEM((slots, slots), F32)] * 2 + [pltpu.VMEM((width + 8, slots), F32)],
        limit=24,
    )
    others = call(
        functools.partial(others_kernel, order[2:]), "others", [row] * (lanes - 2),
        [near_own, far_own, prepared[6], *middle[:2], *shared],
        flops=6 * members * slots * width, limit=16,
    )
    analysed = dict(zip(order, [first, second, *others]))

    def swapped(x):
        return lax.ppermute(analysed[x], "member", [(i, i ^ x) for i in range(lanes)]) if x else analysed[0]

    return call(
        functools.partial(unpack_kernel, order), "unpack", array(step, rows, width),
        [swapped(x) for x in order], [pltpu.VMEM((step, rows, width), F32), pltpu.SemaphoreType.DMA((4,))],
        limit=48, out=pl.BlockSpec(memory_space=pltpu.HBM),
    )


def solution(mesh):
    return jax.shard_map(
        per_device,
        mesh=mesh,
        in_specs=(
            P("member", "patch", None),
            P(None, "patch", None),
            P("member"),
            P(("patch", "member"), None),
            P(("patch", "member")),
            P(("patch", "member"), None),
            P(("patch", "member"), None),
        ),
        out_specs=P("member", "patch", None),
        check_vma=False,
    )
```

```python
import functools
import math

import jax
import jax.numpy as jnp
from jax import lax
from jax.experimental import pallas as pl
from jax.experimental.pallas import tpu as pltpu
from jax.sharding import PartitionSpec as P

STEPS = 2
COARSE = 0.35
DONE = 0.03
LARGE = 2e4
PART = 256
PADDING = 8
F32 = jnp.float32
BF16 = jnp.bfloat16


def pack_kernel(info, field_ref, flow_ref, first_ref, second_ref):
    members, rows, width = field_ref.shape
    even = info[2] == 0
    for place in range(STEPS):
        tail, head = field_ref[:, rows - STEPS + place, :], field_ref[:, place, :]
        at = pl.ds(place * members, members)
        first_ref[at, :] = jnp.where(even, tail, head)
        second_ref[at, :] = jnp.where(even, head, tail)
    tail, head = flow_ref[:, rows - 1, :], flow_ref[:, 0, :]
    at = pl.ds(STEPS * members, 8)
    first_ref[at, :] = jnp.concatenate([jnp.where(even, tail, head)] * 2, axis=0)
    second_ref[at, :] = jnp.concatenate([jnp.where(even, head, tail)] * 2, axis=0)


def doubled(x):
    return jnp.concatenate([x, x], axis=1)


def weights_of(flow):
    row_flow, col_flow, kept, source = flow[0:1], flow[1:2], 1.0 - flow[2:3], flow[3:4]
    behind, ahead = jnp.maximum(row_flow, 0.0), -jnp.minimum(row_flow, 0.0)
    left, right = jnp.maximum(col_flow, 0.0), -jnp.minimum(col_flow, 0.0)
    stays = 1.0 - behind - ahead - left - right
    return [kept * stays, kept * behind, kept * ahead, kept * left, kept * right, source]


def advance(weights, emission, behind, field, ahead):
    width = field.shape[1]
    return (
        weights[0] * field
        + weights[1] * behind
        + weights[2] * ahead
        + weights[3] * pltpu.roll(field, 1, 1)
        + weights[4] * pltpu.roll(field, width - 1, 1)
        + emission * weights[5]
    )


def inner_kernel(targets, info, field_ref, flow_ref, member_ref, kept_ref, emission_ref, *refs):
    out_refs, (wide_ref, weight_ref) = refs[:-2], refs[-2:]
    members, rows, _ = field_ref.shape
    diagonal = lax.broadcasted_iota(jnp.int32, (members, members), 0) == lax.broadcasted_iota(
        jnp.int32, (members, members), 1
    )
    column = jnp.sum(jnp.where(diagonal, member_ref[...], 0.0), axis=1, keepdims=True)
    emission_ref[...] = jnp.broadcast_to(column, emission_ref.shape)
    emission = doubled(emission_ref[...])
    for row in range(1, rows - 1):
        weights = weights_of(flow_ref[:, row, :])
        for i, weight in enumerate(weights):
            weight_ref[row, pl.ds(i, 1), :] = weight
        wide_ref[row] = advance(
            weights, emission, field_ref[:, row - 1, :], field_ref[:, row, :], field_ref[:, row + 1, :]
        )
    for place, row in enumerate((1, 2, rows - 3, rows - 2)):
        kept_ref[place] = wide_ref[row]
    for out_ref, hops in zip(out_refs, targets):
        chip = sum(jnp.where(info[0] == source, to, 0) for source, to in hops)

        @pl.when(chip > 0)
        def _():
            for place in range(2):
                position = 2 * chip + jnp.abs(info[1] - 1 + place)
                row = position + info[2] * (rows - 1 - 2 * position)
                weights = weight_ref[row]
                out_ref[place] = advance(
                    [weights[i : i + 1] for i in range(6)],
                    emission, wide_ref[row - 1], wide_ref[row], wide_ref[row + 1],
                )


def end_rows(info, last, field_ref, flow_ref, emission_ref, kept_ref, halo_ref, out_ref):
    members, rows, width = field_ref.shape
    emission = doubled(emission_ref[...])

    def halo_row(place):
        return halo_ref[pl.ds(place * members, members), :]

    halo_weights = weights_of(halo_ref[pl.ds(STEPS * members, 4), :])
    for parity in range(2):

        @pl.when(info[2] == parity)
        def _():
            if parity == last:
                end, near, outside, beyond = 0, 1, halo_row(1), halo_row(0)
                inside, further = kept_ref[0], kept_ref[1]
            else:
                end, near, outside, beyond = rows - 1, rows - 2, halo_row(0), halo_row(1)
                inside, further = kept_ref[3], kept_ref[2]

            def ordered(weights, outer, own, inner):
                behind, ahead = (outer, inner) if end == 0 else (inner, outer)
                return advance(weights, emission, behind, own, ahead)

            end_weights = weights_of(flow_ref[:, end, :])
            end_field = field_ref[:, end, :]
            outer = ordered(halo_weights, beyond, outside, end_field)
            own = ordered(end_weights, outside, end_field, field_ref[:, near, :])
            out_ref[last] = ordered(end_weights, outer, own, inside)
            out_ref[1 - last] = ordered(weights_of(flow_ref[:, near, :]), own, inside, further)


def edge_kernel(info, field_ref, flow_ref, emission_ref, kept_ref, last_ref, first_ref, *refs):
    out_refs, scratch = refs[:-1], refs[-1]
    chips = len(out_refs)
    core = info[1]
    for last, halo_ref in enumerate((first_ref, last_ref)):
        end_rows(info, last, field_ref, flow_ref, emission_ref, kept_ref, halo_ref, scratch)
        for s, out_ref in enumerate(out_refs):

            @pl.when(info[0] == (chips - 1 - s if last else s))
            def _():
                out_ref[0] = scratch[1 - core]
                out_ref[1] = scratch[core]


def source_of(chip, chips, hops, k):
    inner = sum(jnp.where(chip == to, source, 0) for source, to in hops)
    return jnp.where(chip == 0, k, jnp.where(chip == chips - 1, chips - 1 - k, inner))


def collect_kernel(order, info, mine_ref, other_ref, *refs):
    chips = len(order)
    near_other, near_own, observed_ref = refs[-3:]
    step = near_other.shape[1]
    observed_ref[...] = jnp.where(info[2] == 1, other_ref[...], mine_ref[...])
    near_own[pl.ds(chips * step, PADDING), :] = jnp.zeros((PADDING, near_own.shape[1]), F32)
    chip = info[0]
    at_edge = jnp.logical_or(chip == 0, chip == chips - 1)
    for index, (s, k) in enumerate(order):
        block = source_of(chip, chips, s, k)
        rows = pl.ds(pl.multiple_of(block * step, step), step)
        for ref, here in ((refs[index], jnp.logical_not(at_edge)), (refs[chips + index], at_edge)):

            @pl.when(here)
            def _():
                near_other[block] = ref[0]
                near_own[rows, :] = ref[1]


def unpack_kernel(order, info, *refs):
    row_refs, (out_hbm, out_ref, sems) = refs[:-3], refs[-3:]
    members, rows, _ = out_ref.shape
    part = members // 4
    moves = []
    for index in range(4):
        some = pl.ds(index * part, part)
        for x, ref in zip(order, row_refs):
            position = (2 * info[0] + info[1]) ^ x
            row = position + info[2] * (rows - 1 - 2 * position)
            out_ref[some, pl.ds(row, 1), :] = ref[some, :][:, None, :]
        moves.append(pltpu.make_async_copy(out_ref.at[some], out_hbm.at[some], sems.at[index]))
        moves[-1].start()
    for move in moves:
        move.wait()


def pieces(x, count):
    parts = []
    for _ in range(count - 1):
        part = x.astype(BF16)
        parts.append(part)
        x = x - part.astype(F32)
    return parts + [x.astype(BF16)]


def dot(a, b):
    return lax.dot_general(a, b, (((1,), (0,)), ((), ())), preferred_element_type=F32)


def dot_t(a, b):
    return lax.dot_general(a, b, (((0,), (0,)), ((), ())), preferred_element_type=F32)


def product(a, b):
    total = None
    for i, left in enumerate(a):
        for j, right in enumerate(b):
            if i + j < max(len(a), len(b)):
                term = dot(left, right)
                total = term if total is None else total + term
    return total


def observations(info, observed_ref, width, root):
    slots = observed_ref.shape[1]
    cells, values, scales, count = (observed_ref[pl.ds(i, 1), :] for i in range(4))
    cells = cells.astype(jnp.int32)
    offset = sum((cells >= i * width).astype(jnp.int32) for i in (1, 2)) - 1
    column = cells - (offset + 1) * width
    side = offset * jnp.where(info[2] == 1, -1, 1) * (1 - 2 * info[1])
    cells = column + width * jnp.where(side == 0, 2, jnp.where(side < 0, 0, 1))
    active = lax.broadcasted_iota(jnp.int32, (1, slots), 1) < count.astype(jnp.int32)
    slot_weight = jnp.where(active, scales, 0.0)
    return cells, slot_weight, values, slot_weight * (1.0 / root)


def one_hot(cells, first, count):
    return (
        lax.broadcasted_iota(jnp.int32, (count, cells.shape[1]), 0) + first == cells
    ).astype(F32).astype(BF16)


def mean_of(blocks, members):
    total = blocks[0]
    for block in blocks[1:]:
        total = total + block
    return jnp.sum(total, axis=0, keepdims=True) * (1.0 / members)


def at_cells(row, chosen):
    parts = pieces(jnp.broadcast_to(row, (8, row.shape[1])), 3)
    return (dot(parts[0], chosen) + (dot(parts[1], chosen) + dot(parts[2], chosen)))[:1]


def prepare_kernel(
    info, observed_ref, near_other, near_own, far_other, far_own,
    spread_high, spread_low, own_high, own_low, own_part, seen_ref, direction_ref,
    anomaly, high_ref, low_ref,
):
    chips, step, width = near_other.shape
    members = 2 * chips * step
    cells, _, _, scale = observations(info, observed_ref, width, math.sqrt(members - 1))
    chosen = one_hot(cells, width, 2 * width)
    blocks = [pl.ds(index * step, step) for index in range(2 * chips)]
    means = []
    for place in range(2):
        columns = pl.ds(place * width, width)
        if place:
            rows = [near_own.at[block, :] for block in blocks[:chips]] + [far_own.at[chip] for chip in range(chips)]
        else:
            rows = [near_other.at[chip] for chip in range(chips)] + [far_other.at[block, :] for block in blocks[:chips]]
        means.append(mean_of([row[...] for row in rows], members))
        for block, row in zip(blocks, rows):
            part = row[...] - means[-1]
            anomaly[block, columns] = part
            high_ref[block, columns] = part.astype(BF16)

    def unit(x):
        return x * (1.0 / jnp.maximum(jnp.max(jnp.abs(x)), 1e-30))

    high = high_ref[...]
    along = lax.dot_general(high[:16], high, (((1,), (1,)), ((), ())), preferred_element_type=F32)
    rows = unit(dot(unit(along).astype(BF16), high))
    weight = jnp.sum(rows * rows[:1], axis=1, keepdims=True)
    weight = weight + jnp.where(jnp.max(jnp.abs(weight)) > 0.0, 0.0, 1.0)
    pattern = unit(jnp.sum(rows * weight, axis=0, keepdims=True))
    total = jnp.zeros((1, 1), F32)
    for block in blocks:
        along = jnp.sum(anomaly[block, :] * pattern, axis=1, keepdims=True)
        total = total + jnp.sum(along * along, axis=0, keepdims=True)
        direction_ref[block, :] = jnp.broadcast_to(along, (step, direction_ref.shape[1]))
    length = lax.rsqrt(jnp.maximum(total, 1e-30))
    taken = None
    for block in blocks:
        direction = direction_ref[block, :] * length
        direction_ref[block, :] = direction
        term = anomaly[block, :] * doubled(doubled(direction))
        taken = term if taken is None else taken + term
    taken = jnp.sum(taken, axis=0, keepdims=True)
    own_part[...] = jnp.broadcast_to(taken[:, width:], (own_part.shape[1], width)).T

    for block in blocks:
        rest = anomaly[block, :] - doubled(doubled(direction_ref[block, :])) * taken
        high, low = pieces(rest, 2)
        high_ref[block, :] = high
        low_ref[block, :] = low
        own = rest[:, width:].T
        own_high[:, block], own_low[:, block] = pieces(own, 2)
    seen_ref[pl.ds(0, 1), :] = at_cells(jnp.concatenate(means, axis=1), chosen)
    seen_ref[pl.ds(1, 1), :] = at_cells(taken, chosen)
    for first in range(0, members, PART):
        rows = pl.ds(first, PART)
        spread = (dot(high_ref[rows, :], chosen) + dot(low_ref[rows, :], chosen)) * scale
        high, low = pieces(spread, 2)
        spread_high[rows, :] = high
        spread_low[rows, :] = low


def square(parts):
    half = parts[0].shape[0] // 2
    upper = product([part[:half] for part in parts], parts)
    lower = product([part[half:] for part in parts], [part[:, half:] for part in parts])
    return upper, jnp.concatenate([upper[:, half:].T, lower], axis=1)


def at_border(info):
    chip, core, _, chips = info
    ends = jnp.logical_or(jnp.logical_and(chip == 0, core == 0), jnp.logical_and(chip == chips - 1, core == 1))
    return jnp.where(ends, 0, 1)


def shifted_spread(rows, blocks, direction_ref, shift, along, chosen, scale, high_in, low_in, high_out, low_out):
    total, taken = None, None
    step = rows[0].shape[0]
    for index, (row, block) in enumerate(zip(rows, blocks)):
        here = pl.ds(index * step, step)
        direction = doubled(direction_ref[block, :])
        rest = row[...] - shift - direction * along
        total = rest if total is None else total + rest
        taken = direction * rest if taken is None else taken + direction * rest
        high, low = pieces(rest, 2)
        high, low = pieces((dot(high, chosen) + dot(low, chosen)) * scale, 2)
        high_out[here, :] = high + high_in[block, :]
        low_out[here, :] = low + low_in[block, :]
    return jnp.sum(total, axis=0, keepdims=True), jnp.sum(taken, axis=0, keepdims=True)


def gram(high, low):
    turned = high.T
    cross = dot(turned, low)
    return dot(turned, high) + (cross + cross.T)


def middle_kernel(
    info, observed_ref, high_in, low_in, own_high, own_low, direction_ref, half_ref,
    high_ref, low_ref, gram_ref, right_ref, known_ref,
):
    chips = info[3]
    count, slots = high_ref.shape
    step = count // chips
    width = half_ref.shape[1]
    first = at_border(info) * count
    cells, _, _, scale = observations(info, observed_ref, width, math.sqrt(2 * count - 1))
    chosen = one_hot(cells, 0, width)
    rows = [half_ref.at[pl.ds(chip * step, step), :] for chip in range(chips)]
    blocks = [pl.ds(pl.multiple_of(first + chip * step, step), step) for chip in range(chips)]
    mean = mean_of([row[...] for row in rows], count)
    along, weight = None, None
    for row, block in zip(rows, blocks):
        direction = direction_ref[block, :]
        term = (row[...] - mean) * doubled(direction)
        along = term if along is None else along + term
        weight = direction * direction if weight is None else weight + direction * direction
    weight = doubled(jnp.sum(weight, axis=0, keepdims=True))
    along = jnp.sum(along, axis=0, keepdims=True) / jnp.maximum(weight, 0.1)
    total, taken = shifted_spread(
        rows, blocks, direction_ref, mean, along, chosen, scale, high_in, low_in, high_ref, low_ref
    )
    for index, known in enumerate((mean, along, total, taken)):
        known_ref[pl.ds(index, 1), :] = known
    high, low = high_ref[...], low_ref[...]
    gram_ref[...] = gram(high, low)
    members = pl.ds(pl.multiple_of(first, count), count)
    right_ref[...] = product([own_high[:, members], own_low[:, members]], [high, low])


def analysed_row(info, x, near_own, far_own, direction_ref, halves, rests, parts, sides):
    chips, step, _ = far_own.shape
    chip, mine = info[0] ^ (x // 2), x % 2
    rows = pl.ds(pl.multiple_of(chip * step, step), step)
    spread = [
        jnp.where(at_border(info) == mine, half[rows, :], rest[rows, :]) for half, rest in zip(halves, rests)
    ]
    block = pl.ds(pl.multiple_of((mine * chips + chip) * step, step), step)
    own = far_own[chip] if mine else near_own[rows, :]
    return own + sides[0:1] + product(spread, parts) + doubled(direction_ref[block, :]) * sides[1:2]


def others_kernel(
    order, info, near_own, far_own, direction_ref, high_half, low_half, high_rest, low_rest,
    solved_high, solved_low, sides_ref, *out_refs,
):
    parts = [solved_high[...], solved_low[...]]
    for x, out_ref in zip(order, out_refs):
        out_ref[...] = analysed_row(
            info, x, near_own, far_own, direction_ref, (high_half, low_half), (high_rest, low_rest), parts, sides_ref[...]
        )


def region_kernel(
    order, info, observed_ref, near_own, far_own, high_in, low_in, own_high, own_low, own_part, seen_ref,
    direction_ref, high_half, low_half, gram_half, right_half, known_ref, rest_ref, *refs,
):
    chips, step, width = far_own.shape
    high_rest, low_rest, solved_high, solved_low, sides_ref = refs[:5]
    out_refs, (factor, squared, answer) = refs[5:-3], refs[-3:]
    count = chips * step
    members = 2 * count
    slots = observed_ref.shape[1]
    root = math.sqrt(members - 1)
    part = at_border(info)
    first = (1 - part) * count
    cells, slot_weight, values, scale = observations(info, observed_ref, width, root)
    chosen = one_hot(cells, 0, width)
    shift, along, total, taken = (known_ref[pl.ds(index, 1), :] for index in range(4))
    more, further = shifted_spread(
        [rest_ref.at[chip] for chip in range(chips)],
        [pl.ds(pl.multiple_of(first + chip * step, step), step) for chip in range(chips)],
        direction_ref, shift, along, chosen, scale, high_in, low_in, high_rest, low_rest,
    )
    left = (total + more) * (1.0 / members)
    taken = taken + further
    seen_mean = seen_ref[pl.ds(0, 1), :] + at_cells(shift + left, chosen)
    left, taken_here = at_cells(left, chosen) * scale, at_cells(taken, chosen) * scale
    common = (seen_ref[pl.ds(1, 1), :] + at_cells(along + taken, chosen)) * scale
    innovation = slot_weight * (values - seen_mean)
    place = lax.broadcasted_iota(jnp.int32, (8, slots), 0)
    excess = jnp.where(place == 0, left * math.sqrt(members), jnp.where(place == 1, taken_here, 0.0))
    excess = pieces(excess, 2)

    eye = lax.broadcasted_iota(jnp.int32, (slots, slots), 0) == lax.broadcasted_iota(
        jnp.int32, (slots, slots), 1
    )
    high, low = high_rest[...], low_rest[...]
    over = dot_t(excess[0], excess[0]) + (dot_t(excess[0], excess[1]) + dot_t(excess[1], excess[0]))
    factor[...] = gram(high, low) + (gram_half[...] - over) + jnp.where(eye, 1.0, 0.0)
    rows = pl.ds(pl.multiple_of(first, count), count)
    answer[pl.ds(0, width), :] = right_half[...] + product([own_high[:, rows], own_low[:, rows]], [high, low])
    answer[pl.ds(width, 8), :] = jnp.where(
        lax.broadcasted_iota(jnp.int32, (8, slots), 0) == 0, jnp.broadcast_to(common, (8, slots)), 0.0
    )
    half = slots // 2
    upper, lower = pl.ds(0, half), pl.ds(half, half)

    def after(bound):
        return bound * bound / (2.0 - bound * bound)

    def size(matrix):
        return jnp.sum(jnp.sum(matrix * matrix, axis=0, keepdims=True))

    def begin(parts, count):
        if count > 2:
            squared[upper, :], squared[lower, :] = square(parts)
        bound = 1.0 - start
        gain = 2.0 / (2.0 - bound * bound)
        answer[...] = (gain * start) * (2.0 * answer[...] - start * product(pieces(answer[...], count), parts))
        factor[...] = (gain * start) * (2.0 * factor[...] - start * squared[...])
        return after(bound)

    def refine(bound, count):
        gain = 2.0 / (2.0 - bound * bound)
        parts = pieces(factor[...], count)
        answer[...] = gain * (2.0 * answer[...] - product(pieces(answer[...], count), parts))
        top, bottom = square(parts)
        factor[upper, :] = gain * (2.0 * factor[upper, :] - top)
        factor[lower, :] = gain * (2.0 * factor[lower, :] - bottom)
        return after(bound)

    def close(bound, rest):
        gain = 2.0 / (2.0 - bound * bound)
        answer[...] = gain * (answer[...] + dot(answer[...].astype(BF16), rest))
        return gain

    def finish(bound):
        rest = factor[...].astype(BF16)
        gain = close(bound, rest)
        factor[...] = gain * (dot(rest, rest) - jnp.where(eye, 0.5 * bound * bound, 0.0))
        return after(bound)

    parts = pieces(factor[...], 2)
    top, bottom = square(parts)
    squared[upper, :] = top
    squared[lower, :] = bottom
    limit = 1.0001 * jnp.sqrt(jnp.sqrt(size(top) + size(bottom)))
    start = 2.0 / (1.0 + limit)
    large = limit > LARGE
    bound = lax.cond(large, lambda: begin(pieces(factor[...], 3), 3), lambda: begin(parts, 2))
    bound = lax.while_loop(lambda b: jnp.logical_and(b > COARSE, large), lambda b: refine(b, 3), bound)
    bound = lax.while_loop(lambda b: b > COARSE, lambda b: refine(b, 2), bound)
    factor[...] = jnp.where(eye, 1.0, 0.0) - factor[...]
    bound = lax.while_loop(lambda b: b > DONE, finish, bound)
    close(bound, factor[...].astype(BF16))

    solved = answer[pl.ds(0, width), :]
    alone = answer[pl.ds(width, 1), :]
    share = own_part[:, :1] - jnp.sum(solved * common, axis=1, keepdims=True)
    solved = solved + (share / (1.0 + jnp.sum(common * alone, axis=1, keepdims=True))) * alone
    solved = solved.T
    which = lax.broadcasted_iota(jnp.int32, (8, slots), 0)
    sides = jnp.where(
        which == 0, innovation * (1.0 / root) + 0.5 * left, jnp.where(which == 1, 0.5 * (taken_here - common), 0.0)
    )
    parts = pieces(solved, 2)
    sides = product(pieces(sides, 2), parts)
    parts = [part * jnp.asarray(-0.5, BF16) for part in parts]
    sides_ref[...] = sides
    solved_high[...], solved_low[...] = parts
    for x, out_ref in zip(order, out_refs):
        out_ref[...] = analysed_row(
            info, x, near_own, far_own, direction_ref, (high_half, low_half), (high_rest, low_rest), parts, sides
        )


VMEM = pl.BlockSpec(memory_space=pltpu.VMEM)


def position():
    lane, patch = lax.axis_index("member"), lax.axis_index("patch")
    return lax.div(lane, 2), lax.rem(lane, 2), lax.rem(patch, 2), lax.axis_size("member") // 2


def call(kernel, name, out_shape, args, scratch=(), flops=None, limit=8, out=VMEM):
    several = isinstance(out_shape, (list, tuple))
    return pl.pallas_call(
        lambda *refs: kernel(position(), *refs),
        out_shape=out_shape,
        in_specs=[VMEM] * len(args),
        out_specs=[out] * len(out_shape) if several else out,
        scratch_shapes=scratch,
        compiler_params=pltpu.CompilerParams(vmem_limit_bytes=limit * 1024 * 1024),
        cost_estimate=flops and pl.CostEstimate(flops=flops, bytes_accessed=0, transcendentals=0),
        name=name,
    )(*args)


def bfloat(*shape):
    return jax.ShapeDtypeStruct(shape, BF16)


def array(*shape):
    return jax.ShapeDtypeStruct(shape, F32)


def per_device(
    init_field, flow_fields, emission, observed_cell, observed_count, observed_value, observed_scale
):
    step, rows, width = init_field.shape
    slots = observed_cell.shape[1]
    patches, lanes = lax.axis_size("patch"), lax.axis_size("member")
    chips = lanes // 2
    members = lanes * step
    axes = ("patch", "member")
    count = patches * lanes

    edge = array(STEPS * step + 8, width)
    to_last, to_first = call(pack_kernel, "pack", [edge, edge], [init_field, flow_fields], limit=32)

    def swap(message, start):
        lower = range(start, patches - 1, 2)
        return lax.ppermute(message, "patch", [(p, p + 1) for p in lower] + [(p + 1, p) for p in lower])

    halo_last, halo_first = swap(to_last, 0), swap(to_first, 1)

    mine = jnp.concatenate(
        [
            observed_cell.astype(F32),
            observed_value,
            observed_scale,
            jnp.broadcast_to(observed_count.astype(F32)[:, None], observed_cell.shape),
        ]
        * 2,
        axis=0,
    )

    def between(message, hops):
        return lax.ppermute(message, "member", [(2 * a + core, 2 * b + core) for a, b in hops for core in range(2)])

    mirrored = [
        [hop for to in range(1, chips // 2) for hop in (((to + s) % chips, to), (chips - 1 - (to + s) % chips, chips - 1 - to))]
        for s in range(chips)
    ]
    turning = [[((to - s) % chips, to) for to in range(1, chips - 1)] for s in range(chips)]
    single = all(len({source for source, _ in hops}) == len(hops) for hops in mirrored)
    targets = mirrored if single else turning
    pair = array(2, step, width)
    kept, emitted, *inner = call(
        functools.partial(inner_kernel, targets), "inner",
        [array(4, step, width), array(step, width // 2)] + [pair] * chips,
        [init_field, flow_fields, emission[None, :]],
        [pltpu.VMEM((rows, step, width), F32), pltpu.VMEM((rows, 8, width), F32)], limit=32,
    )
    got_inner = [inner[0]] + [between(inner[s], targets[s]) for s in range(1, chips)]
    outer = call(
        edge_kernel, "edge", [pair] * chips, [init_field, flow_fields, emitted, kept, halo_last, halo_first],
        [pltpu.VMEM((2, step, width), F32)], limit=32,
    )
    got_outer = [outer[0]] + [
        between(outer[s], [(s, 0), (chips - 1 - s, chips - 1)]) for s in range(1, chips)
    ]
    turns = [0, chips - 1, *range(1, chips - 1)]
    order = [(targets[s], k) for k, s in enumerate(turns)]
    pieces_in = [got_inner[s] for s in turns] + got_outer
    mine, _ = lax.optimization_barrier((mine, outer[0]))
    other = lax.ppermute(
        mine, axes,
        [(p * lanes + i, p * lanes + lanes - 1 - i) for p in range(1, patches, 2) for i in range(lanes)],
    )

    def device(p, chip, core):
        return p * lanes + 2 * chip + core

    borders, siblings = [], []
    for p in range(patches):
        for chip in range(chips):
            for core, away in ((0, -1), (1, 1)):
                siblings.append((device(p, chip, core), device(p, chip, 1 - core)))
                if 0 <= chip + away < chips:
                    borders.append((device(p, chip, core), device(p, chip + away, 1 - core)))
                else:
                    to = p + 1 if (p % 2 == 0) == (away == 1) else p - 1
                    if 0 <= to < patches:
                        borders.append((device(p, chip, core), device(to, chip, core)))

    half = array(chips, step, width)
    near_other, near_own, observed = call(
        functools.partial(collect_kernel, order), "collect",
        [half, array(chips * step + PADDING, width), array(8, slots)], [mine, other] + pieces_in,
    )
    far_own = lax.ppermute(near_other, axes, siblings)
    got_half = lax.ppermute(near_own, axes, borders)
    far_other = lax.ppermute(near_own, axes, siblings)
    got_rest = lax.ppermute(far_own, axes, borders)

    prepared = call(
        prepare_kernel, "prepare",
        [bfloat(members, slots)] * 2 + [bfloat(width, members)] * 2
        + [array(width, width // 2), array(8, slots), array(members, width // 2)],
        [observed, near_other, near_own, far_other, far_own],
        [pltpu.VMEM((members, 2 * width), F32)] + [pltpu.VMEM((members, 2 * width), BF16)] * 2,
        flops=8 * members * slots * width, limit=20,
    )
    halves = members // 2
    middle = call(
        middle_kernel, "middle",
        [bfloat(halves, slots)] * 2 + [array(slots, slots), array(width, slots), array(8, width)],
        [observed, *prepared[:4], prepared[6], got_half],
        flops=10 * halves * slots * slots, limit=20,
    )
    order = sorted(range(lanes), key=lambda x: (x.bit_length() != lanes.bit_length() - 1, -x))
    row = array(step, width)
    *shared, first, second = call(
        functools.partial(region_kernel, order[:2]), "region",
        [bfloat(halves, slots)] * 2 + [bfloat(slots, width)] * 2 + [array(8, width)] + [row] * 2,
        [observed, near_own, far_own, *prepared, *middle, got_rest],
        [pltpu.VMEM((slots, slots), F32)] * 2 + [pltpu.VMEM((width + 8, slots), F32)],
        limit=24,
    )
    others = call(
        functools.partial(others_kernel, order[2:]), "others", [row] * (lanes - 2),
        [near_own, far_own, prepared[6], *middle[:2], *shared],
        flops=6 * members * slots * width, limit=16,
    )
    analysed = dict(zip(order, [first, second, *others]))

    def swapped(x):
        return lax.ppermute(analysed[x], "member", [(i, i ^ x) for i in range(lanes)]) if x else analysed[0]

    return call(
        functools.partial(unpack_kernel, order), "unpack", array(step, rows, width),
        [swapped(x) for x in order], [pltpu.VMEM((step, rows, width), F32), pltpu.SemaphoreType.DMA((4,))],
        limit=48, out=pl.BlockSpec(memory_space=pltpu.HBM),
    )


def solution(mesh):
    return jax.shard_map(
        per_device,
        mesh=mesh,
        in_specs=(
            P("member", "patch", None),
            P(None, "patch", None),
            P("member"),
            P(("patch", "member"), None),
            P(("patch", "member")),
            P(("patch", "member"), None),
            P(("patch", "member"), None),
        ),
        out_specs=P("member", "patch", None),
        check_vma=False,
    )
```

```python
import functools
import math

import jax
import jax.numpy as jnp
from jax import lax
from jax.experimental import pallas as pl
from jax.experimental.pallas import tpu as pltpu
from jax.sharding import PartitionSpec as P

STEPS = 2
COARSE = 0.35
DONE = 0.03
LARGE = 2e4
PART = 256
PADDING = 8
F32 = jnp.float32
BF16 = jnp.bfloat16


def pack_kernel(info, field_ref, flow_ref, first_ref, second_ref):
    members, rows, width = field_ref.shape
    even = info[2] == 0
    for place in range(STEPS):
        tail, head = field_ref[:, rows - STEPS + place, :], field_ref[:, place, :]
        at = pl.ds(place * members, members)
        first_ref[at, :] = jnp.where(even, tail, head)
        second_ref[at, :] = jnp.where(even, head, tail)
    tail, head = flow_ref[:, rows - 1, :], flow_ref[:, 0, :]
    at = pl.ds(STEPS * members, 8)
    first_ref[at, :] = jnp.concatenate([jnp.where(even, tail, head)] * 2, axis=0)
    second_ref[at, :] = jnp.concatenate([jnp.where(even, head, tail)] * 2, axis=0)


def doubled(x):
    return jnp.concatenate([x, x], axis=1)


def weights_of(flow):
    row_flow, col_flow, kept, source = flow[0:1], flow[1:2], 1.0 - flow[2:3], flow[3:4]
    behind, ahead = jnp.maximum(row_flow, 0.0), -jnp.minimum(row_flow, 0.0)
    left, right = jnp.maximum(col_flow, 0.0), -jnp.minimum(col_flow, 0.0)
    stays = 1.0 - behind - ahead - left - right
    return [kept * stays, kept * behind, kept * ahead, kept * left, kept * right, source]


def advance(weights, emission, behind, field, ahead):
    width = field.shape[1]
    return (
        weights[0] * field
        + weights[1] * behind
        + weights[2] * ahead
        + weights[3] * pltpu.roll(field, 1, 1)
        + weights[4] * pltpu.roll(field, width - 1, 1)
        + emission * weights[5]
    )


def inner_kernel(targets, info, field_ref, flow_ref, member_ref, kept_ref, emission_ref, *refs):
    out_refs, (wide_ref, weight_ref) = refs[:-2], refs[-2:]
    members, rows, _ = field_ref.shape
    diagonal = lax.broadcasted_iota(jnp.int32, (members, members), 0) == lax.broadcasted_iota(
        jnp.int32, (members, members), 1
    )
    column = jnp.sum(jnp.where(diagonal, member_ref[...], 0.0), axis=1, keepdims=True)
    emission_ref[...] = jnp.broadcast_to(column, emission_ref.shape)
    emission = doubled(emission_ref[...])
    for row in range(1, rows - 1):
        weights = weights_of(flow_ref[:, row, :])
        for i, weight in enumerate(weights):
            weight_ref[row, pl.ds(i, 1), :] = weight
        wide_ref[row] = advance(
            weights, emission, field_ref[:, row - 1, :], field_ref[:, row, :], field_ref[:, row + 1, :]
        )
    for place, row in enumerate((1, 2, rows - 3, rows - 2)):
        kept_ref[place] = wide_ref[row]
    for out_ref, hops in zip(out_refs, targets):
        chip = sum(jnp.where(info[0] == source, to, 0) for source, to in hops)

        @pl.when(chip > 0)
        def _():
            for place in range(2):
                position = 2 * chip + jnp.abs(info[1] - 1 + place)
                row = position + info[2] * (rows - 1 - 2 * position)
                weights = weight_ref[row]
                out_ref[place] = advance(
                    [weights[i : i + 1] for i in range(6)],
                    emission, wide_ref[row - 1], wide_ref[row], wide_ref[row + 1],
                )


def end_rows(info, last, field_ref, flow_ref, emission_ref, kept_ref, halo_ref, out_ref):
    members, rows, width = field_ref.shape
    emission = doubled(emission_ref[...])

    def halo_row(place):
        return halo_ref[pl.ds(place * members, members), :]

    halo_weights = weights_of(halo_ref[pl.ds(STEPS * members, 4), :])
    for parity in range(2):

        @pl.when(info[2] == parity)
        def _():
            if parity == last:
                end, near, outside, beyond = 0, 1, halo_row(1), halo_row(0)
                inside, further = kept_ref[0], kept_ref[1]
            else:
                end, near, outside, beyond = rows - 1, rows - 2, halo_row(0), halo_row(1)
                inside, further = kept_ref[3], kept_ref[2]

            def ordered(weights, outer, own, inner):
                behind, ahead = (outer, inner) if end == 0 else (inner, outer)
                return advance(weights, emission, behind, own, ahead)

            end_weights = weights_of(flow_ref[:, end, :])
            end_field = field_ref[:, end, :]
            outer = ordered(halo_weights, beyond, outside, end_field)
            own = ordered(end_weights, outside, end_field, field_ref[:, near, :])
            out_ref[last] = ordered(end_weights, outer, own, inside)
            out_ref[1 - last] = ordered(weights_of(flow_ref[:, near, :]), own, inside, further)


def edge_kernel(info, field_ref, flow_ref, emission_ref, kept_ref, last_ref, first_ref, *refs):
    out_refs, scratch = refs[:-1], refs[-1]
    chips = len(out_refs)
    core = info[1]
    for last, halo_ref in enumerate((first_ref, last_ref)):
        end_rows(info, last, field_ref, flow_ref, emission_ref, kept_ref, halo_ref, scratch)
        for s, out_ref in enumerate(out_refs):

            @pl.when(info[0] == (chips - 1 - s if last else s))
            def _():
                out_ref[0] = scratch[1 - core]
                out_ref[1] = scratch[core]


def source_of(chip, chips, hops, k):
    inner = sum(jnp.where(chip == to, source, 0) for source, to in hops)
    return jnp.where(chip == 0, k, jnp.where(chip == chips - 1, chips - 1 - k, inner))


def collect_kernel(order, info, mine_ref, other_ref, *refs):
    chips = len(order)
    near_other, near_own, observed_ref = refs[-3:]
    step = near_other.shape[1]
    observed_ref[...] = jnp.where(info[2] == 1, other_ref[...], mine_ref[...])
    near_own[pl.ds(chips * step, PADDING), :] = jnp.zeros((PADDING, near_own.shape[1]), F32)
    chip = info[0]
    at_edge = jnp.logical_or(chip == 0, chip == chips - 1)
    for index, (s, k) in enumerate(order):
        block = source_of(chip, chips, s, k)
        rows = pl.ds(pl.multiple_of(block * step, step), step)
        for ref, here in ((refs[index], jnp.logical_not(at_edge)), (refs[chips + index], at_edge)):

            @pl.when(here)
            def _():
                near_other[block] = ref[0]
                near_own[rows, :] = ref[1]


def unpack_kernel(order, info, *refs):
    row_refs, (out_hbm, out_ref, sems) = refs[:-3], refs[-3:]
    members, rows, _ = out_ref.shape
    part = members // 4
    moves = []
    for index in range(4):
        some = pl.ds(index * part, part)
        for x, ref in zip(order, row_refs):
            position = (2 * info[0] + info[1]) ^ x
            row = position + info[2] * (rows - 1 - 2 * position)
            out_ref[some, pl.ds(row, 1), :] = ref[some, :][:, None, :]
        moves.append(pltpu.make_async_copy(out_ref.at[some], out_hbm.at[some], sems.at[index]))
        moves[-1].start()
    for move in moves:
        move.wait()


def pieces(x, count):
    parts = []
    for _ in range(count - 1):
        part = x.astype(BF16)
        parts.append(part)
        x = x - part.astype(F32)
    return parts + [x.astype(BF16)]


def dot(a, b):
    return lax.dot_general(a, b, (((1,), (0,)), ((), ())), preferred_element_type=F32)


def dot_t(a, b):
    return lax.dot_general(a, b, (((0,), (0,)), ((), ())), preferred_element_type=F32)


def product(a, b):
    total = None
    for i, left in enumerate(a):
        for j, right in enumerate(b):
            if i + j < max(len(a), len(b)):
                term = dot(left, right)
                total = term if total is None else total + term
    return total


def observations(info, observed_ref, width, root):
    slots = observed_ref.shape[1]
    cells, values, scales, count = (observed_ref[pl.ds(i, 1), :] for i in range(4))
    cells = cells.astype(jnp.int32)
    offset = sum((cells >= i * width).astype(jnp.int32) for i in (1, 2)) - 1
    column = cells - (offset + 1) * width
    side = offset * jnp.where(info[2] == 1, -1, 1) * (1 - 2 * info[1])
    cells = column + width * jnp.where(side == 0, 2, jnp.where(side < 0, 0, 1))
    active = lax.broadcasted_iota(jnp.int32, (1, slots), 1) < count.astype(jnp.int32)
    slot_weight = jnp.where(active, scales, 0.0)
    return cells, slot_weight, values, slot_weight * (1.0 / root)


def one_hot(cells, first, count):
    return (
        lax.broadcasted_iota(jnp.int32, (count, cells.shape[1]), 0) + first == cells
    ).astype(F32).astype(BF16)


def mean_of(blocks, members):
    total = blocks[0]
    for block in blocks[1:]:
        total = total + block
    return jnp.sum(total, axis=0, keepdims=True) * (1.0 / members)


def at_cells(row, chosen):
    parts = pieces(jnp.broadcast_to(row, (8, row.shape[1])), 3)
    return (dot(parts[0], chosen) + (dot(parts[1], chosen) + dot(parts[2], chosen)))[:1]


def prepare_kernel(
    info, observed_ref, near_other, near_own, far_other, far_own,
    spread_high, spread_low, own_high, own_low, own_part, seen_ref, direction_ref,
    anomaly, high_ref, low_ref,
):
    chips, step, width = near_other.shape
    members = 2 * chips * step
    cells, _, _, scale = observations(info, observed_ref, width, math.sqrt(members - 1))
    chosen = one_hot(cells, width, 2 * width)
    blocks = [pl.ds(index * step, step) for index in range(2 * chips)]
    means = []
    for place in range(2):
        columns = pl.ds(place * width, width)
        if place:
            rows = [near_own.at[block, :] for block in blocks[:chips]] + [far_own.at[chip] for chip in range(chips)]
        else:
            rows = [near_other.at[chip] for chip in range(chips)] + [far_other.at[block, :] for block in blocks[:chips]]
        means.append(mean_of([row[...] for row in rows], members))
        for block, row in zip(blocks, rows):
            part = row[...] - means[-1]
            anomaly[block, columns] = part
            high_ref[block, columns] = part.astype(BF16)

    def unit(x):
        return x * (1.0 / jnp.maximum(jnp.max(jnp.abs(x)), 1e-30))

    high = high_ref[...]
    along = lax.dot_general(high[:16], high, (((1,), (1,)), ((), ())), preferred_element_type=F32)
    rows = unit(dot(unit(along).astype(BF16), high))
    weight = jnp.sum(rows * rows[:1], axis=1, keepdims=True)
    weight = weight + jnp.where(jnp.max(jnp.abs(weight)) > 0.0, 0.0, 1.0)
    pattern = unit(jnp.sum(rows * weight, axis=0, keepdims=True))
    total = jnp.zeros((1, 1), F32)
    for block in blocks:
        along = jnp.sum(anomaly[block, :] * pattern, axis=1, keepdims=True)
        total = total + jnp.sum(along * along, axis=0, keepdims=True)
        direction_ref[block, :] = jnp.broadcast_to(along, (step, direction_ref.shape[1]))
    length = lax.rsqrt(jnp.maximum(total, 1e-30))
    taken = None
    for block in blocks:
        direction = direction_ref[block, :] * length
        direction_ref[block, :] = direction
        term = anomaly[block, :] * doubled(doubled(direction))
        taken = term if taken is None else taken + term
    taken = jnp.sum(taken, axis=0, keepdims=True)
    own_part[...] = jnp.broadcast_to(taken[:, width:], (own_part.shape[1], width)).T

    for block in blocks:
        rest = anomaly[block, :] - doubled(doubled(direction_ref[block, :])) * taken
        high, low = pieces(rest, 2)
        high_ref[block, :] = high
        low_ref[block, :] = low
        own = rest[:, width:].T
        own_high[:, block], own_low[:, block] = pieces(own, 2)
    seen_ref[pl.ds(0, 1), :] = at_cells(jnp.concatenate(means, axis=1), chosen)
    seen_ref[pl.ds(1, 1), :] = at_cells(taken, chosen)
    for first in range(0, members, PART):
        rows = pl.ds(first, PART)
        spread = (dot(high_ref[rows, :], chosen) + dot(low_ref[rows, :], chosen)) * scale
        high, low = pieces(spread, 2)
        spread_high[rows, :] = high
        spread_low[rows, :] = low


def square(parts):
    half = parts[0].shape[0] // 2
    upper = product([part[:half] for part in parts], parts)
    lower = product([part[half:] for part in parts], [part[:, half:] for part in parts])
    return upper, jnp.concatenate([upper[:, half:].T, lower], axis=1)


def at_border(info):
    chip, core, _, chips = info
    ends = jnp.logical_or(jnp.logical_and(chip == 0, core == 0), jnp.logical_and(chip == chips - 1, core == 1))
    return jnp.where(ends, 0, 1)


def shifted_spread(rows, blocks, direction_ref, shift, along, chosen, scale, high_in, low_in, high_out, low_out):
    total, taken = None, None
    step = rows[0].shape[0]
    for index, (row, block) in enumerate(zip(rows, blocks)):
        here = pl.ds(index * step, step)
        direction = doubled(direction_ref[block, :])
        rest = row[...] - shift - direction * along
        total = rest if total is None else total + rest
        taken = direction * rest if taken is None else taken + direction * rest
        high, low = pieces(rest, 2)
        high, low = pieces((dot(high, chosen) + dot(low, chosen)) * scale, 2)
        high_out[here, :] = high + high_in[block, :]
        low_out[here, :] = low + low_in[block, :]
    return jnp.sum(total, axis=0, keepdims=True), jnp.sum(taken, axis=0, keepdims=True)


def gram(high, low):
    turned = high.T
    cross = dot(turned, low)
    return dot(turned, high) + (cross + cross.T)


def middle_kernel(
    info, observed_ref, high_in, low_in, own_high, own_low, direction_ref, half_ref,
    high_ref, low_ref, gram_ref, right_ref, known_ref,
):
    chips = info[3]
    count, slots = high_ref.shape
    step = count // chips
    width = half_ref.shape[1]
    first = at_border(info) * count
    cells, _, _, scale = observations(info, observed_ref, width, math.sqrt(2 * count - 1))
    chosen = one_hot(cells, 0, width)
    rows = [half_ref.at[pl.ds(chip * step, step), :] for chip in range(chips)]
    blocks = [pl.ds(pl.multiple_of(first + chip * step, step), step) for chip in range(chips)]
    mean = mean_of([row[...] for row in rows], count)
    along, weight = None, None
    for row, block in zip(rows, blocks):
        direction = direction_ref[block, :]
        term = (row[...] - mean) * doubled(direction)
        along = term if along is None else along + term
        weight = direction * direction if weight is None else weight + direction * direction
    weight = doubled(jnp.sum(weight, axis=0, keepdims=True))
    along = jnp.sum(along, axis=0, keepdims=True) / jnp.maximum(weight, 0.1)
    total, taken = shifted_spread(
        rows, blocks, direction_ref, mean, along, chosen, scale, high_in, low_in, high_ref, low_ref
    )
    for index, known in enumerate((mean, along, total, taken)):
        known_ref[pl.ds(index, 1), :] = known
    high, low = high_ref[...], low_ref[...]
    gram_ref[...] = gram(high, low)
    members = pl.ds(pl.multiple_of(first, count), count)
    right_ref[...] = product([own_high[:, members], own_low[:, members]], [high, low])


def analysed_row(info, x, near_own, far_own, direction_ref, halves, rests, parts, sides):
    chips, step, _ = far_own.shape
    chip, mine = info[0] ^ (x // 2), x % 2
    rows = pl.ds(pl.multiple_of(chip * step, step), step)
    spread = [
        jnp.where(at_border(info) == mine, half[rows, :], rest[rows, :]) for half, rest in zip(halves, rests)
    ]
    block = pl.ds(pl.multiple_of((mine * chips + chip) * step, step), step)
    own = far_own[chip] if mine else near_own[rows, :]
    return own + sides[0:1] + product(spread, parts) + doubled(direction_ref[block, :]) * sides[1:2]


def others_kernel(
    order, info, near_own, far_own, direction_ref, high_half, low_half, high_rest, low_rest,
    solved_high, solved_low, sides_ref, *out_refs,
):
    parts = [solved_high[...], solved_low[...]]
    for x, out_ref in zip(order, out_refs):
        out_ref[...] = analysed_row(
            info, x, near_own, far_own, direction_ref, (high_half, low_half), (high_rest, low_rest), parts, sides_ref[...]
        )


def region_kernel(
    order, info, observed_ref, near_own, far_own, high_in, low_in, own_high, own_low, own_part, seen_ref,
    direction_ref, high_half, low_half, gram_half, right_half, known_ref, rest_ref, *refs,
):
    chips, step, width = far_own.shape
    high_rest, low_rest, solved_high, solved_low, sides_ref = refs[:5]
    out_refs, (factor, squared, answer) = refs[5:-3], refs[-3:]
    count = chips * step
    members = 2 * count
    slots = observed_ref.shape[1]
    root = math.sqrt(members - 1)
    part = at_border(info)
    first = (1 - part) * count
    cells, slot_weight, values, scale = observations(info, observed_ref, width, root)
    chosen = one_hot(cells, 0, width)
    shift, along, total, taken = (known_ref[pl.ds(index, 1), :] for index in range(4))
    more, further = shifted_spread(
        [rest_ref.at[chip] for chip in range(chips)],
        [pl.ds(pl.multiple_of(first + chip * step, step), step) for chip in range(chips)],
        direction_ref, shift, along, chosen, scale, high_in, low_in, high_rest, low_rest,
    )
    left = (total + more) * (1.0 / members)
    taken = taken + further
    seen_mean = seen_ref[pl.ds(0, 1), :] + at_cells(shift + left, chosen)
    left, taken_here = at_cells(left, chosen) * scale, at_cells(taken, chosen) * scale
    common = (seen_ref[pl.ds(1, 1), :] + at_cells(along + taken, chosen)) * scale
    innovation = slot_weight * (values - seen_mean)
    place = lax.broadcasted_iota(jnp.int32, (8, slots), 0)
    excess = jnp.where(place == 0, left * math.sqrt(members), jnp.where(place == 1, taken_here, 0.0))
    excess = pieces(excess, 2)

    eye = lax.broadcasted_iota(jnp.int32, (slots, slots), 0) == lax.broadcasted_iota(
        jnp.int32, (slots, slots), 1
    )
    high, low = high_rest[...], low_rest[...]
    over = dot_t(excess[0], excess[0]) + (dot_t(excess[0], excess[1]) + dot_t(excess[1], excess[0]))
    factor[...] = gram(high, low) + (gram_half[...] - over) + jnp.where(eye, 1.0, 0.0)
    rows = pl.ds(pl.multiple_of(first, count), count)
    answer[pl.ds(0, width), :] = right_half[...] + product([own_high[:, rows], own_low[:, rows]], [high, low])
    answer[pl.ds(width, 8), :] = jnp.where(
        lax.broadcasted_iota(jnp.int32, (8, slots), 0) == 0, jnp.broadcast_to(common, (8, slots)), 0.0
    )
    half = slots // 2
    upper, lower = pl.ds(0, half), pl.ds(half, half)

    def after(bound):
        return bound * bound / (2.0 - bound * bound)

    def size(matrix):
        return jnp.sum(jnp.sum(matrix * matrix, axis=0, keepdims=True))

    def begin(parts, count):
        if count > 2:
            squared[upper, :], squared[lower, :] = square(parts)
        bound = 1.0 - start
        gain = 2.0 / (2.0 - bound * bound)
        answer[...] = (gain * start) * (2.0 * answer[...] - start * product(pieces(answer[...], count), parts))
        factor[...] = (gain * start) * (2.0 * factor[...] - start * squared[...])
        return after(bound)

    def refine(bound, count):
        gain = 2.0 / (2.0 - bound * bound)
        parts = pieces(factor[...], count)
        answer[...] = gain * (2.0 * answer[...] - product(pieces(answer[...], count), parts))
        top, bottom = square(parts)
        factor[upper, :] = gain * (2.0 * factor[upper, :] - top)
        factor[lower, :] = gain * (2.0 * factor[lower, :] - bottom)
        return after(bound)

    def close(bound, rest):
        gain = 2.0 / (2.0 - bound * bound)
        answer[...] = gain * (answer[...] + dot(answer[...].astype(BF16), rest))
        return gain

    def finish(bound):
        rest = factor[...].astype(BF16)
        gain = close(bound, rest)
        factor[...] = gain * (dot(rest, rest) - jnp.where(eye, 0.5 * bound * bound, 0.0))
        return after(bound)

    parts = pieces(factor[...], 2)
    top, bottom = square(parts)
    squared[upper, :] = top
    squared[lower, :] = bottom
    limit = 1.0001 * jnp.sqrt(jnp.sqrt(size(top) + size(bottom)))
    start = 2.0 / (1.0 + limit)
    large = limit > LARGE
    bound = lax.cond(large, lambda: begin(pieces(factor[...], 3), 3), lambda: begin(parts, 2))
    bound = lax.while_loop(lambda b: jnp.logical_and(b > COARSE, large), lambda b: refine(b, 3), bound)
    bound = lax.while_loop(lambda b: b > COARSE, lambda b: refine(b, 2), bound)
    factor[...] = jnp.where(eye, 1.0, 0.0) - factor[...]
    bound = lax.while_loop(lambda b: b > DONE, finish, bound)
    close(bound, factor[...].astype(BF16))

    solved = answer[pl.ds(0, width), :]
    alone = answer[pl.ds(width, 1), :]
    share = own_part[:, :1] - jnp.sum(solved * common, axis=1, keepdims=True)
    solved = solved + (share / (1.0 + jnp.sum(common * alone, axis=1, keepdims=True))) * alone
    solved = solved.T
    which = lax.broadcasted_iota(jnp.int32, (8, slots), 0)
    sides = jnp.where(
        which == 0, innovation * (1.0 / root) + 0.5 * left, jnp.where(which == 1, 0.5 * (taken_here - common), 0.0)
    )
    parts = pieces(solved, 2)
    sides = product(pieces(sides, 2), parts)
    parts = [part * jnp.asarray(-0.5, BF16) for part in parts]
    sides_ref[...] = sides
    solved_high[...], solved_low[...] = parts
    for x, out_ref in zip(order, out_refs):
        out_ref[...] = analysed_row(
            info, x, near_own, far_own, direction_ref, (high_half, low_half), (high_rest, low_rest), parts, sides
        )


VMEM = pl.BlockSpec(memory_space=pltpu.VMEM)


def position():
    lane, patch = lax.axis_index("member"), lax.axis_index("patch")
    return lax.div(lane, 2), lax.rem(lane, 2), lax.rem(patch, 2), lax.axis_size("member") // 2


def call(kernel, name, out_shape, args, scratch=(), flops=None, limit=8, out=VMEM):
    several = isinstance(out_shape, (list, tuple))
    return pl.pallas_call(
        lambda *refs: kernel(position(), *refs),
        out_shape=out_shape,
        in_specs=[VMEM] * len(args),
        out_specs=[out] * len(out_shape) if several else out,
        scratch_shapes=scratch,
        compiler_params=pltpu.CompilerParams(vmem_limit_bytes=limit * 1024 * 1024),
        cost_estimate=flops and pl.CostEstimate(flops=flops, bytes_accessed=0, transcendentals=0),
        name=name,
    )(*args)


def bfloat(*shape):
    return jax.ShapeDtypeStruct(shape, BF16)


def array(*shape):
    return jax.ShapeDtypeStruct(shape, F32)


def per_device(
    init_field, flow_fields, emission, observed_cell, observed_count, observed_value, observed_scale
):
    step, rows, width = init_field.shape
    slots = observed_cell.shape[1]
    patches, lanes = lax.axis_size("patch"), lax.axis_size("member")
    chips = lanes // 2
    members = lanes * step
    axes = ("patch", "member")
    count = patches * lanes

    edge = array(STEPS * step + 8, width)
    to_last, to_first = call(pack_kernel, "pack", [edge, edge], [init_field, flow_fields], limit=32)

    def swap(message, start):
        lower = range(start, patches - 1, 2)
        return lax.ppermute(message, "patch", [(p, p + 1) for p in lower] + [(p + 1, p) for p in lower])

    halo_last, halo_first = swap(to_last, 0), swap(to_first, 1)

    mine = jnp.concatenate(
        [
            observed_cell.astype(F32),
            observed_value,
            observed_scale,
            jnp.broadcast_to(observed_count.astype(F32)[:, None], observed_cell.shape),
        ]
        * 2,
        axis=0,
    )

    def between(message, hops):
        return lax.ppermute(message, "member", [(2 * a + core, 2 * b + core) for a, b in hops for core in range(2)])

    mirrored = [
        [hop for to in range(1, chips // 2) for hop in (((to + s) % chips, to), (chips - 1 - (to + s) % chips, chips - 1 - to))]
        for s in range(chips)
    ]
    turning = [[((to - s) % chips, to) for to in range(1, chips - 1)] for s in range(chips)]
    single = all(len({source for source, _ in hops}) == len(hops) for hops in mirrored)
    targets = mirrored if single else turning
    pair = array(2, step, width)
    kept, emitted, *inner = call(
        functools.partial(inner_kernel, targets), "inner",
        [array(4, step, width), array(step, width // 2)] + [pair] * chips,
        [init_field, flow_fields, emission[None, :]],
        [pltpu.VMEM((rows, step, width), F32), pltpu.VMEM((rows, 8, width), F32)], limit=32,
    )
    got_inner = [inner[0]] + [between(inner[s], targets[s]) for s in range(1, chips)]
    outer = call(
        edge_kernel, "edge", [pair] * chips, [init_field, flow_fields, emitted, kept, halo_last, halo_first],
        [pltpu.VMEM((2, step, width), F32)], limit=32,
    )
    got_outer = [outer[0]] + [
        between(outer[s], [(s, 0), (chips - 1 - s, chips - 1)]) for s in range(1, chips)
    ]
    turns = [0, chips - 1, *range(1, chips - 1)]
    order = [(targets[s], k) for k, s in enumerate(turns)]
    pieces_in = [got_inner[s] for s in turns] + got_outer
    mine, _ = lax.optimization_barrier((mine, outer[0]))
    other = lax.ppermute(
        mine, axes,
        [(p * lanes + i, p * lanes + lanes - 1 - i) for p in range(1, patches, 2) for i in range(lanes)],
    )

    def device(p, chip, core):
        return p * lanes + 2 * chip + core

    borders, siblings = [], []
    for p in range(patches):
        for chip in range(chips):
            for core, away in ((0, -1), (1, 1)):
                siblings.append((device(p, chip, core), device(p, chip, 1 - core)))
                if 0 <= chip + away < chips:
                    borders.append((device(p, chip, core), device(p, chip + away, 1 - core)))
                else:
                    to = p + 1 if (p % 2 == 0) == (away == 1) else p - 1
                    if 0 <= to < patches:
                        borders.append((device(p, chip, core), device(to, chip, core)))

    half = array(chips, step, width)
    near_other, near_own, observed = call(
        functools.partial(collect_kernel, order), "collect",
        [half, array(chips * step + PADDING, width), array(8, slots)], [mine, other] + pieces_in,
    )
    far_own = lax.ppermute(near_other, axes, siblings)
    got_half = lax.ppermute(near_own, axes, borders)
    far_other = lax.ppermute(near_own, axes, siblings)
    got_rest = lax.ppermute(far_own, axes, borders)

    prepared = call(
        prepare_kernel, "prepare",
        [bfloat(members, slots)] * 2 + [bfloat(width, members)] * 2
        + [array(width, width // 2), array(8, slots), array(members, width // 2)],
        [observed, near_other, near_own, far_other, far_own],
        [pltpu.VMEM((members, 2 * width), F32)] + [pltpu.VMEM((members, 2 * width), BF16)] * 2,
        flops=8 * members * slots * width, limit=20,
    )
    halves = members // 2
    middle = call(
        middle_kernel, "middle",
        [bfloat(halves, slots)] * 2 + [array(slots, slots), array(width, slots), array(8, width)],
        [observed, *prepared[:4], prepared[6], got_half],
        flops=10 * halves * slots * slots, limit=20,
    )
    order = sorted(range(lanes), key=lambda x: (-x.bit_length(), x))
    row = array(step, width)
    *shared, first, second = call(
        functools.partial(region_kernel, order[:2]), "region",
        [bfloat(halves, slots)] * 2 + [bfloat(slots, width)] * 2 + [array(8, width)] + [row] * 2,
        [observed, near_own, far_own, *prepared, *middle, got_rest],
        [pltpu.VMEM((slots, slots), F32)] * 2 + [pltpu.VMEM((width + 8, slots), F32)],
        limit=24,
    )
    others = call(
        functools.partial(others_kernel, order[2:]), "others", [row] * (lanes - 2),
        [near_own, far_own, prepared[6], *middle[:2], *shared],
        flops=6 * members * slots * width, limit=16,
    )
    analysed = dict(zip(order, [first, second, *others]))

    def swapped(x):
        return lax.ppermute(analysed[x], "member", [(i, i ^ x) for i in range(lanes)]) if x else analysed[0]

    return call(
        functools.partial(unpack_kernel, order), "unpack", array(step, rows, width),
        [swapped(x) for x in order], [pltpu.VMEM((step, rows, width), F32), pltpu.SemaphoreType.DMA((4,))],
        limit=48, out=pl.BlockSpec(memory_space=pltpu.HBM),
    )


def solution(mesh):
    return jax.shard_map(
        per_device,
        mesh=mesh,
        in_specs=(
            P("member", "patch", None),
            P(None, "patch", None),
            P("member"),
            P(("patch", "member"), None),
            P(("patch", "member")),
            P(("patch", "member"), None),
            P(("patch", "member"), None),
        ),
        out_specs=P("member", "patch", None),
        check_vma=False,
    )
```
